32 devices in a mesh: row: 8 (over y, x, core), col: 4 (over z).
Axes of the slice: x: 2, y: 2, z: 4, core: 2. Of those that a mesh axis runs over, the one named last changes fastest.
Arguments:
- tokens: bfloat16 [8192, 2048], P(('row', 'col')), may hold values from -6 to 6
- seq_lens: int32 [8, 3], P('row'), may hold values from 1 to 512, 1024 in all within a row
- attn_gain: bfloat16 [2048], replicated, may hold values from 0.099609375 to 1.8984375
- query_weight: bfloat16 [2048, 2048], P('row', 'col'), may hold values from -0.125 to 0.125
- keyvalue_weight: bfloat16 [2048, 8, 128], P('row', 'col'), may hold values from -0.125 to 0.125
- output_weight: bfloat16 [2048, 2048], P('row', 'col'), may hold values from -0.5 to 0.5
- mlp_gain: bfloat16 [2048], replicated, may hold values from 0.099609375 to 1.8984375
- hidden_weight: bfloat16 [2048, 2, 8192], P('row', None, 'col'), may hold values from -0.125 to 0.125
- down_weight: bfloat16 [2048, 8192], P('row', 'col'), may hold values from -0.09375 to 0.09375
- out_grad: bfloat16 [8192, 2048], P(('row', 'col')), may hold values from -6 to 6
Outputs:
- block_out: bfloat16 [8192, 2048], P(('row', 'col'))
- grad_tokens: bfloat16 [8192, 2048], P(('row', 'col'))
- grad_attn_gain: float32 [2048], replicated
- grad_query: float32 [2048, 2048], P('row', 'col')
- grad_keyvalue: float32 [2048, 8, 128], P('row', 'col')
- grad_output: float32 [2048, 2048], P('row', 'col')
- grad_mlp_gain: float32 [2048], replicated
- grad_hidden: float32 [2048, 2, 8192], P('row', None, 'col')
- grad_down: float32 [2048, 8192], P('row', 'col')
The draws below stay inside these ranges and needn't reach their ends.
Inputs may be any that keep to these rules, and one draw needn't show every extreme that they name: Each row of seq_lens belongs to one block of 1024 tokens, sums to 1024, and its largest entry is 512.
All inputs are finite; a program needn't handle non-finite values.
Results may differ from the reference program's by a relative error of at most 0.023.
Values may be sent and summed in bfloat16 or wider, within the bound.
A program may use at most 256 MiB of HBM per device.

```python
import math
import jax
import jax.numpy as jnp
import numpy as np
from jax import lax

D = 2048
H = 32
KV = 8
HD = 64
FF = 8192
TOK_ROW = 1024
SEQS = 3
SEQ_MAX = 512
TOKENS = 8192
N_ROW = 8


def steps_of(own_key, shape, split, low, top_value):
    loudness, own = 1.0, jax.random.fold_in(own_key, 6)
    for axis_at, blocks in split:
        heights = jnp.exp(jax.random.uniform(jax.random.fold_in(own, axis_at), (blocks,), jnp.float32, low / len(split), top_value / len(split)))
        loudness = loudness * jnp.repeat(heights, shape[axis_at] // blocks).reshape([-1 if axis == axis_at else 1 for axis in range(len(shape))])
    return loudness


def profile(count, total, reach, slope):
    loads = [(1 << 20) // math.isqrt(rank ** slope) + 1 for rank in range(2, count + 1)]
    rest, given = total - reach - (count - 1), [1] * (count - 1)
    while rest > 0:
        movable = [i for i in range(count - 1) if given[i] < reach]
        pool, left = sum([loads[i] for i in movable]), rest
        for i in movable:
            extra = min(reach - given[i], max(1, left * loads[i] // pool), rest)
            given[i] = given[i] + extra
            rest = rest - extra
    return np.array([reach] + given)


def uneven_parts(stream_key, number_of, total, bound, slope):
    if number_of == 2:
        one = jax.random.randint(stream_key, (), max(1, total - bound), min(bound, total - 1) + 1)
        return jnp.stack([one, total - one])
    lengths = jnp.asarray(profile(number_of, total, bound, slope), jnp.int32)
    twos = (number_of - 1) // 2
    donor, receiver = lengths[1:1 + 2 * twos:2], lengths[2:2 + 2 * twos:2]
    margin = jnp.minimum(donor - 1, bound - receiver)
    shifted = jax.random.randint(jax.random.fold_in(stream_key, 1), (twos,), 0, 1 << 20) % (margin + 1)
    lengths = lengths.at[1:1 + 2 * twos:2].set(donor - shifted).at[2:2 + 2 * twos:2].set(receiver + shifted)
    return lengths[jax.random.permutation(jax.random.fold_in(stream_key, 2), number_of)]


def gaussian(rng, shape, spread, most, shards=(), kind=jnp.bfloat16):
    factor_of = steps_of(rng, shape, shards, -0.22, 0.18) if shards else 1.0
    values = jax.random.normal(rng, shape, jnp.float32) * spread * factor_of
    return jnp.minimum(jnp.maximum(values, -most), most).astype(kind)


def setup_inputs(seed: int = 0) -> dict:
    seeds = jax.random.split(jax.random.key(seed), 11)
    return {
        "tokens": gaussian(seeds[0], (TOKENS, D), 1.0, 6.0, ((0, 32),)),
        "seq_lens": jax.vmap(lambda own: uneven_parts(own, SEQS, TOK_ROW, SEQ_MAX, 2))(jax.random.split(seeds[1], N_ROW)).reshape((N_ROW, SEQS)).astype(jnp.int32),
        "attn_gain": jnp.clip(1.0 + 0.18 * jax.random.normal(seeds[2], (D,), jnp.float32), 0.099609375, 1.8984375).astype(jnp.bfloat16),
        "query_weight": gaussian(seeds[3], (D, H * HD), D ** -0.5, 0.125, ((0, 8), (1, 4))),
        "keyvalue_weight": gaussian(seeds[4], (D, KV, 2 * HD), D ** -0.5, 0.125, ((0, 8), (1, 4))),
        "output_weight": gaussian(seeds[5], (D, H * HD), (H * HD // 16) ** -0.5, 0.5, ((0, 8), (1, 4))),
        "mlp_gain": jnp.clip(1.0 + 0.18 * jax.random.normal(seeds[6], (D,), jnp.float32), 0.099609375, 1.8984375).astype(jnp.bfloat16),
        "hidden_weight": gaussian(seeds[7], (D, 2, FF), D ** -0.5, 0.125, ((0, 8), (2, 4))),
        "down_weight": gaussian(seeds[8], (D, FF), (FF // 2) ** -0.5, 0.09375, ((0, 8), (1, 4))),
        "out_grad": gaussian(seeds[9], (TOKENS, D), 1.0, 6.0, ((0, 32),)),
    }


highest = lax.Precision.HIGHEST
epsilon = 1e-05
rope_base = 500000.0

@jax.custom_vjp
def low(v):
    return lax.optimization_barrier(v.astype(jnp.bfloat16)).astype(jnp.float32)

@jax.custom_vjp
def low_back(v):
    return v

def low_keep(v):
    return (low(v), None)

def low_pass(kept, grad):
    return (grad,)

def back_keep(v):
    return (v, None)

def back_low(kept, grad):
    return (low(grad),)
low.defvjp(low_keep, low_pass)
low_back.defvjp(back_keep, back_low)

def rope_tables(position):
    indices = jnp.arange(HD // 2, dtype=jnp.float32)
    frequency = rope_base ** (-(indices * 2.0 / HD))
    wavelen = 2.0 * jnp.pi / frequency
    smooth = (8192.0 / wavelen - 1.0) / 3.0
    scaled = jnp.where(wavelen > 8192.0, frequency / 32.0, (1.0 - smooth) * frequency / 32.0 + smooth * frequency)
    frequency = jnp.where(wavelen < 2048.0, frequency, scaled)
    angles = position.astype(jnp.float32)[:, None] * frequency[None, :]
    return (jnp.cos(angles), jnp.sin(angles))

def rotate(values, cosine, sinusoid):
    halfway = values.shape[-1] // 2
    former = values[..., :halfway]
    latter = values[..., halfway:]
    cos_wide = cosine[:, None, :]
    sin_wide = sinusoid[:, None, :]
    return jnp.concatenate([former * cos_wide - latter * sin_wide, latter * cos_wide + former * sin_wide], axis=-1)

def normed(values, gain):
    scale = lax.rsqrt(lax.optimization_barrier(jnp.mean(values * values, axis=-1, keepdims=True)) + epsilon)
    return values * scale * gain

def sequence_marks(seq_lens):
    finish = jnp.cumsum(seq_lens, axis=1)
    indices = jnp.arange(TOK_ROW, dtype=jnp.int32)
    passed = indices[None, :, None] >= finish[:, None, :]
    segment = lax.optimization_barrier(jnp.sum(passed.astype(jnp.int32), axis=2, dtype=jnp.int32))
    position = indices[None, :] - lax.optimization_barrier(jnp.sum(jnp.where(passed, seq_lens[:, None, :], 0), axis=2, dtype=jnp.int32))
    return (segment, position)

def attend_rows(queries, key_rows, values, segment):
    indices = jnp.arange(TOK_ROW, dtype=jnp.int32)
    allowed = (segment[:, None] == segment[None, :]) & (indices[None, :] <= indices[:, None])
    factor = HD ** (-0.5)

    def one_head(bundle):
        head_query, head_key, head_value = bundle
        scores = low_back(jnp.einsum('qgd,sd->gqs', head_query, head_key, precision=highest) * factor)
        scores = jnp.where(allowed[None], scores, -1e+30)
        summit = lax.optimization_barrier(jnp.max(scores, axis=-1, keepdims=True))
        weights = jnp.exp(scores - summit)
        chances = low(weights / lax.optimization_barrier(jnp.sum(weights, axis=-1, keepdims=True)))
        return jnp.einsum('gqs,sd->qgd', chances, head_value, precision=highest)
    mixed_heads = lax.map(jax.checkpoint(one_head), (jnp.transpose(queries, (1, 0, 2, 3)), jnp.transpose(key_rows, (1, 0, 2)), jnp.transpose(values, (1, 0, 2))))
    return jnp.transpose(mixed_heads, (1, 0, 2, 3))

def block_forward(rows_in, segment, cosine, sinusoid, attn_gain, query_weight, keyvalue_weight, output_weight, mlp_gain, hidden_weight, down_weight):
    group_size = H // KV
    normal_in = low(normed(rows_in, attn_gain))
    queries = low_back(jnp.dot(normal_in, query_weight, precision=highest)).reshape(TOK_ROW, H, HD)
    keyvals = low_back(jnp.dot(normal_in, keyvalue_weight.reshape(D, KV * 2 * HD), precision=highest)).reshape(TOK_ROW, KV, 2, HD)
    queries = low(rotate(queries, cosine, sinusoid)).reshape(TOK_ROW, KV, group_size, HD)
    key_rows = low(rotate(keyvals[:, :, 0], cosine, sinusoid))
    values = low(keyvals[:, :, 1])
    mixed_heads = attend_rows(queries, key_rows, values, segment)
    mixed_heads = low_back(low(mixed_heads.reshape(TOK_ROW, H * HD)))
    attended = low_back(jnp.dot(mixed_heads, output_weight.T, precision=highest))
    hidden_in = rows_in + attended
    normal_mid = low(normed(hidden_in, mlp_gain))
    gate_up = low_back(jnp.dot(normal_mid, hidden_weight.reshape(D, 2 * FF), precision=highest))
    gated_act = low(jax.nn.silu(gate_up[:, :FF]) * gate_up[:, FF:])
    return hidden_in + low_back(jnp.dot(gated_act, down_weight.T, precision=highest))

def reference(tokens, seq_lens, attn_gain, query_weight, keyvalue_weight, output_weight, mlp_gain, hidden_weight, down_weight, out_grad):
    segment, position = sequence_marks(seq_lens)
    cosine, sinusoid = rope_tables(position.reshape(TOKENS))
    cosine = cosine.reshape(N_ROW, TOK_ROW, HD // 2)
    sinusoid = sinusoid.reshape(N_ROW, TOK_ROW, HD // 2)
    primals = tuple((member.astype(jnp.float32) for member in (tokens, attn_gain, query_weight, keyvalue_weight, output_weight, mlp_gain, hidden_weight, down_weight)))

    def whole(token_block, gain_a, weight_q, weight_kv, weight_o, gain_m, weight_h, weight_d):

        def one_block(bundle):
            rows_in, seg_row, cos_row, sin_row = bundle
            return block_forward(rows_in, seg_row, cos_row, sin_row, gain_a, weight_q, weight_kv, weight_o, gain_m, weight_h, weight_d)
        stacked = lax.map(jax.checkpoint(one_block), (token_block.reshape(N_ROW, TOK_ROW, D), segment, cosine, sinusoid))
        return stacked.reshape(TOKENS, D)
    result, pullback = jax.vjp(whole, primals[0], primals[1], primals[2], primals[3], primals[4], primals[5], primals[6], primals[7])
    grads = pullback(out_grad.astype(jnp.float32))
    return (result.astype(jnp.bfloat16), grads[0].astype(jnp.bfloat16), grads[1], grads[2], grads[3], grads[4], grads[5], grads[6], grads[7])
```

```python
import functools

import jax
import jax.numpy as jnp
from jax import lax
from jax.experimental import pallas as pl
from jax.experimental.pallas import tpu as pltpu
from jax.sharding import PartitionSpec as P

HD = 64
SEQ_MAX = 512
MESH = pl.DeviceIdType.MESH
ANY = pl.BlockSpec(memory_space=pl.ANY)

epsilon = 1e-05
rope_base = 500000.0
blocked = -1e30
bf16 = jnp.bfloat16
f32 = jnp.float32


def plane_sizes(row_count):
    cores = 2 if row_count % 2 == 0 else 1
    chips = row_count // cores
    first = 2 if chips % 2 == 0 else 1
    return first, chips // first, cores


class Place:
    def __init__(self, row_count, col_count):
        self.rows, self.cols = row_count, col_count
        self.sizes = plane_sizes(row_count)
        na, nb, nk = self.sizes
        self.row = lax.axis_index("row")
        self.col = lax.axis_index("col")
        self.at = (self.row // (nb * nk), (self.row // nk) % nb, self.row % nk)

    def row_of(self, at):
        _, nb, nk = self.sizes
        return (at[0] * nb + at[1]) * nk + at[2]

    def chip_of(self, at):
        return at[0] * self.sizes[1] + at[1]

    def moved(self, axis, step, at=None):
        at = list(self.at if at is None else at)
        size = self.sizes[axis]
        at[axis] = lax.rem(at[axis] + (step % size), size)
        return tuple(at)

    def device(self, axis, step):
        return (self.row_of(self.moved(axis, step)), self.col)

    def greet(self, plane, line):
        barrier = pltpu.get_barrier_semaphore()
        count = 0
        if plane:
            for axis in range(3):
                size = self.sizes[axis]
                for step in {1 % size, (size - 1) % size} - {0}:
                    pl.semaphore_signal(
                        barrier, inc=1, device_id=self.device(axis, step), device_id_type=MESH
                    )
                    count += 1
        if line and self.cols > 1:
            for step, there in self.line_ways():

                @pl.when(there)
                def _(step=step):
                    pl.semaphore_signal(
                        barrier, inc=1, device_id=(self.row, self.col + step), device_id_type=MESH
                    )

        if line and self.cols > 1:
            last = self.cols - 1
            count = count + jnp.minimum(self.col, 1) + jnp.minimum(last - self.col, 1)
        if not isinstance(count, int) or count:
            pl.semaphore_wait(barrier, count)

    def line_ways(self):
        return ((1, self.col < self.cols - 1), (-1, self.col > 0))


def when(condition, action):
    if condition is None:
        action()
    else:
        pl.when(condition)(action)


def remote(src, dst, send_sem, recv_sem, device):
    return pltpu.make_async_remote_copy(
        src_ref=src,
        dst_ref=dst,
        send_sem=send_sem,
        recv_sem=recv_sem,
        device_id=device,
        device_id_type=MESH,
    )


class LineGather:
    def __init__(self, place, own, block, send_sems, recv_sems):
        self.place, self.own, self.block = place, own, block
        self.sends, self.recvs = send_sems, recv_sems

    def copy(self, way, step, origin):
        place = self.place
        source = self.own if step == 1 else self.block(origin)
        return remote(
            source,
            self.block(origin),
            self.sends.at[way, step - 1],
            self.recvs.at[way, step - 1],
            (place.row, place.col + (1, -1)[way]),
        )

    def sends_at(self, way, step):
        col, last = self.place.col, self.place.cols - 1
        if way == 0:
            return (col >= step - 1) & (col < last), col - (step - 1)
        return (col + step - 1 <= last) & (col > 0), col + (step - 1)

    def gets_at(self, way, step):
        col, last = self.place.col, self.place.cols - 1
        if way == 0:
            return col >= step, col - step
        return col + step <= last, col + step

    def send(self, way, step):
        condition, origin = self.sends_at(way, step)
        when(condition, lambda: self.copy(way, step, origin).start())

    def receive(self, way, step):
        condition, origin = self.gets_at(way, step)

        def action():
            self.copy(way, step, origin).wait_recv()

        when(condition, action)
        if step < self.place.cols - 1:
            self.send(way, step + 1)

    def finish(self):
        for step in range(1, self.place.cols):
            for way in (0, 1):
                condition, origin = self.sends_at(way, step)
                when(condition, lambda: self.copy(way, step, origin).wait_send())


class PlaneGather:
    def __init__(self, place, block, send_sems, recv_sems):
        self.place, self.block = place, block
        self.sends, self.recvs = send_sems, recv_sems

    @staticmethod
    def sem_count(sizes):
        na, nb, _ = sizes
        return 2 * na * nb - 1

    def axes(self, half):
        return (1, 0) if half == 0 else (0, 1)

    def counts(self, half):
        first, second = self.axes(half)
        return self.place.sizes[first], self.place.sizes[second]

    def origin(self, half, i, j, core_step=0):
        first, second = self.axes(half)
        at = self.place.moved(first, -i)
        at = self.place.moved(second, -j, at)
        if core_step:
            at = self.place.moved(2, 1, at)
        return self.place.row_of(at)

    def copy(self, half, kind, i, j):
        np_, nq = self.counts(half)
        if kind == 0:
            number, device = i - 1, self.place.device(self.axes(half)[0], 1)
        elif kind == 1:
            number = (np_ - 1) + i * (nq - 1) + (j - 1)
            device = self.place.device(self.axes(half)[1], 1)
        else:
            number = (np_ * nq - 1) + i * nq + j
            device = self.place.device(2, 1)
        return number, device

    def sender(self, half, kind, i, j):
        number, device = self.copy(half, kind, i, j)
        oi, oj = (i - 1, j) if kind == 0 else ((i, j - 1) if kind == 1 else (i, j))
        ref = self.block(self.origin(half, oi, oj), half)
        return remote(ref, ref, self.sends.at[half, number], self.recvs.at[half, number], device)

    def receiver(self, half, kind, i, j):
        number, device = self.copy(half, kind, i, j)
        ref = self.block(self.origin(half, i, j, 1 if kind == 2 else 0), half)
        return remote(ref, ref, self.sends.at[half, number], self.recvs.at[half, number], device)

    def all_copies(self):
        for half in (0, 1):
            np_, nq = self.counts(half)
            for i in range(1, np_):
                yield half, 0, i, 0
            for i in range(np_):
                for j in range(1, nq):
                    yield half, 1, i, j
            if self.place.sizes[2] > 1:
                for i in range(np_):
                    for j in range(nq):
                        yield half, 2, i, j

    def share(self, half, i, j):
        if self.place.sizes[2] > 1:
            self.sender(half, 2, i, j).start()

    def first(self):
        for half in (0, 1):
            if self.counts(half)[0] > 1:
                self.sender(half, 0, 1, 0).start()
        for half in (0, 1):
            self.share(half, 0, 0)

    def second(self):
        for half in (0, 1):
            np_, nq = self.counts(half)
            for i in range(np_):
                if i > 0:
                    self.receiver(half, 0, i, 0).wait_recv()
                    if i < np_ - 1:
                        self.sender(half, 0, i + 1, 0).start()
                if nq > 1:
                    self.sender(half, 1, i, 1).start()
                if i > 0:
                    self.share(half, i, 0)

    def third(self):
        for half in (0, 1):
            np_, nq = self.counts(half)
            for j in range(1, nq):
                for i in range(np_):
                    self.receiver(half, 1, i, j).wait_recv()
                    if j < nq - 1:
                        self.sender(half, 1, i, j + 1).start()
                    self.share(half, i, j)

    def finish(self):
        for copy in self.all_copies():
            self.sender(*copy).wait_send()
            if copy[1] == 2:
                self.receiver(*copy).wait_recv()


def gather_kernel(sizes, count, *refs):
    row_count, col_count = sizes
    own = refs[:count]
    own_act = refs[count]
    full = refs[count + 1 : 2 * count + 1]
    full_act = refs[2 * count + 1]
    local_sems, zs, zr, ps, pr = refs[2 * count + 2 :]
    place = Place(row_count, col_count)
    place.greet(True, True)
    deep = own[0].shape[0]
    half_deep = deep // 2
    token_rows = own_act.shape[0]

    lines = [
        LineGather(
            place,
            own[n],
            lambda j, n=n: full[n].at[j, pl.ds(place.row * deep, deep)],
            zs.at[n],
            zr.at[n],
        )
        for n in range(count)
    ]
    acts = LineGather(
        place,
        own_act,
        lambda j: full_act.at[pl.ds(j * token_rows, token_rows)],
        zs.at[count],
        zr.at[count],
    )

    def keep(n):
        target = (
            full[n].at[place.col, pl.ds(place.row * deep, deep)]
            if n < count
            else full_act.at[pl.ds(place.col * token_rows, token_rows)]
        )
        return pltpu.make_async_copy(own[n] if n < count else own_act, target, local_sems.at[n])

    for n in range(count + 1):
        keep(n).start()
    for line in lines + [acts]:
        for way in (0, 1):
            line.send(way, 1)
    for n in range(count + 1):
        keep(n).wait()

    def inside(n, col):
        return PlaneGather(
            place,
            lambda row, half: full[n].at[
                col, pl.ds(row * deep + half * half_deep, half_deep)
            ],
            ps.at[n, col],
            pr.at[n, col],
        )

    slots = [(0, 0)] + [(way, step) for step in range(1, col_count) for way in (0, 1)]
    entries = [(way, step, n) for way, step in slots for n in range(count)]

    def at_entry(entry):
        way, step, n = entry
        if step == 0:
            return None, place.col
        return lines[n].gets_at(way, step)

    for number in range(len(entries) + 2):
        if number < len(entries):
            way, step, n = entries[number]
            condition, col = at_entry(entries[number])
            if step > 0:
                lines[n].receive(way, step)
            when(condition, lambda: inside(n, col).first())
        if 1 <= number <= len(entries):
            condition, col = at_entry(entries[number - 1])
            m = entries[number - 1][2]
            when(condition, lambda: inside(m, col).second())
        if 2 <= number:
            condition, col = at_entry(entries[number - 2])
            m = entries[number - 2][2]
            when(condition, lambda: inside(m, col).third())
        if number < len(entries):
            way, step, n = entries[number]
            if step > 1 and way == 1 and n == count - 1:
                for other in (0, 1):
                    acts.receive(other, step - 1)
    for other in (0, 1):
        acts.receive(other, col_count - 1)
    for entry in entries:
        condition, col = at_entry(entry)
        m = entry[2]
        when(condition, lambda: inside(m, col).finish())
    for line in lines + [acts]:
        line.finish()


def gather_all(weights, act, row_count, col_count):
    count = len(weights)
    sizes = plane_sizes(row_count)
    deep = weights[0].shape[0]
    steps = max(col_count - 1, 1)
    plane_sems = (count, col_count, 2, PlaneGather.sem_count(sizes))
    moved = sum(w.size for w in weights) * row_count * col_count * 2
    return pl.pallas_call(
        functools.partial(gather_kernel, (row_count, col_count), count),
        out_shape=[
            jax.ShapeDtypeStruct((col_count, row_count * deep, w.shape[1]), bf16) for w in weights
        ]
        + [jax.ShapeDtypeStruct((col_count * act.shape[0], act.shape[1]), bf16)],
        in_specs=[ANY] * (count + 1),
        out_specs=[ANY] * (count + 1),
        scratch_shapes=[
            pltpu.SemaphoreType.DMA((count + 1,)),
            pltpu.SemaphoreType.DMA((count + 1, 2, steps)),
            pltpu.SemaphoreType.DMA((count + 1, 2, steps)),
            pltpu.SemaphoreType.DMA(plane_sems),
            pltpu.SemaphoreType.DMA(plane_sems),
        ],
        compiler_params=pltpu.CompilerParams(collective_id=0, has_side_effects=True),
        cost_estimate=pl.CostEstimate(flops=0, bytes_accessed=moved, transcendentals=0),
        name="gather_weights",
    )(*weights, act)


def line_gather_kernel(sizes, own, full, local_sem, sends, recvs):
    place = Place(*sizes)
    place.greet(False, True)
    rows = own.shape[0]
    line = LineGather(place, own, lambda j: full.at[pl.ds(j * rows, rows)], sends, recvs)
    for way in (0, 1):
        line.send(way, 1)
    keep = pltpu.make_async_copy(own, full.at[pl.ds(place.col * rows, rows)], local_sem)
    keep.start()
    for step in range(1, place.cols):
        for way in (0, 1):
            line.receive(way, step)
    keep.wait()
    line.finish()


def line_gather(own, row_count, col_count, collective_id):
    steps = max(col_count - 1, 1)
    return pl.pallas_call(
        functools.partial(line_gather_kernel, (row_count, col_count)),
        out_shape=jax.ShapeDtypeStruct((col_count * own.shape[0], own.shape[1]), own.dtype),
        in_specs=[ANY],
        out_specs=ANY,
        scratch_shapes=[
            pltpu.SemaphoreType.DMA,
            pltpu.SemaphoreType.DMA((2, steps)),
            pltpu.SemaphoreType.DMA((2, steps)),
        ],
        compiler_params=pltpu.CompilerParams(collective_id=collective_id, has_side_effects=True),
        cost_estimate=pl.CostEstimate(
            flops=0, bytes_accessed=own.size * 2 * col_count, transcendentals=0
        ),
        name="gather_line",
    )(own)


def add_rows(target, source):
    rows = target.shape[0]
    piece = 32 if rows % 32 == 0 else 16

    def body(n, carry):
        at = pl.ds(pl.multiple_of(n * piece, piece), piece)
        target[at] = (target[at].astype(f32) + source[at].astype(f32)).astype(target.dtype)
        return carry

    lax.fori_loop(0, rows // piece, body, 0)


class LineSum:
    def __init__(self, place, own, held, send_sems, recv_sems):
        self.place, self.own, self.held = place, own, held
        self.sends, self.recvs = send_sems, recv_sems

    def target(self, way, distance):
        col, last = self.place.col, self.place.cols - 1
        if way == 0:
            return col + distance <= last, col + distance
        return col >= distance, col - distance

    def gets(self, way, distance):
        col, last = self.place.col, self.place.cols - 1
        there, _ = self.target(way, distance)
        return there & ((col > 0) if way == 0 else (col < last))

    def copy(self, way, distance, source):
        return remote(
            source,
            self.held.at[way, distance - 1],
            self.sends.at[way, distance - 1],
            self.recvs.at[way, distance - 1],
            (self.place.row, self.place.col + (1, -1)[way]),
        )

    def arrived(self, way, distance):
        ref = self.held.at[way, distance]
        return remote(
            ref,
            ref,
            self.sends.at[way, distance],
            self.recvs.at[way, distance],
            (self.place.row, self.place.col + (1, -1)[way]),
        )

    def step(self, way, distance):
        condition, col = self.target(way, distance)
        if distance < self.place.cols - 1:

            def add():
                self.arrived(way, distance).wait_recv()
                add_rows(self.own(col), self.held.at[way, distance])

            when(self.gets(way, distance), add)
        when(condition, lambda: self.copy(way, distance, self.own(col)).start())

    def last(self, out):
        if self.place.cols > 1:
            for way in (0, 1):
                when(self.gets(way, 0), lambda: self.arrived(way, 0).wait_recv())
        own = self.own(self.place.col)
        rows = own.shape[0]
        piece = 32 if rows % 32 == 0 else 16
        has = [self.gets(way, 0) for way in (0, 1)]

        def body(n, carry):
            at = pl.ds(pl.multiple_of(n * piece, piece), piece)
            total = own[at].astype(f32)
            if self.place.cols > 1:
                for way in (0, 1):
                    term = self.held[way, 0, at].astype(f32)
                    total = total + jnp.where(has[way], term, 0.0)
            out[at] = total.astype(out.dtype)
            return carry

        lax.fori_loop(0, rows // piece, body, 0)

    def finish(self):
        for distance in range(1, self.place.cols):
            for way in (0, 1):
                condition, col = self.target(way, distance)
                when(condition, lambda: self.copy(way, distance, self.own(col)).wait_send())


def line_sum_kernel(sizes, terms, out, held, sends, recvs):
    place = Place(*sizes)
    place.greet(False, True)
    rows = out.shape[0]
    line = LineSum(
        place, lambda j: terms.at[pl.ds(pl.multiple_of(j * rows, rows), rows)], held, sends, recvs
    )
    for distance in range(place.cols - 1, 0, -1):
        for way in (0, 1):
            line.step(way, distance)
    line.last(out)
    line.finish()


def line_sum(terms, row_count, col_count, collective_id):
    steps = max(col_count - 1, 1)
    rows, width = terms.shape[0] // col_count, terms.shape[1]
    return pl.pallas_call(
        functools.partial(line_sum_kernel, (row_count, col_count)),
        out_shape=jax.ShapeDtypeStruct((rows, width), f32),
        in_specs=[pl.BlockSpec(memory_space=pltpu.VMEM)],
        out_specs=pl.BlockSpec(memory_space=pltpu.VMEM),
        scratch_shapes=[
            pltpu.VMEM((2, steps, rows, width), bf16),
            pltpu.SemaphoreType.DMA((2, steps)),
            pltpu.SemaphoreType.DMA((2, steps)),
        ],
        compiler_params=pltpu.CompilerParams(
            collective_id=collective_id, has_side_effects=True, vmem_limit_bytes=48 << 20
        ),
        cost_estimate=pl.CostEstimate(
            flops=terms.size, bytes_accessed=terms.size * 2, transcendentals=0
        ),
        name="sum_line",
    )(terms)


class PlaneSum:
    def __init__(self, place, acc, held_core, held_second, held_first, sems):
        self.place, self.acc = place, acc
        self.held = (held_first, held_second, held_core)
        self.sends, self.recvs = sems
        self.half_deep = acc.shape[1] // 2

    @staticmethod
    def counts_of(sizes):
        na, nb, _ = sizes
        return max(na, nb) - 1, max((na - 1) * nb, (nb - 1) * na)

    @staticmethod
    def sem_count(sizes):
        na, nb, _ = sizes
        return na * nb - 1

    def axes(self, half):
        return (1, 0) if half == 0 else (0, 1)

    def counts(self, half):
        first, second = self.axes(half)
        return self.place.sizes[first], self.place.sizes[second]

    def part(self, half, i, j):
        first, second = self.axes(half)
        at = self.place.moved(second, j, self.place.moved(first, i))
        return self.acc.at[
            self.place.chip_of(at), pl.ds(half * self.half_deep, self.half_deep)
        ]

    def copy(self, half, kind, step, i):
        np_, nq = self.counts(half)
        if kind == 1:
            number = (step - 1) * np_ + i
            source = self.part(half, i, nq - step)
            target = self.held[1].at[half, number]
            sem = number
        else:
            source = self.part(half, np_ - step, 0)
            target = self.held[0].at[half, step - 1]
            sem = (nq - 1) * np_ + step - 1
        device = self.place.device(self.axes(half)[1 if kind == 1 else 0], 1)
        return remote(source, target, self.sends.at[half, sem], self.recvs.at[half, sem], device)

    def add(self, half, kind, step, i):
        np_, nq = self.counts(half)
        self.copy(half, kind, step, i).wait_recv()
        if kind == 1:
            add_rows(
                self.part(half, i, nq - step - 1), self.held[1].at[half, (step - 1) * np_ + i]
            )
        else:
            add_rows(self.part(half, np_ - step - 1, 0), self.held[0].at[half, step - 1])

    def first(self):
        for half in (0, 1):
            np_, nq = self.counts(half)
            if nq > 1:
                for i in range(np_ - 1, -1, -1):
                    self.copy(half, 1, 1, i).start()

    def second(self):
        for half in (0, 1):
            np_, nq = self.counts(half)
            for step in range(1, nq):
                for i in range(np_ - 1, -1, -1):
                    self.add(half, 1, step, i)
                    if step < nq - 1:
                        self.copy(half, 1, step + 1, i).start()
                    elif i == np_ - 1 and np_ > 1:
                        self.copy(half, 0, 1, 0).start()
            if nq == 1 and np_ > 1:
                self.copy(half, 0, 1, 0).start()

    def third(self):
        for half in (0, 1):
            np_, _ = self.counts(half)
            for step in range(1, np_):
                self.add(half, 0, step, 0)
                if step < np_ - 1:
                    self.copy(half, 0, step + 1, 0).start()

    def finish(self):
        for half in (0, 1):
            np_, nq = self.counts(half)
            for step in range(1, nq):
                for i in range(np_):
                    self.copy(half, 1, step, i).wait_send()
            for step in range(1, np_):
                self.copy(half, 0, step, 0).wait_send()


def sum_kernel(sizes, count, *refs):
    row_count, col_count = sizes
    terms = refs[:count]
    act_terms = refs[count]
    outs = refs[count + 1 : 2 * count + 1]
    act_out = refs[2 * count + 1]
    refs = refs[2 * count + 2 :]
    per = [refs[6 * n : 6 * n + 6] for n in range(count)]
    act_held, load_sems, cs, cr, ps, pr, zs, zr = refs[6 * count :]
    place = Place(row_count, col_count)
    cores = place.sizes[2]
    core = place.at[2]
    token_rows = act_out.shape[0]

    slots = [(way, step) for step in range(col_count - 1, 0, -1) for way in (0, 1)] + [(0, 0)]
    entries = [(way, step, n) for way, step in slots for n in range(count)]

    acts = LineSum(
        place,
        lambda j: act_terms.at[pl.ds(pl.multiple_of(j * token_rows, token_rows), token_rows)],
        act_held,
        zs.at[count],
        zr.at[count],
    )
    acc = [per[n][0] for n in range(count)]
    lines = [
        LineSum(
            place,
            lambda j, n=n: acc[n].at[j, place.chip_of(place.at)],
            per[n][4],
            zs.at[n],
            zr.at[n],
        )
        for n in range(count)
    ]

    def at_entry(entry):
        way, step, n = entry
        if step == 0:
            return None, place.col
        return lines[n].target(way, step)

    def load(n, col):
        return pltpu.make_async_copy(
            terms[n].at[col, :, core], acc[n].at[col], load_sems.at[n, col]
        )

    def share(n, col):
        return remote(
            terms[n].at[col, :, lax.rem(core + 1, cores)],
            per[n][1].at[col],
            cs.at[n, col],
            cr.at[n, col],
            place.device(2, 1),
        )

    def inside(n, col):
        return PlaneSum(
            place,
            acc[n].at[col],
            per[n][1].at[col],
            per[n][2].at[col],
            per[n][3].at[col],
            (ps.at[n, col], pr.at[n, col]),
        )

    for entry in entries:
        condition, col = at_entry(entry)
        n = entry[2]
        when(condition, lambda: load(n, col).start())
    place.greet(True, True)
    if cores > 1:
        for entry in entries:
            condition, col = at_entry(entry)
            n = entry[2]
            when(condition, lambda: share(n, col).start())
    for way in (0, 1):
        if col_count > 1:
            acts.step(way, col_count - 1)

    def start(n, col):
        load(n, col).wait()
        if cores > 1:
            share(n, col).wait_recv()
            for chip in range(acc[n].shape[1]):
                add_rows(acc[n].at[col, chip], per[n][1].at[col, chip])
        inside(n, col).first()

    for number in range(len(entries) + 2):
        if number < len(entries):
            condition, col = at_entry(entries[number])
            n = entries[number][2]
            when(condition, lambda: start(n, col))
        if 1 <= number <= len(entries):
            condition, col = at_entry(entries[number - 1])
            n = entries[number - 1][2]
            when(condition, lambda: inside(n, col).second())
        if 2 <= number:
            way, step, n = entries[number - 2]
            condition, col = at_entry(entries[number - 2])
            when(condition, lambda: inside(n, col).third())
            if step > 0:
                lines[n].step(way, step)
            else:
                lines[n].last(per[n][5])
                pltpu.make_async_copy(per[n][5], outs[n], load_sems.at[n, place.col]).start()
        if number < len(entries):
            way, step, n = entries[number]
            if 1 < step and way == 1 and n == count - 1:
                for other in (0, 1):
                    acts.step(other, step - 1)
    acts.last(act_out)
    for n in range(count):
        pltpu.make_async_copy(per[n][5], outs[n], load_sems.at[n, place.col]).wait()
    for entry in entries:
        condition, col = at_entry(entry)
        n = entry[2]

        def done():
            if cores > 1:
                share(n, col).wait_send()
            inside(n, col).finish()

        when(condition, done)
    for line in lines + [acts]:
        line.finish()


def sum_all(terms, act_terms, row_count, col_count, act_type):
    count = len(terms)
    sizes = plane_sizes(row_count)
    na, nb, nk = sizes
    chips = na * nb
    deep = terms[0].shape[1] // row_count
    steps = max(col_count - 1, 1)
    firsts, seconds = PlaneSum.counts_of(sizes)
    widths = [t.shape[2] for t in terms]
    token_rows = act_terms.shape[0] // col_count
    scratch = []
    for width in widths:
        scratch += [
            pltpu.VMEM((col_count, chips, deep, width), bf16),
            pltpu.VMEM((col_count, chips, deep, width), bf16),
            pltpu.VMEM((col_count, 2, max(seconds, 1), deep // 2, width), bf16),
            pltpu.VMEM((col_count, 2, max(firsts, 1), deep // 2, width), bf16),
            pltpu.VMEM((2, steps, deep, width), bf16),
            pltpu.VMEM((deep, width), f32),
        ]
    plane_sems = (count, col_count, 2, max(PlaneSum.sem_count(sizes), 1))
    scratch += [
        pltpu.VMEM((2, steps, token_rows, act_terms.shape[1]), bf16),
        pltpu.SemaphoreType.DMA((count, col_count)),
        pltpu.SemaphoreType.DMA((count, col_count)),
        pltpu.SemaphoreType.DMA((count, col_count)),
        pltpu.SemaphoreType.DMA(plane_sems),
        pltpu.SemaphoreType.DMA(plane_sems),
        pltpu.SemaphoreType.DMA((count + 1, 2, steps)),
        pltpu.SemaphoreType.DMA((count + 1, 2, steps)),
    ]
    vmem = pl.BlockSpec(memory_space=pltpu.VMEM)
    return pl.pallas_call(
        functools.partial(sum_kernel, (row_count, col_count), count),
        out_shape=[jax.ShapeDtypeStruct((deep, width), f32) for width in widths]
        + [jax.ShapeDtypeStruct((token_rows, act_terms.shape[1]), act_type)],
        in_specs=[ANY] * count + [vmem],
        out_specs=[ANY] * count + [vmem],
        scratch_shapes=scratch,
        compiler_params=pltpu.CompilerParams(
            collective_id=1, has_side_effects=True, vmem_limit_bytes=60 << 20
        ),
        cost_estimate=pl.CostEstimate(
            flops=0, bytes_accessed=sum(t.size for t in terms) * 4, transcendentals=0
        ),
        name="sum_weights",
    )(
        *[t.reshape(col_count, chips, nk, deep, t.shape[2]) for t in terms],
        act_terms,
    )


def rope_tables(position):
    indices = jnp.arange(HD // 2, dtype=f32)
    frequency = rope_base ** (-(indices * 2.0 / HD))
    wavelen = 2.0 * jnp.pi / frequency
    smooth = (8192.0 / wavelen - 1.0) / 3.0
    scaled = jnp.where(
        wavelen > 8192.0, frequency / 32.0, (1.0 - smooth) * frequency / 32.0 + smooth * frequency
    )
    frequency = jnp.where(wavelen < 2048.0, frequency, scaled)
    angles = position.astype(f32)[:, None] * frequency[None, :]
    return (jnp.cos(angles), jnp.sin(angles))


def rotate(values, cosine, sinusoid):
    halfway = values.shape[-1] // 2
    former = values[..., :halfway]
    latter = values[..., halfway:]
    cos_wide = cosine[:, None, :]
    sin_wide = sinusoid[:, None, :]
    return jnp.concatenate(
        [former * cos_wide - latter * sin_wide, latter * cos_wide + former * sin_wide], axis=-1
    )


def normalize(values, gain):
    scale = lax.rsqrt(jnp.mean(values * values, axis=1, keepdims=True) + epsilon)
    return ((values * scale * gain).astype(bf16), scale)


def norm_back(grad_in, values, scale, gain):
    weighted = grad_in * gain
    inner_sum = jnp.mean(weighted * values, axis=1, keepdims=True)
    return (
        scale * weighted - values * (scale * scale * scale) * inner_sum,
        jnp.sum(grad_in * values * scale, axis=0),
    )


def against(left, right):
    return lax.dot_general(left, right, (((1,), (1,)), ((), ())), preferred_element_type=f32)


def over_rows(left, right):
    return lax.dot_general(left, right, (((0,), (0,)), ((), ())), preferred_element_type=f32)


def matmul(left, right):
    return jnp.dot(left, right, preferred_element_type=f32)


def shift(values, step, col_count):
    if step > 0:
        pairs = [(i, i + step) for i in range(col_count - step)]
    else:
        pairs = [(i, i + step) for i in range(-step, col_count)]
    return lax.ppermute(values, "col", pairs)


def shards(
    tokens,
    seq_lens,
    attn_gain,
    query_weight,
    keyvalue_weight,
    output_weight,
    mlp_gain,
    hidden_weight,
    down_weight,
    out_grad,
):
    row_count, col_count = lax.axis_size("row"), lax.axis_size("col")
    local = tokens.shape[0]
    block_rows = local * col_count
    col = lax.axis_index("col")
    deep = query_weight.shape[0]
    width = tokens.shape[1]
    query_width = query_weight.shape[1]
    pairs = keyvalue_weight.shape[1]
    heads = query_width // HD
    group = heads // pairs
    hidden = down_weight.shape[1]
    back = min(-(-(SEQ_MAX - 1) // local), col_count - 1)

    lengths = seq_lens[0]
    finish = jnp.cumsum(lengths)
    indices = jnp.arange(block_rows, dtype=jnp.int32)
    passed = indices[:, None] >= finish[None, :]
    segment = jnp.sum(passed.astype(jnp.int32), axis=1, dtype=jnp.int32)
    position = indices - jnp.sum(jnp.where(passed, lengths[None, :], 0), axis=1, dtype=jnp.int32)
    own_position = lax.dynamic_slice(position, (col * local,), (local,))
    own_segment = lax.dynamic_slice(segment, (col * local,), (local,))
    padded = jnp.concatenate([jnp.full((back * local,), -1, jnp.int32), segment])
    key_segment = lax.dynamic_slice(padded, (col * local,), ((back + 1) * local,))
    key_index = jnp.arange((back + 1) * local, dtype=jnp.int32) - back * local
    query_index = jnp.arange(local, dtype=jnp.int32)
    allowed = (own_segment[:, None] == key_segment[None, :]) & (
        key_index[None, :] <= query_index[:, None]
    )
    cosine, sinusoid = rope_tables(own_position)
    gain_first = attn_gain.astype(f32)
    gain_second = mlp_gain.astype(f32)

    full_hidden = lax.all_gather(
        hidden_weight.reshape(deep, 2 * hidden), "row", axis=0, tiled=True
    )
    full_down = lax.all_gather(down_weight, "row", axis=0, tiled=True)

    first_weight = jnp.concatenate(
        [query_weight, keyvalue_weight.reshape(deep, pairs * 2 * HD)], axis=1
    )
    full_first, full_output, rows_grad = gather_all(
        [first_weight, output_weight], out_grad, row_count, col_count
    )

    inputs = tokens.astype(f32)
    normal_in, scale_in = normalize(inputs, gain_first)
    projected = jnp.stack([matmul(normal_in, full_first[z]) for z in range(col_count)])
    queries = (
        rotate(projected[:, :, :query_width].reshape(col_count, local, heads, HD), cosine, sinusoid)
        .astype(bf16)
        .reshape(col_count, local, pairs, group, HD)
    )
    keyvals = projected[:, :, query_width:].reshape(col_count, local, pairs, 2, HD)
    keyvals = jnp.stack(
        [rotate(keyvals[:, :, :, 0], cosine, sinusoid), keyvals[:, :, :, 1]], axis=3
    ).astype(bf16)
    chunks = [keyvals]
    for _ in range(back):
        chunks.insert(0, shift(chunks[0], 1, col_count))
    all_keyvals = jnp.concatenate(chunks, axis=1)
    key_rows, values = all_keyvals[:, :, :, 0], all_keyvals[:, :, :, 1]

    factor = HD ** (-0.5)
    scores = jnp.einsum("ztkgd,zskd->zkgts", queries, key_rows, preferred_element_type=f32) * factor
    scores = jnp.where(allowed, scores, blocked)
    summit = jnp.max(scores, axis=-1, keepdims=True)
    weights = jnp.exp(scores - summit)
    totals = jnp.sum(weights, axis=-1, keepdims=True)
    chances = weights / totals
    rounded = chances.astype(bf16)
    mixed = (
        jnp.einsum("zkgts,zskd->ztkgd", rounded, values, preferred_element_type=f32)
        .astype(bf16)
        .reshape(col_count, local, query_width)
    )
    attended = sum(against(mixed[z], full_output[z]) for z in range(col_count))
    hidden_in = inputs + attended
    normal_mid, scale_mid = normalize(hidden_in, gain_second)

    rows_mid = line_gather(normal_mid, row_count, col_count, 2)
    gate_up = matmul(rows_mid, full_hidden)
    gate_part = gate_up[:, :hidden]
    up_part = gate_up[:, hidden:]
    sigmoid_gate = jax.nn.sigmoid(gate_part)
    silu_gate = gate_part * sigmoid_gate
    gated_act = (silu_gate * up_part).astype(bf16)
    grad_gated = matmul(rows_grad, full_down)
    grad_gate = grad_gated * up_part * sigmoid_gate * (1.0 + gate_part * (1.0 - sigmoid_gate))
    grad_up = grad_gated * silu_gate
    grad_gate_up = jnp.concatenate([grad_gate, grad_up], axis=1).astype(bf16)
    grad_mid = line_sum(
        against(grad_gate_up, full_hidden).astype(bf16), row_count, col_count, 3
    )
    out_terms = against(gated_act, full_down).astype(bf16)
    grad_down_part = over_rows(rows_grad, gated_act).astype(bf16)
    grad_hidden_part = over_rows(rows_mid, grad_gate_up).astype(bf16)
    sum_hidden = lax.psum_scatter(grad_hidden_part, "row", scatter_dimension=0, tiled=True)
    sum_down = lax.psum_scatter(grad_down_part, "row", scatter_dimension=0, tiled=True)

    back_mid, gain_mid_part = norm_back(grad_mid, hidden_in, scale_mid, gain_second)
    grad_hidden_in = out_grad.astype(f32) + back_mid
    grad_low = grad_hidden_in.astype(bf16)
    grad_mixed = jnp.stack(
        [matmul(grad_low, full_output[z]).astype(bf16) for z in range(col_count)]
    ).reshape(col_count, local, pairs, group, HD)
    grad_output_part = jnp.stack(
        [over_rows(grad_low, mixed[z]).astype(bf16) for z in range(col_count)]
    )

    grad_chance = jnp.einsum("ztkgd,zskd->zkgts", grad_mixed, values, preferred_element_type=f32)
    centre = jnp.sum(chances * grad_chance, axis=-1, keepdims=True)
    grad_score = (chances * (grad_chance - centre)).astype(bf16)
    grad_query = (
        jnp.einsum("zkgts,zskd->ztkgd", grad_score, key_rows, preferred_element_type=f32) * factor
    )
    grad_key = (
        jnp.einsum("zkgts,ztkgd->zskd", grad_score, queries, preferred_element_type=f32) * factor
    )
    grad_value = jnp.einsum("zkgts,ztkgd->zskd", rounded, grad_mixed, preferred_element_type=f32)
    grad_keyval = jnp.stack([grad_key, grad_value], axis=3)
    carried = None
    for number in range(back + 1):
        part = grad_keyval[:, number * local : (number + 1) * local]
        if carried is not None:
            part = part + carried.astype(f32)
        if number < back:
            carried = shift(part.astype(bf16), -1, col_count)
    grad_query = rotate(
        grad_query.reshape(col_count, local, heads, HD), cosine, -sinusoid
    ).reshape(col_count, local, query_width)
    grad_keyval = jnp.stack(
        [rotate(part[:, :, :, 0], cosine, -sinusoid), part[:, :, :, 1]], axis=3
    ).reshape(col_count, local, pairs * 2 * HD)
    grad_first = jnp.concatenate([grad_query, grad_keyval], axis=2).astype(bf16)
    grad_first_part = jnp.stack(
        [over_rows(normal_in, grad_first[z]).astype(bf16) for z in range(col_count)]
    )
    sum_first, sum_output, out_sum = sum_all(
        [grad_first_part, grad_output_part], out_terms, row_count, col_count, f32
    )
    block_out = hidden_in + out_sum
    grad_in = sum(against(grad_first[z], full_first[z]) for z in range(col_count))
    back_in, gain_in_part = norm_back(grad_in, inputs, scale_in, gain_first)
    grad_tokens = (grad_hidden_in + back_in).astype(bf16)
    gain_in_sum, gain_mid_sum = lax.psum((gain_in_part, gain_mid_part), ("row", "col"))
    return (
        block_out.astype(bf16),
        grad_tokens,
        gain_in_sum,
        sum_first[:, :query_width],
        sum_first[:, query_width:].reshape(deep, pairs, 2 * HD),
        sum_output,
        gain_mid_sum,
        sum_hidden.astype(f32).reshape(deep, 2, hidden),
        sum_down.astype(f32),
    )


def solution(mesh):
    return jax.shard_map(
        shards,
        mesh=mesh,
        in_specs=(
            P(("row", "col"), None),
            P("row", None),
            P(),
            P("row", "col"),
            P("row", "col", None),
            P("row", "col"),
            P(),
            P("row", None, "col"),
            P("row", "col"),
            P(("row", "col"), None),
        ),
        out_specs=(
            P(("row", "col"), None),
            P(("row", "col"), None),
            P(),
            P("row", "col"),
            P("row", "col", None),
            P("row", "col"),
            P(),
            P("row", None, "col"),
            P("row", "col"),
        ),
        check_vma=False,
    )
```

```python
import functools

import jax
import jax.numpy as jnp
from jax import lax
from jax.experimental import pallas as pl
from jax.experimental.pallas import tpu as pltpu
from jax.sharding import PartitionSpec as P

HD = 64
SEQ_MAX = 512
MESH = pl.DeviceIdType.MESH
ANY = pl.BlockSpec(memory_space=pl.ANY)

epsilon = 1e-05
rope_base = 500000.0
blocked = -1e30
bf16 = jnp.bfloat16
f32 = jnp.float32


def plane_sizes(row_count):
    cores = 2 if row_count % 2 == 0 else 1
    chips = row_count // cores
    first = 2 if chips % 2 == 0 else 1
    return first, chips // first, cores


class Place:
    def __init__(self, row_count, col_count):
        self.rows, self.cols = row_count, col_count
        self.sizes = plane_sizes(row_count)
        na, nb, nk = self.sizes
        self.row = lax.axis_index("row")
        self.col = lax.axis_index("col")
        self.at = (self.row // (nb * nk), (self.row // nk) % nb, self.row % nk)

    def row_of(self, at):
        _, nb, nk = self.sizes
        return (at[0] * nb + at[1]) * nk + at[2]

    def chip_of(self, at):
        return at[0] * self.sizes[1] + at[1]

    def moved(self, axis, step, at=None):
        at = list(self.at if at is None else at)
        size = self.sizes[axis]
        at[axis] = lax.rem(at[axis] + (step % size), size)
        return tuple(at)

    def device(self, axis, step):
        return (self.row_of(self.moved(axis, step)), self.col)

    def greet(self, plane, line):
        barrier = pltpu.get_barrier_semaphore()
        count = 0
        if plane:
            for axis in range(3):
                size = self.sizes[axis]
                for step in {1 % size, (size - 1) % size} - {0}:
                    pl.semaphore_signal(
                        barrier, inc=1, device_id=self.device(axis, step), device_id_type=MESH
                    )
                    count += 1
        if line and self.cols > 1:
            for step, there in self.line_ways():

                @pl.when(there)
                def _(step=step):
                    pl.semaphore_signal(
                        barrier, inc=1, device_id=(self.row, self.col + step), device_id_type=MESH
                    )

        if line and self.cols > 1:
            last = self.cols - 1
            count = count + jnp.minimum(self.col, 1) + jnp.minimum(last - self.col, 1)
        if not isinstance(count, int) or count:
            pl.semaphore_wait(barrier, count)

    def line_ways(self):
        return ((1, self.col < self.cols - 1), (-1, self.col > 0))


def when(condition, action):
    if condition is None:
        action()
    else:
        pl.when(condition)(action)


def remote(src, dst, send_sem, recv_sem, device):
    return pltpu.make_async_remote_copy(
        src_ref=src,
        dst_ref=dst,
        send_sem=send_sem,
        recv_sem=recv_sem,
        device_id=device,
        device_id_type=MESH,
    )


class LineGather:
    def __init__(self, place, own, block, send_sems, recv_sems):
        self.place, self.own, self.block = place, own, block
        self.sends, self.recvs = send_sems, recv_sems

    def copy(self, way, step, origin):
        place = self.place
        source = self.own if step == 1 else self.block(origin)
        return remote(
            source,
            self.block(origin),
            self.sends.at[way, step - 1],
            self.recvs.at[way, step - 1],
            (place.row, place.col + (1, -1)[way]),
        )

    def sends_at(self, way, step):
        col, last = self.place.col, self.place.cols - 1
        if way == 0:
            return (col >= step - 1) & (col < last), col - (step - 1)
        return (col + step - 1 <= last) & (col > 0), col + (step - 1)

    def gets_at(self, way, step):
        col, last = self.place.col, self.place.cols - 1
        if way == 0:
            return col >= step, col - step
        return col + step <= last, col + step

    def send(self, way, step):
        condition, origin = self.sends_at(way, step)
        when(condition, lambda: self.copy(way, step, origin).start())

    def receive(self, way, step):
        condition, origin = self.gets_at(way, step)

        def action():
            self.copy(way, step, origin).wait_recv()

        when(condition, action)
        if step < self.place.cols - 1:
            self.send(way, step + 1)

    def finish(self):
        for step in range(1, self.place.cols):
            for way in (0, 1):
                condition, origin = self.sends_at(way, step)
                when(condition, lambda: self.copy(way, step, origin).wait_send())


class PlaneGather:
    def __init__(self, place, block, send_sems, recv_sems):
        self.place, self.block = place, block
        self.sends, self.recvs = send_sems, recv_sems

    @staticmethod
    def sem_count(sizes):
        na, nb, _ = sizes
        return 2 * na * nb - 1

    def axes(self, half):
        return (1, 0) if half == 0 else (0, 1)

    def counts(self, half):
        first, second = self.axes(half)
        return self.place.sizes[first], self.place.sizes[second]

    def origin(self, half, i, j, core_step=0):
        first, second = self.axes(half)
        at = self.place.moved(first, -i)
        at = self.place.moved(second, -j, at)
        if core_step:
            at = self.place.moved(2, 1, at)
        return self.place.row_of(at)

    def copy(self, half, kind, i, j):
        np_, nq = self.counts(half)
        if kind == 0:
            number, device = i - 1, self.place.device(self.axes(half)[0], 1)
        elif kind == 1:
            number = (np_ - 1) + i * (nq - 1) + (j - 1)
            device = self.place.device(self.axes(half)[1], 1)
        else:
            number = (np_ * nq - 1) + i * nq + j
            device = self.place.device(2, 1)
        return number, device

    def sender(self, half, kind, i, j):
        number, device = self.copy(half, kind, i, j)
        oi, oj = (i - 1, j) if kind == 0 else ((i, j - 1) if kind == 1 else (i, j))
        ref = self.block(self.origin(half, oi, oj), half)
        return remote(ref, ref, self.sends.at[half, number], self.recvs.at[half, number], device)

    def receiver(self, half, kind, i, j):
        number, device = self.copy(half, kind, i, j)
        ref = self.block(self.origin(half, i, j, 1 if kind == 2 else 0), half)
        return remote(ref, ref, self.sends.at[half, number], self.recvs.at[half, number], device)

    def all_copies(self):
        for half in (0, 1):
            np_, nq = self.counts(half)
            for i in range(1, np_):
                yield half, 0, i, 0
            for i in range(np_):
                for j in range(1, nq):
                    yield half, 1, i, j
            if self.place.sizes[2] > 1:
                for i in range(np_):
                    for j in range(nq):
                        yield half, 2, i, j

    def share(self, half, i, j):
        if self.place.sizes[2] > 1:
            self.sender(half, 2, i, j).start()

    def first(self):
        for half in (0, 1):
            if self.counts(half)[0] > 1:
                self.sender(half, 0, 1, 0).start()
        for half in (0, 1):
            self.share(half, 0, 0)

    def second(self):
        for half in (0, 1):
            np_, nq = self.counts(half)
            for i in range(np_):
                if i > 0:
                    self.receiver(half, 0, i, 0).wait_recv()
                    if i < np_ - 1:
                        self.sender(half, 0, i + 1, 0).start()
                if nq > 1:
                    self.sender(half, 1, i, 1).start()
                if i > 0:
                    self.share(half, i, 0)

    def third(self):
        for half in (0, 1):
            np_, nq = self.counts(half)
            for j in range(1, nq):
                for i in range(np_):
                    self.receiver(half, 1, i, j).wait_recv()
                    if j < nq - 1:
                        self.sender(half, 1, i, j + 1).start()
                    self.share(half, i, j)

    def finish(self):
        for copy in self.all_copies():
            self.sender(*copy).wait_send()
            if copy[1] == 2:
                self.receiver(*copy).wait_recv()


def gather_kernel(sizes, count, *refs):
    row_count, col_count = sizes
    own = refs[:count]
    full = refs[count : 2 * count]
    local_sems, zs, zr, ps, pr = refs[2 * count :]
    place = Place(row_count, col_count)
    place.greet(True, True)
    deep = own[0].shape[0]
    half_deep = deep // 2

    lines = [
        LineGather(
            place,
            own[n],
            lambda j, n=n: full[n].at[j, pl.ds(place.row * deep, deep)],
            zs.at[n],
            zr.at[n],
        )
        for n in range(count)
    ]
    def keep(n):
        return pltpu.make_async_copy(
            own[n], full[n].at[place.col, pl.ds(place.row * deep, deep)], local_sems.at[n]
        )

    for n in range(count):
        keep(n).start()
    for line in lines:
        for way in (0, 1):
            line.send(way, 1)
    for n in range(count):
        keep(n).wait()

    def inside(n, col):
        return PlaneGather(
            place,
            lambda row, half: full[n].at[
                col, pl.ds(row * deep + half * half_deep, half_deep)
            ],
            ps.at[n, col],
            pr.at[n, col],
        )

    slots = [(0, 0)] + [(way, step) for step in range(1, col_count) for way in (0, 1)]
    entries = [(way, step, n) for way, step in slots for n in range(count)]

    def at_entry(entry):
        way, step, n = entry
        if step == 0:
            return None, place.col
        return lines[n].gets_at(way, step)

    for number in range(len(entries) + 2):
        if number < len(entries):
            way, step, n = entries[number]
            condition, col = at_entry(entries[number])
            if step > 0:
                lines[n].receive(way, step)
            when(condition, lambda: inside(n, col).first())
        if 1 <= number <= len(entries):
            condition, col = at_entry(entries[number - 1])
            m = entries[number - 1][2]
            when(condition, lambda: inside(m, col).second())
        if 2 <= number:
            condition, col = at_entry(entries[number - 2])
            m = entries[number - 2][2]
            when(condition, lambda: inside(m, col).third())
    for entry in entries:
        condition, col = at_entry(entry)
        m = entry[2]
        when(condition, lambda: inside(m, col).finish())
    for line in lines:
        line.finish()


def gather_all(weights, row_count, col_count):
    count = len(weights)
    sizes = plane_sizes(row_count)
    deep = weights[0].shape[0]
    steps = max(col_count - 1, 1)
    plane_sems = (count, col_count, 2, PlaneGather.sem_count(sizes))
    moved = sum(w.size for w in weights) * row_count * col_count * 2
    return pl.pallas_call(
        functools.partial(gather_kernel, (row_count, col_count), count),
        out_shape=[
            jax.ShapeDtypeStruct((col_count, row_count * deep, w.shape[1]), bf16) for w in weights
        ],
        in_specs=[ANY] * count,
        out_specs=[ANY] * count,
        scratch_shapes=[
            pltpu.SemaphoreType.DMA((count,)),
            pltpu.SemaphoreType.DMA((count, 2, steps)),
            pltpu.SemaphoreType.DMA((count, 2, steps)),
            pltpu.SemaphoreType.DMA(plane_sems),
            pltpu.SemaphoreType.DMA(plane_sems),
        ],
        compiler_params=pltpu.CompilerParams(collective_id=0, has_side_effects=True),
        cost_estimate=pl.CostEstimate(flops=0, bytes_accessed=moved, transcendentals=0),
        name="gather_weights",
    )(*weights)


def line_gather_kernel(sizes, own, full, local_sem, sends, recvs):
    place = Place(*sizes)
    place.greet(False, True)
    rows = own.shape[0]
    line = LineGather(place, own, lambda j: full.at[pl.ds(j * rows, rows)], sends, recvs)
    for way in (0, 1):
        line.send(way, 1)
    keep = pltpu.make_async_copy(own, full.at[pl.ds(place.col * rows, rows)], local_sem)
    keep.start()
    for step in range(1, place.cols):
        for way in (0, 1):
            line.receive(way, step)
    keep.wait()
    line.finish()


def line_gather(own, row_count, col_count, collective_id):
    steps = max(col_count - 1, 1)
    return pl.pallas_call(
        functools.partial(line_gather_kernel, (row_count, col_count)),
        out_shape=jax.ShapeDtypeStruct((col_count * own.shape[0], own.shape[1]), own.dtype),
        in_specs=[ANY],
        out_specs=ANY,
        scratch_shapes=[
            pltpu.SemaphoreType.DMA,
            pltpu.SemaphoreType.DMA((2, steps)),
            pltpu.SemaphoreType.DMA((2, steps)),
        ],
        compiler_params=pltpu.CompilerParams(collective_id=collective_id, has_side_effects=True),
        cost_estimate=pl.CostEstimate(
            flops=0, bytes_accessed=own.size * 2 * col_count, transcendentals=0
        ),
        name="gather_line",
    )(own)


def add_rows(target, source):
    rows = target.shape[0]
    piece = 32 if rows % 32 == 0 else 16

    def body(n, carry):
        at = pl.ds(pl.multiple_of(n * piece, piece), piece)
        target[at] = (target[at].astype(f32) + source[at].astype(f32)).astype(target.dtype)
        return carry

    lax.fori_loop(0, rows // piece, body, 0)


class LineSum:
    def __init__(self, place, own, held, send_sems, recv_sems):
        self.place, self.own, self.held = place, own, held
        self.sends, self.recvs = send_sems, recv_sems

    def target(self, way, distance):
        col, last = self.place.col, self.place.cols - 1
        if way == 0:
            return col + distance <= last, col + distance
        return col >= distance, col - distance

    def gets(self, way, distance):
        col, last = self.place.col, self.place.cols - 1
        there, _ = self.target(way, distance)
        return there & ((col > 0) if way == 0 else (col < last))

    def copy(self, way, distance, source):
        return remote(
            source,
            self.held.at[way, distance - 1],
            self.sends.at[way, distance - 1],
            self.recvs.at[way, distance - 1],
            (self.place.row, self.place.col + (1, -1)[way]),
        )

    def arrived(self, way, distance):
        ref = self.held.at[way, distance]
        return remote(
            ref,
            ref,
            self.sends.at[way, distance],
            self.recvs.at[way, distance],
            (self.place.row, self.place.col + (1, -1)[way]),
        )

    def step(self, way, distance):
        condition, col = self.target(way, distance)
        if distance < self.place.cols - 1:

            def add():
                self.arrived(way, distance).wait_recv()
                add_rows(self.own(col), self.held.at[way, distance])

            when(self.gets(way, distance), add)
        when(condition, lambda: self.copy(way, distance, self.own(col)).start())

    def last(self, out):
        if self.place.cols > 1:
            for way in (0, 1):
                when(self.gets(way, 0), lambda: self.arrived(way, 0).wait_recv())
        own = self.own(self.place.col)
        rows = own.shape[0]
        piece = 32 if rows % 32 == 0 else 16
        has = [self.gets(way, 0) for way in (0, 1)]

        def body(n, carry):
            at = pl.ds(pl.multiple_of(n * piece, piece), piece)
            total = own[at].astype(f32)
            if self.place.cols > 1:
                for way in (0, 1):
                    term = self.held[way, 0, at].astype(f32)
                    total = total + jnp.where(has[way], term, 0.0)
            out[at] = total.astype(out.dtype)
            return carry

        lax.fori_loop(0, rows // piece, body, 0)

    def finish(self):
        for distance in range(1, self.place.cols):
            for way in (0, 1):
                condition, col = self.target(way, distance)
                when(condition, lambda: self.copy(way, distance, self.own(col)).wait_send())


def line_sum_kernel(sizes, terms, out, held, sends, recvs):
    place = Place(*sizes)
    place.greet(False, True)
    rows = out.shape[0]
    line = LineSum(
        place, lambda j: terms.at[pl.ds(pl.multiple_of(j * rows, rows), rows)], held, sends, recvs
    )
    for distance in range(place.cols - 1, 0, -1):
        for way in (0, 1):
            line.step(way, distance)
    line.last(out)
    line.finish()


def line_sum(terms, row_count, col_count, collective_id):
    steps = max(col_count - 1, 1)
    rows, width = terms.shape[0] // col_count, terms.shape[1]
    return pl.pallas_call(
        functools.partial(line_sum_kernel, (row_count, col_count)),
        out_shape=jax.ShapeDtypeStruct((rows, width), f32),
        in_specs=[pl.BlockSpec(memory_space=pltpu.VMEM)],
        out_specs=pl.BlockSpec(memory_space=pltpu.VMEM),
        scratch_shapes=[
            pltpu.VMEM((2, steps, rows, width), bf16),
            pltpu.SemaphoreType.DMA((2, steps)),
            pltpu.SemaphoreType.DMA((2, steps)),
        ],
        compiler_params=pltpu.CompilerParams(
            collective_id=collective_id, has_side_effects=True, vmem_limit_bytes=48 << 20
        ),
        cost_estimate=pl.CostEstimate(
            flops=terms.size, bytes_accessed=terms.size * 2, transcendentals=0
        ),
        name="sum_line",
    )(terms)


class PlaneSum:
    def __init__(self, place, acc, held_core, held_second, held_first, sems):
        self.place, self.acc = place, acc
        self.held = (held_first, held_second, held_core)
        self.sends, self.recvs = sems
        self.half_deep = acc.shape[1] // 2

    @staticmethod
    def counts_of(sizes):
        na, nb, _ = sizes
        return max(na, nb) - 1, max((na - 1) * nb, (nb - 1) * na)

    @staticmethod
    def sem_count(sizes):
        na, nb, _ = sizes
        return na * nb - 1

    def axes(self, half):
        return (1, 0) if half == 0 else (0, 1)

    def counts(self, half):
        first, second = self.axes(half)
        return self.place.sizes[first], self.place.sizes[second]

    def part(self, half, i, j):
        first, second = self.axes(half)
        at = self.place.moved(second, j, self.place.moved(first, i))
        return self.acc.at[
            self.place.chip_of(at), pl.ds(half * self.half_deep, self.half_deep)
        ]

    def copy(self, half, kind, step, i):
        np_, nq = self.counts(half)
        if kind == 1:
            number = (step - 1) * np_ + i
            source = self.part(half, i, nq - step)
            target = self.held[1].at[half, number]
            sem = number
        else:
            source = self.part(half, np_ - step, 0)
            target = self.held[0].at[half, step - 1]
            sem = (nq - 1) * np_ + step - 1
        device = self.place.device(self.axes(half)[1 if kind == 1 else 0], 1)
        return remote(source, target, self.sends.at[half, sem], self.recvs.at[half, sem], device)

    def add(self, half, kind, step, i):
        np_, nq = self.counts(half)
        self.copy(half, kind, step, i).wait_recv()
        if kind == 1:
            add_rows(
                self.part(half, i, nq - step - 1), self.held[1].at[half, (step - 1) * np_ + i]
            )
        else:
            add_rows(self.part(half, np_ - step - 1, 0), self.held[0].at[half, step - 1])

    def first(self):
        for half in (0, 1):
            np_, nq = self.counts(half)
            if nq > 1:
                for i in range(np_ - 1, -1, -1):
                    self.copy(half, 1, 1, i).start()

    def second(self):
        for half in (0, 1):
            np_, nq = self.counts(half)
            for step in range(1, nq):
                for i in range(np_ - 1, -1, -1):
                    self.add(half, 1, step, i)
                    if step < nq - 1:
                        self.copy(half, 1, step + 1, i).start()
                    elif i == np_ - 1 and np_ > 1:
                        self.copy(half, 0, 1, 0).start()
            if nq == 1 and np_ > 1:
                self.copy(half, 0, 1, 0).start()

    def third(self):
        for half in (0, 1):
            np_, _ = self.counts(half)
            for step in range(1, np_):
                self.add(half, 0, step, 0)
                if step < np_ - 1:
                    self.copy(half, 0, step + 1, 0).start()

    def finish(self):
        for half in (0, 1):
            np_, nq = self.counts(half)
            for step in range(1, nq):
                for i in range(np_):
                    self.copy(half, 1, step, i).wait_send()
            for step in range(1, np_):
                self.copy(half, 0, step, 0).wait_send()


class SmallSum:
    def __init__(self, place, own, total, ring_held, line_held, ring_sems, line_sems):
        self.place, self.own, self.total = place, own, total
        self.held, self.sems = ring_held, ring_sems
        self.line = LineGather(
            place, total, lambda j: line_held.at[j], line_sems.at[0], line_sems.at[1]
        )
        self.line_held = line_held
        self.stages = []
        for axis in range(3):
            for step in range(1, place.sizes[axis]):
                self.stages.append(functools.partial(self.ring_send, axis, step))
                self.stages.append(functools.partial(self.ring_receive, axis, step))
            if place.sizes[axis] > 1:
                self.stages.append(functools.partial(self.ring_add, axis))
        self.stages.append(self.line_start)
        for step in range(1, place.cols):
            self.stages.append(functools.partial(self.line_step, step))
        self.stages.append(self.line_add)

    def begin(self):
        self.total[...] = self.own[...]

    def block(self, axis, step):
        at = self.place.moved(axis, -step)[axis]
        return self.held.at[axis, at]

    def ring_copy(self, axis, step):
        source = self.total if step == 1 else self.block(axis, step - 1)
        target = self.held.at[axis, self.place.moved(axis, 1 - step)[axis]]
        return remote(
            source,
            target,
            self.sems.at[0, axis, step - 1],
            self.sems.at[1, axis, step - 1],
            self.place.device(axis, 1),
        )

    def ring_send(self, axis, step):
        self.ring_copy(axis, step).start()

    def ring_receive(self, axis, step):
        ref = self.block(axis, step)
        remote(
            ref,
            ref,
            self.sems.at[0, axis, step - 1],
            self.sems.at[1, axis, step - 1],
            self.place.device(axis, 1),
        ).wait_recv()

    def ring_add(self, axis):
        for step in range(1, self.place.sizes[axis]):
            self.ring_copy(axis, step).wait_send()
        own_at = self.place.at[axis]
        total = None
        for at in range(self.place.sizes[axis]):
            term = jnp.where(own_at == at, self.total[...], self.held[axis, at])
            total = term if total is None else total + term
        self.total[...] = total

    def line_start(self):
        for way in (0, 1):
            self.line.send(way, 1)

    def line_step(self, step):
        for way in (0, 1):
            self.line.receive(way, step)

    def line_add(self):
        self.line.finish()
        total = None
        for at in range(self.place.cols):
            term = jnp.where(self.place.col == at, self.total[...], self.line_held[at])
            total = term if total is None else total + term
        self.total[...] = total


def sum_kernel(sizes, count, *refs):
    row_count, col_count = sizes
    terms = refs[:count]
    act_terms, small = refs[count : count + 2]
    outs = refs[count + 2 : 2 * count + 2]
    act_out, small_out = refs[2 * count + 2 : 2 * count + 4]
    refs = refs[2 * count + 4 :]
    per = [refs[6 * n : 6 * n + 6] for n in range(count)]
    act_held, load_sems, cs, cr, ps, pr, zs, zr = refs[6 * count : 6 * count + 8]
    ring_held, line_held, ring_sems, line_sems = refs[6 * count + 8 :]
    place = Place(row_count, col_count)
    cores = place.sizes[2]
    core = place.at[2]
    token_rows = act_out.shape[0]

    slots = [(way, step) for step in range(col_count - 1, 0, -1) for way in (0, 1)] + [(0, 0)]
    entries = [(way, step, n) for way, step in slots for n in range(count)]

    acts = LineSum(
        place,
        lambda j: act_terms.at[pl.ds(pl.multiple_of(j * token_rows, token_rows), token_rows)],
        act_held,
        zs.at[count],
        zr.at[count],
    )
    acc = [per[n][0] for n in range(count)]
    lines = [
        LineSum(
            place,
            lambda j, n=n: acc[n].at[j, place.chip_of(place.at)],
            per[n][4],
            zs.at[n],
            zr.at[n],
        )
        for n in range(count)
    ]

    def at_entry(entry):
        way, step, n = entry
        if step == 0:
            return None, place.col
        return lines[n].target(way, step)

    def load(n, col):
        return pltpu.make_async_copy(
            terms[n].at[col, :, core], acc[n].at[col], load_sems.at[n, col]
        )

    def share(n, col):
        return remote(
            terms[n].at[col, :, lax.rem(core + 1, cores)],
            per[n][1].at[col],
            cs.at[n, col],
            cr.at[n, col],
            place.device(2, 1),
        )

    def inside(n, col):
        return PlaneSum(
            place,
            acc[n].at[col],
            per[n][1].at[col],
            per[n][2].at[col],
            per[n][3].at[col],
            (ps.at[n, col], pr.at[n, col]),
        )

    for entry in entries:
        condition, col = at_entry(entry)
        n = entry[2]
        when(condition, lambda: load(n, col).start())
    place.greet(True, True)
    if cores > 1:
        for entry in entries:
            condition, col = at_entry(entry)
            n = entry[2]
            when(condition, lambda: share(n, col).start())
    for way in (0, 1):
        if col_count > 1:
            acts.step(way, col_count - 1)
    smalls = SmallSum(place, small, small_out, ring_held, line_held, ring_sems, line_sems)
    smalls.begin()
    stages = list(smalls.stages)

    def start(n, col):
        load(n, col).wait()
        if cores > 1:
            share(n, col).wait_recv()
            for chip in range(acc[n].shape[1]):
                add_rows(acc[n].at[col, chip], per[n][1].at[col, chip])
        inside(n, col).first()

    for number in range(len(entries) + 2):
        if number < len(entries):
            condition, col = at_entry(entries[number])
            n = entries[number][2]
            when(condition, lambda: start(n, col))
        if 1 <= number <= len(entries):
            condition, col = at_entry(entries[number - 1])
            n = entries[number - 1][2]
            when(condition, lambda: inside(n, col).second())
        if 2 <= number:
            way, step, n = entries[number - 2]
            condition, col = at_entry(entries[number - 2])
            when(condition, lambda: inside(n, col).third())
            if step > 0:
                lines[n].step(way, step)
            else:
                lines[n].last(per[n][5])
                pltpu.make_async_copy(per[n][5], outs[n], load_sems.at[n, place.col]).start()
        if number < len(entries):
            way, step, n = entries[number]
            if 1 < step and way == 1 and n == count - 1:
                for other in (0, 1):
                    acts.step(other, step - 1)
        if stages:
            stages.pop(0)()
    for stage in stages:
        stage()
    acts.last(act_out)
    for n in range(count):
        pltpu.make_async_copy(per[n][5], outs[n], load_sems.at[n, place.col]).wait()
    for entry in entries:
        condition, col = at_entry(entry)
        n = entry[2]

        def done():
            if cores > 1:
                share(n, col).wait_send()
            inside(n, col).finish()

        when(condition, done)
    for line in lines + [acts]:
        line.finish()


def sum_all(terms, act_terms, small, row_count, col_count, act_type):
    count = len(terms)
    sizes = plane_sizes(row_count)
    na, nb, nk = sizes
    chips = na * nb
    deep = terms[0].shape[1] // row_count
    steps = max(col_count - 1, 1)
    firsts, seconds = PlaneSum.counts_of(sizes)
    widths = [t.shape[2] for t in terms]
    token_rows = act_terms.shape[0] // col_count
    scratch = []
    for width in widths:
        scratch += [
            pltpu.VMEM((col_count, chips, deep, width), bf16),
            pltpu.VMEM((col_count, chips, deep, width), bf16),
            pltpu.VMEM((col_count, 2, max(seconds, 1), deep // 2, width), bf16),
            pltpu.VMEM((col_count, 2, max(firsts, 1), deep // 2, width), bf16),
            pltpu.VMEM((2, steps, deep, width), bf16),
            pltpu.VMEM((deep, width), f32),
        ]
    plane_sems = (count, col_count, 2, max(PlaneSum.sem_count(sizes), 1))
    scratch += [
        pltpu.VMEM((2, steps, token_rows, act_terms.shape[1]), bf16),
        pltpu.SemaphoreType.DMA((count, col_count)),
        pltpu.SemaphoreType.DMA((count, col_count)),
        pltpu.SemaphoreType.DMA((count, col_count)),
        pltpu.SemaphoreType.DMA(plane_sems),
        pltpu.SemaphoreType.DMA(plane_sems),
        pltpu.SemaphoreType.DMA((count + 1, 2, steps)),
        pltpu.SemaphoreType.DMA((count + 1, 2, steps)),
        pltpu.VMEM((3, max(sizes)) + small.shape, f32),
        pltpu.VMEM((col_count,) + small.shape, f32),
        pltpu.SemaphoreType.DMA((2, 3, max(max(sizes) - 1, 1))),
        pltpu.SemaphoreType.DMA((2, 2, steps)),
    ]
    vmem = pl.BlockSpec(memory_space=pltpu.VMEM)
    return pl.pallas_call(
        functools.partial(sum_kernel, (row_count, col_count), count),
        out_shape=[jax.ShapeDtypeStruct((deep, width), f32) for width in widths]
        + [
            jax.ShapeDtypeStruct((token_rows, act_terms.shape[1]), act_type),
            jax.ShapeDtypeStruct(small.shape, f32),
        ],
        in_specs=[ANY] * count + [vmem, vmem],
        out_specs=[ANY] * count + [vmem, vmem],
        scratch_shapes=scratch,
        compiler_params=pltpu.CompilerParams(
            collective_id=1, has_side_effects=True, vmem_limit_bytes=60 << 20
        ),
        cost_estimate=pl.CostEstimate(
            flops=0, bytes_accessed=sum(t.size for t in terms) * 4, transcendentals=0
        ),
        name="sum_weights",
    )(
        *[t.reshape(col_count, chips, nk, deep, t.shape[2]) for t in terms],
        act_terms,
        small,
    )


def rope_tables(position):
    indices = jnp.arange(HD // 2, dtype=f32)
    frequency = rope_base ** (-(indices * 2.0 / HD))
    wavelen = 2.0 * jnp.pi / frequency
    smooth = (8192.0 / wavelen - 1.0) / 3.0
    scaled = jnp.where(
        wavelen > 8192.0, frequency / 32.0, (1.0 - smooth) * frequency / 32.0 + smooth * frequency
    )
    frequency = jnp.where(wavelen < 2048.0, frequency, scaled)
    angles = position.astype(f32)[:, None] * frequency[None, :]
    return (jnp.cos(angles), jnp.sin(angles))


def rotate(values, cosine, sinusoid):
    halfway = values.shape[-1] // 2
    former = values[..., :halfway]
    latter = values[..., halfway:]
    cos_wide = cosine[:, None, :]
    sin_wide = sinusoid[:, None, :]
    return jnp.concatenate(
        [former * cos_wide - latter * sin_wide, latter * cos_wide + former * sin_wide], axis=-1
    )


def normalize(values, gain):
    scale = lax.rsqrt(jnp.mean(values * values, axis=1, keepdims=True) + epsilon)
    return ((values * scale * gain).astype(bf16), scale)


def norm_back(grad_in, values, scale, gain):
    weighted = grad_in * gain
    inner_sum = jnp.mean(weighted * values, axis=1, keepdims=True)
    return (
        scale * weighted - values * (scale * scale * scale) * inner_sum,
        jnp.sum(grad_in * values * scale, axis=0),
    )


def against(left, right):
    return lax.dot_general(left, right, (((1,), (1,)), ((), ())), preferred_element_type=f32)


def over_rows(left, right):
    return lax.dot_general(left, right, (((0,), (0,)), ((), ())), preferred_element_type=f32)


def matmul(left, right):
    return jnp.dot(left, right, preferred_element_type=f32)


def shift(values, step, col_count):
    if step > 0:
        pairs = [(i, i + step) for i in range(col_count - step)]
    else:
        pairs = [(i, i + step) for i in range(-step, col_count)]
    return lax.ppermute(values, "col", pairs)


def shards(
    tokens,
    seq_lens,
    attn_gain,
    query_weight,
    keyvalue_weight,
    output_weight,
    mlp_gain,
    hidden_weight,
    down_weight,
    out_grad,
):
    row_count, col_count = lax.axis_size("row"), lax.axis_size("col")
    local = tokens.shape[0]
    block_rows = local * col_count
    col = lax.axis_index("col")
    deep = query_weight.shape[0]
    width = tokens.shape[1]
    query_width = query_weight.shape[1]
    pairs = keyvalue_weight.shape[1]
    heads = query_width // HD
    group = heads // pairs
    hidden = down_weight.shape[1]
    back = min(-(-(SEQ_MAX - 1) // local), col_count - 1)

    lengths = seq_lens[0]
    finish = jnp.cumsum(lengths)
    indices = jnp.arange(block_rows, dtype=jnp.int32)
    passed = indices[:, None] >= finish[None, :]
    segment = jnp.sum(passed.astype(jnp.int32), axis=1, dtype=jnp.int32)
    position = indices - jnp.sum(jnp.where(passed, lengths[None, :], 0), axis=1, dtype=jnp.int32)
    own_position = lax.dynamic_slice(position, (col * local,), (local,))
    own_segment = lax.dynamic_slice(segment, (col * local,), (local,))
    padded = jnp.concatenate([jnp.full((back * local,), -1, jnp.int32), segment])
    key_segment = lax.dynamic_slice(padded, (col * local,), ((back + 1) * local,))
    key_index = jnp.arange((back + 1) * local, dtype=jnp.int32) - back * local
    query_index = jnp.arange(local, dtype=jnp.int32)
    allowed = (own_segment[:, None] == key_segment[None, :]) & (
        key_index[None, :] <= query_index[:, None]
    )
    cosine, sinusoid = rope_tables(own_position)
    gain_first = attn_gain.astype(f32)
    gain_second = mlp_gain.astype(f32)

    rows_grad = lax.all_gather(out_grad, "col", axis=0, tiled=True)

    first_weight = jnp.concatenate(
        [query_weight, keyvalue_weight.reshape(deep, pairs * 2 * HD)], axis=1
    )
    full_first, full_output = gather_all([first_weight, output_weight], row_count, col_count)

    hidden_flat, down_flat, full_first = lax.optimization_barrier(
        (hidden_weight.reshape(deep, 2 * hidden), down_weight, full_first)
    )
    full_hidden = lax.all_gather(hidden_flat, "row", axis=0, tiled=True)
    full_down = lax.all_gather(down_flat, "row", axis=0, tiled=True)

    inputs = tokens.astype(f32)
    normal_in, scale_in = normalize(inputs, gain_first)
    projected = jnp.stack([matmul(normal_in, full_first[z]) for z in range(col_count)])
    queries = (
        rotate(projected[:, :, :query_width].reshape(col_count, local, heads, HD), cosine, sinusoid)
        .astype(bf16)
        .reshape(col_count, local, pairs, group, HD)
    )
    keyvals = projected[:, :, query_width:].reshape(col_count, local, pairs, 2, HD)
    keyvals = jnp.stack(
        [rotate(keyvals[:, :, :, 0], cosine, sinusoid), keyvals[:, :, :, 1]], axis=3
    ).astype(bf16)
    chunks = [keyvals]
    for _ in range(back):
        chunks.insert(0, shift(chunks[0], 1, col_count))
    all_keyvals = jnp.concatenate(chunks, axis=1)
    key_rows, values = all_keyvals[:, :, :, 0], all_keyvals[:, :, :, 1]

    factor = HD ** (-0.5)
    scores = jnp.einsum("ztkgd,zskd->zkgts", queries, key_rows, preferred_element_type=f32) * factor
    scores = jnp.where(allowed, scores, blocked)
    summit = jnp.max(scores, axis=-1, keepdims=True)
    weights = jnp.exp(scores - summit)
    totals = jnp.sum(weights, axis=-1, keepdims=True)
    chances = weights / totals
    rounded = chances.astype(bf16)
    mixed = (
        jnp.einsum("zkgts,zskd->ztkgd", rounded, values, preferred_element_type=f32)
        .astype(bf16)
        .reshape(col_count, local, query_width)
    )
    attended = sum(against(mixed[z], full_output[z]) for z in range(col_count))
    hidden_in = inputs + attended
    normal_mid, scale_mid = normalize(hidden_in, gain_second)

    rows_mid = line_gather(normal_mid, row_count, col_count, 2)
    gate_up = matmul(rows_mid, full_hidden)
    gate_part = gate_up[:, :hidden]
    up_part = gate_up[:, hidden:]
    sigmoid_gate = jax.nn.sigmoid(gate_part)
    silu_gate = gate_part * sigmoid_gate
    gated_act = (silu_gate * up_part).astype(bf16)
    grad_gated = matmul(rows_grad, full_down)
    grad_gate = grad_gated * up_part * sigmoid_gate * (1.0 + gate_part * (1.0 - sigmoid_gate))
    grad_up = grad_gated * silu_gate
    grad_gate_up = jnp.concatenate([grad_gate, grad_up], axis=1).astype(bf16)
    grad_mid = line_sum(
        against(grad_gate_up, full_hidden).astype(bf16), row_count, col_count, 3
    )
    out_terms = against(gated_act, full_down).astype(bf16)
    grad_down_part = over_rows(rows_grad, gated_act).astype(bf16)
    grad_hidden_part = over_rows(rows_mid, grad_gate_up).astype(bf16)
    sum_hidden = lax.psum_scatter(grad_hidden_part, "row", scatter_dimension=0, tiled=True)
    sum_down = lax.psum_scatter(grad_down_part, "row", scatter_dimension=0, tiled=True)

    back_mid, gain_mid_part = norm_back(grad_mid, hidden_in, scale_mid, gain_second)
    grad_hidden_in = out_grad.astype(f32) + back_mid
    grad_low = grad_hidden_in.astype(bf16)
    grad_mixed = jnp.stack(
        [matmul(grad_low, full_output[z]).astype(bf16) for z in range(col_count)]
    ).reshape(col_count, local, pairs, group, HD)
    grad_output_part = jnp.stack(
        [over_rows(grad_low, mixed[z]).astype(bf16) for z in range(col_count)]
    )

    grad_chance = jnp.einsum("ztkgd,zskd->zkgts", grad_mixed, values, preferred_element_type=f32)
    centre = jnp.sum(chances * grad_chance, axis=-1, keepdims=True)
    grad_score = (chances * (grad_chance - centre)).astype(bf16)
    grad_query = (
        jnp.einsum("zkgts,zskd->ztkgd", grad_score, key_rows, preferred_element_type=f32) * factor
    )
    grad_key = (
        jnp.einsum("zkgts,ztkgd->zskd", grad_score, queries, preferred_element_type=f32) * factor
    )
    grad_value = jnp.einsum("zkgts,ztkgd->zskd", rounded, grad_mixed, preferred_element_type=f32)
    grad_keyval = jnp.stack([grad_key, grad_value], axis=3)
    carried = None
    for number in range(back + 1):
        part = grad_keyval[:, number * local : (number + 1) * local]
        if carried is not None:
            part = part + carried.astype(f32)
        if number < back:
            carried = shift(part.astype(bf16), -1, col_count)
    grad_query = rotate(
        grad_query.reshape(col_count, local, heads, HD), cosine, -sinusoid
    ).reshape(col_count, local, query_width)
    grad_keyval = jnp.stack(
        [rotate(part[:, :, :, 0], cosine, -sinusoid), part[:, :, :, 1]], axis=3
    ).reshape(col_count, local, pairs * 2 * HD)
    grad_first = jnp.concatenate([grad_query, grad_keyval], axis=2).astype(bf16)
    grad_first_part = jnp.stack(
        [over_rows(normal_in, grad_first[z]).astype(bf16) for z in range(col_count)]
    )
    grad_in = sum(against(grad_first[z], full_first[z]) for z in range(col_count))
    back_in, gain_in_part = norm_back(grad_in, inputs, scale_in, gain_first)
    grad_tokens = (grad_hidden_in + back_in).astype(bf16)
    gain_parts = jnp.concatenate([gain_in_part, gain_mid_part]).reshape(-1, 128)
    sum_first, sum_output, out_sum, gain_sums = sum_all(
        [grad_first_part, grad_output_part], out_terms, gain_parts, row_count, col_count, f32
    )
    block_out = hidden_in + out_sum
    gain_in_sum, gain_mid_sum = gain_sums.reshape(2, width)
    return (
        block_out.astype(bf16),
        grad_tokens,
        gain_in_sum,
        sum_first[:, :query_width],
        sum_first[:, query_width:].reshape(deep, pairs, 2 * HD),
        sum_output,
        gain_mid_sum,
        sum_hidden.astype(f32).reshape(deep, 2, hidden),
        sum_down.astype(f32),
    )


def solution(mesh):
    return jax.shard_map(
        shards,
        mesh=mesh,
        in_specs=(
            P(("row", "col"), None),
            P("row", None),
            P(),
            P("row", "col"),
            P("row", "col", None),
            P("row", "col"),
            P(),
            P("row", None, "col"),
            P("row", "col"),
            P(("row", "col"), None),
        ),
        out_specs=(
            P(("row", "col"), None),
            P(("row", "col"), None),
            P(),
            P("row", "col"),
            P("row", "col", None),
            P("row", "col"),
            P(),
            P("row", None, "col"),
            P("row", "col"),
        ),
        check_vma=False,
    )
```

```python
import functools

import jax
import jax.numpy as jnp
from jax import lax
from jax.experimental import pallas as pl
from jax.experimental.pallas import tpu as pltpu
from jax.sharding import PartitionSpec as P

HD = 64
SEQ_MAX = 512
MESH = pl.DeviceIdType.MESH
ANY = pl.BlockSpec(memory_space=pl.ANY)

epsilon = 1e-05
rope_base = 500000.0
blocked = -1e30
bf16 = jnp.bfloat16
f32 = jnp.float32


def plane_sizes(row_count):
    cores = 2 if row_count % 2 == 0 else 1
    chips = row_count // cores
    first = 2 if chips % 2 == 0 else 1
    return first, chips // first, cores


class Place:
    def __init__(self, row_count, col_count):
        self.rows, self.cols = row_count, col_count
        self.sizes = plane_sizes(row_count)
        na, nb, nk = self.sizes
        self.row = lax.axis_index("row")
        self.col = lax.axis_index("col")
        self.at = (self.row // (nb * nk), (self.row // nk) % nb, self.row % nk)

    def row_of(self, at):
        _, nb, nk = self.sizes
        return (at[0] * nb + at[1]) * nk + at[2]

    def chip_of(self, at):
        return at[0] * self.sizes[1] + at[1]

    def moved(self, axis, step, at=None):
        at = list(self.at if at is None else at)
        size = self.sizes[axis]
        at[axis] = lax.rem(at[axis] + (step % size), size)
        return tuple(at)

    def device(self, axis, step):
        return (self.row_of(self.moved(axis, step)), self.col)

    def greet(self, plane, line):
        barrier = pltpu.get_barrier_semaphore()
        count = 0
        if plane:
            for axis in range(3):
                size = self.sizes[axis]
                for step in {1 % size, (size - 1) % size} - {0}:
                    pl.semaphore_signal(
                        barrier, inc=1, device_id=self.device(axis, step), device_id_type=MESH
                    )
                    count += 1
        if line and self.cols > 1:
            for step, there in self.line_ways():

                @pl.when(there)
                def _(step=step):
                    pl.semaphore_signal(
                        barrier, inc=1, device_id=(self.row, self.col + step), device_id_type=MESH
                    )

        if line and self.cols > 1:
            last = self.cols - 1
            count = count + jnp.minimum(self.col, 1) + jnp.minimum(last - self.col, 1)
        if not isinstance(count, int) or count:
            pl.semaphore_wait(barrier, count)

    def line_ways(self):
        return ((1, self.col < self.cols - 1), (-1, self.col > 0))


def when(condition, action):
    if condition is None:
        action()
    else:
        pl.when(condition)(action)


def remote(src, dst, send_sem, recv_sem, device):
    return pltpu.make_async_remote_copy(
        src_ref=src,
        dst_ref=dst,
        send_sem=send_sem,
        recv_sem=recv_sem,
        device_id=device,
        device_id_type=MESH,
    )


class LineGather:
    def __init__(self, place, own, block, send_sems, recv_sems):
        self.place, self.own, self.block = place, own, block
        self.sends, self.recvs = send_sems, recv_sems

    def copy(self, way, step, origin):
        place = self.place
        source = self.own if step == 1 else self.block(origin)
        return remote(
            source,
            self.block(origin),
            self.sends.at[way, step - 1],
            self.recvs.at[way, step - 1],
            (place.row, place.col + (1, -1)[way]),
        )

    def sends_at(self, way, step):
        col, last = self.place.col, self.place.cols - 1
        if way == 0:
            return (col >= step - 1) & (col < last), col - (step - 1)
        return (col + step - 1 <= last) & (col > 0), col + (step - 1)

    def gets_at(self, way, step):
        col, last = self.place.col, self.place.cols - 1
        if way == 0:
            return col >= step, col - step
        return col + step <= last, col + step

    def send(self, way, step):
        condition, origin = self.sends_at(way, step)
        when(condition, lambda: self.copy(way, step, origin).start())

    def receive(self, way, step):
        condition, origin = self.gets_at(way, step)

        def action():
            self.copy(way, step, origin).wait_recv()

        when(condition, action)
        if step < self.place.cols - 1:
            self.send(way, step + 1)

    def finish(self):
        for step in range(1, self.place.cols):
            for way in (0, 1):
                condition, origin = self.sends_at(way, step)
                when(condition, lambda: self.copy(way, step, origin).wait_send())


class PlaneGather:
    def __init__(self, place, block, own, send_sems, recv_sems):
        self.place, self.block, self.own = place, block, own
        self.sends, self.recvs = send_sems, recv_sems

    @staticmethod
    def sem_count(sizes):
        na, nb, _ = sizes
        return 2 * na * nb - 1

    def axes(self, half):
        return (1, 0) if half == 0 else (0, 1)

    def counts(self, half):
        first, second = self.axes(half)
        return self.place.sizes[first], self.place.sizes[second]

    def origin(self, half, i, j, core_step=0):
        first, second = self.axes(half)
        at = self.place.moved(first, -i)
        at = self.place.moved(second, -j, at)
        if core_step:
            at = self.place.moved(2, 1, at)
        return self.place.row_of(at)

    def copy(self, half, kind, i, j):
        np_, nq = self.counts(half)
        if kind == 0:
            number, device = i - 1, self.place.device(self.axes(half)[0], 1)
        elif kind == 1:
            number = (np_ - 1) + i * (nq - 1) + (j - 1)
            device = self.place.device(self.axes(half)[1], 1)
        else:
            number = (np_ * nq - 1) + i * nq + j
            device = self.place.device(2, 1)
        return number, device

    def sender(self, half, kind, i, j):
        number, device = self.copy(half, kind, i, j)
        oi, oj = (i - 1, j) if kind == 0 else ((i, j - 1) if kind == 1 else (i, j))
        ref = self.block(self.origin(half, oi, oj), half)
        source = self.own(half) if (oi, oj) == (0, 0) else ref
        return remote(source, ref, self.sends.at[half, number], self.recvs.at[half, number], device)

    def receiver(self, half, kind, i, j):
        number, device = self.copy(half, kind, i, j)
        ref = self.block(self.origin(half, i, j, 1 if kind == 2 else 0), half)
        return remote(ref, ref, self.sends.at[half, number], self.recvs.at[half, number], device)

    def all_copies(self):
        for half in (0, 1):
            np_, nq = self.counts(half)
            for i in range(1, np_):
                yield half, 0, i, 0
            for i in range(np_):
                for j in range(1, nq):
                    yield half, 1, i, j
            if self.place.sizes[2] > 1:
                for i in range(np_):
                    for j in range(nq):
                        yield half, 2, i, j

    def share(self, half, i, j):
        if self.place.sizes[2] > 1:
            self.sender(half, 2, i, j).start()

    def first(self):
        for half in (0, 1):
            if self.counts(half)[0] > 1:
                self.sender(half, 0, 1, 0).start()
        for half in (0, 1):
            self.share(half, 0, 0)

    def second(self):
        for half in (0, 1):
            np_, nq = self.counts(half)
            for i in range(np_):
                if i > 0:
                    self.receiver(half, 0, i, 0).wait_recv()
                    if i < np_ - 1:
                        self.sender(half, 0, i + 1, 0).start()
                if nq > 1:
                    self.sender(half, 1, i, 1).start()
                if i > 0:
                    self.share(half, i, 0)

    def third(self):
        for half in (0, 1):
            np_, nq = self.counts(half)
            for j in range(1, nq):
                for i in range(np_):
                    self.receiver(half, 1, i, j).wait_recv()
                    if j < nq - 1:
                        self.sender(half, 1, i, j + 1).start()
                    self.share(half, i, j)

    def finish(self):
        for copy in self.all_copies():
            self.sender(*copy).wait_send()
            if copy[1] == 2:
                self.receiver(*copy).wait_recv()


def nearby(place, number):
    low, high = place.col, place.cols - 1 - place.col
    both = jnp.minimum(low, high)
    way = jnp.minimum(jnp.maximum(high - low, -1), 1)
    step = (number + 1) // 2 * (-1 if number % 2 else 1)
    paired = jnp.minimum(jnp.maximum(2 * both - number + 1, 0), 1)
    return place.col + paired * step + (1 - paired) * way * (number - both)


def gather_kernel(sizes, count, inner, *refs):
    row_count, col_count = sizes
    every = count + inner
    own, own_act = refs[:every], refs[every]
    full, full_act = refs[every + 1 : 2 * every + 1], refs[2 * every + 1]
    local_sems, zs, zr, ps, pr = refs[2 * every + 2 :]
    place = Place(row_count, col_count)
    place.greet(True, True)
    token_rows = own_act.shape[0]

    def at(n, col, row):
        deep = own[n].shape[0]
        if n < count:
            return full[n].at[col, pl.ds(row * deep, deep)]
        return full[n].at[pl.ds(row * deep, deep)]

    lines = [
        LineGather(place, own[n], lambda j, n=n: at(n, j, place.row), zs.at[n], zr.at[n])
        for n in range(count)
    ]
    acts = LineGather(
        place,
        own_act,
        lambda j: full_act.at[pl.ds(j * token_rows, token_rows)],
        zs.at[count],
        zr.at[count],
    )

    def keep(n):
        if n == every:
            return pltpu.make_async_copy(own_act, acts.block(place.col), local_sems.at[n])
        return pltpu.make_async_copy(own[n], at(n, place.col, place.row), local_sems.at[n])

    for n in range(every + 1):
        keep(n).start()
    for line in lines:
        for way in (0, 1):
            line.send(way, 1)

    def inside(n, col, near):
        deep = own[n].shape[0]
        half = deep // 2

        def block(row, number):
            rows = pl.ds(row * deep + number * half, half)
            return full[n].at[col, rows] if n < count else full[n].at[rows]

        def mine(number):
            return own[n].at[pl.ds(number * half, half)] if near else block(place.row, number)

        return PlaneGather(place, block, mine, ps.at[n, col], pr.at[n, col])

    entries = [(n, k) for k in range(col_count) for n in range(count)]
    entries += [(n, 0) for n in range(count, every)]
    parts = [inside(n, nearby(place, k), k == 0) for n, k in entries]
    act_steps = list(range(1, col_count))

    def act_step():
        if act_steps:
            for way in (0, 1):
                acts.receive(way, act_steps[0])
            act_steps.pop(0)

    for number in range(len(parts) + 2):
        if number < len(parts):
            n, k = entries[number]
            if n == 0 and k > 0:
                for line in lines:
                    for way in (0, 1):
                        line.receive(way, k)
                if k == 1:
                    for way in (0, 1):
                        acts.send(way, 1)
                if k >= 3:
                    act_step()
            parts[number].first()
        if 1 <= number <= len(parts):
            parts[number - 1].second()
        if 2 <= number:
            parts[number - 2].third()
        if number >= len(parts):
            act_step()
    while act_steps:
        act_step()
    for n in range(every + 1):
        keep(n).wait()
    for part in parts:
        part.finish()
    for line in lines + [acts]:
        line.finish()


def gather_all(weights, inner_weights, act, row_count, col_count):
    count, inner = len(weights), len(inner_weights)
    sizes = plane_sizes(row_count)
    steps = max(col_count - 1, 1)
    every = list(weights) + list(inner_weights)
    plane_sems = (count + inner, col_count, 2, PlaneGather.sem_count(sizes))
    moved = sum(w.size for w in weights) * row_count * col_count * 2
    return pl.pallas_call(
        functools.partial(gather_kernel, (row_count, col_count), count, inner),
        out_shape=[
            jax.ShapeDtypeStruct((col_count, row_count * w.shape[0], w.shape[1]), bf16)
            for w in weights
        ]
        + [
            jax.ShapeDtypeStruct((row_count * w.shape[0], w.shape[1]), bf16) for w in inner_weights
        ]
        + [jax.ShapeDtypeStruct((col_count * act.shape[0], act.shape[1]), bf16)],
        in_specs=[pl.BlockSpec(memory_space=pltpu.VMEM)] * (len(every) + 1),
        out_specs=[ANY] * (len(every) + 1),
        scratch_shapes=[
            pltpu.SemaphoreType.DMA((len(every) + 1,)),
            pltpu.SemaphoreType.DMA((count + 1, 2, steps)),
            pltpu.SemaphoreType.DMA((count + 1, 2, steps)),
            pltpu.SemaphoreType.DMA(plane_sems),
            pltpu.SemaphoreType.DMA(plane_sems),
        ],
        compiler_params=pltpu.CompilerParams(collective_id=0, has_side_effects=True),
        cost_estimate=pl.CostEstimate(flops=0, bytes_accessed=moved, transcendentals=0),
        name="gather_weights",
    )(*every, act)


def line_gather_kernel(sizes, own, full, local_sem, sends, recvs):
    place = Place(*sizes)
    place.greet(False, True)
    rows = own.shape[0]
    line = LineGather(place, own, lambda j: full.at[pl.ds(j * rows, rows)], sends, recvs)
    for way in (0, 1):
        line.send(way, 1)
    keep = pltpu.make_async_copy(own, full.at[pl.ds(place.col * rows, rows)], local_sem)
    keep.start()
    for step in range(1, place.cols):
        for way in (0, 1):
            line.receive(way, step)
    keep.wait()
    line.finish()


def line_gather(own, row_count, col_count, collective_id):
    steps = max(col_count - 1, 1)
    return pl.pallas_call(
        functools.partial(line_gather_kernel, (row_count, col_count)),
        out_shape=jax.ShapeDtypeStruct((col_count * own.shape[0], own.shape[1]), own.dtype),
        in_specs=[pl.BlockSpec(memory_space=pltpu.VMEM)],
        out_specs=ANY,
        scratch_shapes=[
            pltpu.SemaphoreType.DMA,
            pltpu.SemaphoreType.DMA((2, steps)),
            pltpu.SemaphoreType.DMA((2, steps)),
        ],
        compiler_params=pltpu.CompilerParams(collective_id=collective_id, has_side_effects=True),
        cost_estimate=pl.CostEstimate(
            flops=0, bytes_accessed=own.size * 2 * col_count, transcendentals=0
        ),
        name="gather_line",
    )(own)


def add_rows(target, source):
    rows = target.shape[0]
    piece = 32 if rows % 32 == 0 else 16

    def body(n, carry):
        at = pl.ds(pl.multiple_of(n * piece, piece), piece)
        target[at] = (target[at].astype(f32) + source[at].astype(f32)).astype(target.dtype)
        return carry

    lax.fori_loop(0, rows // piece, body, 0)


class LineSum:
    def __init__(self, place, own, held, send_sems, recv_sems):
        self.place, self.own, self.held = place, own, held
        self.sends, self.recvs = send_sems, recv_sems

    def distance(self, way, col):
        return col - self.place.col if way == 0 else self.place.col - col

    def feeds(self, way):
        return self.place.col > 0 if way == 0 else self.place.col < self.place.cols - 1

    def copy(self, way, distance, source):
        return remote(
            source,
            self.held.at[way, distance - 1],
            self.sends.at[way, distance - 1],
            self.recvs.at[way, distance - 1],
            (self.place.row, self.place.col + (1, -1)[way]),
        )

    def arrived(self, way, distance):
        ref = self.held.at[way, distance]
        return remote(
            ref,
            ref,
            self.sends.at[way, distance],
            self.recvs.at[way, distance],
            (self.place.row, self.place.col + (1, -1)[way]),
        )

    def early(self, col, allowed):
        for way in (0, 1):
            far = self.distance(way, col)

            @pl.when(allowed & (far > 0) & jnp.logical_not(self.feeds(way)))
            def _():
                self.copy(way, far, self.own(col)).start()

    def late(self, col, allowed):
        for way in (0, 1):
            far = self.distance(way, col)

            @pl.when(allowed & (far > 0) & self.feeds(way))
            def _():
                self.arrived(way, far).wait_recv()
                add_rows(self.own(col), self.held.at[way, far])
                self.copy(way, far, self.own(col)).start()

    def last(self, out):
        if self.place.cols > 1:
            for way in (0, 1):
                when(self.feeds(way), lambda: self.arrived(way, 0).wait_recv())
        own = self.own(self.place.col)
        rows = own.shape[0]
        piece = 32 if rows % 32 == 0 else 16
        has = [self.feeds(way) for way in (0, 1)]

        def body(n, carry):
            at = pl.ds(pl.multiple_of(n * piece, piece), piece)
            total = own[at].astype(f32)
            if self.place.cols > 1:
                for way in (0, 1):
                    term = self.held[way, 0, at].astype(f32)
                    total = total + jnp.where(has[way], term, 0.0)
            out[at] = total.astype(out.dtype)
            return carry

        lax.fori_loop(0, rows // piece, body, 0)

    def finish(self):
        for distance in range(1, self.place.cols):
            for way in (0, 1):
                col = self.place.col + (distance if way == 0 else -distance)
                there = col < self.place.cols if way == 0 else col >= 0
                when(there, lambda: self.copy(way, distance, self.own(col)).wait_send())


def dot_tokens(left, right):
    return lax.dot_general(left, right, (((0,), (0,)), ((), ())), preferred_element_type=f32)


def mlp_kernel(sizes, tile, wide, *refs):
    hn_in, dy_in, wh_in, wd_in, grad_out, y_out, dwh_out, dwd_out = refs[:8]
    hn, dy, wh, wd, act, dgu, terms, staged, held = refs[8:17]
    token_sems, weight_sems, y_sems, dw_sems, sends, recvs = refs[17:]
    place = Place(*sizes)
    cols = place.cols
    hidden = wd.shape[1]
    width = wd.shape[0]
    tiles = hidden // tile
    wides = width // wide
    tokens = hn.shape[1]
    line = LineSum(place, lambda j: terms.at[j], held, sends, recvs)

    def token_copies(j):
        return (
            pltpu.make_async_copy(hn_in.at[j], hn.at[j], token_sems.at[0, j]),
            pltpu.make_async_copy(dy_in.at[j], dy.at[j], token_sems.at[1, j]),
        )

    def part(number, base=0):
        return pl.ds(pl.multiple_of(base + number * tile, tile), tile)

    def weight_copies(f):
        gate, up = part(f), part(f, hidden)
        return (
            pltpu.make_async_copy(wh_in.at[:, gate], wh.at[:, gate], weight_sems.at[0, f]),
            pltpu.make_async_copy(wh_in.at[:, up], wh.at[:, up], weight_sems.at[1, f]),
            pltpu.make_async_copy(wd_in.at[:, gate], wd.at[:, gate], weight_sems.at[2, f]),
        )

    def order(number):
        return nearby(place, cols - 1 - number)

    for copy in token_copies(order(0)):
        copy.start()
    for f in range(tiles):
        for copy in weight_copies(f):
            copy.start()
    for number in range(1, cols):
        for copy in token_copies(order(number)):
            copy.start()
    place.greet(False, True)

    def out_copy(slot, j):
        return pltpu.make_async_copy(staged.at[slot], y_out.at[j], y_sems.at[slot])

    for number in range(cols):
        j = order(number)
        for copy in token_copies(j):
            copy.wait()

        def hidden_tile(f, carry):
            if number == 0:
                for copy in weight_copies(f):
                    copy.wait()
            gate_at, up_at = part(f), part(f, hidden)
            gate = matmul(hn[j], wh[:, gate_at])
            up = matmul(hn[j], wh[:, up_at])
            back = matmul(dy[j], wd[:, gate_at])
            sigmoid = jax.nn.sigmoid(gate)
            silu = gate * sigmoid
            act[j, :, gate_at] = (silu * up).astype(bf16)
            dgu[j, :, gate_at] = (back * up * sigmoid * (1.0 + gate * (1.0 - sigmoid))).astype(bf16)
            dgu[j, :, up_at] = (back * silu).astype(bf16)
            return carry

        lax.fori_loop(0, tiles, hidden_tile, 0)

        def grad_tile(n, carry):
            at = pl.ds(pl.multiple_of(n * wide, wide), wide)
            terms[j, :, at] = against(dgu[j], wh[at]).astype(bf16)
            return carry

        lax.fori_loop(0, wides, grad_tile, 0)
        line.early(j, True)
        slot = number % 2
        if number >= 2:
            out_copy(slot, order(number - 2)).wait()

        def y_tile(n, carry):
            at = pl.ds(pl.multiple_of(n * wide, wide), wide)
            staged[slot, :, at] = against(act[j], wd[at]).astype(bf16)
            return carry

        lax.fori_loop(0, wides, y_tile, 0)
        out_copy(slot, j).start()
        if number >= 2:
            line.late(order(number - 2), True)

    rest = [number for number in range(max(cols - 2, 0), cols - 1)]
    strips = width // 256
    calls = [functools.partial(line.late, order(number), True) for number in rest]

    def flat(ref):
        return ref[...].reshape(cols * tokens, ref.shape[2])

    def weight_strip(left, right, store, target, sem, at):
        columns = jnp.concatenate([left[j, :, at] for j in range(cols)], axis=0)
        store[at] = dot_tokens(columns, flat(right)).astype(bf16)
        pltpu.make_async_copy(store.at[at], target.at[at], sem).start()

    def down_strip(n, carry):
        at = pl.ds(pl.multiple_of(n * 256, 256), 256)
        weight_strip(dy, act, wd, dwd_out, dw_sems.at[0, n], at)
        return carry

    def hidden_strip(n, carry):
        at = pl.ds(pl.multiple_of(n * 256, 256), 256)
        weight_strip(hn, dgu, wh, dwh_out, dw_sems.at[1, n], at)
        return carry

    pieces = [(down_strip, 0, strips // 2), (down_strip, strips // 2, strips)]
    pieces += [(hidden_strip, n, n + 2) for n in range(0, strips, 2)]
    for body, begin, end in pieces:
        lax.fori_loop(begin, end, body, 0)
        if calls:
            calls.pop(0)()
    for call in calls:
        call()
    line.last(grad_out)
    for number in range(max(cols - 2, 0), cols):
        out_copy(number % 2, order(number)).wait()

    def finish(n, carry):
        at = pl.ds(pl.multiple_of(n * 256, 256), 256)
        pltpu.make_async_copy(wd.at[at], dwd_out.at[at], dw_sems.at[0, n]).wait()
        pltpu.make_async_copy(wh.at[at], dwh_out.at[at], dw_sems.at[1, n]).wait()
        return carry

    lax.fori_loop(0, strips, finish, 0)
    line.finish()


def mlp(hn, dy, wh, wd, row_count, col_count, collective_id):
    steps = max(col_count - 1, 1)
    rows, width = hn.shape[0] // col_count, hn.shape[1]
    hidden = wd.shape[1]
    tile = min(512, hidden)
    wide = min(512, width)
    shape = (col_count, rows, width)
    vmem = pl.BlockSpec(memory_space=pltpu.VMEM)
    total = col_count * rows
    grad, y, dwh, dwd = pl.pallas_call(
        functools.partial(mlp_kernel, (row_count, col_count), tile, wide),
        out_shape=[
            jax.ShapeDtypeStruct((rows, width), f32),
            jax.ShapeDtypeStruct(shape, bf16),
            jax.ShapeDtypeStruct(wh.shape, bf16),
            jax.ShapeDtypeStruct(wd.shape, bf16),
        ],
        in_specs=[ANY] * 4,
        out_specs=[vmem, ANY, ANY, ANY],
        scratch_shapes=[
            pltpu.VMEM(shape, bf16),
            pltpu.VMEM(shape, bf16),
            pltpu.VMEM(wh.shape, bf16),
            pltpu.VMEM(wd.shape, bf16),
            pltpu.VMEM((col_count, rows, hidden), bf16),
            pltpu.VMEM((col_count, rows, 2 * hidden), bf16),
            pltpu.VMEM(shape, bf16),
            pltpu.VMEM((2, rows, width), bf16),
            pltpu.VMEM((2, steps, rows, width), bf16),
            pltpu.SemaphoreType.DMA((2, col_count)),
            pltpu.SemaphoreType.DMA((3, hidden // tile)),
            pltpu.SemaphoreType.DMA((2,)),
            pltpu.SemaphoreType.DMA((2, width // 256)),
            pltpu.SemaphoreType.DMA((2, steps)),
            pltpu.SemaphoreType.DMA((2, steps)),
        ],
        compiler_params=pltpu.CompilerParams(
            collective_id=collective_id, has_side_effects=True, vmem_limit_bytes=63 << 20
        ),
        cost_estimate=pl.CostEstimate(
            flops=2 * 9 * total * width * hidden,
            bytes_accessed=(wh.size + wd.size) * 4,
            transcendentals=total * hidden,
        ),
        name="feed_forward",
    )(hn.reshape(shape), dy.reshape(shape), wh, wd)
    return grad, y.reshape(total, width), dwh, dwd


class PlaneSum:
    def __init__(self, place, acc, held_core, held_second, held_first, sems):
        self.place, self.acc = place, acc
        self.held = (held_first, held_second, held_core)
        self.sends, self.recvs = sems
        self.half_deep = acc.shape[1] // 2

    @staticmethod
    def counts_of(sizes):
        na, nb, _ = sizes
        return max(na, nb) - 1, max((na - 1) * nb, (nb - 1) * na)

    @staticmethod
    def sem_count(sizes):
        na, nb, _ = sizes
        return na * nb - 1

    def axes(self, half):
        return (1, 0) if half == 0 else (0, 1)

    def counts(self, half):
        first, second = self.axes(half)
        return self.place.sizes[first], self.place.sizes[second]

    def part(self, half, i, j):
        first, second = self.axes(half)
        at = self.place.moved(second, j, self.place.moved(first, i))
        return self.acc.at[
            self.place.chip_of(at), pl.ds(half * self.half_deep, self.half_deep)
        ]

    def copy(self, half, kind, step, i):
        np_, nq = self.counts(half)
        if kind == 1:
            number = (step - 1) * np_ + i
            source = self.part(half, i, nq - step)
            target = self.held[1].at[half, number]
            sem = number
        else:
            source = self.part(half, np_ - step, 0)
            target = self.held[0].at[half, step - 1]
            sem = (nq - 1) * np_ + step - 1
        device = self.place.device(self.axes(half)[1 if kind == 1 else 0], 1)
        return remote(source, target, self.sends.at[half, sem], self.recvs.at[half, sem], device)

    def add(self, half, kind, step, i):
        np_, nq = self.counts(half)
        self.copy(half, kind, step, i).wait_recv()
        if kind == 1:
            add_rows(
                self.part(half, i, nq - step - 1), self.held[1].at[half, (step - 1) * np_ + i]
            )
        else:
            add_rows(self.part(half, np_ - step - 1, 0), self.held[0].at[half, step - 1])

    def first(self):
        for half in (0, 1):
            np_, nq = self.counts(half)
            if nq > 1:
                for i in range(np_ - 1, -1, -1):
                    self.copy(half, 1, 1, i).start()

    def second(self):
        for half in (0, 1):
            np_, nq = self.counts(half)
            for step in range(1, nq):
                for i in range(np_ - 1, -1, -1):
                    self.add(half, 1, step, i)
                    if step < nq - 1:
                        self.copy(half, 1, step + 1, i).start()
                    elif i == np_ - 1 and np_ > 1:
                        self.copy(half, 0, 1, 0).start()
            if nq == 1 and np_ > 1:
                self.copy(half, 0, 1, 0).start()

    def third(self):
        for half in (0, 1):
            np_, _ = self.counts(half)
            for step in range(1, np_):
                self.add(half, 0, step, 0)
                if step < np_ - 1:
                    self.copy(half, 0, step + 1, 0).start()

    def finish(self):
        for half in (0, 1):
            np_, nq = self.counts(half)
            for step in range(1, nq):
                for i in range(np_):
                    self.copy(half, 1, step, i).wait_send()
            for step in range(1, np_):
                self.copy(half, 0, step, 0).wait_send()


class SmallSum:
    def __init__(self, place, own, total, ring_held, line_held, ring_sems, line_sems):
        self.place, self.own, self.total = place, own, total
        self.held, self.sems = ring_held, ring_sems
        self.line = LineGather(
            place, total, lambda j: line_held.at[j], line_sems.at[0], line_sems.at[1]
        )
        self.line_held = line_held
        self.stages = []
        for axis in range(3):
            for step in range(1, place.sizes[axis]):
                self.stages.append(functools.partial(self.ring_send, axis, step))
                self.stages.append(functools.partial(self.ring_receive, axis, step))
            if place.sizes[axis] > 1:
                self.stages.append(functools.partial(self.ring_add, axis))
        self.stages.append(self.line_start)
        for step in range(1, place.cols):
            self.stages.append(functools.partial(self.line_step, step))
        self.stages.append(self.line_add)

    def begin(self):
        self.total[...] = self.own[...]

    def block(self, axis, step):
        at = self.place.moved(axis, -step)[axis]
        return self.held.at[axis, at]

    def ring_copy(self, axis, step):
        source = self.total if step == 1 else self.block(axis, step - 1)
        target = self.held.at[axis, self.place.moved(axis, 1 - step)[axis]]
        return remote(
            source,
            target,
            self.sems.at[0, axis, step - 1],
            self.sems.at[1, axis, step - 1],
            self.place.device(axis, 1),
        )

    def ring_send(self, axis, step):
        self.ring_copy(axis, step).start()

    def ring_receive(self, axis, step):
        ref = self.block(axis, step)
        remote(
            ref,
            ref,
            self.sems.at[0, axis, step - 1],
            self.sems.at[1, axis, step - 1],
            self.place.device(axis, 1),
        ).wait_recv()

    def ring_add(self, axis):
        for step in range(1, self.place.sizes[axis]):
            self.ring_copy(axis, step).wait_send()
        own_at = self.place.at[axis]
        total = None
        for at in range(self.place.sizes[axis]):
            term = jnp.where(own_at == at, self.total[...], self.held[axis, at])
            total = term if total is None else total + term
        self.total[...] = total

    def line_start(self):
        for way in (0, 1):
            self.line.send(way, 1)

    def line_step(self, step):
        for way in (0, 1):
            self.line.receive(way, step)

    def line_add(self):
        self.line.finish()
        total = None
        for at in range(self.place.cols):
            term = jnp.where(self.place.col == at, self.total[...], self.line_held[at])
            total = term if total is None else total + term
        self.total[...] = total


def sum_kernel(sizes, count, *refs):
    row_count, col_count = sizes
    terms = refs[:count]
    act_terms, small = refs[count : count + 2]
    outs = refs[count + 2 : 2 * count + 2]
    act_out, small_out = refs[2 * count + 2 : 2 * count + 4]
    refs = refs[2 * count + 4 :]
    per = [refs[6 * n : 6 * n + 6] for n in range(count)]
    act_held, load_sems, cs, cr, ps, pr, zs, zr = refs[6 * count : 6 * count + 8]
    ring_held, line_held, ring_sems, line_sems = refs[6 * count + 8 :]
    place = Place(row_count, col_count)
    cores = place.sizes[2]
    core = place.at[2]
    token_rows = act_out.shape[0]

    entries = [(n, nearby(place, k)) for k in range(col_count - 1, -1, -1) for n in range(count)]

    acts = LineSum(
        place,
        lambda j: act_terms.at[pl.ds(pl.multiple_of(j * token_rows, token_rows), token_rows)],
        act_held,
        zs.at[count],
        zr.at[count],
    )
    acc = [per[n][0] for n in range(count)]
    lines = [
        LineSum(
            place,
            lambda j, n=n: acc[n].at[j, place.chip_of(place.at)],
            per[n][4],
            zs.at[n],
            zr.at[n],
        )
        for n in range(count)
    ]

    def load(n, col):
        return pltpu.make_async_copy(
            terms[n].at[col, :, core], acc[n].at[col], load_sems.at[n, col]
        )

    def share(n, col):
        return remote(
            terms[n].at[col, :, lax.rem(core + 1, cores)],
            per[n][1].at[col],
            cs.at[n, col],
            cr.at[n, col],
            place.device(2, 1),
        )

    def inside(n, col):
        return PlaneSum(
            place,
            acc[n].at[col],
            per[n][1].at[col],
            per[n][2].at[col],
            per[n][3].at[col],
            (ps.at[n, col], pr.at[n, col]),
        )

    for n, col in entries:
        load(n, col).start()
    place.greet(True, True)
    if cores > 1:
        for n, col in entries:
            share(n, col).start()
    act_order = [nearby(place, k) for k in range(col_count - 1, 0, -1)]
    for col in act_order:
        acts.early(col, True)
    smalls = SmallSum(place, small, small_out, ring_held, line_held, ring_sems, line_sems)
    smalls.begin()
    stages = list(smalls.stages)

    def start(n, col):
        load(n, col).wait()
        if cores > 1:
            share(n, col).wait_recv()
            for chip in range(acc[n].shape[1]):
                add_rows(acc[n].at[col, chip], per[n][1].at[col, chip])
        inside(n, col).first()

    parts = [inside(n, col) for n, col in entries]
    final = len(entries) - count
    for number in range(len(entries) + 2):
        if number < len(entries):
            start(*entries[number])
        if 1 <= number <= len(entries):
            parts[number - 1].second()
        if 2 <= number:
            parts[number - 2].third()
            n, col = entries[number - 2]
            if number - 2 < final:
                lines[n].early(col, True)
                if number - 2 >= count:
                    lines[n].late(entries[number - 2 - count][1], True)
        if act_order and number % 2 == 1:
            acts.late(act_order.pop(0), True)
        if stages:
            stages.pop(0)()
    for stage in stages:
        stage()
    for col in act_order:
        acts.late(col, True)
    if col_count > 1:
        for n in range(count):
            lines[n].late(entries[final - count][1], True)
    for n in range(count):
        lines[n].last(per[n][5])
        pltpu.make_async_copy(per[n][5], outs[n], load_sems.at[n, place.col]).start()
    acts.last(act_out)
    for n in range(count):
        pltpu.make_async_copy(per[n][5], outs[n], load_sems.at[n, place.col]).wait()
    for number, (n, col) in enumerate(entries):
        if cores > 1:
            share(n, col).wait_send()
        parts[number].finish()
    for line in lines + [acts]:
        line.finish()


def sum_all(terms, act_terms, small, row_count, col_count, act_type):
    count = len(terms)
    sizes = plane_sizes(row_count)
    na, nb, nk = sizes
    chips = na * nb
    deep = terms[0].shape[1] // row_count
    steps = max(col_count - 1, 1)
    firsts, seconds = PlaneSum.counts_of(sizes)
    widths = [t.shape[2] for t in terms]
    token_rows = act_terms.shape[0] // col_count
    scratch = []
    for width in widths:
        scratch += [
            pltpu.VMEM((col_count, chips, deep, width), bf16),
            pltpu.VMEM((col_count, chips, deep, width), bf16),
            pltpu.VMEM((col_count, 2, max(seconds, 1), deep // 2, width), bf16),
            pltpu.VMEM((col_count, 2, max(firsts, 1), deep // 2, width), bf16),
            pltpu.VMEM((2, steps, deep, width), bf16),
            pltpu.VMEM((deep, width), f32),
        ]
    plane_sems = (count, col_count, 2, max(PlaneSum.sem_count(sizes), 1))
    scratch += [
        pltpu.VMEM((2, steps, token_rows, act_terms.shape[1]), bf16),
        pltpu.SemaphoreType.DMA((count, col_count)),
        pltpu.SemaphoreType.DMA((count, col_count)),
        pltpu.SemaphoreType.DMA((count, col_count)),
        pltpu.SemaphoreType.DMA(plane_sems),
        pltpu.SemaphoreType.DMA(plane_sems),
        pltpu.SemaphoreType.DMA((count + 1, 2, steps)),
        pltpu.SemaphoreType.DMA((count + 1, 2, steps)),
        pltpu.VMEM((3, max(sizes)) + small.shape, f32),
        pltpu.VMEM((col_count,) + small.shape, f32),
        pltpu.SemaphoreType.DMA((2, 3, max(max(sizes) - 1, 1))),
        pltpu.SemaphoreType.DMA((2, 2, steps)),
    ]
    vmem = pl.BlockSpec(memory_space=pltpu.VMEM)
    return pl.pallas_call(
        functools.partial(sum_kernel, (row_count, col_count), count),
        out_shape=[jax.ShapeDtypeStruct((deep, width), f32) for width in widths]
        + [
            jax.ShapeDtypeStruct((token_rows, act_terms.shape[1]), act_type),
            jax.ShapeDtypeStruct(small.shape, f32),
        ],
        in_specs=[ANY] * count + [vmem, vmem],
        out_specs=[ANY] * count + [vmem, vmem],
        scratch_shapes=scratch,
        compiler_params=pltpu.CompilerParams(
            collective_id=1, has_side_effects=True, vmem_limit_bytes=60 << 20
        ),
        cost_estimate=pl.CostEstimate(
            flops=0, bytes_accessed=sum(t.size for t in terms) * 4, transcendentals=0
        ),
        name="sum_weights",
    )(
        *[t.reshape(col_count, chips, nk, deep, t.shape[2]) for t in terms],
        act_terms,
        small,
    )


def rope_tables(position):
    indices = jnp.arange(HD // 2, dtype=f32)
    frequency = rope_base ** (-(indices * 2.0 / HD))
    wavelen = 2.0 * jnp.pi / frequency
    smooth = (8192.0 / wavelen - 1.0) / 3.0
    scaled = jnp.where(
        wavelen > 8192.0, frequency / 32.0, (1.0 - smooth) * frequency / 32.0 + smooth * frequency
    )
    frequency = jnp.where(wavelen < 2048.0, frequency, scaled)
    angles = position.astype(f32)[:, None] * frequency[None, :]
    return (jnp.cos(angles), jnp.sin(angles))


def rotate(values, cosine, sinusoid):
    halfway = values.shape[-1] // 2
    former = values[..., :halfway]
    latter = values[..., halfway:]
    cos_wide = cosine[:, None, :]
    sin_wide = sinusoid[:, None, :]
    return jnp.concatenate(
        [former * cos_wide - latter * sin_wide, latter * cos_wide + former * sin_wide], axis=-1
    )


def normalize(values, gain):
    scale = lax.rsqrt(jnp.mean(values * values, axis=1, keepdims=True) + epsilon)
    return ((values * scale * gain).astype(bf16), scale)


def norm_back(grad_in, values, scale, gain):
    weighted = grad_in * gain
    inner_sum = jnp.mean(weighted * values, axis=1, keepdims=True)
    return (
        scale * weighted - values * (scale * scale * scale) * inner_sum,
        jnp.sum(grad_in * values * scale, axis=0),
    )


def against(left, right):
    return lax.dot_general(left, right, (((1,), (1,)), ((), ())), preferred_element_type=f32)


def over_rows(left, right):
    return lax.dot_general(left, right, (((0,), (0,)), ((), ())), preferred_element_type=f32)


def matmul(left, right):
    return jnp.dot(left, right, preferred_element_type=f32)


def shift(values, step, col_count):
    if step > 0:
        pairs = [(i, i + step) for i in range(col_count - step)]
    else:
        pairs = [(i, i + step) for i in range(-step, col_count)]
    return lax.ppermute(values, "col", pairs)


def shards(
    tokens,
    seq_lens,
    attn_gain,
    query_weight,
    keyvalue_weight,
    output_weight,
    mlp_gain,
    hidden_weight,
    down_weight,
    out_grad,
):
    row_count, col_count = lax.axis_size("row"), lax.axis_size("col")
    local = tokens.shape[0]
    block_rows = local * col_count
    col = lax.axis_index("col")
    deep = query_weight.shape[0]
    width = tokens.shape[1]
    query_width = query_weight.shape[1]
    pairs = keyvalue_weight.shape[1]
    heads = query_width // HD
    group = heads // pairs
    hidden = down_weight.shape[1]
    back = min(-(-(SEQ_MAX - 1) // local), col_count - 1)

    lengths = seq_lens[0]
    finish = jnp.cumsum(lengths)
    indices = jnp.arange(block_rows, dtype=jnp.int32)
    passed = indices[:, None] >= finish[None, :]
    segment = jnp.sum(passed.astype(jnp.int32), axis=1, dtype=jnp.int32)
    position = indices - jnp.sum(jnp.where(passed, lengths[None, :], 0), axis=1, dtype=jnp.int32)
    own_position = lax.dynamic_slice(position, (col * local,), (local,))
    own_segment = lax.dynamic_slice(segment, (col * local,), (local,))
    padded = jnp.concatenate([jnp.full((back * local,), -1, jnp.int32), segment])
    key_segment = lax.dynamic_slice(padded, (col * local,), ((back + 1) * local,))
    key_index = jnp.arange((back + 1) * local, dtype=jnp.int32) - back * local
    query_index = jnp.arange(local, dtype=jnp.int32)
    allowed = (own_segment[:, None] == key_segment[None, :]) & (
        key_index[None, :] <= query_index[:, None]
    )
    cosine, sinusoid = rope_tables(own_position)
    gain_first = attn_gain.astype(f32)
    gain_second = mlp_gain.astype(f32)

    first_weight = jnp.concatenate(
        [query_weight, keyvalue_weight.reshape(deep, pairs * 2 * HD)], axis=1
    )
    full_first, full_output, full_down, rows_grad = gather_all(
        [first_weight, output_weight], [down_weight], out_grad, row_count, col_count
    )

    hidden_flat, full_first = lax.optimization_barrier(
        (hidden_weight.reshape(deep, 2 * hidden), full_first)
    )
    full_hidden = lax.all_gather(hidden_flat, "row", axis=0, tiled=True)

    inputs = tokens.astype(f32)
    normal_in, scale_in = normalize(inputs, gain_first)
    projected = jnp.stack([matmul(normal_in, full_first[z]) for z in range(col_count)])
    queries = (
        rotate(projected[:, :, :query_width].reshape(col_count, local, heads, HD), cosine, sinusoid)
        .astype(bf16)
        .reshape(col_count, local, pairs, group, HD)
    )
    keyvals = projected[:, :, query_width:].reshape(col_count, local, pairs, 2, HD)
    keyvals = jnp.stack(
        [rotate(keyvals[:, :, :, 0], cosine, sinusoid), keyvals[:, :, :, 1]], axis=3
    ).astype(bf16)
    chunks = [keyvals]
    for _ in range(back):
        chunks.insert(0, shift(chunks[0], 1, col_count))
    all_keyvals = jnp.concatenate(chunks, axis=1)
    key_rows, values = all_keyvals[:, :, :, 0], all_keyvals[:, :, :, 1]

    factor = HD ** (-0.5)
    scores = jnp.einsum("ztkgd,zskd->zkgts", queries, key_rows, preferred_element_type=f32) * factor
    scores = jnp.where(allowed, scores, blocked)
    summit = jnp.max(scores, axis=-1, keepdims=True)
    weights = jnp.exp(scores - summit)
    totals = jnp.sum(weights, axis=-1, keepdims=True)
    chances = weights / totals
    rounded = chances.astype(bf16)
    mixed = (
        jnp.einsum("zkgts,zskd->ztkgd", rounded, values, preferred_element_type=f32)
        .astype(bf16)
        .reshape(col_count, local, query_width)
    )
    attended = sum(against(mixed[z], full_output[z]) for z in range(col_count))
    hidden_in = inputs + attended
    normal_mid, scale_mid = normalize(hidden_in, gain_second)

    rows_mid = line_gather(normal_mid, row_count, col_count, 2)
    grad_mid, out_terms, grad_hidden_part, grad_down_part = mlp(
        rows_mid, rows_grad, full_hidden, full_down, row_count, col_count, 3
    )
    sum_hidden = lax.psum_scatter(grad_hidden_part, "row", scatter_dimension=0, tiled=True)
    sum_down = lax.psum_scatter(grad_down_part, "row", scatter_dimension=0, tiled=True)

    back_mid, gain_mid_part = norm_back(grad_mid, hidden_in, scale_mid, gain_second)
    grad_hidden_in = out_grad.astype(f32) + back_mid
    grad_low = grad_hidden_in.astype(bf16)
    grad_mixed = jnp.stack(
        [matmul(grad_low, full_output[z]).astype(bf16) for z in range(col_count)]
    ).reshape(col_count, local, pairs, group, HD)
    grad_output_part = jnp.stack(
        [over_rows(grad_low, mixed[z]).astype(bf16) for z in range(col_count)]
    )

    grad_chance = jnp.einsum("ztkgd,zskd->zkgts", grad_mixed, values, preferred_element_type=f32)
    centre = jnp.sum(chances * grad_chance, axis=-1, keepdims=True)
    grad_score = (chances * (grad_chance - centre)).astype(bf16)
    grad_query = (
        jnp.einsum("zkgts,zskd->ztkgd", grad_score, key_rows, preferred_element_type=f32) * factor
    )
    grad_key = (
        jnp.einsum("zkgts,ztkgd->zskd", grad_score, queries, preferred_element_type=f32) * factor
    )
    grad_value = jnp.einsum("zkgts,ztkgd->zskd", rounded, grad_mixed, preferred_element_type=f32)
    grad_keyval = jnp.stack([grad_key, grad_value], axis=3)
    carried = None
    for number in range(back + 1):
        part = grad_keyval[:, number * local : (number + 1) * local]
        if carried is not None:
            part = part + carried.astype(f32)
        if number < back:
            carried = shift(part.astype(bf16), -1, col_count)
    grad_query = rotate(
        grad_query.reshape(col_count, local, heads, HD), cosine, -sinusoid
    ).reshape(col_count, local, query_width)
    grad_keyval = jnp.stack(
        [rotate(part[:, :, :, 0], cosine, -sinusoid), part[:, :, :, 1]], axis=3
    ).reshape(col_count, local, pairs * 2 * HD)
    grad_first = jnp.concatenate([grad_query, grad_keyval], axis=2).astype(bf16)
    grad_first_part = jnp.stack(
        [over_rows(normal_in, grad_first[z]).astype(bf16) for z in range(col_count)]
    )
    grad_in = sum(against(grad_first[z], full_first[z]) for z in range(col_count))
    back_in, gain_in_part = norm_back(grad_in, inputs, scale_in, gain_first)
    grad_tokens = (grad_hidden_in + back_in).astype(bf16)
    gain_parts = jnp.concatenate([gain_in_part, gain_mid_part]).reshape(-1, 128)
    sum_first, sum_output, out_sum, gain_sums = sum_all(
        [grad_first_part, grad_output_part], out_terms, gain_parts, row_count, col_count, f32
    )
    block_out = hidden_in + out_sum
    gain_in_sum, gain_mid_sum = gain_sums.reshape(2, width)
    return (
        block_out.astype(bf16),
        grad_tokens,
        gain_in_sum,
        sum_first[:, :query_width],
        sum_first[:, query_width:].reshape(deep, pairs, 2 * HD),
        sum_output,
        gain_mid_sum,
        sum_hidden.astype(f32).reshape(deep, 2, hidden),
        sum_down.astype(f32),
    )


def solution(mesh):
    return jax.shard_map(
        shards,
        mesh=mesh,
        in_specs=(
            P(("row", "col"), None),
            P("row", None),
            P(),
            P("row", "col"),
            P("row", "col", None),
            P("row", "col"),
            P(),
            P("row", None, "col"),
            P("row", "col"),
            P(("row", "col"), None),
        ),
        out_specs=(
            P(("row", "col"), None),
            P(("row", "col"), None),
            P(),
            P("row", "col"),
            P("row", "col", None),
            P("row", "col"),
            P(),
            P("row", None, "col"),
            P("row", "col"),
        ),
        check_vma=False,
    )
```

```python
import functools

import jax
import jax.numpy as jnp
from jax import lax
from jax.experimental import pallas as pl
from jax.experimental.pallas import tpu as pltpu
from jax.sharding import PartitionSpec as P

HD = 64
SEQ_MAX = 512
MESH = pl.DeviceIdType.MESH
ANY = pl.BlockSpec(memory_space=pl.ANY)

epsilon = 1e-05
rope_base = 500000.0
blocked = -1e30
bf16 = jnp.bfloat16
f32 = jnp.float32


def plane_sizes(row_count):
    cores = 2 if row_count % 2 == 0 else 1
    chips = row_count // cores
    first = 2 if chips % 2 == 0 else 1
    return first, chips // first, cores


class Place:
    def __init__(self, row_count, col_count):
        self.rows, self.cols = row_count, col_count
        self.sizes = plane_sizes(row_count)
        na, nb, nk = self.sizes
        self.row = lax.axis_index("row")
        self.col = lax.axis_index("col")
        self.at = (self.row // (nb * nk), (self.row // nk) % nb, self.row % nk)

    def row_of(self, at):
        _, nb, nk = self.sizes
        return (at[0] * nb + at[1]) * nk + at[2]

    def chip_of(self, at):
        return at[0] * self.sizes[1] + at[1]

    def moved(self, axis, step, at=None):
        at = list(self.at if at is None else at)
        size = self.sizes[axis]
        at[axis] = lax.rem(at[axis] + (step % size), size)
        return tuple(at)

    def device(self, axis, step):
        return (self.row_of(self.moved(axis, step)), self.col)

    def greet(self, plane, line):
        barrier = pltpu.get_barrier_semaphore()
        count = 0
        if plane:
            for axis in range(3):
                size = self.sizes[axis]
                for step in {1 % size, (size - 1) % size} - {0}:
                    pl.semaphore_signal(
                        barrier, inc=1, device_id=self.device(axis, step), device_id_type=MESH
                    )
                    count += 1
        if line and self.cols > 1:
            for step, there in self.line_ways():

                @pl.when(there)
                def _(step=step):
                    pl.semaphore_signal(
                        barrier, inc=1, device_id=(self.row, self.col + step), device_id_type=MESH
                    )

        if line and self.cols > 1:
            last = self.cols - 1
            count = count + jnp.minimum(self.col, 1) + jnp.minimum(last - self.col, 1)
        if not isinstance(count, int) or count:
            pl.semaphore_wait(barrier, count)

    def line_ways(self):
        return ((1, self.col < self.cols - 1), (-1, self.col > 0))


def when(condition, action):
    if condition is None or condition is True:
        action()
    elif condition is False:
        pass
    else:
        pl.when(condition)(action)


def remote(src, dst, send_sem, recv_sem, device):
    return pltpu.make_async_remote_copy(
        src_ref=src,
        dst_ref=dst,
        send_sem=send_sem,
        recv_sem=recv_sem,
        device_id=device,
        device_id_type=MESH,
    )


class LineGather:
    def __init__(self, place, own, block, send_sems, recv_sems):
        self.place, self.own, self.block = place, own, block
        self.sends, self.recvs = send_sems, recv_sems

    def copy(self, way, step, origin):
        place = self.place
        source = self.own if step == 1 else self.block(origin)
        return remote(
            source,
            self.block(origin),
            self.sends.at[way, step - 1],
            self.recvs.at[way, step - 1],
            (place.row, place.col + (1, -1)[way]),
        )

    def sends_at(self, way, step):
        col, last = self.place.col, self.place.cols - 1
        if way == 0:
            return (col >= step - 1) & (col < last), col - (step - 1)
        return (col + step - 1 <= last) & (col > 0), col + (step - 1)

    def gets_at(self, way, step):
        col, last = self.place.col, self.place.cols - 1
        if way == 0:
            return col >= step, col - step
        return col + step <= last, col + step

    def send(self, way, step):
        condition, origin = self.sends_at(way, step)
        when(condition, lambda: self.copy(way, step, origin).start())

    def receive(self, way, step):
        condition, origin = self.gets_at(way, step)

        def action():
            self.copy(way, step, origin).wait_recv()

        when(condition, action)
        if step < self.place.cols - 1:
            self.send(way, step + 1)

    def finish(self):
        for step in range(1, self.place.cols):
            for way in (0, 1):
                condition, origin = self.sends_at(way, step)
                when(condition, lambda: self.copy(way, step, origin).wait_send())


class PlaneGather:
    def __init__(self, place, block, own, send_sems, recv_sems):
        self.place, self.block, self.own = place, block, own
        self.sends, self.recvs = send_sems, recv_sems

    @staticmethod
    def sem_count(sizes):
        na, nb, _ = sizes
        return 2 * na * nb - 1

    def axes(self, half):
        return (1, 0) if half == 0 else (0, 1)

    def counts(self, half):
        first, second = self.axes(half)
        return self.place.sizes[first], self.place.sizes[second]

    def origin(self, half, i, j, core_step=0):
        first, second = self.axes(half)
        at = self.place.moved(first, -i)
        at = self.place.moved(second, -j, at)
        if core_step:
            at = self.place.moved(2, 1, at)
        return self.place.row_of(at)

    def copy(self, half, kind, i, j):
        np_, nq = self.counts(half)
        if kind == 0:
            number, device = i - 1, self.place.device(self.axes(half)[0], 1)
        elif kind == 1:
            number = (np_ - 1) + i * (nq - 1) + (j - 1)
            device = self.place.device(self.axes(half)[1], 1)
        else:
            number = (np_ * nq - 1) + i * nq + j
            device = self.place.device(2, 1)
        return number, device

    def sender(self, half, kind, i, j):
        number, device = self.copy(half, kind, i, j)
        oi, oj = (i - 1, j) if kind == 0 else ((i, j - 1) if kind == 1 else (i, j))
        ref = self.block(self.origin(half, oi, oj), half)
        source = self.own(half) if (oi, oj) == (0, 0) else ref
        return remote(source, ref, self.sends.at[half, number], self.recvs.at[half, number], device)

    def receiver(self, half, kind, i, j):
        number, device = self.copy(half, kind, i, j)
        ref = self.block(self.origin(half, i, j, 1 if kind == 2 else 0), half)
        return remote(ref, ref, self.sends.at[half, number], self.recvs.at[half, number], device)

    def all_copies(self):
        for half in (0, 1):
            np_, nq = self.counts(half)
            for i in range(1, np_):
                yield half, 0, i, 0
            for i in range(np_):
                for j in range(1, nq):
                    yield half, 1, i, j
            if self.place.sizes[2] > 1:
                for i in range(np_):
                    for j in range(nq):
                        yield half, 2, i, j

    def share(self, half, i, j):
        if self.place.sizes[2] > 1:
            self.sender(half, 2, i, j).start()

    def first(self):
        for half in (0, 1):
            if self.counts(half)[0] > 1:
                self.sender(half, 0, 1, 0).start()
        for half in (0, 1):
            self.share(half, 0, 0)

    def second(self):
        for half in (0, 1):
            np_, nq = self.counts(half)
            for i in range(np_):
                if i > 0:
                    self.receiver(half, 0, i, 0).wait_recv()
                    if i < np_ - 1:
                        self.sender(half, 0, i + 1, 0).start()
                if nq > 1:
                    self.sender(half, 1, i, 1).start()
                if i > 0:
                    self.share(half, i, 0)

    def third(self):
        for half in (0, 1):
            np_, nq = self.counts(half)
            for j in range(1, nq):
                for i in range(np_):
                    self.receiver(half, 1, i, j).wait_recv()
                    if j < nq - 1:
                        self.sender(half, 1, i, j + 1).start()
                    self.share(half, i, j)

    def finish(self):
        for copy in self.all_copies():
            self.sender(*copy).wait_send()
            if copy[1] == 2:
                self.receiver(*copy).wait_recv()


def nearby(place, number):
    low, high = place.col, place.cols - 1 - place.col
    both = jnp.minimum(low, high)
    way = jnp.minimum(jnp.maximum(high - low, -1), 1)
    step = (number + 1) // 2 * (-1 if number % 2 else 1)
    paired = jnp.minimum(jnp.maximum(2 * both - number + 1, 0), 1)
    return place.col + paired * step + (1 - paired) * way * (number - both)


def gather_kernel(sizes, count, inner, *refs):
    row_count, col_count = sizes
    every = count + inner
    own, own_act = refs[:every], refs[every]
    full, full_act = refs[every + 1 : 2 * every + 1], refs[2 * every + 1]
    local_sems, zs, zr, ps, pr = refs[2 * every + 2 :]
    place = Place(row_count, col_count)
    place.greet(True, True)
    token_rows = own_act.shape[0]

    def at(n, col, row):
        deep = own[n].shape[0]
        if n < count:
            return full[n].at[col, pl.ds(row * deep, deep)]
        return full[n].at[pl.ds(row * deep, deep)]

    lines = [
        LineGather(place, own[n], lambda j, n=n: at(n, j, place.row), zs.at[n], zr.at[n])
        for n in range(count)
    ]
    acts = LineGather(
        place,
        own_act,
        lambda j: full_act.at[pl.ds(j * token_rows, token_rows)],
        zs.at[count],
        zr.at[count],
    )

    def keep(n):
        if n == every:
            return pltpu.make_async_copy(own_act, acts.block(place.col), local_sems.at[n])
        return pltpu.make_async_copy(own[n], at(n, place.col, place.row), local_sems.at[n])

    for n in range(every + 1):
        keep(n).start()
    for line in lines:
        for way in (0, 1):
            line.send(way, 1)

    def inside(n, col, near):
        deep = own[n].shape[0]
        half = deep // 2

        def block(row, number):
            rows = pl.ds(row * deep + number * half, half)
            return full[n].at[col, rows] if n < count else full[n].at[rows]

        def mine(number):
            return own[n].at[pl.ds(number * half, half)] if near else block(place.row, number)

        return PlaneGather(place, block, mine, ps.at[n, col], pr.at[n, col])

    entries = [(n, k) for k in range(col_count) for n in range(count)]
    entries += [(n, 0) for n in range(count, every)]
    parts = [inside(n, nearby(place, k), k == 0) for n, k in entries]
    act_steps = list(range(1, col_count))

    def act_step():
        if act_steps:
            for way in (0, 1):
                acts.receive(way, act_steps[0])
            act_steps.pop(0)

    for number in range(len(parts) + 2):
        if number < len(parts):
            n, k = entries[number]
            if n == 0 and k > 0:
                for line in lines:
                    for way in (0, 1):
                        line.receive(way, k)
                if k == 1:
                    for way in (0, 1):
                        acts.send(way, 1)
                if k >= 3:
                    act_step()
            parts[number].first()
        if 1 <= number <= len(parts):
            parts[number - 1].second()
        if 2 <= number:
            parts[number - 2].third()
        if number >= len(parts):
            act_step()
    while act_steps:
        act_step()
    for n in range(every + 1):
        keep(n).wait()
    for part in parts:
        part.finish()
    for line in lines + [acts]:
        line.finish()


def gather_all(weights, inner_weights, act, row_count, col_count):
    count, inner = len(weights), len(inner_weights)
    sizes = plane_sizes(row_count)
    steps = max(col_count - 1, 1)
    every = list(weights) + list(inner_weights)
    plane_sems = (count + inner, col_count, 2, PlaneGather.sem_count(sizes))
    moved = sum(w.size for w in weights) * row_count * col_count * 2
    return pl.pallas_call(
        functools.partial(gather_kernel, (row_count, col_count), count, inner),
        out_shape=[
            jax.ShapeDtypeStruct((col_count, row_count * w.shape[0], w.shape[1]), bf16)
            for w in weights
        ]
        + [
            jax.ShapeDtypeStruct((row_count * w.shape[0], w.shape[1]), bf16) for w in inner_weights
        ]
        + [jax.ShapeDtypeStruct((col_count * act.shape[0], act.shape[1]), bf16)],
        in_specs=[pl.BlockSpec(memory_space=pltpu.VMEM)] * (len(every) + 1),
        out_specs=[ANY] * (len(every) + 1),
        scratch_shapes=[
            pltpu.SemaphoreType.DMA((len(every) + 1,)),
            pltpu.SemaphoreType.DMA((count + 1, 2, steps)),
            pltpu.SemaphoreType.DMA((count + 1, 2, steps)),
            pltpu.SemaphoreType.DMA(plane_sems),
            pltpu.SemaphoreType.DMA(plane_sems),
        ],
        compiler_params=pltpu.CompilerParams(collective_id=0, has_side_effects=True),
        cost_estimate=pl.CostEstimate(flops=0, bytes_accessed=moved, transcendentals=0),
        name="gather_weights",
    )(*every, act)


def line_gather_kernel(sizes, own, full, local_sem, sends, recvs):
    place = Place(*sizes)
    place.greet(False, True)
    rows = own.shape[0]
    line = LineGather(place, own, lambda j: full.at[pl.ds(j * rows, rows)], sends, recvs)
    for way in (0, 1):
        line.send(way, 1)
    keep = pltpu.make_async_copy(own, full.at[pl.ds(place.col * rows, rows)], local_sem)
    keep.start()
    for step in range(1, place.cols):
        for way in (0, 1):
            line.receive(way, step)
    keep.wait()
    line.finish()


def line_gather(own, row_count, col_count, collective_id):
    steps = max(col_count - 1, 1)
    return pl.pallas_call(
        functools.partial(line_gather_kernel, (row_count, col_count)),
        out_shape=jax.ShapeDtypeStruct((col_count * own.shape[0], own.shape[1]), own.dtype),
        in_specs=[pl.BlockSpec(memory_space=pltpu.VMEM)],
        out_specs=ANY,
        scratch_shapes=[
            pltpu.SemaphoreType.DMA,
            pltpu.SemaphoreType.DMA((2, steps)),
            pltpu.SemaphoreType.DMA((2, steps)),
        ],
        compiler_params=pltpu.CompilerParams(collective_id=collective_id, has_side_effects=True),
        cost_estimate=pl.CostEstimate(
            flops=0, bytes_accessed=own.size * 2 * col_count, transcendentals=0
        ),
        name="gather_line",
    )(own)


def add_rows(target, source):
    rows = target.shape[0]
    piece = 32 if rows % 32 == 0 else 16

    def body(n, carry):
        at = pl.ds(pl.multiple_of(n * piece, piece), piece)
        target[at] = (target[at].astype(f32) + source[at].astype(f32)).astype(target.dtype)
        return carry

    lax.fori_loop(0, rows // piece, body, 0)


class LineSum:
    def __init__(self, place, own, held, send_sems, recv_sems):
        self.place, self.own, self.held = place, own, held
        self.sends, self.recvs = send_sems, recv_sems

    def distance(self, way, col):
        return col - self.place.col if way == 0 else self.place.col - col

    def feeds(self, way):
        return self.place.col > 0 if way == 0 else self.place.col < self.place.cols - 1

    def copy(self, way, distance, source):
        return remote(
            source,
            self.held.at[way, distance - 1],
            self.sends.at[way, distance - 1],
            self.recvs.at[way, distance - 1],
            (self.place.row, self.place.col + (1, -1)[way]),
        )

    def arrived(self, way, distance):
        ref = self.held.at[way, distance]
        return remote(
            ref,
            ref,
            self.sends.at[way, distance],
            self.recvs.at[way, distance],
            (self.place.row, self.place.col + (1, -1)[way]),
        )

    def early(self, col, allowed):
        for way in (0, 1):
            far = self.distance(way, col)

            @pl.when(allowed & (far > 0) & jnp.logical_not(self.feeds(way)))
            def _():
                self.copy(way, far, self.own(col)).start()

    def late(self, col, allowed):
        for way in (0, 1):
            far = self.distance(way, col)

            @pl.when(allowed & (far > 0) & self.feeds(way))
            def _():
                self.arrived(way, far).wait_recv()
                add_rows(self.own(col), self.held.at[way, far])
                self.copy(way, far, self.own(col)).start()

    def last(self, out):
        if self.place.cols > 1:
            for way in (0, 1):
                when(self.feeds(way), lambda: self.arrived(way, 0).wait_recv())
        own = self.own(self.place.col)
        rows = own.shape[0]
        piece = 32 if rows % 32 == 0 else 16
        has = [self.feeds(way) for way in (0, 1)]

        def body(n, carry):
            at = pl.ds(pl.multiple_of(n * piece, piece), piece)
            total = own[at].astype(f32)
            if self.place.cols > 1:
                for way in (0, 1):
                    term = self.held[way, 0, at].astype(f32)
                    total = total + jnp.where(has[way], term, 0.0)
            out[at] = total.astype(out.dtype)
            return carry

        lax.fori_loop(0, rows // piece, body, 0)

    def finish(self):
        for distance in range(1, self.place.cols):
            for way in (0, 1):
                col = self.place.col + (distance if way == 0 else -distance)
                there = col < self.place.cols if way == 0 else col >= 0
                when(there, lambda: self.copy(way, distance, self.own(col)).wait_send())


def dot_tokens(left, right):
    return lax.dot_general(left, right, (((0,), (0,)), ((), ())), preferred_element_type=f32)


def mlp_kernel(sizes, tile, wide, *refs):
    hn_in, dy_in, wh_in, wd_in, grad_out, y_out, dwh_out, dwd_out = refs[:8]
    hn, dy, wh, wd, act, dgu, terms, staged, held = refs[8:17]
    token_sems, weight_sems, y_sems, dw_sems, sends, recvs = refs[17:]
    place = Place(*sizes)
    cols = place.cols
    hidden = wd.shape[1]
    width = wd.shape[0]
    tiles = hidden // tile
    wides = width // wide
    tokens = hn.shape[1]
    line = LineSum(place, lambda j: terms.at[j], held, sends, recvs)

    def token_copies(j):
        return (
            pltpu.make_async_copy(hn_in.at[j], hn.at[j], token_sems.at[0, j]),
            pltpu.make_async_copy(dy_in.at[j], dy.at[j], token_sems.at[1, j]),
        )

    def part(number, base=0):
        return pl.ds(pl.multiple_of(base + number * tile, tile), tile)

    def weight_copies(f):
        gate, up = part(f), part(f, hidden)
        return (
            pltpu.make_async_copy(wh_in.at[:, gate], wh.at[:, gate], weight_sems.at[0, f]),
            pltpu.make_async_copy(wh_in.at[:, up], wh.at[:, up], weight_sems.at[1, f]),
            pltpu.make_async_copy(wd_in.at[:, gate], wd.at[:, gate], weight_sems.at[2, f]),
        )

    def order(number):
        return nearby(place, cols - 1 - number)

    for copy in token_copies(order(0)):
        copy.start()
    for f in range(tiles):
        for copy in weight_copies(f):
            copy.start()
    for number in range(1, cols):
        for copy in token_copies(order(number)):
            copy.start()
    place.greet(False, True)

    def out_copy(slot, j):
        return pltpu.make_async_copy(staged.at[slot], y_out.at[j], y_sems.at[slot])

    for number in range(cols):
        j = order(number)
        for copy in token_copies(j):
            copy.wait()

        def hidden_tile(f, carry):
            if number == 0:
                for copy in weight_copies(f):
                    copy.wait()
            gate_at, up_at = part(f), part(f, hidden)
            gate = matmul(hn[j], wh[:, gate_at])
            up = matmul(hn[j], wh[:, up_at])
            back = matmul(dy[j], wd[:, gate_at])
            sigmoid = jax.nn.sigmoid(gate)
            silu = gate * sigmoid
            act[j, :, gate_at] = (silu * up).astype(bf16)
            dgu[j, :, gate_at] = (back * up * sigmoid * (1.0 + gate * (1.0 - sigmoid))).astype(bf16)
            dgu[j, :, up_at] = (back * silu).astype(bf16)
            return carry

        lax.fori_loop(0, tiles, hidden_tile, 0)

        def grad_tile(n, carry):
            at = pl.ds(pl.multiple_of(n * wide, wide), wide)
            terms[j, :, at] = against(dgu[j], wh[at]).astype(bf16)
            return carry

        lax.fori_loop(0, wides, grad_tile, 0)
        line.early(j, True)
        slot = number % 2
        if number >= 2:
            out_copy(slot, order(number - 2)).wait()

        def y_tile(n, carry):
            at = pl.ds(pl.multiple_of(n * wide, wide), wide)
            staged[slot, :, at] = against(act[j], wd[at]).astype(bf16)
            return carry

        lax.fori_loop(0, wides, y_tile, 0)
        out_copy(slot, j).start()
        if number >= 2:
            line.late(order(number - 2), True)

    rest = [number for number in range(max(cols - 2, 0), cols - 1)]
    strips = width // 256
    calls = [functools.partial(line.late, order(number), True) for number in rest]

    def flat(ref):
        return ref[...].reshape(cols * tokens, ref.shape[2])

    def weight_strip(left, right, store, target, sem, at):
        columns = jnp.concatenate([left[j, :, at] for j in range(cols)], axis=0)
        store[at] = dot_tokens(columns, flat(right)).astype(bf16)
        pltpu.make_async_copy(store.at[at], target.at[at], sem).start()

    def down_strip(n, carry):
        at = pl.ds(pl.multiple_of(n * 256, 256), 256)
        weight_strip(dy, act, wd, dwd_out, dw_sems.at[0, n], at)
        return carry

    def hidden_strip(n, carry):
        at = pl.ds(pl.multiple_of(n * 256, 256), 256)
        weight_strip(hn, dgu, wh, dwh_out, dw_sems.at[1, n], at)
        return carry

    pieces = [(down_strip, 0, strips // 2), (down_strip, strips // 2, strips)]
    pieces += [(hidden_strip, n, n + 2) for n in range(0, strips, 2)]
    for body, begin, end in pieces:
        lax.fori_loop(begin, end, body, 0)
        if calls:
            calls.pop(0)()
    for call in calls:
        call()
    line.last(grad_out)
    for number in range(max(cols - 2, 0), cols):
        out_copy(number % 2, order(number)).wait()

    def finish(n, carry):
        at = pl.ds(pl.multiple_of(n * 256, 256), 256)
        pltpu.make_async_copy(wd.at[at], dwd_out.at[at], dw_sems.at[0, n]).wait()
        pltpu.make_async_copy(wh.at[at], dwh_out.at[at], dw_sems.at[1, n]).wait()
        return carry

    lax.fori_loop(0, strips, finish, 0)
    line.finish()


def mlp(hn, dy, wh, wd, row_count, col_count, collective_id):
    steps = max(col_count - 1, 1)
    rows, width = hn.shape[0] // col_count, hn.shape[1]
    hidden = wd.shape[1]
    tile = min(512, hidden)
    wide = min(512, width)
    shape = (col_count, rows, width)
    vmem = pl.BlockSpec(memory_space=pltpu.VMEM)
    total = col_count * rows
    grad, y, dwh, dwd = pl.pallas_call(
        functools.partial(mlp_kernel, (row_count, col_count), tile, wide),
        out_shape=[
            jax.ShapeDtypeStruct((rows, width), f32),
            jax.ShapeDtypeStruct(shape, bf16),
            jax.ShapeDtypeStruct(wh.shape, bf16),
            jax.ShapeDtypeStruct(wd.shape, bf16),
        ],
        in_specs=[ANY] * 4,
        out_specs=[vmem, ANY, ANY, ANY],
        scratch_shapes=[
            pltpu.VMEM(shape, bf16),
            pltpu.VMEM(shape, bf16),
            pltpu.VMEM(wh.shape, bf16),
            pltpu.VMEM(wd.shape, bf16),
            pltpu.VMEM((col_count, rows, hidden), bf16),
            pltpu.VMEM((col_count, rows, 2 * hidden), bf16),
            pltpu.VMEM(shape, bf16),
            pltpu.VMEM((2, rows, width), bf16),
            pltpu.VMEM((2, steps, rows, width), bf16),
            pltpu.SemaphoreType.DMA((2, col_count)),
            pltpu.SemaphoreType.DMA((3, hidden // tile)),
            pltpu.SemaphoreType.DMA((2,)),
            pltpu.SemaphoreType.DMA((2, width // 256)),
            pltpu.SemaphoreType.DMA((2, steps)),
            pltpu.SemaphoreType.DMA((2, steps)),
        ],
        compiler_params=pltpu.CompilerParams(
            collective_id=collective_id, has_side_effects=True, vmem_limit_bytes=63 << 20
        ),
        cost_estimate=pl.CostEstimate(
            flops=2 * 9 * total * width * hidden,
            bytes_accessed=(wh.size + wd.size) * 4,
            transcendentals=total * hidden,
        ),
        name="feed_forward",
    )(hn.reshape(shape), dy.reshape(shape), wh, wd)
    return grad, y.reshape(total, width), dwh, dwd


class PlaneSum:
    def __init__(self, place, acc, held_core, held_second, held_first, sems):
        self.place, self.acc = place, acc
        self.held = (held_first, held_second, held_core)
        self.sends, self.recvs = sems
        self.half_deep = acc.shape[1] // 2

    @staticmethod
    def counts_of(sizes):
        na, nb, _ = sizes
        return max(na, nb) - 1, max((na - 1) * nb, (nb - 1) * na)

    @staticmethod
    def sem_count(sizes):
        na, nb, _ = sizes
        return na * nb - 1

    def axes(self, half):
        return (1, 0) if half == 0 else (0, 1)

    def counts(self, half):
        first, second = self.axes(half)
        return self.place.sizes[first], self.place.sizes[second]

    def part(self, half, i, j):
        first, second = self.axes(half)
        at = self.place.moved(second, j, self.place.moved(first, i))
        return self.acc.at[
            self.place.chip_of(at), pl.ds(half * self.half_deep, self.half_deep)
        ]

    def copy(self, half, kind, step, i):
        np_, nq = self.counts(half)
        if kind == 1:
            number = (step - 1) * np_ + i
            source = self.part(half, i, nq - step)
            target = self.held[1].at[half, number]
            sem = number
        else:
            source = self.part(half, np_ - step, 0)
            target = self.held[0].at[half, step - 1]
            sem = (nq - 1) * np_ + step - 1
        device = self.place.device(self.axes(half)[1 if kind == 1 else 0], 1)
        return remote(source, target, self.sends.at[half, sem], self.recvs.at[half, sem], device)

    def add(self, half, kind, step, i):
        np_, nq = self.counts(half)
        self.copy(half, kind, step, i).wait_recv()
        if kind == 1:
            add_rows(
                self.part(half, i, nq - step - 1), self.held[1].at[half, (step - 1) * np_ + i]
            )
        else:
            add_rows(self.part(half, np_ - step - 1, 0), self.held[0].at[half, step - 1])

    def first(self):
        for half in (0, 1):
            np_, nq = self.counts(half)
            if nq > 1:
                for i in range(np_ - 1, -1, -1):
                    self.copy(half, 1, 1, i).start()

    def second(self):
        for half in (0, 1):
            np_, nq = self.counts(half)
            for step in range(1, nq):
                for i in range(np_ - 1, -1, -1):
                    self.add(half, 1, step, i)
                    if step < nq - 1:
                        self.copy(half, 1, step + 1, i).start()
                    elif i == np_ - 1 and np_ > 1:
                        self.copy(half, 0, 1, 0).start()
            if nq == 1 and np_ > 1:
                self.copy(half, 0, 1, 0).start()

    def third(self):
        for half in (0, 1):
            np_, _ = self.counts(half)
            for step in range(1, np_):
                self.add(half, 0, step, 0)
                if step < np_ - 1:
                    self.copy(half, 0, step + 1, 0).start()

    def finish(self):
        for half in (0, 1):
            np_, nq = self.counts(half)
            for step in range(1, nq):
                for i in range(np_):
                    self.copy(half, 1, step, i).wait_send()
            for step in range(1, np_):
                self.copy(half, 0, step, 0).wait_send()


def core_rows(place, chip, step, deep):
    cores = place.sizes[2]
    row = chip * cores + lax.rem(place.at[2] + step, cores)
    return pl.ds(pl.multiple_of(row * deep, deep), deep)


class InnerSum:
    def __init__(self, place, terms, out, chunk, refs):
        self.place, self.terms, self.out, self.chunk = place, terms, out, chunk
        self.acc, self.core_held, self.second, self.first, self.staged = refs[:5]
        self.load_sems, self.core_sems, self.plane_sems, self.out_sems = refs[5:]
        self.count = out.shape[1] // chunk
        self.ahead = min(3, self.count)

    @staticmethod
    def scratch(sizes, deep, width, chunk):
        na, nb, _ = sizes
        count = width // chunk
        firsts, seconds = PlaneSum.counts_of(sizes)
        sems = (2, count, 2, max(PlaneSum.sem_count(sizes), 1))
        return [
            pltpu.VMEM((count, na * nb, deep, chunk), bf16),
            pltpu.VMEM((count, na * nb, deep, chunk), bf16),
            pltpu.VMEM((count, 2, max(seconds, 1), deep // 2, chunk), bf16),
            pltpu.VMEM((count, 2, max(firsts, 1), deep // 2, chunk), bf16),
            pltpu.VMEM((2, deep, chunk), f32),
            pltpu.SemaphoreType.DMA((count,)),
            pltpu.SemaphoreType.DMA((2, count)),
            pltpu.SemaphoreType.DMA(sems),
            pltpu.SemaphoreType.DMA((2,)),
        ]

    def columns(self, e):
        return pl.ds(pl.multiple_of(e * self.chunk, self.chunk), self.chunk)

    def load(self, e):
        source = self.terms.at[:, self.place.at[2], :, self.columns(e)]
        return pltpu.make_async_copy(source, self.acc.at[e], self.load_sems.at[e])

    def share(self, e):
        other = lax.rem(self.place.at[2] + 1, self.place.sizes[2])
        return remote(
            self.terms.at[:, other, :, self.columns(e)],
            self.core_held.at[e],
            self.core_sems.at[0, e],
            self.core_sems.at[1, e],
            self.place.device(2, 1),
        )

    def inside(self, e):
        return PlaneSum(
            self.place,
            self.acc.at[e],
            self.core_held.at[e],
            self.second.at[e],
            self.first.at[e],
            (self.plane_sems.at[0, e], self.plane_sems.at[1, e]),
        )

    def out_copy(self, e):
        slot = lax.rem(e, 2)
        return pltpu.make_async_copy(
            self.staged.at[slot], self.out.at[:, self.columns(e)], self.out_sems.at[slot]
        )

    def prepare(self, e):
        self.load(e).start()
        if self.place.sizes[2] > 1:
            self.share(e).start()

    def begin(self):
        for e in range(self.ahead):
            self.prepare(e)

    def start(self, e):
        when(e + self.ahead < self.count, lambda: self.prepare(e + self.ahead))
        self.load(e).wait()
        if self.place.sizes[2] > 1:
            self.share(e).wait_recv()
            for chip in range(self.acc.shape[1]):
                add_rows(self.acc.at[e, chip], self.core_held.at[e, chip])
        self.inside(e).first()

    def middle(self, e):
        self.inside(e).second()

    def close(self, e):
        self.inside(e).third()
        when(e >= 2, lambda: self.out_copy(e - 2).wait())
        slot = lax.rem(e, 2)
        own = self.acc.at[e, self.place.chip_of(self.place.at)]
        self.staged[slot] = own[...].astype(f32)
        self.out_copy(e).start()

    def tick(self, t):
        when(t < self.count, lambda: self.start(t))
        when((t >= 1) & (t - 1 < self.count), lambda: self.middle(t - 1))
        when((t >= 2) & (t - 2 < self.count), lambda: self.close(t - 2))

    def finish(self):
        for e in range(max(self.count - 2, 0), self.count):
            self.out_copy(e).wait()

        def done(e, carry):
            if self.place.sizes[2] > 1:
                self.share(e).wait_send()
            self.inside(e).finish()
            return carry

        lax.fori_loop(0, self.count, done, 0)


class SmallSum:
    def __init__(self, place, own, total, ring_held, line_held, ring_sems, line_sems):
        self.place, self.own, self.total = place, own, total
        self.held, self.sems = ring_held, ring_sems
        self.line = LineGather(
            place, total, lambda j: line_held.at[j], line_sems.at[0], line_sems.at[1]
        )
        self.line_held = line_held
        self.stages = []
        for axis in range(3):
            for step in range(1, place.sizes[axis]):
                self.stages.append(functools.partial(self.ring_send, axis, step))
                self.stages.append(functools.partial(self.ring_receive, axis, step))
            if place.sizes[axis] > 1:
                self.stages.append(functools.partial(self.ring_add, axis))
        self.stages.append(self.line_start)
        for step in range(1, place.cols):
            self.stages.append(functools.partial(self.line_step, step))
        self.stages.append(self.line_add)

    def begin(self):
        self.total[...] = self.own[...]

    def block(self, axis, step):
        at = self.place.moved(axis, -step)[axis]
        return self.held.at[axis, at]

    def ring_copy(self, axis, step):
        source = self.total if step == 1 else self.block(axis, step - 1)
        target = self.held.at[axis, self.place.moved(axis, 1 - step)[axis]]
        return remote(
            source,
            target,
            self.sems.at[0, axis, step - 1],
            self.sems.at[1, axis, step - 1],
            self.place.device(axis, 1),
        )

    def ring_send(self, axis, step):
        self.ring_copy(axis, step).start()

    def ring_receive(self, axis, step):
        ref = self.block(axis, step)
        remote(
            ref,
            ref,
            self.sems.at[0, axis, step - 1],
            self.sems.at[1, axis, step - 1],
            self.place.device(axis, 1),
        ).wait_recv()

    def ring_add(self, axis):
        for step in range(1, self.place.sizes[axis]):
            self.ring_copy(axis, step).wait_send()
        own_at = self.place.at[axis]
        total = None
        for at in range(self.place.sizes[axis]):
            term = jnp.where(own_at == at, self.total[...], self.held[axis, at])
            total = term if total is None else total + term
        self.total[...] = total

    def line_start(self):
        for way in (0, 1):
            self.line.send(way, 1)

    def line_step(self, step):
        for way in (0, 1):
            self.line.receive(way, step)

    def line_add(self):
        self.line.finish()
        total = None
        for at in range(self.place.cols):
            term = jnp.where(self.place.col == at, self.total[...], self.line_held[at])
            total = term if total is None else total + term
        self.total[...] = total


def sum_kernel(sizes, count, chunk, *refs):
    row_count, col_count = sizes
    place = Place(row_count, col_count)
    cores = place.sizes[2]
    lefts, rights = refs[: cores * count], refs[cores * count : 2 * cores * count]
    refs = refs[2 * cores * count :]
    inner_terms, act_terms, small = refs[:3]
    outs = refs[3 : 3 + count]
    inner_out, act_out, small_out = refs[3 + count : 6 + count]
    refs = refs[6 + count :]
    per = [refs[7 * n : 7 * n + 7] for n in range(count)]
    inner = InnerSum(place, inner_terms, inner_out, chunk, refs[7 * count : 7 * count + 9])
    act_held, load_sems, out_sems, ps, pr, zs, zr = refs[7 * count + 9 : 7 * count + 16]
    ring_held, line_held, ring_sems, line_sems, chip_sems = refs[7 * count + 16 :]
    token_rows = act_out.shape[0]

    entries = [(n, nearby(place, k)) for k in range(col_count - 1, -1, -1) for n in range(count)]

    acts = LineSum(
        place,
        lambda j: act_terms.at[pl.ds(pl.multiple_of(j * token_rows, token_rows), token_rows)],
        act_held,
        zs.at[count],
        zr.at[count],
    )
    acc = [per[n][0] for n in range(count)]
    lines = [
        LineSum(
            place,
            lambda j, n=n: acc[n].at[j, place.chip_of(place.at)],
            per[n][3],
            zs.at[n],
            zr.at[n],
        )
        for n in range(count)
    ]
    tokens = lefts[0].shape[0]
    chips, deep = acc[0].shape[1:3]

    def loads():
        for n in range(count):
            left, right = per[n][5], per[n][6]
            for k in range(cores):
                at = pl.ds(k * tokens, tokens)
                if k == 0:
                    for chip in range(chips):
                        yield pltpu.make_async_copy(
                            lefts[n * cores].at[:, core_rows(place, chip, 0, deep)],
                            left.at[at, pl.ds(chip * deep, deep)],
                            chip_sems.at[n, chip],
                        )
                else:
                    yield pltpu.make_async_copy(
                        lefts[n * cores + k], left.at[at], load_sems.at[0, n * cores + k]
                    )
                yield pltpu.make_async_copy(
                    rights[n * cores + k], right.at[:, at], load_sems.at[1, n * cores + k]
                )

    for copy in loads():
        copy.start()
    place.greet(True, True)
    inner.begin()
    act_order = [nearby(place, k) for k in range(col_count - 1, 0, -1)]
    act_early, act_late = list(act_order), list(act_order)
    acts.early(act_early.pop(0), True) if act_early else None
    smalls = SmallSum(place, small, small_out, ring_held, line_held, ring_sems, line_sems)
    smalls.begin()
    stages = list(smalls.stages)
    for copy in loads():
        copy.wait()

    def inside(n, col):
        return PlaneSum(
            place,
            acc[n].at[col],
            None,
            per[n][1].at[col],
            per[n][2].at[col],
            (ps.at[n, col], pr.at[n, col]),
        )

    parts = [inside(n, col) for n, col in entries]
    final = len(entries) - count
    total = len(entries) + inner.count

    def start(number):
        if number >= len(entries):
            inner.start(number - len(entries))
            return
        n, col = entries[number]
        left, right = per[n][5], per[n][6]
        deep = acc[n].shape[2]

        def chip_rows(chip, carry):
            at = pl.ds(pl.multiple_of(chip * deep, deep), deep)
            acc[n][col, chip] = dot_tokens(left[:, at], right[col]).astype(bf16)
            return carry

        lax.fori_loop(0, acc[n].shape[1], chip_rows, 0)
        parts[number].first()

    def middle(number):
        if number >= len(entries):
            inner.middle(number - len(entries))
        else:
            parts[number].second()

    def out_copy(n):
        return pltpu.make_async_copy(per[n][4], outs[n], out_sems.at[n])

    def close(number):
        if number >= len(entries):
            inner.close(number - len(entries))
            if number == len(entries) + 1 or total == len(entries) + 1:
                finish_lines()
            return
        parts[number].third()
        n, col = entries[number]
        if number < final:
            lines[n].early(col, True)
        if number >= 2 * count:
            waiting.pop(0)()

    waiting = [functools.partial(lines[n].late, col, True) for n, col in entries[:final]]

    def finish_lines():
        while waiting:
            waiting.pop(0)()
        for n in range(count):
            lines[n].last(per[n][4])
            out_copy(n).start()

    for number in range(total + 2):
        if number < total:
            start(number)
        if 1 <= number <= total:
            middle(number - 1)
        if 2 <= number:
            close(number - 2)
        if act_early and number % 2 == 1:
            acts.early(act_early.pop(0), True)
        if act_late and number >= 3 and number % 2 == 1:
            acts.late(act_late.pop(0), True)
        if stages:
            stages.pop(0)()
    for stage in stages:
        stage()
    for col in act_early:
        acts.early(col, True)
    for col in act_late:
        acts.late(col, True)
    acts.last(act_out)
    for n in range(count):
        out_copy(n).wait()
    for part in parts:
        part.finish()
    inner.finish()
    for line in lines + [acts]:
        line.finish()


def sum_all(lefts, rights, inner_terms, act_terms, small, row_count, col_count, act_type):
    count = len(rights)
    sizes = plane_sizes(row_count)
    na, nb, nk = sizes
    chips = na * nb
    tokens = lefts[0][0].shape[0]
    deep = lefts[0][0].shape[1] // row_count
    steps = max(col_count - 1, 1)
    firsts, seconds = PlaneSum.counts_of(sizes)
    widths = [right[0].shape[2] for right in rights]
    token_rows = act_terms.shape[0] // col_count
    inner_width = inner_terms.shape[1]
    chunk = min(512, inner_width)
    scratch = []
    for width in widths:
        scratch += [
            pltpu.VMEM((col_count, chips, deep, width), bf16),
            pltpu.VMEM((col_count, 2, max(seconds, 1), deep // 2, width), bf16),
            pltpu.VMEM((col_count, 2, max(firsts, 1), deep // 2, width), bf16),
            pltpu.VMEM((2, steps, deep, width), bf16),
            pltpu.VMEM((deep, width), f32),
            pltpu.VMEM((nk * tokens, chips * deep), bf16),
            pltpu.VMEM((col_count, nk * tokens, width), bf16),
        ]
    scratch += InnerSum.scratch(sizes, deep, inner_width, chunk)
    plane_sems = (count, col_count, 2, max(PlaneSum.sem_count(sizes), 1))
    scratch += [
        pltpu.VMEM((2, steps, token_rows, act_terms.shape[1]), bf16),
        pltpu.SemaphoreType.DMA((2, count * nk)),
        pltpu.SemaphoreType.DMA((count,)),
        pltpu.SemaphoreType.DMA(plane_sems),
        pltpu.SemaphoreType.DMA(plane_sems),
        pltpu.SemaphoreType.DMA((count + 1, 2, steps)),
        pltpu.SemaphoreType.DMA((count + 1, 2, steps)),
        pltpu.VMEM((3, max(sizes)) + small.shape, f32),
        pltpu.VMEM((col_count,) + small.shape, f32),
        pltpu.SemaphoreType.DMA((2, 3, max(max(sizes) - 1, 1))),
        pltpu.SemaphoreType.DMA((2, 2, steps)),
        pltpu.SemaphoreType.DMA((count, chips)),
    ]
    vmem = pl.BlockSpec(memory_space=pltpu.VMEM)
    flops = sum(2 * nk * tokens * chips * deep * width * col_count for width in widths)
    return pl.pallas_call(
        functools.partial(sum_kernel, (row_count, col_count), count, chunk),
        out_shape=[jax.ShapeDtypeStruct((deep, width), f32) for width in widths]
        + [
            jax.ShapeDtypeStruct((deep, inner_width), f32),
            jax.ShapeDtypeStruct((token_rows, act_terms.shape[1]), act_type),
            jax.ShapeDtypeStruct(small.shape, f32),
        ],
        in_specs=[ANY] * (2 * count * nk) + [ANY, vmem, vmem],
        out_specs=[ANY] * (count + 1) + [vmem, vmem],
        scratch_shapes=scratch,
        compiler_params=pltpu.CompilerParams(
            collective_id=1, has_side_effects=True, vmem_limit_bytes=63 << 20
        ),
        cost_estimate=pl.CostEstimate(
            flops=flops, bytes_accessed=inner_terms.size * 2, transcendentals=0
        ),
        name="sum_weights",
    )(
        *[left for pair in lefts for left in pair],
        *[right for pair in rights for right in pair],
        inner_terms.reshape(chips, nk, deep, inner_width),
        act_terms,
        small,
    )


LANES = 2 * HD


def lower_lanes():
    return lax.broadcasted_iota(jnp.int32, (1, LANES), 1) < HD


def rope_lanes(values, cosine, sinusoid):
    lane = lax.broadcasted_iota(jnp.int32, (1, LANES), 1)
    other = jnp.where(
        lane % HD < HD // 2,
        pltpu.roll(values, LANES - HD // 2, 1),
        pltpu.roll(values, HD // 2, 1),
    )
    return values * cosine + other * sinusoid


def head_at(tile, head, upper):
    if (head % 2 == 1) != upper:
        tile = pltpu.roll(tile, HD, 1)
    keep = lower_lanes()
    if upper:
        keep = jnp.logical_not(keep)
    return jnp.where(keep, tile, 0.0)


def tile_of(head):
    return slice(head // 2 * LANES, head // 2 * LANES + LANES)


def pair_tile(even, odd, upper):
    if upper:
        even = pltpu.roll(even, HD, 1)
    else:
        odd = pltpu.roll(odd, HD, 1)
    return jnp.where(lower_lanes(), even, odd)


def attend_kernel(sizes, heads, group, back, *refs):
    xn, x, wf_in, wo_in, bias, cosq, sinq, coskv, sinkv, gain = refs[:10]
    q_out, kv_out, mixed_out, lse_out, hidden, hn = refs[10:16]
    q, kv, mixed, lse, wf, wo, w_sems, o_sems, sends, recvs = refs[16:]
    place = Place(*sizes)
    cols, col = place.cols, place.col
    tokens = xn.shape[0]
    query_width = heads * HD
    own_rows = pl.ds(back * tokens, tokens)
    pairs = heads // group

    def weight_copies(z):
        return (
            pltpu.make_async_copy(wf_in.at[z], wf.at[z], w_sems.at[0, z]),
            pltpu.make_async_copy(wo_in.at[z], wo.at[z], w_sems.at[1, z]),
        )

    for number in (0, 1):
        for z in range(cols):
            weight_copies(z)[number].start()
    for step in range(1, back + 1):

        @pl.when(col < step)
        def _():
            kv[:, (back - step) * tokens : (back - step + 1) * tokens] = jnp.zeros(
                (cols, tokens, kv.shape[2]), bf16
            )

    place.greet(False, True)

    def hop(z, step):
        source = kv.at[z, pl.ds((back - step + 1) * tokens, tokens)]
        target = kv.at[z, pl.ds((back - step) * tokens, tokens)]
        return remote(
            source, target, sends.at[step - 1, z], recvs.at[step - 1, z], (place.row, col + 1)
        )

    def goes(step):
        return (col < cols - 1) & (col >= step - 1)

    def send(z, step):
        pl.when(goes(step))(lambda: hop(z, step).start())

    def receive(z, step):
        ref = kv.at[z, pl.ds((back - step) * tokens, tokens)]

        @pl.when(col >= step)
        def _():
            remote(
                ref, ref, sends.at[step - 1, z], recvs.at[step - 1, z], (place.row, col + 1)
            ).wait_recv()

    def project(z, carry):
        weight_copies(z)[0].wait()
        pre = matmul(xn[...], wf[z])
        for n in range(query_width // LANES):
            at = slice(n * LANES, (n + 1) * LANES)
            q[z, :, at] = rope_lanes(pre[:, at], cosq[...], sinq[...]).astype(bf16)
        for n in range(pairs):
            at = slice(n * LANES, (n + 1) * LANES)
            tile = pre[:, query_width + n * LANES : query_width + (n + 1) * LANES]
            kv[z, own_rows, at] = rope_lanes(tile, coskv[...], sinkv[...]).astype(bf16)
        if back > 0:
            send(z, 1)
        return carry

    lax.fori_loop(0, cols, project, 0)
    for step in range(1, back):
        for z in range(cols):
            receive(z, step)
            send(z, step + 1)

    def attend(z, carry):
        if back > 0:
            receive(z, back)
        lane = lax.broadcasted_iota(jnp.int32, (1, LANES), 1)
        logs = jnp.zeros((tokens, LANES), f32)
        outs = []
        for head in range(heads):
            pair = head // group
            keyval = kv[z, :, pair * LANES : (pair + 1) * LANES]
            query = head_at(q[z, :, tile_of(head)].astype(f32), head, False) * HD**-0.5
            scores = against(query.astype(bf16), keyval) + bias[...]
            summit = jnp.max(scores, axis=1, keepdims=True)
            weights = jnp.exp(scores - summit)
            total = jnp.sum(weights, axis=1, keepdims=True)
            chances = (weights * (1.0 / total)).astype(bf16)
            outs.append(matmul(chances, keyval))
            logs = jnp.where(lane == head, summit + jnp.log(total), logs)
            if head % 2 == 1:
                mixed[z, :, tile_of(head)] = pair_tile(outs[-2], outs[-1], True).astype(bf16)
        lse[z] = jnp.transpose(logs)[:heads]
        return carry

    lax.fori_loop(0, cols, attend, 0)
    outputs = [
        pltpu.make_async_copy(source, target, o_sems.at[n])
        for n, (source, target) in enumerate(
            ((q, q_out), (kv, kv_out), (mixed, mixed_out), (lse, lse_out))
        )
    ]
    for copy in outputs:
        copy.start()
    hidden[...] = x[...].astype(f32)

    def project_out(z, carry):
        weight_copies(z)[1].wait()
        hidden[...] += against(mixed[z], wo[z])
        return carry

    lax.fori_loop(0, cols, project_out, 0)
    total = hidden[...]
    scale = lax.rsqrt(jnp.mean(total * total, axis=1, keepdims=True) + epsilon)
    hn[...] = (total * scale * gain[...]).astype(bf16)
    for copy in outputs:
        copy.wait()
    for step in range(1, back + 1):
        for z in range(cols):
            pl.when(goes(step))(lambda: hop(z, step).wait_send())


def attend(xn, x, wf, wo, bias, tables, gain, heads, group, back, row_count, col_count, cid):
    tokens, width = xn.shape
    query_width = heads * HD
    kv_shape = (col_count, (back + 1) * tokens, heads // group * LANES)
    q_shape = (col_count, tokens, query_width)
    lse_shape = (col_count, heads, tokens)
    vmem = pl.BlockSpec(memory_space=pltpu.VMEM)
    keys = (back + 1) * tokens
    return pl.pallas_call(
        functools.partial(attend_kernel, (row_count, col_count), heads, group, back),
        out_shape=[
            jax.ShapeDtypeStruct(q_shape, bf16),
            jax.ShapeDtypeStruct(kv_shape, bf16),
            jax.ShapeDtypeStruct(q_shape, bf16),
            jax.ShapeDtypeStruct(lse_shape, f32),
            jax.ShapeDtypeStruct((tokens, width), f32),
            jax.ShapeDtypeStruct((tokens, width), bf16),
        ],
        in_specs=[vmem, vmem, ANY, ANY] + [vmem] * 6,
        out_specs=[ANY] * 4 + [vmem] * 2,
        scratch_shapes=[
            pltpu.VMEM(q_shape, bf16),
            pltpu.VMEM(kv_shape, bf16),
            pltpu.VMEM(q_shape, bf16),
            pltpu.VMEM(lse_shape, f32),
            pltpu.VMEM(wf.shape, bf16),
            pltpu.VMEM(wo.shape, bf16),
            pltpu.SemaphoreType.DMA((2, col_count)),
            pltpu.SemaphoreType.DMA((4,)),
            pltpu.SemaphoreType.DMA((max(back, 1), col_count)),
            pltpu.SemaphoreType.DMA((max(back, 1), col_count)),
        ],
        compiler_params=pltpu.CompilerParams(
            collective_id=cid, has_side_effects=True, vmem_limit_bytes=56 << 20
        ),
        cost_estimate=pl.CostEstimate(
            flops=2 * tokens * (wf.size + wo.size) + 4 * col_count * heads * tokens * keys * HD,
            bytes_accessed=(wf.size + wo.size) * 2,
            transcendentals=col_count * heads * tokens * keys,
        ),
        name="attend",
    )(xn, x, wf, wo, bias, *tables, gain)


def attend_back_kernel(sizes, heads, group, back, chunk, *refs):
    dhb, xn, lse, bias, cosq, sinq, coskv, sinkv = refs[:8]
    mixed_in, q_in, kv_in, wo_in, wf_in, terms = refs[8:14]
    dxn, dqkv_out, sum_out, xn_sib, dhb_sib, mixed_sib, dqkv_sib = refs[14:21]
    q, kv, wo, wf, dmix, dkv, dqkv, going, coming, dst, pst, rhs_q, rhs_o = refs[21:34]
    in_sems, wo_sems, wf_sems, out_sems, pair_sems, row_sems, sends, recvs = refs[34:42]
    place = Place(*sizes)
    cols, col = place.cols, place.col
    cores = place.sizes[2]
    tokens = dhb.shape[0]
    query_width = heads * HD
    pairs = heads // group
    inner = InnerSum(place, terms, sum_out, chunk, refs[42:])

    in_copies = [
        pltpu.make_async_copy(q_in, q, in_sems.at[0]),
        pltpu.make_async_copy(kv_in, kv, in_sems.at[1]),
    ]

    def wo_copy(z):
        slot = lax.rem(z, 2)
        return pltpu.make_async_copy(wo_in.at[z], wo.at[slot], wo_sems.at[slot])

    def wf_copy(z):
        slot = lax.rem(z, 2)
        return pltpu.make_async_copy(wf_in.at[z], wf.at[slot], wf_sems.at[slot])

    wo_copy(0).start()
    for copy in in_copies:
        copy.start()
    for z in range(min(2, cols)):
        wf_copy(z).start()
    place.greet(True, True)

    other = place.device(2, 1)
    exchanges = []
    if cores > 1:
        chips, deep = terms.shape[0], terms.shape[2]
        moves = [(mixed_in, mixed_sib)]
        for chip in range(chips):
            to, rows = pl.ds(chip * deep, deep), core_rows(place, chip, 1, deep)
            moves += [(xn.at[:, rows], xn_sib.at[:, to]), (dhb.at[:, rows], dhb_sib.at[:, to])]
        exchanges = [
            remote(source, target, pair_sems.at[0, n], pair_sems.at[1, n], other)
            for n, (source, target) in enumerate(moves)
        ]

    def row_exchange(z):
        return remote(dqkv.at[z], dqkv_sib.at[z], row_sems.at[0, z], row_sems.at[1, z], other)

    def out_copy(z):
        return pltpu.make_async_copy(dqkv.at[z], dqkv_out.at[z], out_sems.at[z])

    inner.begin()
    for exchange in exchanges:
        exchange.start()
    dxn[...] = jnp.zeros_like(dxn)
    for copy in in_copies:
        copy.wait()

    def hop(z, step):
        return remote(
            going.at[step - 1, z],
            coming.at[step - 1, z],
            sends.at[step - 1, z],
            recvs.at[step - 1, z],
            (place.row, col - 1),
        )

    def goes(step):
        return col - back + step - 1 >= 0

    def comes(step):
        return (col < cols - 1) & (col + step - back >= 0)

    def send(z, step):
        pl.when(goes(step))(lambda: hop(z, step).start())

    def chunk_rows(step):
        return slice(step * tokens, (step + 1) * tokens)

    def halo(step, z):
        if step > 0:
            pl.when(comes(step))(lambda: hop(z, step).wait_recv())
            term = jnp.where(comes(step), coming[step - 1, z].astype(f32), 0.0)
            total = dkv[z, chunk_rows(step)] + term
        else:
            total = dkv[z, chunk_rows(step)]
        if step < back:
            going[step, z] = total.astype(bf16)
            send(z, step + 1)
            return
        for n in range(pairs):
            at = slice(n * LANES, (n + 1) * LANES)
            dqkv[z, :, query_width + n * LANES : query_width + (n + 1) * LANES] = rope_lanes(
                total[:, at], coskv[...], sinkv[...]
            ).astype(bf16)
        out_copy(z).start()
        if cores > 1:
            row_exchange(z).start()
        wf_copy(z).wait()
        dxn[...] += against(dqkv[z], wf[lax.rem(z, 2)])
        when(z + 2 < cols, lambda: wf_copy(z + 2).start())

    def halos(z):
        for step in range(1, back + 1):
            at = z - step
            when((at >= 0) & (at < cols), lambda: halo(step, at))

    def one_col(z, carry):
        wo_copy(z).wait()
        when(z + 1 < cols, lambda: wo_copy(z + 1).start())
        dmix[...] = matmul(dhb[...], wo[lax.rem(z, 2)]).astype(bf16)
        for n in range(pairs):
            keyval = kv[z, :, n * LANES : (n + 1) * LANES]
            for i in range(group):
                head = n * group + i
                at = slice(i * tokens, (i + 1) * tokens)
                query = head_at(q[z, :, tile_of(head)].astype(f32), head, False) * HD**-0.5
                query = query.astype(bf16)
                grad = head_at(dmix[:, tile_of(head)].astype(f32), head, True).astype(bf16)
                rhs_q[at] = query
                rhs_o[at] = grad
                chances = jnp.exp(against(keyval, query) + bias[...] - lse[z, head : head + 1])
                grad_chance = against(keyval, grad)
                centre = jnp.sum(chances * grad_chance, axis=0, keepdims=True)
                dst[:, at] = (chances * (grad_chance - centre)).astype(bf16)
                pst[:, at] = chances.astype(bf16)
            dkv[z, :, n * LANES : (n + 1) * LANES] = matmul(dst[...], rhs_q[...]) + matmul(
                pst[...], rhs_o[...]
            )
            grad_rows = dot_tokens(keyval, dst[...])
            for i in range(0, group, 2):
                tile = jnp.concatenate(
                    [
                        grad_rows[:HD, i * tokens : (i + 1) * tokens],
                        grad_rows[:HD, (i + 1) * tokens : (i + 2) * tokens],
                    ],
                    axis=0,
                )
                turned = rope_lanes(jnp.transpose(tile), cosq[...], sinq[...]) * HD**-0.5
                dqkv[z, :, tile_of(n * group + i)] = turned.astype(bf16)
            inner.tick(z * pairs + n)
        halo(0, z)
        halos(z)
        return carry

    lax.fori_loop(0, cols, one_col, 0)
    ticks = list(range(cols * pairs, inner.count + 2))
    for z in range(cols, cols + back):
        if ticks:
            inner.tick(ticks.pop(0))
        halos(z)
    for t in ticks:
        inner.tick(t)
    for z in range(cols):
        out_copy(z).wait()
        if cores > 1:
            row_exchange(z).wait_send()
            row_exchange(z).wait_recv()
    for exchange in exchanges:
        exchange.wait_send()
        exchange.wait_recv()
    for step in range(1, back + 1):
        for z in range(cols):
            pl.when(goes(step))(lambda: hop(z, step).wait_send())
    inner.finish()


def attend_back(
    dhb, xn, lse, bias, tables, mixed, q, kv, wo, wf, terms, group, sizes, cid
):
    row_count, col_count = sizes
    plane = plane_sizes(row_count)
    chips = plane[0] * plane[1]
    tokens, width = dhb.shape
    heads = lse.shape[1]
    back = kv.shape[1] // tokens - 1
    pairs = heads // group
    keys = kv.shape[1]
    all_width = wf.shape[2]
    inner_width = terms.shape[1]
    chunk = min(512, inner_width)
    deep = terms.shape[0] // row_count
    row_shape = (col_count, tokens, all_width)
    halo_shape = (max(back, 1), col_count, tokens, kv.shape[2])
    vmem = pl.BlockSpec(memory_space=pltpu.VMEM)
    return pl.pallas_call(
        functools.partial(attend_back_kernel, sizes, heads, group, back, chunk),
        out_shape=[
            jax.ShapeDtypeStruct((tokens, width), f32),
            jax.ShapeDtypeStruct(row_shape, bf16),
            jax.ShapeDtypeStruct((deep, inner_width), f32),
            jax.ShapeDtypeStruct((tokens, chips * deep), bf16),
            jax.ShapeDtypeStruct((tokens, chips * deep), bf16),
            jax.ShapeDtypeStruct(mixed.shape, bf16),
            jax.ShapeDtypeStruct(row_shape, bf16),
        ],
        in_specs=[vmem] * 8 + [ANY] * 6,
        out_specs=[vmem] + [ANY] * 6,
        scratch_shapes=[
            pltpu.VMEM(q.shape, bf16),
            pltpu.VMEM(kv.shape, bf16),
            pltpu.VMEM((2,) + wo.shape[1:], bf16),
            pltpu.VMEM((2,) + wf.shape[1:], bf16),
            pltpu.VMEM((tokens, heads * HD), bf16),
            pltpu.VMEM(kv.shape, f32),
            pltpu.VMEM(row_shape, bf16),
            pltpu.VMEM(halo_shape, bf16),
            pltpu.VMEM(halo_shape, bf16),
            pltpu.VMEM((keys, group * tokens), bf16),
            pltpu.VMEM((keys, group * tokens), bf16),
            pltpu.VMEM((group * tokens, LANES), bf16),
            pltpu.VMEM((group * tokens, LANES), bf16),
            pltpu.SemaphoreType.DMA((2,)),
            pltpu.SemaphoreType.DMA((2,)),
            pltpu.SemaphoreType.DMA((2,)),
            pltpu.SemaphoreType.DMA((col_count,)),
            pltpu.SemaphoreType.DMA((2, 1 + 2 * chips)),
            pltpu.SemaphoreType.DMA((2, col_count)),
            pltpu.SemaphoreType.DMA((max(back, 1), col_count)),
            pltpu.SemaphoreType.DMA((max(back, 1), col_count)),
        ]
        + InnerSum.scratch(plane, deep, inner_width, chunk),
        compiler_params=pltpu.CompilerParams(
            collective_id=cid, has_side_effects=True, vmem_limit_bytes=62 << 20
        ),
        cost_estimate=pl.CostEstimate(
            flops=2 * tokens * (wf.size + wo.size) + 10 * col_count * heads * tokens * keys * HD,
            bytes_accessed=(wf.size + wo.size + terms.size) * 2,
            transcendentals=col_count * heads * tokens * keys,
        ),
        name="attend_back",
    )(
        dhb,
        xn,
        lse,
        bias,
        *tables,
        mixed,
        q,
        kv,
        wo,
        wf,
        terms.reshape(chips, plane[2], deep, inner_width),
    )


def rope_tables(position):
    indices = jnp.arange(HD // 2, dtype=f32)
    frequency = rope_base ** (-(indices * 2.0 / HD))
    wavelen = 2.0 * jnp.pi / frequency
    smooth = (8192.0 / wavelen - 1.0) / 3.0
    scaled = jnp.where(
        wavelen > 8192.0, frequency / 32.0, (1.0 - smooth) * frequency / 32.0 + smooth * frequency
    )
    frequency = jnp.where(wavelen < 2048.0, frequency, scaled)
    angles = position.astype(f32)[:, None] * frequency[None, :]
    return (jnp.cos(angles), jnp.sin(angles))


def rotate(values, cosine, sinusoid):
    halfway = values.shape[-1] // 2
    former = values[..., :halfway]
    latter = values[..., halfway:]
    cos_wide = cosine[:, None, :]
    sin_wide = sinusoid[:, None, :]
    return jnp.concatenate(
        [former * cos_wide - latter * sin_wide, latter * cos_wide + former * sin_wide], axis=-1
    )


def normalize(values, gain):
    scale = lax.rsqrt(jnp.mean(values * values, axis=1, keepdims=True) + epsilon)
    return ((values * scale * gain).astype(bf16), scale)


def norm_back(grad_in, values, scale, gain):
    weighted = grad_in * gain
    inner_sum = jnp.mean(weighted * values, axis=1, keepdims=True)
    return (
        scale * weighted - values * (scale * scale * scale) * inner_sum,
        jnp.sum(grad_in * values * scale, axis=0),
    )


def against(left, right):
    return lax.dot_general(left, right, (((1,), (1,)), ((), ())), preferred_element_type=f32)


def over_rows(left, right):
    return lax.dot_general(left, right, (((0,), (0,)), ((), ())), preferred_element_type=f32)


def matmul(left, right):
    return jnp.dot(left, right, preferred_element_type=f32)


def shift(values, step, col_count):
    if step > 0:
        pairs = [(i, i + step) for i in range(col_count - step)]
    else:
        pairs = [(i, i + step) for i in range(-step, col_count)]
    return lax.ppermute(values, "col", pairs)


def shards(
    tokens,
    seq_lens,
    attn_gain,
    query_weight,
    keyvalue_weight,
    output_weight,
    mlp_gain,
    hidden_weight,
    down_weight,
    out_grad,
):
    row_count, col_count = lax.axis_size("row"), lax.axis_size("col")
    local = tokens.shape[0]
    block_rows = local * col_count
    col = lax.axis_index("col")
    deep = query_weight.shape[0]
    width = tokens.shape[1]
    query_width = query_weight.shape[1]
    pairs = keyvalue_weight.shape[1]
    heads = query_width // HD
    group = heads // pairs
    hidden = down_weight.shape[1]
    back = min(-(-(SEQ_MAX - 1) // local), col_count - 1)

    lengths = seq_lens[0]
    finish = jnp.cumsum(lengths)
    indices = jnp.arange(block_rows, dtype=jnp.int32)
    passed = indices[:, None] >= finish[None, :]
    segment = jnp.sum(passed.astype(jnp.int32), axis=1, dtype=jnp.int32)
    position = indices - jnp.sum(jnp.where(passed, lengths[None, :], 0), axis=1, dtype=jnp.int32)
    own_position = lax.dynamic_slice(position, (col * local,), (local,))
    own_segment = lax.dynamic_slice(segment, (col * local,), (local,))
    padded = jnp.concatenate([jnp.full((back * local,), -1, jnp.int32), segment])
    key_segment = lax.dynamic_slice(padded, (col * local,), ((back + 1) * local,))
    key_index = jnp.arange((back + 1) * local, dtype=jnp.int32) - back * local
    query_index = jnp.arange(local, dtype=jnp.int32)
    allowed = (own_segment[:, None] == key_segment[None, :]) & (
        key_index[None, :] <= query_index[:, None]
    )
    cosine, sinusoid = rope_tables(own_position)
    gain_first = attn_gain.astype(f32)
    gain_second = mlp_gain.astype(f32)

    first_weight = jnp.concatenate(
        [query_weight, keyvalue_weight.reshape(deep, pairs * 2 * HD)], axis=1
    )
    full_first, full_output, full_down, rows_grad = gather_all(
        [first_weight, output_weight], [down_weight], out_grad, row_count, col_count
    )

    hidden_flat, full_first = lax.optimization_barrier(
        (hidden_weight.reshape(deep, 2 * hidden), full_first)
    )
    full_hidden = lax.all_gather(hidden_flat, "row", axis=0, tiled=True)

    inputs = tokens.astype(f32)
    normal_in, scale_in = normalize(inputs, gain_first)
    halves = jnp.concatenate([cosine, cosine], axis=1)
    signed = jnp.concatenate([-sinusoid, sinusoid], axis=1)
    tables = (
        jnp.concatenate([halves, halves], axis=1),
        jnp.concatenate([signed, signed], axis=1),
        jnp.concatenate([halves, jnp.ones_like(halves)], axis=1),
        jnp.concatenate([signed, jnp.zeros_like(signed)], axis=1),
    )
    bias = jnp.where(allowed, 0.0, blocked).astype(f32)
    queries, all_keyvals, mixed, lse, hidden_in, normal_mid = attend(
        normal_in,
        tokens,
        full_first,
        full_output,
        bias,
        tables,
        gain_second[None],
        heads,
        group,
        back,
        row_count,
        col_count,
        4,
    )
    scale_mid = lax.rsqrt(jnp.mean(hidden_in * hidden_in, axis=1, keepdims=True) + epsilon)

    rows_mid = line_gather(normal_mid, row_count, col_count, 2)
    grad_mid, out_terms, grad_hidden_part, grad_down_part = mlp(
        rows_mid, rows_grad, full_hidden, full_down, row_count, col_count, 3
    )
    back_mid, gain_mid_part = norm_back(grad_mid, hidden_in, scale_mid, gain_second)
    grad_hidden_in = out_grad.astype(f32) + back_mid
    grad_low = grad_hidden_in.astype(bf16)
    cores = plane_sizes(row_count)[2]
    tables_back = (tables[0], -tables[1], tables[2], -tables[3])
    grad_in, grad_first, sum_hidden, normal_sib, grad_low_sib, mixed_sib, grad_first_sib = (
        attend_back(
            grad_low,
            normal_in,
            lse,
            bias.T,
            tables_back,
            mixed,
            queries,
            all_keyvals,
            full_output,
            full_first,
            grad_hidden_part,
            group,
            (row_count, col_count),
            5,
        )
    )
    back_in, gain_in_part = norm_back(grad_in, inputs, scale_in, gain_first)
    grad_tokens = (grad_hidden_in + back_in).astype(bf16)
    gain_parts = jnp.concatenate([gain_in_part, gain_mid_part]).reshape(-1, 128)
    lefts = [
        (normal_in, normal_sib)[:cores],
        (grad_low, grad_low_sib)[:cores],
    ]
    rights = [(grad_first, grad_first_sib)[:cores], (mixed, mixed_sib)[:cores]]
    sum_first, sum_output, sum_down, out_sum, gain_sums = sum_all(
        lefts, rights, grad_down_part, out_terms, gain_parts, row_count, col_count, f32
    )
    block_out = hidden_in + out_sum
    gain_in_sum, gain_mid_sum = gain_sums.reshape(2, width)
    return (
        block_out.astype(bf16),
        grad_tokens,
        gain_in_sum,
        sum_first[:, :query_width],
        sum_first[:, query_width:].reshape(deep, pairs, 2 * HD),
        sum_output,
        gain_mid_sum,
        sum_hidden.reshape(deep, 2, hidden),
        sum_down,
    )


def solution(mesh):
    return jax.shard_map(
        shards,
        mesh=mesh,
        in_specs=(
            P(("row", "col"), None),
            P("row", None),
            P(),
            P("row", "col"),
            P("row", "col", None),
            P("row", "col"),
            P(),
            P("row", None, "col"),
            P("row", "col"),
            P(("row", "col"), None),
        ),
        out_specs=(
            P(("row", "col"), None),
            P(("row", "col"), None),
            P(),
            P("row", "col"),
            P("row", "col", None),
            P("row", "col"),
            P(),
            P("row", None, "col"),
            P("row", "col"),
        ),
        check_vma=False,
    )
```

```python
import functools

import jax
import jax.numpy as jnp
from jax import lax
from jax.experimental import pallas as pl
from jax.experimental.pallas import tpu as pltpu
from jax.sharding import PartitionSpec as P

HD = 64
SEQ_MAX = 512
MESH = pl.DeviceIdType.MESH
ANY = pl.BlockSpec(memory_space=pl.ANY)

epsilon = 1e-05
rope_base = 500000.0
blocked = -1e30
bf16 = jnp.bfloat16
f32 = jnp.float32


def plane_sizes(row_count):
    cores = 2 if row_count % 2 == 0 else 1
    chips = row_count // cores
    first = 2 if chips % 2 == 0 else 1
    return first, chips // first, cores


class Place:
    def __init__(self, row_count, col_count):
        self.rows, self.cols = row_count, col_count
        self.sizes = plane_sizes(row_count)
        na, nb, nk = self.sizes
        self.row = lax.axis_index("row")
        self.col = lax.axis_index("col")
        self.at = (self.row // (nb * nk), (self.row // nk) % nb, self.row % nk)

    def row_of(self, at):
        _, nb, nk = self.sizes
        return (at[0] * nb + at[1]) * nk + at[2]

    def chip_of(self, at):
        return at[0] * self.sizes[1] + at[1]

    def moved(self, axis, step, at=None):
        at = list(self.at if at is None else at)
        size = self.sizes[axis]
        at[axis] = lax.rem(at[axis] + (step % size), size)
        return tuple(at)

    def device(self, axis, step):
        return (self.row_of(self.moved(axis, step)), self.col)

    def greet(self, plane, line):
        barrier = pltpu.get_barrier_semaphore()
        count = 0
        if plane:
            for axis in range(3):
                size = self.sizes[axis]
                for step in {1 % size, (size - 1) % size} - {0}:
                    pl.semaphore_signal(
                        barrier, inc=1, device_id=self.device(axis, step), device_id_type=MESH
                    )
                    count += 1
        if line and self.cols > 1:
            for step, there in self.line_ways():

                @pl.when(there)
                def _(step=step):
                    pl.semaphore_signal(
                        barrier, inc=1, device_id=(self.row, self.col + step), device_id_type=MESH
                    )

        if line and self.cols > 1:
            last = self.cols - 1
            count = count + jnp.minimum(self.col, 1) + jnp.minimum(last - self.col, 1)
        if not isinstance(count, int) or count:
            pl.semaphore_wait(barrier, count)

    def line_ways(self):
        return ((1, self.col < self.cols - 1), (-1, self.col > 0))


def when(condition, action):
    if condition is None or condition is True:
        action()
    elif condition is False:
        pass
    else:
        pl.when(condition)(action)


def remote(src, dst, send_sem, recv_sem, device):
    return pltpu.make_async_remote_copy(
        src_ref=src,
        dst_ref=dst,
        send_sem=send_sem,
        recv_sem=recv_sem,
        device_id=device,
        device_id_type=MESH,
    )


class LineGather:
    def __init__(self, place, own, block, send_sems, recv_sems):
        self.place, self.own, self.block = place, own, block
        self.sends, self.recvs = send_sems, recv_sems

    def copy(self, way, step, origin):
        place = self.place
        source = self.own if step == 1 else self.block(origin)
        return remote(
            source,
            self.block(origin),
            self.sends.at[way, step - 1],
            self.recvs.at[way, step - 1],
            (place.row, place.col + (1, -1)[way]),
        )

    def sends_at(self, way, step):
        col, last = self.place.col, self.place.cols - 1
        if way == 0:
            return (col >= step - 1) & (col < last), col - (step - 1)
        return (col + step - 1 <= last) & (col > 0), col + (step - 1)

    def gets_at(self, way, step):
        col, last = self.place.col, self.place.cols - 1
        if way == 0:
            return col >= step, col - step
        return col + step <= last, col + step

    def send(self, way, step):
        condition, origin = self.sends_at(way, step)
        when(condition, lambda: self.copy(way, step, origin).start())

    def receive(self, way, step):
        condition, origin = self.gets_at(way, step)

        def action():
            self.copy(way, step, origin).wait_recv()

        when(condition, action)
        if step < self.place.cols - 1:
            self.send(way, step + 1)

    def finish(self):
        for step in range(1, self.place.cols):
            for way in (0, 1):
                condition, origin = self.sends_at(way, step)
                when(condition, lambda: self.copy(way, step, origin).wait_send())


class PlaneGather:
    def __init__(self, place, block, own, send_sems, recv_sems):
        self.place, self.block, self.own = place, block, own
        self.sends, self.recvs = send_sems, recv_sems

    @staticmethod
    def sem_count(sizes):
        na, nb, _ = sizes
        return 2 * na * nb - 1

    def axes(self, half):
        return (1, 0) if half == 0 else (0, 1)

    def counts(self, half):
        first, second = self.axes(half)
        return self.place.sizes[first], self.place.sizes[second]

    def origin(self, half, i, j, core_step=0):
        first, second = self.axes(half)
        at = self.place.moved(first, -i)
        at = self.place.moved(second, -j, at)
        if core_step:
            at = self.place.moved(2, 1, at)
        return self.place.row_of(at)

    def copy(self, half, kind, i, j):
        np_, nq = self.counts(half)
        if kind == 0:
            number, device = i - 1, self.place.device(self.axes(half)[0], 1)
        elif kind == 1:
            number = (np_ - 1) + i * (nq - 1) + (j - 1)
            device = self.place.device(self.axes(half)[1], 1)
        else:
            number = (np_ * nq - 1) + i * nq + j
            device = self.place.device(2, 1)
        return number, device

    def sender(self, half, kind, i, j):
        number, device = self.copy(half, kind, i, j)
        oi, oj = (i - 1, j) if kind == 0 else ((i, j - 1) if kind == 1 else (i, j))
        ref = self.block(self.origin(half, oi, oj), half)
        source = self.own(half) if (oi, oj) == (0, 0) else ref
        return remote(source, ref, self.sends.at[half, number], self.recvs.at[half, number], device)

    def receiver(self, half, kind, i, j):
        number, device = self.copy(half, kind, i, j)
        ref = self.block(self.origin(half, i, j, 1 if kind == 2 else 0), half)
        return remote(ref, ref, self.sends.at[half, number], self.recvs.at[half, number], device)

    def all_copies(self):
        for half in (0, 1):
            np_, nq = self.counts(half)
            for i in range(1, np_):
                yield half, 0, i, 0
            for i in range(np_):
                for j in range(1, nq):
                    yield half, 1, i, j
            if self.place.sizes[2] > 1:
                for i in range(np_):
                    for j in range(nq):
                        yield half, 2, i, j

    def share(self, half, i, j):
        if self.place.sizes[2] > 1:
            self.sender(half, 2, i, j).start()

    def first(self):
        for half in (0, 1):
            if self.counts(half)[0] > 1:
                self.sender(half, 0, 1, 0).start()
        for half in (0, 1):
            self.share(half, 0, 0)

    def second(self):
        for half in (0, 1):
            np_, nq = self.counts(half)
            for i in range(np_):
                if i > 0:
                    self.receiver(half, 0, i, 0).wait_recv()
                    if i < np_ - 1:
                        self.sender(half, 0, i + 1, 0).start()
                if nq > 1:
                    self.sender(half, 1, i, 1).start()
                if i > 0:
                    self.share(half, i, 0)

    def third(self):
        for half in (0, 1):
            np_, nq = self.counts(half)
            for j in range(1, nq):
                for i in range(np_):
                    self.receiver(half, 1, i, j).wait_recv()
                    if j < nq - 1:
                        self.sender(half, 1, i, j + 1).start()
                    self.share(half, i, j)

    def shared(self):
        for copy in self.all_copies():
            if copy[1] == 2:
                self.receiver(*copy).wait_recv()

    def sent(self):
        for copy in self.all_copies():
            self.sender(*copy).wait_send()

    def finish(self):
        self.shared()
        self.sent()


def tile_gather(place, full, own, send_sems, recv_sems):
    deep = full.shape[0] // place.rows
    half = deep // 2

    def block(row, number):
        return full.at[pl.ds(row * deep + number * half, half)]

    def mine(number):
        if own is None:
            return block(place.row, number)
        return own.at[pl.ds(number * half, half)]

    return PlaneGather(place, block, mine, send_sems, recv_sems)


def nearby(place, number):
    low, high = place.col, place.cols - 1 - place.col
    both = jnp.minimum(low, high)
    way = jnp.minimum(jnp.maximum(high - low, -1), 1)
    step = (number + 1) // 2 * (-1 if number % 2 else 1)
    paired = jnp.minimum(jnp.maximum(2 * both - number + 1, 0), 1)
    return place.col + paired * step + (1 - paired) * way * (number - both)


def gather_kernel(sizes, count, inner, *refs):
    row_count, col_count = sizes
    every = count + inner
    own, own_act = refs[:every], refs[every]
    full, full_act = refs[every + 1 : 2 * every + 1], refs[2 * every + 1]
    local_sems, zs, zr, ps, pr = refs[2 * every + 2 :]
    place = Place(row_count, col_count)
    place.greet(True, True)
    token_rows = own_act.shape[0]

    def at(n, col, row):
        deep = own[n].shape[0]
        if n < count:
            return full[n].at[col, pl.ds(row * deep, deep)]
        return full[n].at[pl.ds(row * deep, deep)]

    lines = [
        LineGather(place, own[n], lambda j, n=n: at(n, j, place.row), zs.at[n], zr.at[n])
        for n in range(count)
    ]
    acts = LineGather(
        place,
        own_act,
        lambda j: full_act.at[pl.ds(j * token_rows, token_rows)],
        zs.at[count],
        zr.at[count],
    )

    def keep(n):
        if n == every:
            return pltpu.make_async_copy(own_act, acts.block(place.col), local_sems.at[n])
        return pltpu.make_async_copy(own[n], at(n, place.col, place.row), local_sems.at[n])

    for n in range(every + 1):
        keep(n).start()
    for line in lines:
        for way in (0, 1):
            line.send(way, 1)

    def inside(n, col, near):
        deep = own[n].shape[0]
        half = deep // 2

        def block(row, number):
            rows = pl.ds(row * deep + number * half, half)
            return full[n].at[col, rows] if n < count else full[n].at[rows]

        def mine(number):
            return own[n].at[pl.ds(number * half, half)] if near else block(place.row, number)

        return PlaneGather(place, block, mine, ps.at[n, col], pr.at[n, col])

    entries = [(n, k) for k in range(col_count) for n in range(count)]
    entries += [(n, 0) for n in range(count, every)]
    parts = [inside(n, nearby(place, k), k == 0) for n, k in entries]
    act_steps = list(range(1, col_count))

    def act_step():
        if act_steps:
            for way in (0, 1):
                acts.receive(way, act_steps[0])
            act_steps.pop(0)

    for number in range(len(parts) + 2):
        if number < len(parts):
            n, k = entries[number]
            if n == 0 and k > 0:
                for line in lines:
                    for way in (0, 1):
                        line.receive(way, k)
                if k == 1:
                    for way in (0, 1):
                        acts.send(way, 1)
                if k >= 3:
                    act_step()
            parts[number].first()
        if 1 <= number <= len(parts):
            parts[number - 1].second()
        if 2 <= number:
            parts[number - 2].third()
        if number >= len(parts):
            act_step()
    while act_steps:
        act_step()
    for n in range(every + 1):
        keep(n).wait()
    for part in parts:
        part.finish()
    for line in lines + [acts]:
        line.finish()


def gather_all(weights, inner_weights, act, row_count, col_count):
    count, inner = len(weights), len(inner_weights)
    sizes = plane_sizes(row_count)
    steps = max(col_count - 1, 1)
    every = list(weights) + list(inner_weights)
    plane_sems = (count + inner, col_count, 2, PlaneGather.sem_count(sizes))
    moved = sum(w.size for w in weights) * row_count * col_count * 2
    return pl.pallas_call(
        functools.partial(gather_kernel, (row_count, col_count), count, inner),
        out_shape=[
            jax.ShapeDtypeStruct((col_count, row_count * w.shape[0], w.shape[1]), bf16)
            for w in weights
        ]
        + [
            jax.ShapeDtypeStruct((row_count * w.shape[0], w.shape[1]), bf16) for w in inner_weights
        ]
        + [jax.ShapeDtypeStruct((col_count * act.shape[0], act.shape[1]), bf16)],
        in_specs=[pl.BlockSpec(memory_space=pltpu.VMEM)] * (len(every) + 1),
        out_specs=[ANY] * (len(every) + 1),
        scratch_shapes=[
            pltpu.SemaphoreType.DMA((len(every) + 1,)),
            pltpu.SemaphoreType.DMA((count + 1, 2, steps)),
            pltpu.SemaphoreType.DMA((count + 1, 2, steps)),
            pltpu.SemaphoreType.DMA(plane_sems),
            pltpu.SemaphoreType.DMA(plane_sems),
        ],
        compiler_params=pltpu.CompilerParams(collective_id=0, has_side_effects=True),
        cost_estimate=pl.CostEstimate(flops=0, bytes_accessed=moved, transcendentals=0),
        name="gather_weights",
    )(*every, act)


def line_gather_kernel(sizes, own, full, local_sem, sends, recvs):
    place = Place(*sizes)
    place.greet(False, True)
    rows = own.shape[0]
    line = LineGather(place, own, lambda j: full.at[pl.ds(j * rows, rows)], sends, recvs)
    for way in (0, 1):
        line.send(way, 1)
    keep = pltpu.make_async_copy(own, full.at[pl.ds(place.col * rows, rows)], local_sem)
    keep.start()
    for step in range(1, place.cols):
        for way in (0, 1):
            line.receive(way, step)
    keep.wait()
    line.finish()


def line_gather(own, row_count, col_count, collective_id):
    steps = max(col_count - 1, 1)
    return pl.pallas_call(
        functools.partial(line_gather_kernel, (row_count, col_count)),
        out_shape=jax.ShapeDtypeStruct((col_count * own.shape[0], own.shape[1]), own.dtype),
        in_specs=[pl.BlockSpec(memory_space=pltpu.VMEM)],
        out_specs=ANY,
        scratch_shapes=[
            pltpu.SemaphoreType.DMA,
            pltpu.SemaphoreType.DMA((2, steps)),
            pltpu.SemaphoreType.DMA((2, steps)),
        ],
        compiler_params=pltpu.CompilerParams(collective_id=collective_id, has_side_effects=True),
        cost_estimate=pl.CostEstimate(
            flops=0, bytes_accessed=own.size * 2 * col_count, transcendentals=0
        ),
        name="gather_line",
    )(own)


def add_rows(target, source):
    rows = target.shape[0]
    piece = 32 if rows % 32 == 0 else 16

    def body(n, carry):
        at = pl.ds(pl.multiple_of(n * piece, piece), piece)
        target[at] = (target[at].astype(f32) + source[at].astype(f32)).astype(target.dtype)
        return carry

    lax.fori_loop(0, rows // piece, body, 0)


class LineSum:
    def __init__(self, place, own, held, send_sems, recv_sems):
        self.place, self.own, self.held = place, own, held
        self.sends, self.recvs = send_sems, recv_sems

    def distance(self, way, col):
        return col - self.place.col if way == 0 else self.place.col - col

    def feeds(self, way):
        return self.place.col > 0 if way == 0 else self.place.col < self.place.cols - 1

    def copy(self, way, distance, source):
        return remote(
            source,
            self.held.at[way, distance - 1],
            self.sends.at[way, distance - 1],
            self.recvs.at[way, distance - 1],
            (self.place.row, self.place.col + (1, -1)[way]),
        )

    def arrived(self, way, distance):
        ref = self.held.at[way, distance]
        return remote(
            ref,
            ref,
            self.sends.at[way, distance],
            self.recvs.at[way, distance],
            (self.place.row, self.place.col + (1, -1)[way]),
        )

    def early(self, col, allowed):
        for way in (0, 1):
            far = self.distance(way, col)

            @pl.when(allowed & (far > 0) & jnp.logical_not(self.feeds(way)))
            def _():
                self.copy(way, far, self.own(col)).start()

    def late(self, col, allowed):
        for way in (0, 1):
            far = self.distance(way, col)

            @pl.when(allowed & (far > 0) & self.feeds(way))
            def _():
                self.arrived(way, far).wait_recv()
                add_rows(self.own(col), self.held.at[way, far])
                self.copy(way, far, self.own(col)).start()

    def last(self, out):
        if self.place.cols > 1:
            for way in (0, 1):
                when(self.feeds(way), lambda: self.arrived(way, 0).wait_recv())
        own = self.own(self.place.col)
        rows = own.shape[0]
        piece = 32 if rows % 32 == 0 else 16
        has = [self.feeds(way) for way in (0, 1)]

        def body(n, carry):
            at = pl.ds(pl.multiple_of(n * piece, piece), piece)
            total = own[at].astype(f32)
            if self.place.cols > 1:
                for way in (0, 1):
                    term = self.held[way, 0, at].astype(f32)
                    total = total + jnp.where(has[way], term, 0.0)
            out[at] = total.astype(out.dtype)
            return carry

        lax.fori_loop(0, rows // piece, body, 0)

    def finish(self):
        for distance in range(1, self.place.cols):
            for way in (0, 1):
                col = self.place.col + (distance if way == 0 else -distance)
                there = col < self.place.cols if way == 0 else col >= 0
                when(there, lambda: self.copy(way, distance, self.own(col)).wait_send())


def dot_tokens(left, right):
    return lax.dot_general(left, right, (((0,), (0,)), ((), ())), preferred_element_type=f32)


def plan_units(cols, tiles, early, hop_us, tile_us, unit_us):
    begin = 4.0
    chunk_at = [0.0] + [begin + hop_us * k for k in range(1, cols)]
    tile_at = [0.0] * early + [begin + 2.0 + tile_us * (n + 1) for n in range(tiles - early)]
    events = [(chunk_at[k], ("chunk", k)) for k in range(1, cols)]
    for f in range(early, tiles):
        second_at = begin + 1.0 + 0.35 * tile_us * (f - early + 1)
        events.append((second_at, ("second", f)))
        events.append((tile_at[f], ("third", f)))
    events.sort(key=lambda event: event[0])
    units = [(max(chunk_at[k], tile_at[f]), k, f) for k in range(cols) for f in range(tiles)]
    units.sort()
    plan, now, after = [], 0.0, []
    while units or events or after:
        while events and events[0][0] <= now:
            plan.append(events.pop(0)[1])
        if after and (not units or units[0][0] > now):
            step, cost = after.pop(0)
            plan.append(step)
            now += cost
            continue
        if units and units[0][0] <= now:
            _, k, f = units.pop(0)
            plan.append(("unit", k, f))
            now += unit_us
            if not any(unit[1] == k for unit in units):
                if k > 0:
                    after.append((("grad", k), 2.6 * unit_us))
                after.append((("y", k), 1.3 * unit_us))
                after.sort(key=lambda item: -item[0][1] if item[0][0] == "grad" else 1)
            continue
        now = min([events[0][0]] * bool(events) + [units[0][0]] * bool(units))
    return plan + [("grad", 0)]


def mlp_kernel(sizes, early, wide, *refs):
    hn_own, dy_in, wh_in, wh_own, wd_in, grad_out, y_out, dwh_out, dwd_out = refs[:9]
    hn, dy, wh, wd, act, dgu, terms, staged, held = refs[9:18]
    token_sems, tile_sems, wd_sems, y_sems, dw_sems, sends, recvs = refs[18:25]
    hs, hr, ps, pr, own_sem = refs[25:]
    place = Place(*sizes)
    cols = place.cols
    width, hidden = wd.shape
    tiles = wh.shape[0]
    tile = hidden // tiles
    wides = width // wide
    tokens = hn.shape[1]
    deep = wh_own.shape[1]

    def wide_at(n):
        return pl.ds(pl.multiple_of(n * wide, wide), wide)

    def piece(n):
        return LineSum(
            place, lambda j: terms.at[j, :, wide_at(n)], held.at[n], sends.at[n], recvs.at[n]
        )

    near = [nearby(place, k) for k in range(cols)]

    def dy_copy(j):
        return pltpu.make_async_copy(dy_in.at[j], dy.at[j], token_sems.at[j])

    def wd_copy(f):
        at = slice(f * tile, (f + 1) * tile)
        return pltpu.make_async_copy(wd_in.at[:, at], wd.at[:, at], wd_sems.at[f])

    def tile_copy(f):
        if f < early:
            return pltpu.make_async_copy(wh_in.at[f], wh.at[f], tile_sems.at[f])
        rows = pl.ds(place.row * deep, deep)
        return pltpu.make_async_copy(wh_own.at[f - early], wh.at[f, rows], tile_sems.at[f])

    own_copy = pltpu.make_async_copy(hn_own, hn.at[place.col], own_sem)
    own_copy.start()
    for f in range(early, tiles):
        tile_copy(f).start()
    dy_copy(near[0]).start()
    for f in range(tiles):
        if f < early:
            tile_copy(f).start()
        wd_copy(f).start()
    for k in range(1, cols):
        dy_copy(near[k]).start()
    place.greet(True, True)
    own_copy.wait()
    line = LineGather(place, hn.at[place.col], lambda j: hn.at[j], hs, hr)
    for way in (0, 1):
        line.send(way, 1)
    parts = {
        f: tile_gather(place, wh.at[f], None, ps.at[f - early], pr.at[f - early])
        for f in range(early, tiles)
    }
    for f in range(early, tiles):
        tile_copy(f).wait()
        parts[f].first()

    def out_copy(slot, j):
        return pltpu.make_async_copy(staged.at[slot], y_out.at[j], y_sems.at[slot])

    def unit(k, f):
        j = near[k]
        at = slice(f * tile, (f + 1) * tile)
        gate_up = matmul(hn[j], wh[f])
        gate, up = gate_up[:, :tile], gate_up[:, tile:]
        back = matmul(dy[j], wd[:, at])
        sigmoid = jax.nn.sigmoid(gate)
        silu = gate * sigmoid
        act[j, :, at] = (silu * up).astype(bf16)
        dgate = back * up * sigmoid * (1.0 + gate * (1.0 - sigmoid))
        dgu[j, :, 2 * f * tile : (2 * f + 1) * tile] = dgate.astype(bf16)
        dgu[j, :, (2 * f + 1) * tile : (2 * f + 2) * tile] = (back * silu).astype(bf16)

    def grad(k):
        j = near[k]

        def body(n, carry):
            at = wide_at(n)
            total = 0.0
            for f in range(tiles):
                total += against(dgu[j, :, 2 * f * tile : 2 * (f + 1) * tile], wh[f, at])
            terms[j, :, at] = total.astype(bf16)
            piece(n).early(j, True)
            return carry

        lax.fori_loop(0, wides, body, 0)

    stored = []

    def y_part(k):
        j = near[k]
        slot = len(stored) % 2
        if len(stored) >= 2:
            out_copy(slot, near[stored[-2]]).wait()

        def body(n, carry):
            at = wide_at(n)
            staged[slot, :, at] = against(act[j], wd[at]).astype(bf16)
            return carry

        lax.fori_loop(0, wides, body, 0)
        out_copy(slot, j).start()
        stored.append(k)

    def late(number):
        low, high = place.col, cols - 1 - place.col
        up_first = jnp.minimum(jnp.maximum(high - low, 0), 1)
        side = up_first * high + (1 - up_first) * low
        way = 2 * up_first - 1
        first = jnp.minimum(jnp.maximum(side - number, 0), 1)
        col = place.col + first * way * (number + 1) - (1 - first) * way * (number + 1 - side)
        return col

    calls = [(number, n) for number in range(cols - 1) for n in range(wides)]

    def next_late():
        if calls:
            number, n = calls.pop(0)
            piece(n).late(late(number), True)

    seen_tiles, seen_chunks = set(), set()
    for step in plan_units(cols, tiles, early, 24.0, 18.0, 2.1):
        if step[0] == "chunk":
            for way in (0, 1):
                line.receive(way, step[1])
        elif step[0] == "second":
            parts[step[1]].second()
        elif step[0] == "third":
            parts[step[1]].third()
            parts[step[1]].shared()
        elif step[0] == "unit":
            _, k, f = step
            if f not in seen_tiles:
                seen_tiles.add(f)
                if f < early:
                    tile_copy(f).wait()
                wd_copy(f).wait()
            if k not in seen_chunks:
                seen_chunks.add(k)
                dy_copy(near[k]).wait()
            unit(k, f)
        elif step[0] == "grad":
            grad(step[1])
            if step[1] in (0, cols - 1):
                next_late()
        else:
            y_part(step[1])
            if step[1] == cols - 1:
                next_late()

    for f in parts:
        parts[f].sent()
    strips = width // 256

    def flat(ref):
        return ref[...].reshape(cols * tokens, ref.shape[2])

    def columns(ref, at):
        return jnp.concatenate([ref[j, :, at] for j in range(cols)], axis=0)

    def down_strip(n, carry):
        at = pl.ds(pl.multiple_of(n * 256, 256), 256)
        wd[at] = dot_tokens(columns(dy, at), flat(act)).astype(bf16)
        pltpu.make_async_copy(wd.at[at], dwd_out.at[at], dw_sems.at[0, n]).start()
        return carry

    def hidden_strip(n, carry):
        at = pl.ds(pl.multiple_of(n * 256, 256), 256)
        result = dot_tokens(columns(hn, at), flat(dgu)).astype(bf16)
        for f in range(tiles):
            wh[f, at] = result[:, 2 * f * tile : 2 * (f + 1) * tile]
        pltpu.make_async_copy(wh.at[:, at], dwh_out.at[:, at], dw_sems.at[1, n]).start()
        return carry

    for begin, end in ((0, strips // 2), (strips // 2, strips)):
        lax.fori_loop(begin, end, down_strip, 0)
        if begin == 0:
            next_late()
    for begin, end in ((0, 1), (1, 3), (3, 5), (5, 7), (7, strips)):
        lax.fori_loop(begin, end, hidden_strip, 0)
        next_late()
    while calls:
        next_late()
    for n in range(wides):
        piece(n).last(grad_out.at[:, wide_at(n)])
    for number in range(max(cols - 2, 0), cols):
        out_copy(number % 2, near[stored[number]]).wait()

    def finish(n, carry):
        at = pl.ds(pl.multiple_of(n * 256, 256), 256)
        pltpu.make_async_copy(wd.at[at], dwd_out.at[at], dw_sems.at[0, n]).wait()
        pltpu.make_async_copy(wh.at[:, at], dwh_out.at[:, at], dw_sems.at[1, n]).wait()
        return carry

    lax.fori_loop(0, strips, finish, 0)
    line.finish()
    for n in range(wides):
        piece(n).finish()


def mlp(hn, dy, wh, wh_own, wd, row_count, col_count, collective_id):
    steps = max(col_count - 1, 1)
    rows, width = hn.shape
    hidden = wd.shape[1]
    early, left = wh.shape[0], wh_own.shape[0]
    tiles = early + left
    tile = hidden // tiles
    wide = min(512, width)
    shape = (col_count, rows, width)
    vmem = pl.BlockSpec(memory_space=pltpu.VMEM)
    total = col_count * rows
    wh_shape = (tiles, width, 2 * tile)
    plane_sems = (left, 2, PlaneGather.sem_count(plane_sizes(row_count)))
    grad, y, dwh, dwd = pl.pallas_call(
        functools.partial(mlp_kernel, (row_count, col_count), early, wide),
        out_shape=[
            jax.ShapeDtypeStruct((rows, width), f32),
            jax.ShapeDtypeStruct(shape, bf16),
            jax.ShapeDtypeStruct(wh_shape, bf16),
            jax.ShapeDtypeStruct(wd.shape, bf16),
        ],
        in_specs=[ANY] * 5,
        out_specs=[vmem, ANY, ANY, ANY],
        scratch_shapes=[
            pltpu.VMEM(shape, bf16),
            pltpu.VMEM(shape, bf16),
            pltpu.VMEM(wh_shape, bf16),
            pltpu.VMEM(wd.shape, bf16),
            pltpu.VMEM((col_count, rows, hidden), bf16),
            pltpu.VMEM((col_count, rows, 2 * hidden), bf16),
            pltpu.VMEM(shape, bf16),
            pltpu.VMEM((2, rows, width), bf16),
            pltpu.VMEM((width // wide, 2, steps, rows, wide), bf16),
            pltpu.SemaphoreType.DMA((col_count,)),
            pltpu.SemaphoreType.DMA((tiles,)),
            pltpu.SemaphoreType.DMA((tiles,)),
            pltpu.SemaphoreType.DMA((2,)),
            pltpu.SemaphoreType.DMA((2, width // 256)),
            pltpu.SemaphoreType.DMA((width // wide, 2, steps)),
            pltpu.SemaphoreType.DMA((width // wide, 2, steps)),
            pltpu.SemaphoreType.DMA((2, steps)),
            pltpu.SemaphoreType.DMA((2, steps)),
            pltpu.SemaphoreType.DMA(plane_sems),
            pltpu.SemaphoreType.DMA(plane_sems),
            pltpu.SemaphoreType.DMA,
        ],
        compiler_params=pltpu.CompilerParams(
            collective_id=collective_id, has_side_effects=True, vmem_limit_bytes=63 << 20
        ),
        cost_estimate=pl.CostEstimate(
            flops=2 * 9 * total * width * hidden,
            bytes_accessed=6 * width * hidden * 2,
            transcendentals=total * hidden,
        ),
        name="feed_forward",
    )(hn, dy.reshape(shape), wh, wh_own, wd)
    return grad, y.reshape(total, width), dwh, dwd


class PlaneSum:
    def __init__(self, place, acc, held_core, held_second, held_first, sems):
        self.place, self.acc = place, acc
        self.held = (held_first, held_second, held_core)
        self.sends, self.recvs = sems
        self.half_deep = acc.shape[1] // 2

    @staticmethod
    def counts_of(sizes):
        na, nb, _ = sizes
        return max(na, nb) - 1, max((na - 1) * nb, (nb - 1) * na)

    @staticmethod
    def sem_count(sizes):
        na, nb, _ = sizes
        return na * nb - 1

    def axes(self, half):
        return (1, 0) if half == 0 else (0, 1)

    def counts(self, half):
        first, second = self.axes(half)
        return self.place.sizes[first], self.place.sizes[second]

    def part(self, half, i, j):
        first, second = self.axes(half)
        at = self.place.moved(second, j, self.place.moved(first, i))
        return self.acc.at[
            self.place.chip_of(at), pl.ds(half * self.half_deep, self.half_deep)
        ]

    def copy(self, half, kind, step, i):
        np_, nq = self.counts(half)
        if kind == 1:
            number = (step - 1) * np_ + i
            source = self.part(half, i, nq - step)
            target = self.held[1].at[half, number]
            sem = number
        else:
            source = self.part(half, np_ - step, 0)
            target = self.held[0].at[half, step - 1]
            sem = (nq - 1) * np_ + step - 1
        device = self.place.device(self.axes(half)[1 if kind == 1 else 0], 1)
        return remote(source, target, self.sends.at[half, sem], self.recvs.at[half, sem], device)

    def add(self, half, kind, step, i):
        np_, nq = self.counts(half)
        self.copy(half, kind, step, i).wait_recv()
        if kind == 1:
            add_rows(
                self.part(half, i, nq - step - 1), self.held[1].at[half, (step - 1) * np_ + i]
            )
        else:
            add_rows(self.part(half, np_ - step - 1, 0), self.held[0].at[half, step - 1])

    def first(self):
        for half in (0, 1):
            np_, nq = self.counts(half)
            if nq > 1:
                for i in range(np_ - 1, -1, -1):
                    self.copy(half, 1, 1, i).start()

    def second(self):
        for half in (0, 1):
            np_, nq = self.counts(half)
            for step in range(1, nq):
                for i in range(np_ - 1, -1, -1):
                    self.add(half, 1, step, i)
                    if step < nq - 1:
                        self.copy(half, 1, step + 1, i).start()
                    elif i == np_ - 1 and np_ > 1:
                        self.copy(half, 0, 1, 0).start()
            if nq == 1 and np_ > 1:
                self.copy(half, 0, 1, 0).start()

    def third(self):
        for half in (0, 1):
            np_, _ = self.counts(half)
            for step in range(1, np_):
                self.add(half, 0, step, 0)
                if step < np_ - 1:
                    self.copy(half, 0, step + 1, 0).start()

    def finish(self):
        for half in (0, 1):
            np_, nq = self.counts(half)
            for step in range(1, nq):
                for i in range(np_):
                    self.copy(half, 1, step, i).wait_send()
            for step in range(1, np_):
                self.copy(half, 0, step, 0).wait_send()


def core_rows(place, chip, step, deep):
    cores = place.sizes[2]
    row = chip * cores + lax.rem(place.at[2] + step, cores)
    return pl.ds(pl.multiple_of(row * deep, deep), deep)


class InnerSum:
    def __init__(self, place, count, terms, target, refs):
        self.place, self.count, self.terms, self.target = place, count, terms, target
        self.acc, self.core_held, self.second, self.first, self.staged = refs[:5]
        self.load_sems, self.core_sems, self.plane_sems, self.out_sems = refs[5:]
        self.ahead = min(3, self.count)

    @staticmethod
    def scratch(sizes, deep, width, chunk):
        na, nb, _ = sizes
        count = width // chunk
        firsts, seconds = PlaneSum.counts_of(sizes)
        sems = (2, count, 2, max(PlaneSum.sem_count(sizes), 1))
        return [
            pltpu.VMEM((count, na * nb, deep, chunk), bf16),
            pltpu.VMEM((count, na * nb, deep, chunk), bf16),
            pltpu.VMEM((count, 2, max(seconds, 1), deep // 2, chunk), bf16),
            pltpu.VMEM((count, 2, max(firsts, 1), deep // 2, chunk), bf16),
            pltpu.VMEM((2, deep, chunk), f32),
            pltpu.SemaphoreType.DMA((count,)),
            pltpu.SemaphoreType.DMA((2, count)),
            pltpu.SemaphoreType.DMA(sems),
            pltpu.SemaphoreType.DMA((2,)),
        ]

    def load(self, e):
        source = self.terms(e, self.place.at[2])
        return pltpu.make_async_copy(source, self.acc.at[e], self.load_sems.at[e])

    def share(self, e):
        other = lax.rem(self.place.at[2] + 1, self.place.sizes[2])
        return remote(
            self.terms(e, other),
            self.core_held.at[e],
            self.core_sems.at[0, e],
            self.core_sems.at[1, e],
            self.place.device(2, 1),
        )

    def inside(self, e):
        return PlaneSum(
            self.place,
            self.acc.at[e],
            self.core_held.at[e],
            self.second.at[e],
            self.first.at[e],
            (self.plane_sems.at[0, e], self.plane_sems.at[1, e]),
        )

    def out_copy(self, e):
        slot = lax.rem(e, 2)
        return pltpu.make_async_copy(
            self.staged.at[slot], self.target(e), self.out_sems.at[slot]
        )

    def prepare(self, e):
        self.load(e).start()
        if self.place.sizes[2] > 1:
            self.share(e).start()

    def begin(self):
        for e in range(self.ahead):
            self.prepare(e)

    def start(self, e):
        when(e + self.ahead < self.count, lambda: self.prepare(e + self.ahead))
        self.load(e).wait()
        if self.place.sizes[2] > 1:
            self.share(e).wait_recv()
            for chip in range(self.acc.shape[1]):
                add_rows(self.acc.at[e, chip], self.core_held.at[e, chip])
        self.inside(e).first()

    def middle(self, e):
        self.inside(e).second()

    def close(self, e):
        self.inside(e).third()
        when(e >= 2, lambda: self.out_copy(e - 2).wait())
        slot = lax.rem(e, 2)
        own = self.acc.at[e, self.place.chip_of(self.place.at)]
        self.staged[slot] = own[...].astype(f32)
        self.out_copy(e).start()

    def tick(self, t):
        when(t < self.count, lambda: self.start(t))
        when((t >= 1) & (t - 1 < self.count), lambda: self.middle(t - 1))
        when((t >= 2) & (t - 2 < self.count), lambda: self.close(t - 2))

    def finish(self):
        for e in range(max(self.count - 2, 0), self.count):
            self.out_copy(e).wait()

        def done(e, carry):
            if self.place.sizes[2] > 1:
                self.share(e).wait_send()
            self.inside(e).finish()
            return carry

        lax.fori_loop(0, self.count, done, 0)


class SmallSum:
    def __init__(self, place, own, total, ring_held, line_held, ring_sems, line_sems):
        self.place, self.own, self.total = place, own, total
        self.held, self.sems = ring_held, ring_sems
        self.line = LineGather(
            place, total, lambda j: line_held.at[j], line_sems.at[0], line_sems.at[1]
        )
        self.line_held = line_held
        self.stages = []
        for axis in range(3):
            for step in range(1, place.sizes[axis]):
                self.stages.append(functools.partial(self.ring_send, axis, step))
                self.stages.append(functools.partial(self.ring_receive, axis, step))
            if place.sizes[axis] > 1:
                self.stages.append(functools.partial(self.ring_add, axis))
        self.stages.append(self.line_start)
        for step in range(1, place.cols):
            self.stages.append(functools.partial(self.line_step, step))
        self.stages.append(self.line_add)

    def begin(self):
        self.total[...] = self.own[...]

    def block(self, axis, step):
        at = self.place.moved(axis, -step)[axis]
        return self.held.at[axis, at]

    def ring_copy(self, axis, step):
        source = self.total if step == 1 else self.block(axis, step - 1)
        target = self.held.at[axis, self.place.moved(axis, 1 - step)[axis]]
        return remote(
            source,
            target,
            self.sems.at[0, axis, step - 1],
            self.sems.at[1, axis, step - 1],
            self.place.device(axis, 1),
        )

    def ring_send(self, axis, step):
        self.ring_copy(axis, step).start()

    def ring_receive(self, axis, step):
        ref = self.block(axis, step)
        remote(
            ref,
            ref,
            self.sems.at[0, axis, step - 1],
            self.sems.at[1, axis, step - 1],
            self.place.device(axis, 1),
        ).wait_recv()

    def ring_add(self, axis):
        for step in range(1, self.place.sizes[axis]):
            self.ring_copy(axis, step).wait_send()
        own_at = self.place.at[axis]
        total = None
        for at in range(self.place.sizes[axis]):
            term = jnp.where(own_at == at, self.total[...], self.held[axis, at])
            total = term if total is None else total + term
        self.total[...] = total

    def line_start(self):
        for way in (0, 1):
            self.line.send(way, 1)

    def line_step(self, step):
        for way in (0, 1):
            self.line.receive(way, step)

    def line_add(self):
        self.line.finish()
        total = None
        for at in range(self.place.cols):
            term = jnp.where(self.place.col == at, self.total[...], self.line_held[at])
            total = term if total is None else total + term
        self.total[...] = total


def sum_kernel(sizes, count, chunk, *refs):
    row_count, col_count = sizes
    place = Place(row_count, col_count)
    cores = place.sizes[2]
    lefts, rights = refs[: cores * count], refs[cores * count : 2 * cores * count]
    refs = refs[2 * cores * count :]
    inner_terms, act_terms, small = refs[:3]
    outs = refs[3 : 3 + count]
    inner_out, act_out, small_out = refs[3 + count : 6 + count]
    refs = refs[6 + count :]
    per = [refs[7 * n : 7 * n + 7] for n in range(count)]

    def inner_columns(e):
        return pl.ds(pl.multiple_of(e * chunk, chunk), chunk)

    inner = InnerSum(
        place,
        inner_out.shape[1] // chunk,
        lambda e, core: inner_terms.at[:, core, :, inner_columns(e)],
        lambda e: inner_out.at[:, inner_columns(e)],
        refs[7 * count : 7 * count + 9],
    )
    act_held, load_sems, out_sems, ps, pr, zs, zr = refs[7 * count + 9 : 7 * count + 16]
    ring_held, line_held, ring_sems, line_sems, chip_sems = refs[7 * count + 16 :]
    token_rows = act_out.shape[0]

    entries = [(n, nearby(place, k)) for k in range(col_count - 1, -1, -1) for n in range(count)]

    acts = LineSum(
        place,
        lambda j: act_terms.at[pl.ds(pl.multiple_of(j * token_rows, token_rows), token_rows)],
        act_held,
        zs.at[count],
        zr.at[count],
    )
    acc = [per[n][0] for n in range(count)]
    lines = [
        LineSum(
            place,
            lambda j, n=n: acc[n].at[j, place.chip_of(place.at)],
            per[n][3],
            zs.at[n],
            zr.at[n],
        )
        for n in range(count)
    ]
    tokens = lefts[0].shape[0]
    chips, deep = acc[0].shape[1:3]

    def loads():
        for n in range(count):
            left, right = per[n][5], per[n][6]
            for k in range(cores):
                at = pl.ds(k * tokens, tokens)
                if k == 0:
                    for chip in range(chips):
                        yield pltpu.make_async_copy(
                            lefts[n * cores].at[:, core_rows(place, chip, 0, deep)],
                            left.at[at, pl.ds(chip * deep, deep)],
                            chip_sems.at[n, chip],
                        )
                else:
                    yield pltpu.make_async_copy(
                        lefts[n * cores + k], left.at[at], load_sems.at[0, n * cores + k]
                    )
                yield pltpu.make_async_copy(
                    rights[n * cores + k], right.at[:, at], load_sems.at[1, n * cores + k]
                )

    for copy in loads():
        copy.start()
    place.greet(True, True)
    inner.begin()
    act_order = [nearby(place, k) for k in range(col_count - 1, 0, -1)]
    act_early, act_late = list(act_order), list(act_order)
    acts.early(act_early.pop(0), True) if act_early else None
    smalls = SmallSum(place, small, small_out, ring_held, line_held, ring_sems, line_sems)
    smalls.begin()
    stages = list(smalls.stages)
    for copy in loads():
        copy.wait()

    def inside(n, col):
        return PlaneSum(
            place,
            acc[n].at[col],
            None,
            per[n][1].at[col],
            per[n][2].at[col],
            (ps.at[n, col], pr.at[n, col]),
        )

    parts = [inside(n, col) for n, col in entries]
    final = len(entries) - count
    total = len(entries) + inner.count

    def start(number):
        if number >= len(entries):
            inner.start(number - len(entries))
            return
        n, col = entries[number]
        left, right = per[n][5], per[n][6]
        deep = acc[n].shape[2]

        def chip_rows(chip, carry):
            at = pl.ds(pl.multiple_of(chip * deep, deep), deep)
            acc[n][col, chip] = dot_tokens(left[:, at], right[col]).astype(bf16)
            return carry

        lax.fori_loop(0, acc[n].shape[1], chip_rows, 0)
        parts[number].first()

    def middle(number):
        if number >= len(entries):
            inner.middle(number - len(entries))
        else:
            parts[number].second()

    def out_copy(n):
        return pltpu.make_async_copy(per[n][4], outs[n], out_sems.at[n])

    def close(number):
        if number >= len(entries):
            inner.close(number - len(entries))
            if number == len(entries) + 1 or total == len(entries) + 1:
                finish_lines()
            return
        parts[number].third()
        n, col = entries[number]
        if number < final:
            lines[n].early(col, True)
        if number >= 2 * count:
            waiting.pop(0)()

    waiting = [functools.partial(lines[n].late, col, True) for n, col in entries[:final]]

    def finish_lines():
        while waiting:
            waiting.pop(0)()
        for n in range(count):
            lines[n].last(per[n][4])
            out_copy(n).start()

    for number in range(total + 2):
        if number < total:
            start(number)
        if 1 <= number <= total:
            middle(number - 1)
        if 2 <= number:
            close(number - 2)
        if act_early and number % 2 == 1:
            acts.early(act_early.pop(0), True)
        if act_late and number >= 3 and number % 2 == 1:
            acts.late(act_late.pop(0), True)
        if stages:
            stages.pop(0)()
    for stage in stages:
        stage()
    for col in act_early:
        acts.early(col, True)
    for col in act_late:
        acts.late(col, True)
    acts.last(act_out)
    for n in range(count):
        out_copy(n).wait()
    for part in parts:
        part.finish()
    inner.finish()
    for line in lines + [acts]:
        line.finish()


def sum_all(lefts, rights, inner_terms, act_terms, small, row_count, col_count, act_type):
    count = len(rights)
    sizes = plane_sizes(row_count)
    na, nb, nk = sizes
    chips = na * nb
    tokens = lefts[0][0].shape[0]
    deep = lefts[0][0].shape[1] // row_count
    steps = max(col_count - 1, 1)
    firsts, seconds = PlaneSum.counts_of(sizes)
    widths = [right[0].shape[2] for right in rights]
    token_rows = act_terms.shape[0] // col_count
    inner_width = inner_terms.shape[1]
    chunk = min(512, inner_width)
    scratch = []
    for width in widths:
        scratch += [
            pltpu.VMEM((col_count, chips, deep, width), bf16),
            pltpu.VMEM((col_count, 2, max(seconds, 1), deep // 2, width), bf16),
            pltpu.VMEM((col_count, 2, max(firsts, 1), deep // 2, width), bf16),
            pltpu.VMEM((2, steps, deep, width), bf16),
            pltpu.VMEM((deep, width), f32),
            pltpu.VMEM((nk * tokens, chips * deep), bf16),
            pltpu.VMEM((col_count, nk * tokens, width), bf16),
        ]
    scratch += InnerSum.scratch(sizes, deep, inner_width, chunk)
    plane_sems = (count, col_count, 2, max(PlaneSum.sem_count(sizes), 1))
    scratch += [
        pltpu.VMEM((2, steps, token_rows, act_terms.shape[1]), bf16),
        pltpu.SemaphoreType.DMA((2, count * nk)),
        pltpu.SemaphoreType.DMA((count,)),
        pltpu.SemaphoreType.DMA(plane_sems),
        pltpu.SemaphoreType.DMA(plane_sems),
        pltpu.SemaphoreType.DMA((count + 1, 2, steps)),
        pltpu.SemaphoreType.DMA((count + 1, 2, steps)),
        pltpu.VMEM((3, max(sizes)) + small.shape, f32),
        pltpu.VMEM((col_count,) + small.shape, f32),
        pltpu.SemaphoreType.DMA((2, 3, max(max(sizes) - 1, 1))),
        pltpu.SemaphoreType.DMA((2, 2, steps)),
        pltpu.SemaphoreType.DMA((count, chips)),
    ]
    vmem = pl.BlockSpec(memory_space=pltpu.VMEM)
    flops = sum(2 * nk * tokens * chips * deep * width * col_count for width in widths)
    return pl.pallas_call(
        functools.partial(sum_kernel, (row_count, col_count), count, chunk),
        out_shape=[jax.ShapeDtypeStruct((deep, width), f32) for width in widths]
        + [
            jax.ShapeDtypeStruct((deep, inner_width), f32),
            jax.ShapeDtypeStruct((token_rows, act_terms.shape[1]), act_type),
            jax.ShapeDtypeStruct(small.shape, f32),
        ],
        in_specs=[ANY] * (2 * count * nk) + [ANY, vmem, vmem],
        out_specs=[ANY] * (count + 1) + [vmem, vmem],
        scratch_shapes=scratch,
        compiler_params=pltpu.CompilerParams(
            collective_id=1, has_side_effects=True, vmem_limit_bytes=63 << 20
        ),
        cost_estimate=pl.CostEstimate(
            flops=flops, bytes_accessed=inner_terms.size * 2, transcendentals=0
        ),
        name="sum_weights",
    )(
        *[left for pair in lefts for left in pair],
        *[right for pair in rights for right in pair],
        inner_terms.reshape(chips, nk, deep, inner_width),
        act_terms,
        small,
    )


LANES = 2 * HD


def lower_lanes():
    return lax.broadcasted_iota(jnp.int32, (1, LANES), 1) < HD


def rope_lanes(values, cosine, sinusoid):
    lane = lax.broadcasted_iota(jnp.int32, (1, LANES), 1)
    other = jnp.where(
        lane % HD < HD // 2,
        pltpu.roll(values, LANES - HD // 2, 1),
        pltpu.roll(values, HD // 2, 1),
    )
    return values * cosine + other * sinusoid


def head_at(tile, head, upper):
    if (head % 2 == 1) != upper:
        tile = pltpu.roll(tile, HD, 1)
    keep = lower_lanes()
    if upper:
        keep = jnp.logical_not(keep)
    return jnp.where(keep, tile, 0.0)


def tile_of(head):
    return slice(head // 2 * LANES, head // 2 * LANES + LANES)


def pair_tile(even, odd, upper):
    if upper:
        even = pltpu.roll(even, HD, 1)
    else:
        odd = pltpu.roll(odd, HD, 1)
    return jnp.where(lower_lanes(), even, odd)


def attend_kernel(sizes, heads, group, back, *refs):
    xn, x, wf_in, wo_in, bias, cosq, sinq, coskv, sinkv, gain, tiles = refs[:11]
    q_out, kv_out, mixed_out, lse_out, full_tiles, hidden, hn = refs[11:18]
    q, kv, mixed, lse, wf, wo, w_sems, o_sems, sends, recvs, t_sems, ps, pr = refs[18:]
    place = Place(*sizes)
    cols, col = place.cols, place.col
    tokens = xn.shape[0]
    query_width = heads * HD
    own_rows = pl.ds(back * tokens, tokens)
    pairs = heads // group

    def weight_copies(z):
        return (
            pltpu.make_async_copy(wf_in.at[z], wf.at[z], w_sems.at[0, z]),
            pltpu.make_async_copy(wo_in.at[z], wo.at[z], w_sems.at[1, z]),
        )

    for number in (0, 1):
        for z in range(cols):
            weight_copies(z)[number].start()
    for step in range(1, back + 1):

        @pl.when(col < step)
        def _():
            kv[:, (back - step) * tokens : (back - step + 1) * tokens] = jnp.zeros(
                (cols, tokens, kv.shape[2]), bf16
            )

    keeps = [
        pltpu.make_async_copy(
            tiles.at[f],
            full_tiles.at[f, pl.ds(place.row * tiles.shape[1], tiles.shape[1])],
            t_sems.at[f],
        )
        for f in range(tiles.shape[0])
    ]
    for keep in keeps:
        keep.start()
    place.greet(True, True)
    parts = [
        tile_gather(place, full_tiles.at[f], tiles.at[f], ps.at[f], pr.at[f])
        for f in range(tiles.shape[0])
    ]
    for part in parts:
        part.first()

    def hop(z, step):
        source = kv.at[z, pl.ds((back - step + 1) * tokens, tokens)]
        target = kv.at[z, pl.ds((back - step) * tokens, tokens)]
        return remote(
            source, target, sends.at[step - 1, z], recvs.at[step - 1, z], (place.row, col + 1)
        )

    def goes(step):
        return (col < cols - 1) & (col >= step - 1)

    def send(z, step):
        pl.when(goes(step))(lambda: hop(z, step).start())

    def receive(z, step):
        ref = kv.at[z, pl.ds((back - step) * tokens, tokens)]

        @pl.when(col >= step)
        def _():
            remote(
                ref, ref, sends.at[step - 1, z], recvs.at[step - 1, z], (place.row, col + 1)
            ).wait_recv()

    def project(z, carry):
        weight_copies(z)[0].wait()
        pre = matmul(xn[...], wf[z])
        for n in range(query_width // LANES):
            at = slice(n * LANES, (n + 1) * LANES)
            q[z, :, at] = rope_lanes(pre[:, at], cosq[...], sinq[...]).astype(bf16)
        for n in range(pairs):
            at = slice(n * LANES, (n + 1) * LANES)
            tile = pre[:, query_width + n * LANES : query_width + (n + 1) * LANES]
            kv[z, own_rows, at] = rope_lanes(tile, coskv[...], sinkv[...]).astype(bf16)
        if back > 0:
            send(z, 1)
        return carry

    lax.fori_loop(0, cols, project, 0)
    if parts:
        parts[0].second()
    for step in range(1, back):
        for z in range(cols):
            receive(z, step)
            send(z, step + 1)

    def attend(z, carry):
        if back > 0:
            receive(z, back)
        lane = lax.broadcasted_iota(jnp.int32, (1, LANES), 1)
        logs = jnp.zeros((tokens, LANES), f32)
        outs = []
        for head in range(heads):
            pair = head // group
            keyval = kv[z, :, pair * LANES : (pair + 1) * LANES]
            query = head_at(q[z, :, tile_of(head)].astype(f32), head, False) * HD**-0.5
            scores = against(query.astype(bf16), keyval) + bias[...]
            summit = jnp.max(scores, axis=1, keepdims=True)
            weights = jnp.exp(scores - summit)
            total = jnp.sum(weights, axis=1, keepdims=True)
            chances = (weights * (1.0 / total)).astype(bf16)
            outs.append(matmul(chances, keyval))
            logs = jnp.where(lane == head, summit + jnp.log(total), logs)
            if head % 2 == 1:
                mixed[z, :, tile_of(head)] = pair_tile(outs[-2], outs[-1], True).astype(bf16)
        lse[z] = jnp.transpose(logs)[:heads]

        @pl.when(z == 0)
        def _():
            for part in parts[1:]:
                part.second()

        @pl.when(z == max(cols - 2, 1))
        def _():
            for part in parts[:-1]:
                part.third()

        return carry

    lax.fori_loop(0, cols, attend, 0)
    outputs = [
        pltpu.make_async_copy(source, target, o_sems.at[n])
        for n, (source, target) in enumerate(
            ((q, q_out), (kv, kv_out), (mixed, mixed_out), (lse, lse_out))
        )
    ]
    for copy in outputs:
        copy.start()
    hidden[...] = x[...].astype(f32)

    def project_out(z, carry):
        weight_copies(z)[1].wait()
        hidden[...] += against(mixed[z], wo[z])
        return carry

    lax.fori_loop(0, cols, project_out, 0)
    total = hidden[...]
    scale = lax.rsqrt(jnp.mean(total * total, axis=1, keepdims=True) + epsilon)
    hn[...] = (total * scale * gain[...]).astype(bf16)
    if parts:
        parts[-1].third()
    for part in parts:
        part.finish()
    for copy in keeps + outputs:
        copy.wait()
    for step in range(1, back + 1):
        for z in range(cols):
            pl.when(goes(step))(lambda: hop(z, step).wait_send())


def attend(
    xn, x, wf, wo, bias, tables, gain, tiles, heads, group, back, row_count, col_count, cid
):
    tokens, width = xn.shape
    query_width = heads * HD
    kv_shape = (col_count, (back + 1) * tokens, heads // group * LANES)
    q_shape = (col_count, tokens, query_width)
    lse_shape = (col_count, heads, tokens)
    vmem = pl.BlockSpec(memory_space=pltpu.VMEM)
    keys = (back + 1) * tokens
    count = tiles.shape[0]
    plane_sems = (count, 2, PlaneGather.sem_count(plane_sizes(row_count)))
    return pl.pallas_call(
        functools.partial(attend_kernel, (row_count, col_count), heads, group, back),
        out_shape=[
            jax.ShapeDtypeStruct(q_shape, bf16),
            jax.ShapeDtypeStruct(kv_shape, bf16),
            jax.ShapeDtypeStruct(q_shape, bf16),
            jax.ShapeDtypeStruct(lse_shape, f32),
            jax.ShapeDtypeStruct((count, row_count * tiles.shape[1], tiles.shape[2]), bf16),
            jax.ShapeDtypeStruct((tokens, width), f32),
            jax.ShapeDtypeStruct((tokens, width), bf16),
        ],
        in_specs=[vmem, vmem, ANY, ANY] + [vmem] * 7,
        out_specs=[ANY] * 5 + [vmem] * 2,
        scratch_shapes=[
            pltpu.VMEM(q_shape, bf16),
            pltpu.VMEM(kv_shape, bf16),
            pltpu.VMEM(q_shape, bf16),
            pltpu.VMEM(lse_shape, f32),
            pltpu.VMEM(wf.shape, bf16),
            pltpu.VMEM(wo.shape, bf16),
            pltpu.SemaphoreType.DMA((2, col_count)),
            pltpu.SemaphoreType.DMA((4,)),
            pltpu.SemaphoreType.DMA((max(back, 1), col_count)),
            pltpu.SemaphoreType.DMA((max(back, 1), col_count)),
            pltpu.SemaphoreType.DMA((count,)),
            pltpu.SemaphoreType.DMA(plane_sems),
            pltpu.SemaphoreType.DMA(plane_sems),
        ],
        compiler_params=pltpu.CompilerParams(
            collective_id=cid, has_side_effects=True, vmem_limit_bytes=56 << 20
        ),
        cost_estimate=pl.CostEstimate(
            flops=2 * tokens * (wf.size + wo.size) + 4 * col_count * heads * tokens * keys * HD,
            bytes_accessed=(wf.size + wo.size) * 2,
            transcendentals=col_count * heads * tokens * keys,
        ),
        name="attend",
    )(xn, x, wf, wo, bias, *tables, gain, tiles)


def attend_back_kernel(sizes, heads, group, back, chunk, *refs):
    dhb, xn, lse, bias, cosq, sinq, coskv, sinkv = refs[:8]
    mixed_in, q_in, kv_in, wo_in, wf_in, terms = refs[8:14]
    dxn, dqkv_out, sum_out, xn_sib, dhb_sib, mixed_sib, dqkv_sib = refs[14:21]
    q, kv, wo, wf, dmix, dkv, dqkv, going, coming, dst, pst, rhs_q, rhs_o = refs[21:34]
    in_sems, wo_sems, wf_sems, out_sems, pair_sems, row_sems, sends, recvs = refs[34:42]
    place = Place(*sizes)
    cols, col = place.cols, place.col
    cores = place.sizes[2]
    tokens = dhb.shape[0]
    query_width = heads * HD
    pairs = heads // group
    hidden = sum_out.shape[1] // 2

    def inner_target(e):
        at = lax.rem(e, 2) * hidden + e // 2 * chunk
        return sum_out.at[:, pl.ds(pl.multiple_of(at, chunk), chunk)]

    def inner_terms(e, core):
        at = pl.multiple_of(lax.rem(e, 2) * chunk, chunk)
        return terms.at[e // 2, :, core, :, pl.ds(at, chunk)]

    inner = InnerSum(place, 2 * hidden // chunk, inner_terms, inner_target, refs[42:])

    in_copies = [
        pltpu.make_async_copy(q_in, q, in_sems.at[0]),
        pltpu.make_async_copy(kv_in, kv, in_sems.at[1]),
    ]

    def wo_copy(z):
        slot = lax.rem(z, 2)
        return pltpu.make_async_copy(wo_in.at[z], wo.at[slot], wo_sems.at[slot])

    def wf_copy(z):
        slot = lax.rem(z, 2)
        return pltpu.make_async_copy(wf_in.at[z], wf.at[slot], wf_sems.at[slot])

    wo_copy(0).start()
    for copy in in_copies:
        copy.start()
    for z in range(min(2, cols)):
        wf_copy(z).start()
    place.greet(True, True)

    other = place.device(2, 1)
    exchanges = []
    if cores > 1:
        chips, deep = terms.shape[1], terms.shape[3]
        moves = [(mixed_in, mixed_sib)]
        for chip in range(chips):
            to, rows = pl.ds(chip * deep, deep), core_rows(place, chip, 1, deep)
            moves += [(xn.at[:, rows], xn_sib.at[:, to]), (dhb.at[:, rows], dhb_sib.at[:, to])]
        exchanges = [
            remote(source, target, pair_sems.at[0, n], pair_sems.at[1, n], other)
            for n, (source, target) in enumerate(moves)
        ]

    def row_exchange(z):
        return remote(dqkv.at[z], dqkv_sib.at[z], row_sems.at[0, z], row_sems.at[1, z], other)

    def out_copy(z):
        return pltpu.make_async_copy(dqkv.at[z], dqkv_out.at[z], out_sems.at[z])

    inner.begin()
    for exchange in exchanges:
        exchange.start()
    dxn[...] = jnp.zeros_like(dxn)
    for copy in in_copies:
        copy.wait()

    def hop(z, step):
        return remote(
            going.at[step - 1, z],
            coming.at[step - 1, z],
            sends.at[step - 1, z],
            recvs.at[step - 1, z],
            (place.row, col - 1),
        )

    def goes(step):
        return col - back + step - 1 >= 0

    def comes(step):
        return (col < cols - 1) & (col + step - back >= 0)

    def send(z, step):
        pl.when(goes(step))(lambda: hop(z, step).start())

    def chunk_rows(step):
        return slice(step * tokens, (step + 1) * tokens)

    def halo(step, z):
        if step > 0:
            pl.when(comes(step))(lambda: hop(z, step).wait_recv())
            term = jnp.where(comes(step), coming[step - 1, z].astype(f32), 0.0)
            total = dkv[z, chunk_rows(step)] + term
        else:
            total = dkv[z, chunk_rows(step)]
        if step < back:
            going[step, z] = total.astype(bf16)
            send(z, step + 1)
            return
        for n in range(pairs):
            at = slice(n * LANES, (n + 1) * LANES)
            dqkv[z, :, query_width + n * LANES : query_width + (n + 1) * LANES] = rope_lanes(
                total[:, at], coskv[...], sinkv[...]
            ).astype(bf16)
        out_copy(z).start()
        if cores > 1:
            row_exchange(z).start()
        wf_copy(z).wait()
        dxn[...] += against(dqkv[z], wf[lax.rem(z, 2)])
        when(z + 2 < cols, lambda: wf_copy(z + 2).start())

    def halos(z):
        for step in range(1, back + 1):
            at = z - step
            when((at >= 0) & (at < cols), lambda: halo(step, at))

    def one_col(z, carry):
        wo_copy(z).wait()
        when(z + 1 < cols, lambda: wo_copy(z + 1).start())
        dmix[...] = matmul(dhb[...], wo[lax.rem(z, 2)]).astype(bf16)
        for n in range(pairs):
            keyval = kv[z, :, n * LANES : (n + 1) * LANES]
            for i in range(group):
                head = n * group + i
                at = slice(i * tokens, (i + 1) * tokens)
                query = head_at(q[z, :, tile_of(head)].astype(f32), head, False) * HD**-0.5
                query = query.astype(bf16)
                grad = head_at(dmix[:, tile_of(head)].astype(f32), head, True).astype(bf16)
                rhs_q[at] = query
                rhs_o[at] = grad
                chances = jnp.exp(against(keyval, query) + bias[...] - lse[z, head : head + 1])
                grad_chance = against(keyval, grad)
                centre = jnp.sum(chances * grad_chance, axis=0, keepdims=True)
                dst[:, at] = (chances * (grad_chance - centre)).astype(bf16)
                pst[:, at] = chances.astype(bf16)
            dkv[z, :, n * LANES : (n + 1) * LANES] = matmul(dst[...], rhs_q[...]) + matmul(
                pst[...], rhs_o[...]
            )
            grad_rows = dot_tokens(keyval, dst[...])
            for i in range(0, group, 2):
                tile = jnp.concatenate(
                    [
                        grad_rows[:HD, i * tokens : (i + 1) * tokens],
                        grad_rows[:HD, (i + 1) * tokens : (i + 2) * tokens],
                    ],
                    axis=0,
                )
                turned = rope_lanes(jnp.transpose(tile), cosq[...], sinq[...]) * HD**-0.5
                dqkv[z, :, tile_of(n * group + i)] = turned.astype(bf16)
            inner.tick(z * pairs + n)
        halo(0, z)
        halos(z)
        return carry

    lax.fori_loop(0, cols, one_col, 0)
    ticks = list(range(cols * pairs, inner.count + 2))
    for z in range(cols, cols + back):
        if ticks:
            inner.tick(ticks.pop(0))
        halos(z)
    for t in ticks:
        inner.tick(t)
    for z in range(cols):
        out_copy(z).wait()
        if cores > 1:
            row_exchange(z).wait_send()
            row_exchange(z).wait_recv()
    for exchange in exchanges:
        exchange.wait_send()
        exchange.wait_recv()
    for step in range(1, back + 1):
        for z in range(cols):
            pl.when(goes(step))(lambda: hop(z, step).wait_send())
    inner.finish()


def attend_back(
    dhb, xn, lse, bias, tables, mixed, q, kv, wo, wf, terms, group, sizes, cid
):
    row_count, col_count = sizes
    plane = plane_sizes(row_count)
    chips = plane[0] * plane[1]
    tokens, width = dhb.shape
    heads = lse.shape[1]
    back = kv.shape[1] // tokens - 1
    pairs = heads // group
    keys = kv.shape[1]
    all_width = wf.shape[2]
    tiles, _, chunk = terms.shape
    chunk = chunk // 2
    inner_width = 2 * tiles * chunk
    deep = terms.shape[1] // row_count
    row_shape = (col_count, tokens, all_width)
    halo_shape = (max(back, 1), col_count, tokens, kv.shape[2])
    vmem = pl.BlockSpec(memory_space=pltpu.VMEM)
    return pl.pallas_call(
        functools.partial(attend_back_kernel, sizes, heads, group, back, chunk),
        out_shape=[
            jax.ShapeDtypeStruct((tokens, width), f32),
            jax.ShapeDtypeStruct(row_shape, bf16),
            jax.ShapeDtypeStruct((deep, inner_width), f32),
            jax.ShapeDtypeStruct((tokens, chips * deep), bf16),
            jax.ShapeDtypeStruct((tokens, chips * deep), bf16),
            jax.ShapeDtypeStruct(mixed.shape, bf16),
            jax.ShapeDtypeStruct(row_shape, bf16),
        ],
        in_specs=[vmem] * 8 + [ANY] * 6,
        out_specs=[vmem] + [ANY] * 6,
        scratch_shapes=[
            pltpu.VMEM(q.shape, bf16),
            pltpu.VMEM(kv.shape, bf16),
            pltpu.VMEM((2,) + wo.shape[1:], bf16),
            pltpu.VMEM((2,) + wf.shape[1:], bf16),
            pltpu.VMEM((tokens, heads * HD), bf16),
            pltpu.VMEM(kv.shape, f32),
            pltpu.VMEM(row_shape, bf16),
            pltpu.VMEM(halo_shape, bf16),
            pltpu.VMEM(halo_shape, bf16),
            pltpu.VMEM((keys, group * tokens), bf16),
            pltpu.VMEM((keys, group * tokens), bf16),
            pltpu.VMEM((group * tokens, LANES), bf16),
            pltpu.VMEM((group * tokens, LANES), bf16),
            pltpu.SemaphoreType.DMA((2,)),
            pltpu.SemaphoreType.DMA((2,)),
            pltpu.SemaphoreType.DMA((2,)),
            pltpu.SemaphoreType.DMA((col_count,)),
            pltpu.SemaphoreType.DMA((2, 1 + 2 * chips)),
            pltpu.SemaphoreType.DMA((2, col_count)),
            pltpu.SemaphoreType.DMA((max(back, 1), col_count)),
            pltpu.SemaphoreType.DMA((max(back, 1), col_count)),
        ]
        + InnerSum.scratch(plane, deep, inner_width, chunk),
        compiler_params=pltpu.CompilerParams(
            collective_id=cid, has_side_effects=True, vmem_limit_bytes=62 << 20
        ),
        cost_estimate=pl.CostEstimate(
            flops=2 * tokens * (wf.size + wo.size) + 10 * col_count * heads * tokens * keys * HD,
            bytes_accessed=(wf.size + wo.size + terms.size) * 2,
            transcendentals=col_count * heads * tokens * keys,
        ),
        name="attend_back",
    )(
        dhb,
        xn,
        lse,
        bias,
        *tables,
        mixed,
        q,
        kv,
        wo,
        wf,
        terms.reshape(tiles, chips, plane[2], deep, 2 * chunk),
    )


def rope_tables(position):
    indices = jnp.arange(HD // 2, dtype=f32)
    frequency = rope_base ** (-(indices * 2.0 / HD))
    wavelen = 2.0 * jnp.pi / frequency
    smooth = (8192.0 / wavelen - 1.0) / 3.0
    scaled = jnp.where(
        wavelen > 8192.0, frequency / 32.0, (1.0 - smooth) * frequency / 32.0 + smooth * frequency
    )
    frequency = jnp.where(wavelen < 2048.0, frequency, scaled)
    angles = position.astype(f32)[:, None] * frequency[None, :]
    return (jnp.cos(angles), jnp.sin(angles))


def rotate(values, cosine, sinusoid):
    halfway = values.shape[-1] // 2
    former = values[..., :halfway]
    latter = values[..., halfway:]
    cos_wide = cosine[:, None, :]
    sin_wide = sinusoid[:, None, :]
    return jnp.concatenate(
        [former * cos_wide - latter * sin_wide, latter * cos_wide + former * sin_wide], axis=-1
    )


def normalize(values, gain):
    scale = lax.rsqrt(jnp.mean(values * values, axis=1, keepdims=True) + epsilon)
    return ((values * scale * gain).astype(bf16), scale)


def norm_back(grad_in, values, scale, gain):
    weighted = grad_in * gain
    inner_sum = jnp.mean(weighted * values, axis=1, keepdims=True)
    return (
        scale * weighted - values * (scale * scale * scale) * inner_sum,
        jnp.sum(grad_in * values * scale, axis=0),
    )


def against(left, right):
    return lax.dot_general(left, right, (((1,), (1,)), ((), ())), preferred_element_type=f32)


def over_rows(left, right):
    return lax.dot_general(left, right, (((0,), (0,)), ((), ())), preferred_element_type=f32)


def matmul(left, right):
    return jnp.dot(left, right, preferred_element_type=f32)


def shift(values, step, col_count):
    if step > 0:
        pairs = [(i, i + step) for i in range(col_count - step)]
    else:
        pairs = [(i, i + step) for i in range(-step, col_count)]
    return lax.ppermute(values, "col", pairs)


def shards(
    tokens,
    seq_lens,
    attn_gain,
    query_weight,
    keyvalue_weight,
    output_weight,
    mlp_gain,
    hidden_weight,
    down_weight,
    out_grad,
):
    row_count, col_count = lax.axis_size("row"), lax.axis_size("col")
    local = tokens.shape[0]
    block_rows = local * col_count
    col = lax.axis_index("col")
    deep = query_weight.shape[0]
    width = tokens.shape[1]
    query_width = query_weight.shape[1]
    pairs = keyvalue_weight.shape[1]
    heads = query_width // HD
    group = heads // pairs
    hidden = down_weight.shape[1]
    back = min(-(-(SEQ_MAX - 1) // local), col_count - 1)

    lengths = seq_lens[0]
    finish = jnp.cumsum(lengths)
    indices = jnp.arange(block_rows, dtype=jnp.int32)
    passed = indices[:, None] >= finish[None, :]
    segment = jnp.sum(passed.astype(jnp.int32), axis=1, dtype=jnp.int32)
    position = indices - jnp.sum(jnp.where(passed, lengths[None, :], 0), axis=1, dtype=jnp.int32)
    own_position = lax.dynamic_slice(position, (col * local,), (local,))
    own_segment = lax.dynamic_slice(segment, (col * local,), (local,))
    padded = jnp.concatenate([jnp.full((back * local,), -1, jnp.int32), segment])
    key_segment = lax.dynamic_slice(padded, (col * local,), ((back + 1) * local,))
    key_index = jnp.arange((back + 1) * local, dtype=jnp.int32) - back * local
    query_index = jnp.arange(local, dtype=jnp.int32)
    allowed = (own_segment[:, None] == key_segment[None, :]) & (
        key_index[None, :] <= query_index[:, None]
    )
    cosine, sinusoid = rope_tables(own_position)
    gain_first = attn_gain.astype(f32)
    gain_second = mlp_gain.astype(f32)

    first_weight = jnp.concatenate(
        [query_weight, keyvalue_weight.reshape(deep, pairs * 2 * HD)], axis=1
    )
    full_first, full_output, full_down, rows_grad = gather_all(
        [first_weight, output_weight], [down_weight], out_grad, row_count, col_count
    )

    tile = min(512, hidden)
    tiles = hidden // tile
    early = max(tiles // 2, 1)
    hidden_tiles = jnp.transpose(hidden_weight.reshape(deep, 2, tiles, tile), (2, 0, 1, 3))
    hidden_tiles = hidden_tiles.reshape(tiles, deep, 2 * tile)

    inputs = tokens.astype(f32)
    normal_in, scale_in = normalize(inputs, gain_first)
    halves = jnp.concatenate([cosine, cosine], axis=1)
    signed = jnp.concatenate([-sinusoid, sinusoid], axis=1)
    tables = (
        jnp.concatenate([halves, halves], axis=1),
        jnp.concatenate([signed, signed], axis=1),
        jnp.concatenate([halves, jnp.ones_like(halves)], axis=1),
        jnp.concatenate([signed, jnp.zeros_like(signed)], axis=1),
    )
    bias = jnp.where(allowed, 0.0, blocked).astype(f32)
    queries, all_keyvals, mixed, lse, early_tiles, hidden_in, normal_mid = attend(
        normal_in,
        tokens,
        full_first,
        full_output,
        bias,
        tables,
        gain_second[None],
        hidden_tiles[:early],
        heads,
        group,
        back,
        row_count,
        col_count,
        4,
    )
    scale_mid = lax.rsqrt(jnp.mean(hidden_in * hidden_in, axis=1, keepdims=True) + epsilon)

    grad_mid, out_terms, grad_hidden_part, grad_down_part = mlp(
        normal_mid,
        rows_grad,
        early_tiles,
        hidden_tiles[early:],
        full_down,
        row_count,
        col_count,
        3,
    )
    back_mid, gain_mid_part = norm_back(grad_mid, hidden_in, scale_mid, gain_second)
    grad_hidden_in = out_grad.astype(f32) + back_mid
    grad_low = grad_hidden_in.astype(bf16)
    cores = plane_sizes(row_count)[2]
    tables_back = (tables[0], -tables[1], tables[2], -tables[3])
    grad_in, grad_first, sum_hidden, normal_sib, grad_low_sib, mixed_sib, grad_first_sib = (
        attend_back(
            grad_low,
            normal_in,
            lse,
            bias.T,
            tables_back,
            mixed,
            queries,
            all_keyvals,
            full_output,
            full_first,
            grad_hidden_part,
            group,
            (row_count, col_count),
            5,
        )
    )
    back_in, gain_in_part = norm_back(grad_in, inputs, scale_in, gain_first)
    grad_tokens = (grad_hidden_in + back_in).astype(bf16)
    gain_parts = jnp.concatenate([gain_in_part, gain_mid_part]).reshape(-1, 128)
    lefts = [
        (normal_in, normal_sib)[:cores],
        (grad_low, grad_low_sib)[:cores],
    ]
    rights = [(grad_first, grad_first_sib)[:cores], (mixed, mixed_sib)[:cores]]
    sum_first, sum_output, sum_down, out_sum, gain_sums = sum_all(
        lefts, rights, grad_down_part, out_terms, gain_parts, row_count, col_count, f32
    )
    block_out = hidden_in + out_sum
    gain_in_sum, gain_mid_sum = gain_sums.reshape(2, width)
    return (
        block_out.astype(bf16),
        grad_tokens,
        gain_in_sum,
        sum_first[:, :query_width],
        sum_first[:, query_width:].reshape(deep, pairs, 2 * HD),
        sum_output,
        gain_mid_sum,
        sum_hidden.reshape(deep, 2, hidden),
        sum_down,
    )


def solution(mesh):
    return jax.shard_map(
        shards,
        mesh=mesh,
        in_specs=(
            P(("row", "col"), None),
            P("row", None),
            P(),
            P("row", "col"),
            P("row", "col", None),
            P("row", "col"),
            P(),
            P("row", None, "col"),
            P("row", "col"),
            P(("row", "col"), None),
        ),
        out_specs=(
            P(("row", "col"), None),
            P(("row", "col"), None),
            P(),
            P("row", "col"),
            P("row", "col", None),
            P("row", "col"),
            P(),
            P("row", None, "col"),
            P("row", "col"),
        ),
        check_vma=False,
    )
```

```python
import functools

import jax
import jax.numpy as jnp
from jax import lax
from jax.experimental import pallas as pl
from jax.experimental.pallas import tpu as pltpu
from jax.sharding import PartitionSpec as P

HD = 64
SEQ_MAX = 512
MESH = pl.DeviceIdType.MESH
LAG = 2
ANY = pl.BlockSpec(memory_space=pl.ANY)

epsilon = 1e-05
rope_base = 500000.0
blocked = -1e30
bf16 = jnp.bfloat16
f32 = jnp.float32


def plane_sizes(row_count):
    cores = 2 if row_count % 2 == 0 else 1
    chips = row_count // cores
    first = 2 if chips % 2 == 0 else 1
    return first, chips // first, cores


class Place:
    def __init__(self, row_count, col_count):
        self.rows, self.cols = row_count, col_count
        self.sizes = plane_sizes(row_count)
        na, nb, nk = self.sizes
        self.row = lax.axis_index("row")
        self.col = lax.axis_index("col")
        self.at = (self.row // (nb * nk), (self.row // nk) % nb, self.row % nk)

    def row_of(self, at):
        _, nb, nk = self.sizes
        return (at[0] * nb + at[1]) * nk + at[2]

    def chip_of(self, at):
        return at[0] * self.sizes[1] + at[1]

    def moved(self, axis, step, at=None):
        at = list(self.at if at is None else at)
        size = self.sizes[axis]
        at[axis] = lax.rem(at[axis] + (step % size), size)
        return tuple(at)

    def device(self, axis, step):
        return (self.row_of(self.moved(axis, step)), self.col)

    def greet(self, plane, line):
        barrier = pltpu.get_barrier_semaphore()
        count = 0
        if plane:
            for axis in range(3):
                size = self.sizes[axis]
                for step in {1 % size, (size - 1) % size} - {0}:
                    pl.semaphore_signal(
                        barrier, inc=1, device_id=self.device(axis, step), device_id_type=MESH
                    )
                    count += 1
        if line and self.cols > 1:
            for step, there in self.line_ways():

                @pl.when(there)
                def _(step=step):
                    pl.semaphore_signal(
                        barrier, inc=1, device_id=(self.row, self.col + step), device_id_type=MESH
                    )

        if line and self.cols > 1:
            last = self.cols - 1
            count = count + jnp.minimum(self.col, 1) + jnp.minimum(last - self.col, 1)
        if not isinstance(count, int) or count:
            pl.semaphore_wait(barrier, count)

    def line_ways(self):
        return ((1, self.col < self.cols - 1), (-1, self.col > 0))


def when(condition, action):
    if condition is None or condition is True:
        action()
    elif condition is False:
        pass
    else:
        pl.when(condition)(action)


def remote(src, dst, send_sem, recv_sem, device):
    return pltpu.make_async_remote_copy(
        src_ref=src,
        dst_ref=dst,
        send_sem=send_sem,
        recv_sem=recv_sem,
        device_id=device,
        device_id_type=MESH,
    )


class LineGather:
    def __init__(self, place, own, block, send_sems, recv_sems):
        self.place, self.own, self.block = place, own, block
        self.sends, self.recvs = send_sems, recv_sems

    def copy(self, way, step, origin):
        place = self.place
        source = self.own if step == 1 else self.block(origin)
        return remote(
            source,
            self.block(origin),
            self.sends.at[way, step - 1],
            self.recvs.at[way, step - 1],
            (place.row, place.col + (1, -1)[way]),
        )

    def sends_at(self, way, step):
        col, last = self.place.col, self.place.cols - 1
        if way == 0:
            return (col >= step - 1) & (col < last), col - (step - 1)
        return (col + step - 1 <= last) & (col > 0), col + (step - 1)

    def gets_at(self, way, step):
        col, last = self.place.col, self.place.cols - 1
        if way == 0:
            return col >= step, col - step
        return col + step <= last, col + step

    def send(self, way, step):
        condition, origin = self.sends_at(way, step)
        when(condition, lambda: self.copy(way, step, origin).start())

    def receive(self, way, step):
        condition, origin = self.gets_at(way, step)

        def action():
            self.copy(way, step, origin).wait_recv()

        when(condition, action)
        if step < self.place.cols - 1:
            self.send(way, step + 1)

    def finish(self):
        for step in range(1, self.place.cols):
            for way in (0, 1):
                condition, origin = self.sends_at(way, step)
                when(condition, lambda: self.copy(way, step, origin).wait_send())


class PlaneGather:
    def __init__(self, place, block, own, send_sems, recv_sems):
        self.place, self.block, self.own = place, block, own
        self.sends, self.recvs = send_sems, recv_sems

    @staticmethod
    def sem_count(sizes):
        na, nb, _ = sizes
        return 2 * na * nb - 1

    def axes(self, half):
        return (1, 0) if half == 0 else (0, 1)

    def counts(self, half):
        first, second = self.axes(half)
        return self.place.sizes[first], self.place.sizes[second]

    def origin(self, half, i, j, core_step=0):
        first, second = self.axes(half)
        at = self.place.moved(first, -i)
        at = self.place.moved(second, -j, at)
        if core_step:
            at = self.place.moved(2, 1, at)
        return self.place.row_of(at)

    def copy(self, half, kind, i, j):
        np_, nq = self.counts(half)
        if kind == 0:
            number, device = i - 1, self.place.device(self.axes(half)[0], 1)
        elif kind == 1:
            number = (np_ - 1) + i * (nq - 1) + (j - 1)
            device = self.place.device(self.axes(half)[1], 1)
        else:
            number = (np_ * nq - 1) + i * nq + j
            device = self.place.device(2, 1)
        return number, device

    def sender(self, half, kind, i, j):
        number, device = self.copy(half, kind, i, j)
        oi, oj = (i - 1, j) if kind == 0 else ((i, j - 1) if kind == 1 else (i, j))
        ref = self.block(self.origin(half, oi, oj), half)
        source = self.own(half) if (oi, oj) == (0, 0) else ref
        return remote(source, ref, self.sends.at[half, number], self.recvs.at[half, number], device)

    def receiver(self, half, kind, i, j):
        number, device = self.copy(half, kind, i, j)
        ref = self.block(self.origin(half, i, j, 1 if kind == 2 else 0), half)
        return remote(ref, ref, self.sends.at[half, number], self.recvs.at[half, number], device)

    def all_copies(self):
        for half in (0, 1):
            np_, nq = self.counts(half)
            for i in range(1, np_):
                yield half, 0, i, 0
            for i in range(np_):
                for j in range(1, nq):
                    yield half, 1, i, j
            if self.place.sizes[2] > 1:
                for i in range(np_):
                    for j in range(nq):
                        yield half, 2, i, j

    def share(self, half, i, j):
        if self.place.sizes[2] > 1:
            self.sender(half, 2, i, j).start()

    def first(self):
        for half in (0, 1):
            if self.counts(half)[0] > 1:
                self.sender(half, 0, 1, 0).start()
        for half in (0, 1):
            self.share(half, 0, 0)

    def second(self):
        for half in (0, 1):
            np_, nq = self.counts(half)
            for i in range(np_):
                if i > 0:
                    self.receiver(half, 0, i, 0).wait_recv()
                    if i < np_ - 1:
                        self.sender(half, 0, i + 1, 0).start()
                if nq > 1:
                    self.sender(half, 1, i, 1).start()
                if i > 0:
                    self.share(half, i, 0)

    def third(self):
        for half in (0, 1):
            np_, nq = self.counts(half)
            for j in range(1, nq):
                for i in range(np_):
                    self.receiver(half, 1, i, j).wait_recv()
                    if j < nq - 1:
                        self.sender(half, 1, i, j + 1).start()
                    self.share(half, i, j)

    def shared(self):
        for copy in self.all_copies():
            if copy[1] == 2:
                self.receiver(*copy).wait_recv()

    def sent(self):
        for copy in self.all_copies():
            self.sender(*copy).wait_send()

    def finish(self):
        self.shared()
        self.sent()


def tile_gather(place, full, own, send_sems, recv_sems):
    deep = full.shape[0] // place.rows
    half = deep // 2

    def block(row, number):
        return full.at[pl.ds(row * deep + number * half, half)]

    def mine(number):
        if own is None:
            return block(place.row, number)
        return own.at[pl.ds(number * half, half)]

    return PlaneGather(place, block, mine, send_sems, recv_sems)


def nearby(place, number):
    low, high = place.col, place.cols - 1 - place.col
    both = jnp.minimum(low, high)
    way = jnp.minimum(jnp.maximum(high - low, -1), 1)
    step = (number + 1) // 2 * (-1 if number % 2 else 1)
    paired = jnp.minimum(jnp.maximum(2 * both - number + 1, 0), 1)
    return place.col + paired * step + (1 - paired) * way * (number - both)


def gather_kernel(sizes, count, inner, *refs):
    row_count, col_count = sizes
    every = count + inner
    own, own_act = refs[:every], refs[every]
    full, full_act = refs[every + 1 : 2 * every + 1], refs[2 * every + 1]
    local_sems, zs, zr, ps, pr = refs[2 * every + 2 :]
    place = Place(row_count, col_count)
    place.greet(True, True)
    token_rows = own_act.shape[0]

    def at(n, col, row):
        deep = own[n].shape[0]
        if n < count:
            return full[n].at[col, pl.ds(row * deep, deep)]
        return full[n].at[pl.ds(row * deep, deep)]

    lines = [
        LineGather(place, own[n], lambda j, n=n: at(n, j, place.row), zs.at[n], zr.at[n])
        for n in range(count)
    ]
    acts = LineGather(
        place,
        own_act,
        lambda j: full_act.at[pl.ds(j * token_rows, token_rows)],
        zs.at[count],
        zr.at[count],
    )

    def keep(n):
        if n == every:
            return pltpu.make_async_copy(own_act, acts.block(place.col), local_sems.at[n])
        return pltpu.make_async_copy(own[n], at(n, place.col, place.row), local_sems.at[n])

    for n in range(every + 1):
        keep(n).start()
    for line in lines:
        for way in (0, 1):
            line.send(way, 1)

    def inside(n, col, near):
        deep = own[n].shape[0]
        half = deep // 2

        def block(row, number):
            rows = pl.ds(row * deep + number * half, half)
            return full[n].at[col, rows] if n < count else full[n].at[rows]

        def mine(number):
            return own[n].at[pl.ds(number * half, half)] if near else block(place.row, number)

        return PlaneGather(place, block, mine, ps.at[n, col], pr.at[n, col])

    entries = [(n, k) for k in range(col_count) for n in range(count)]
    entries += [(n, 0) for n in range(count, every)]
    parts = [inside(n, nearby(place, k), k == 0) for n, k in entries]
    act_steps = list(range(1, col_count))

    def act_step():
        if act_steps:
            for way in (0, 1):
                acts.receive(way, act_steps[0])
            act_steps.pop(0)

    for number in range(len(parts) + 2):
        if number < len(parts):
            n, k = entries[number]
            if n == 0 and k > 0:
                for line in lines:
                    for way in (0, 1):
                        line.receive(way, k)
                if k == 1:
                    for way in (0, 1):
                        acts.send(way, 1)
                if k >= 3:
                    act_step()
            parts[number].first()
        if 1 <= number <= len(parts):
            parts[number - 1].second()
        if 2 <= number:
            parts[number - 2].third()
        if number >= len(parts):
            act_step()
    while act_steps:
        act_step()
    for n in range(every + 1):
        keep(n).wait()
    for part in parts:
        part.finish()
    for line in lines + [acts]:
        line.finish()


def gather_all(weights, inner_weights, act, row_count, col_count):
    count, inner = len(weights), len(inner_weights)
    sizes = plane_sizes(row_count)
    steps = max(col_count - 1, 1)
    every = list(weights) + list(inner_weights)
    plane_sems = (count + inner, col_count, 2, PlaneGather.sem_count(sizes))
    moved = sum(w.size for w in weights) * row_count * col_count * 2
    return pl.pallas_call(
        functools.partial(gather_kernel, (row_count, col_count), count, inner),
        out_shape=[
            jax.ShapeDtypeStruct((col_count, row_count * w.shape[0], w.shape[1]), bf16)
            for w in weights
        ]
        + [
            jax.ShapeDtypeStruct((row_count * w.shape[0], w.shape[1]), bf16) for w in inner_weights
        ]
        + [jax.ShapeDtypeStruct((col_count * act.shape[0], act.shape[1]), bf16)],
        in_specs=[pl.BlockSpec(memory_space=pltpu.VMEM)] * (len(every) + 1),
        out_specs=[ANY] * (len(every) + 1),
        scratch_shapes=[
            pltpu.SemaphoreType.DMA((len(every) + 1,)),
            pltpu.SemaphoreType.DMA((count + 1, 2, steps)),
            pltpu.SemaphoreType.DMA((count + 1, 2, steps)),
            pltpu.SemaphoreType.DMA(plane_sems),
            pltpu.SemaphoreType.DMA(plane_sems),
        ],
        compiler_params=pltpu.CompilerParams(collective_id=0, has_side_effects=True),
        cost_estimate=pl.CostEstimate(flops=0, bytes_accessed=moved, transcendentals=0),
        name="gather_weights",
    )(*every, act)


def line_gather_kernel(sizes, own, full, local_sem, sends, recvs):
    place = Place(*sizes)
    place.greet(False, True)
    rows = own.shape[0]
    line = LineGather(place, own, lambda j: full.at[pl.ds(j * rows, rows)], sends, recvs)
    for way in (0, 1):
        line.send(way, 1)
    keep = pltpu.make_async_copy(own, full.at[pl.ds(place.col * rows, rows)], local_sem)
    keep.start()
    for step in range(1, place.cols):
        for way in (0, 1):
            line.receive(way, step)
    keep.wait()
    line.finish()


def line_gather(own, row_count, col_count, collective_id):
    steps = max(col_count - 1, 1)
    return pl.pallas_call(
        functools.partial(line_gather_kernel, (row_count, col_count)),
        out_shape=jax.ShapeDtypeStruct((col_count * own.shape[0], own.shape[1]), own.dtype),
        in_specs=[pl.BlockSpec(memory_space=pltpu.VMEM)],
        out_specs=ANY,
        scratch_shapes=[
            pltpu.SemaphoreType.DMA,
            pltpu.SemaphoreType.DMA((2, steps)),
            pltpu.SemaphoreType.DMA((2, steps)),
        ],
        compiler_params=pltpu.CompilerParams(collective_id=collective_id, has_side_effects=True),
        cost_estimate=pl.CostEstimate(
            flops=0, bytes_accessed=own.size * 2 * col_count, transcendentals=0
        ),
        name="gather_line",
    )(own)


def add_rows(target, source):
    rows = target.shape[0]
    piece = 32 if rows % 32 == 0 else 16

    def body(n, carry):
        at = pl.ds(pl.multiple_of(n * piece, piece), piece)
        target[at] = (target[at].astype(f32) + source[at].astype(f32)).astype(target.dtype)
        return carry

    lax.fori_loop(0, rows // piece, body, 0)


class LineSum:
    def __init__(self, place, own, held, send_sems, recv_sems):
        self.place, self.own, self.held = place, own, held
        self.sends, self.recvs = send_sems, recv_sems

    def distance(self, way, col):
        return col - self.place.col if way == 0 else self.place.col - col

    def feeds(self, way):
        return self.place.col > 0 if way == 0 else self.place.col < self.place.cols - 1

    def copy(self, way, distance, source):
        return remote(
            source,
            self.held.at[way, distance - 1],
            self.sends.at[way, distance - 1],
            self.recvs.at[way, distance - 1],
            (self.place.row, self.place.col + (1, -1)[way]),
        )

    def arrived(self, way, distance):
        ref = self.held.at[way, distance]
        return remote(
            ref,
            ref,
            self.sends.at[way, distance],
            self.recvs.at[way, distance],
            (self.place.row, self.place.col + (1, -1)[way]),
        )

    def early(self, col, allowed):
        for way in (0, 1):
            far = self.distance(way, col)

            @pl.when(allowed & (far > 0) & jnp.logical_not(self.feeds(way)))
            def _():
                self.copy(way, far, self.own(col)).start()

    def late(self, col, allowed):
        for way in (0, 1):
            far = self.distance(way, col)

            @pl.when(allowed & (far > 0) & self.feeds(way))
            def _():
                self.arrived(way, far).wait_recv()
                add_rows(self.own(col), self.held.at[way, far])
                self.copy(way, far, self.own(col)).start()

    def last(self, out):
        if self.place.cols > 1:
            for way in (0, 1):
                when(self.feeds(way), lambda: self.arrived(way, 0).wait_recv())
        own = self.own(self.place.col)
        rows = own.shape[0]
        piece = 32 if rows % 32 == 0 else 16
        has = [self.feeds(way) for way in (0, 1)]

        def body(n, carry):
            at = pl.ds(pl.multiple_of(n * piece, piece), piece)
            total = own[at].astype(f32)
            if self.place.cols > 1:
                for way in (0, 1):
                    term = self.held[way, 0, at].astype(f32)
                    total = total + jnp.where(has[way], term, 0.0)
            out[at] = total.astype(out.dtype)
            return carry

        lax.fori_loop(0, rows // piece, body, 0)

    def finish(self):
        for distance in range(1, self.place.cols):
            for way in (0, 1):
                col = self.place.col + (distance if way == 0 else -distance)
                there = col < self.place.cols if way == 0 else col >= 0
                when(there, lambda: self.copy(way, distance, self.own(col)).wait_send())


def dot_tokens(left, right):
    return lax.dot_general(left, right, (((0,), (0,)), ((), ())), preferred_element_type=f32)


def plan_units(cols, tiles, early, hop_us, tile_us, unit_us):
    begin = 4.0
    chunk_at = [0.0] + [begin + hop_us * k for k in range(1, cols)]
    tile_at = [0.0] * early + [begin + 2.0 + tile_us * (n + 1) for n in range(tiles - early)]
    events = [(chunk_at[k], ("chunk", k)) for k in range(1, cols)]
    for f in range(early, tiles):
        second_at = begin + 1.0 + 0.35 * tile_us * (f - early + 1)
        events.append((second_at, ("second", f)))
        events.append((tile_at[f], ("third", f)))
    events.sort(key=lambda event: event[0])
    units = [(max(chunk_at[k], tile_at[f]), k, f) for k in range(cols) for f in range(tiles)]
    units.sort()
    plan, now, after = [], 0.0, []
    while units or events or after:
        while events and events[0][0] <= now:
            plan.append(events.pop(0)[1])
        if after and (not units or units[0][0] > now):
            step, cost = after.pop(0)
            plan.append(step)
            now += cost
            continue
        if units and units[0][0] <= now:
            _, k, f = units.pop(0)
            plan.append(("unit", k, f))
            now += unit_us
            if not any(unit[1] == k for unit in units):
                if k > 0:
                    after.append((("grad", k), 2.6 * unit_us))
                after.append((("y", k), 1.3 * unit_us))
                after.sort(key=lambda item: -item[0][1] if item[0][0] == "grad" else 1)
            continue
        now = min([events[0][0]] * bool(events) + [units[0][0]] * bool(units))
    return plan


def mlp_kernel(sizes, early, wide, *refs):
    hn_own, dy_in, wh_in, wh_own, wd_in = refs[:5]
    grad_out, y_out, dwh_out, down_out, core_held, second_held, first_held = refs[5:12]
    hn, dy, wh, wd, act, dgu, terms, staged, held, grad_staged, down_staged = refs[12:23]
    token_sems, tile_sems, wd_sems, y_sem, dw_sems, sends, recvs = refs[23:30]
    hs, hr, ps, pr, own_sem, grad_sems = refs[30:36]
    inner_sems, inner_stage = refs[36:39], refs[39:]
    place = Place(*sizes)
    cols = place.cols
    width, hidden = wd.shape
    tiles = wh.shape[0]
    tile = hidden // tiles
    wides = width // wide
    tokens = hn.shape[1]
    deep = wh_own.shape[0]

    def wide_at(n):
        return pl.ds(pl.multiple_of(n * wide, wide), wide)

    def piece(n):
        return LineSum(
            place, lambda j: terms.at[j, :, wide_at(n)], held.at[n], sends.at[n], recvs.at[n]
        )

    near = [nearby(place, k) for k in range(cols)]

    def dy_copy(j):
        return pltpu.make_async_copy(dy_in.at[j], dy.at[j], token_sems.at[j])

    def wd_copy(f):
        at = slice(f * tile, (f + 1) * tile)
        return pltpu.make_async_copy(wd_in.at[:, at], wd.at[:, at], wd_sems.at[f])

    def tile_copies(f):
        if f < early:
            return [pltpu.make_async_copy(wh_in.at[f], wh.at[f], tile_sems.at[f, 0])]
        rows = pl.ds(place.row * deep, deep)
        return [
            pltpu.make_async_copy(
                wh_own.at[:, pl.ds(number * hidden + f * tile, tile)],
                wh.at[f, rows, pl.ds(number * tile, tile)],
                tile_sems.at[f, number],
            )
            for number in (0, 1)
        ]

    own_copy = pltpu.make_async_copy(hn_own, hn.at[place.col], own_sem)
    own_copy.start()
    for f in range(early, tiles):
        for copy in tile_copies(f):
            copy.start()
    place.greet(True, True)
    own_copy.wait()
    line = LineGather(place, hn.at[place.col], lambda j: hn.at[j], hs, hr)
    for way in (0, 1):
        line.send(way, 1)
    parts = {
        f: tile_gather(place, wh.at[f], None, ps.at[f - early], pr.at[f - early])
        for f in range(early, tiles)
    }
    for f in range(early, tiles):
        for copy in tile_copies(f):
            copy.wait()
        parts[f].first()
    dy_copy(near[0]).start()
    for f in range(tiles):
        if f < early:
            tile_copies(f)[0].start()
        wd_copy(f).start()
    for k in range(1, cols):
        dy_copy(near[k]).start()

    def out_copy(j):
        return pltpu.make_async_copy(staged, y_out.at[j], y_sem)

    def unit(k, f):
        j = near[k]
        at = slice(f * tile, (f + 1) * tile)
        gate_up = matmul(hn[j], wh[f])
        gate, up = gate_up[:, :tile], gate_up[:, tile:]
        back = matmul(dy[j], wd[:, at])
        sigmoid = jax.nn.sigmoid(gate)
        silu = gate * sigmoid
        act[j, :, at] = (silu * up).astype(bf16)
        dgate = back * up * sigmoid * (1.0 + gate * (1.0 - sigmoid))
        dgu[j, :, 2 * f * tile : (2 * f + 1) * tile] = dgate.astype(bf16)
        dgu[j, :, (2 * f + 1) * tile : (2 * f + 2) * tile] = (back * silu).astype(bf16)

    def grad(k):
        j = near[k]

        def body(n, carry):
            at = wide_at(n)
            total = 0.0
            for f in range(tiles):
                total += against(dgu[j, :, 2 * f * tile : 2 * (f + 1) * tile], wh[f, at])
            terms[j, :, at] = total.astype(bf16)
            piece(n).early(j, True)
            return carry

        lax.fori_loop(0, wides, body, 0)

    stored = []

    def y_part(k):
        j = near[k]
        if stored:
            out_copy(near[stored[-1]]).wait()

        def body(n, carry):
            at = wide_at(n)
            staged[:, at] = against(act[j], wd[at]).astype(bf16)
            return carry

        lax.fori_loop(0, wides, body, 0)
        out_copy(j).start()
        stored.append(k)

    def late(number):
        low, high = place.col, cols - 1 - place.col
        up_first = jnp.minimum(jnp.maximum(high - low, 0), 1)
        side = up_first * high + (1 - up_first) * low
        way = 2 * up_first - 1
        first = jnp.minimum(jnp.maximum(side - number, 0), 1)
        col = place.col + first * way * (number + 1) - (1 - first) * way * (number + 1 - side)
        return col

    calls = [(number, n) for number in range(cols - 1) for n in range(wides)]

    def do_late(call):
        number, n = call
        piece(n).late(late(number), True)

    def next_late():
        if calls:
            do_late(calls.pop(0))

    seen_tiles, seen_chunks = set(), set()
    for step in plan_units(cols, tiles, early, 24.0, 18.0, 2.1):
        if step[0] == "chunk":
            for way in (0, 1):
                line.receive(way, step[1])
        elif step[0] == "second":
            parts[step[1]].second()
        elif step[0] == "third":
            parts[step[1]].third()
            parts[step[1]].shared()
        elif step[0] == "unit":
            _, k, f = step
            if f not in seen_tiles:
                seen_tiles.add(f)
                if f < early:
                    tile_copies(f)[0].wait()
                wd_copy(f).wait()
            if k not in seen_chunks:
                seen_chunks.add(k)
                dy_copy(near[k]).wait()
            unit(k, f)
        elif step[0] == "grad":
            grad(step[1])
            if step[1] == cols - 1:
                next_late()
        else:
            y_part(step[1])
            if step[1] == cols - 1:
                next_late()

    for f in parts:
        parts[f].sent()
    strips = width // 256

    def flat(ref):
        return ref[...].reshape(cols * tokens, ref.shape[2])

    def columns(ref, at):
        return jnp.concatenate([ref[j, :, at] for j in range(cols)], axis=0)

    def down_strip(n, carry):
        at = pl.ds(pl.multiple_of(n * 256, 256), 256)
        wd[at] = dot_tokens(columns(dy, at), flat(act)).astype(bf16)
        return carry

    for begin, end in ((0, strips // 2), (strips // 2, strips)):
        lax.fori_loop(begin, end, down_strip, 0)
        next_late()
    chunk = down_staged.shape[2]
    inner = InnerSumInPlace(
        place,
        wd,
        lambda e: down_out.at[:, pl.ds(pl.multiple_of(e * chunk, chunk), chunk)],
        chunk,
        (core_held, second_held, first_held, down_staged) + tuple(inner_sems),
        inner_stage,
    )
    inner.begin()
    grad(0)
    beside = []
    for number in ((1, 3) + (2,) * strips)[:strips]:
        beside.append(calls[:number])
        del calls[:number]

    def hidden_strip(n, carry):
        at = pl.ds(pl.multiple_of(n * 256, 256), 256)
        left = columns(hn, at)
        for f in range(tiles):
            span = slice(2 * f * tile, 2 * (f + 1) * tile)
            right = dgu[:, :, span].reshape(cols * tokens, 2 * tile)
            wh[f, at] = dot_tokens(left, right).astype(bf16)
        pltpu.make_async_copy(wh.at[:, at], dwh_out.at[:, at], dw_sems.at[n]).start()
        inner.tick(n)
        for number, some in enumerate(beside):
            for call in some:
                pl.when(n == number)(functools.partial(do_late, call))
        return carry

    lax.fori_loop(0, strips, hidden_strip, 0)
    for t in range(strips, inner.count + 2 * LAG):
        inner.tick(t)
    while calls:
        next_late()

    def grad_copy(n):
        return pltpu.make_async_copy(
            grad_staged.at[n % 2], grad_out.at[:, wide_at(n)], grad_sems.at[n % 2]
        )

    for n in range(wides):
        if n >= 2:
            grad_copy(n - 2).wait()
        piece(n).last(grad_staged.at[n % 2])
        grad_copy(n).start()
    for n in range(max(wides - 2, 0), wides):
        grad_copy(n).wait()
    out_copy(near[stored[-1]]).wait()

    def finish(n, carry):
        at = pl.ds(pl.multiple_of(n * 256, 256), 256)
        pltpu.make_async_copy(wh.at[:, at], dwh_out.at[:, at], dw_sems.at[n]).wait()
        return carry

    lax.fori_loop(0, strips, finish, 0)
    inner.finish()
    line.finish()
    for n in range(wides):
        piece(n).finish()


def mlp(hn, dy, wh, wh_own, wd, row_count, col_count, collective_id):
    steps = max(col_count - 1, 1)
    rows, width = hn.shape
    hidden = wd.shape[1]
    early, tile = wh.shape[0], wh.shape[2] // 2
    tiles = hidden // tile
    left = tiles - early
    wide = min(512, width)
    shape = (col_count, rows, width)
    total = col_count * rows
    wh_shape = (tiles, width, 2 * tile)
    plane = plane_sizes(row_count)
    plane_sems = (left, 2, PlaneGather.sem_count(plane))
    deep = width // row_count
    chunk = min(512, hidden)
    count = hidden // chunk
    inner_sems = InnerSum.sems(plane, count)
    inner_sems[0] = pltpu.SemaphoreType.DMA((2, count, plane[0] * plane[1]))
    grad, y, dwh, sum_down, *_ = pl.pallas_call(
        functools.partial(mlp_kernel, (row_count, col_count), early, wide),
        out_shape=[
            jax.ShapeDtypeStruct((rows, width), f32),
            jax.ShapeDtypeStruct(shape, bf16),
            jax.ShapeDtypeStruct(wh_shape, bf16),
            jax.ShapeDtypeStruct((deep, hidden), f32),
        ]
        + [
            jax.ShapeDtypeStruct(held, bf16)
            for held in InnerSum.held_shapes(plane, deep, hidden, chunk)
        ],
        in_specs=[ANY] * 5,
        out_specs=[ANY] * 7,
        scratch_shapes=[
            pltpu.VMEM(shape, bf16),
            pltpu.VMEM(shape, bf16),
            pltpu.VMEM(wh_shape, bf16),
            pltpu.VMEM(wd.shape, bf16),
            pltpu.VMEM((col_count, rows, hidden), bf16),
            pltpu.VMEM((col_count, rows, 2 * hidden), bf16),
            pltpu.VMEM(shape, bf16),
            pltpu.VMEM((rows, width), bf16),
            pltpu.VMEM((width // wide, 2, steps, rows, wide), bf16),
            pltpu.VMEM((2, rows, wide), f32),
            pltpu.VMEM((2, deep, chunk), f32),
            pltpu.SemaphoreType.DMA((col_count,)),
            pltpu.SemaphoreType.DMA((tiles, 2)),
            pltpu.SemaphoreType.DMA((tiles,)),
            pltpu.SemaphoreType.DMA,
            pltpu.SemaphoreType.DMA((width // 256,)),
            pltpu.SemaphoreType.DMA((width // wide, 2, steps)),
            pltpu.SemaphoreType.DMA((width // wide, 2, steps)),
            pltpu.SemaphoreType.DMA((2, steps)),
            pltpu.SemaphoreType.DMA((2, steps)),
            pltpu.SemaphoreType.DMA(plane_sems),
            pltpu.SemaphoreType.DMA(plane_sems),
            pltpu.SemaphoreType.DMA,
            pltpu.SemaphoreType.DMA((2,)),
        ]
        + inner_sems
        + InnerSumInPlace.stage_scratch(plane, deep, chunk),
        compiler_params=pltpu.CompilerParams(
            collective_id=collective_id, has_side_effects=True, vmem_limit_bytes=63 << 20
        ),
        cost_estimate=pl.CostEstimate(
            flops=2 * 9 * total * width * hidden,
            bytes_accessed=6 * width * hidden * 2,
            transcendentals=total * hidden,
        ),
        name="feed_forward",
    )(hn, dy.reshape(shape), wh, wh_own, wd)
    return grad, y.reshape(total, width), dwh, sum_down


class PlaneSum:
    def __init__(self, place, block, held_second, held_first, sems, stage=None):
        self.place, self.block = place, block
        self.held = (held_first, held_second)
        self.sends, self.recvs = sems
        self.stage = stage

    @staticmethod
    def counts_of(sizes):
        na, nb, _ = sizes
        return max(na, nb) - 1, max((na - 1) * nb, (nb - 1) * na)

    @staticmethod
    def sem_count(sizes):
        na, nb, _ = sizes
        return na * nb - 1

    def axes(self, half):
        return (1, 0) if half == 0 else (0, 1)

    def counts(self, half):
        first, second = self.axes(half)
        return self.place.sizes[first], self.place.sizes[second]

    def part(self, half, i, j):
        first, second = self.axes(half)
        at = self.place.moved(second, j, self.place.moved(first, i))
        return self.block(self.place.chip_of(at), half)

    def number(self, half, kind, step, i):
        return (step - 1) * self.counts(half)[0] + i if kind == 1 else step - 1

    def copy(self, half, kind, step, i):
        np_, nq = self.counts(half)
        number = self.number(half, kind, step, i)
        if kind == 1:
            source, sem = self.part(half, i, nq - step), number
        else:
            source, sem = self.part(half, np_ - step, 0), (nq - 1) * np_ + number
        target = self.held[kind].at[half, number]
        device = self.place.device(self.axes(half)[1 if kind == 1 else 0], 1)
        return remote(source, target, self.sends.at[half, sem], self.recvs.at[half, sem], device)

    def bring(self, half, kind, step, i):
        number = self.number(half, kind, step, i)
        return pltpu.make_async_copy(
            self.held[kind].at[half, number],
            self.stage[kind].at[half, number],
            self.stage[2 + kind].at[half, number],
        )

    def add(self, pieces):
        if self.stage is not None:
            for piece in pieces:
                self.copy(*piece).wait_recv()
                self.bring(*piece).start()
        for half, kind, step, i in pieces:
            np_, nq = self.counts(half)
            if self.stage is None:
                self.copy(half, kind, step, i).wait_recv()
                held = self.held[kind]
            else:
                self.bring(half, kind, step, i).wait()
                held = self.stage[kind]
            if kind == 1:
                target = self.part(half, i, nq - step - 1)
            else:
                target = self.part(half, np_ - step - 1, 0)
            add_rows(target, held.at[half, self.number(half, kind, step, i)])
            yield half, i

    def first(self):
        for half in (0, 1):
            np_, nq = self.counts(half)
            if nq > 1:
                for i in range(np_ - 1, -1, -1):
                    self.copy(half, 1, 1, i).start()

    def second(self):
        for half in (0, 1):
            np_, nq = self.counts(half)
            if nq == 1 and np_ > 1:
                self.copy(half, 0, 1, 0).start()
        for step in range(1, max(self.place.sizes[:2])):
            pieces = []
            for half in (0, 1):
                np_, nq = self.counts(half)
                if step < nq:
                    pieces += [(half, 1, step, i) for i in range(np_ - 1, -1, -1)]
            for half, i in self.add(pieces):
                np_, nq = self.counts(half)
                if step < nq - 1:
                    self.copy(half, 1, step + 1, i).start()
                elif i == np_ - 1 and np_ > 1:
                    self.copy(half, 0, 1, 0).start()

    def third(self):
        for step in range(1, max(self.place.sizes[:2])):
            pieces = [(half, 0, step, 0) for half in (0, 1) if step < self.counts(half)[0]]
            for half, _ in self.add(pieces):
                if step < self.counts(half)[0] - 1:
                    self.copy(half, 0, step + 1, 0).start()

    def finish(self):
        for half in (0, 1):
            np_, nq = self.counts(half)
            for step in range(1, nq):
                for i in range(np_):
                    self.copy(half, 1, step, i).wait_send()
            for step in range(1, np_):
                self.copy(half, 0, step, 0).wait_send()


def halves_of(acc):
    half = acc.shape[1] // 2
    return lambda chip, number: acc.at[chip, pl.ds(number * half, half)]


def core_rows(place, chip, step, deep):
    cores = place.sizes[2]
    row = chip * cores + lax.rem(place.at[2] + step, cores)
    return pl.ds(pl.multiple_of(row * deep, deep), deep)


class InnerSum:
    def __init__(self, place, count, terms, target, refs):
        self.place, self.count, self.terms, self.target = place, count, terms, target
        self.acc, self.core_held, self.second, self.first, self.staged = refs[:5]
        self.load_sems, self.core_sems, self.plane_sems, self.out_sems = refs[5:9]
        self.ahead = min(3, self.count)
        self.chips, self.deep = self.core_held.shape[1:3]
        self.stage = None

    @staticmethod
    def held_shapes(sizes, deep, width, chunk):
        na, nb, _ = sizes
        firsts, seconds = PlaneSum.counts_of(sizes)
        return [
            (width // chunk, na * nb, deep, chunk),
            (width // chunk, 2, max(seconds, 1), deep // 2, chunk),
            (width // chunk, 2, max(firsts, 1), deep // 2, chunk),
        ]

    @staticmethod
    def sems(sizes, count):
        return [
            pltpu.SemaphoreType.DMA((2, count)),
            pltpu.SemaphoreType.DMA((2, count, 2, max(PlaneSum.sem_count(sizes), 1))),
            pltpu.SemaphoreType.DMA((2,)),
        ]

    @staticmethod
    def scratch(sizes, deep, width, chunk):
        shapes = InnerSum.held_shapes(sizes, deep, width, chunk)
        count = width // chunk
        return (
            [pltpu.VMEM(shape, bf16) for shape in shapes[:1] + shapes]
            + [pltpu.VMEM((2, deep, chunk), f32), pltpu.SemaphoreType.DMA((count,))]
            + InnerSum.sems(sizes, count)
        )

    def load(self, e):
        source = self.terms(e, self.place.at[2])
        return pltpu.make_async_copy(source, self.acc.at[e], self.load_sems.at[e])

    def other(self):
        return lax.rem(self.place.at[2] + 1, self.place.sizes[2])

    def shares(self, e):
        return [
            remote(
                self.terms(e, self.other()),
                self.core_held.at[e],
                self.core_sems.at[0, e],
                self.core_sems.at[1, e],
                self.place.device(2, 1),
            )
        ]

    def block(self, e, chip):
        return self.acc.at[e, chip]

    def inside(self, e):
        half = self.deep // 2
        return PlaneSum(
            self.place,
            lambda chip, number: self.block(e, chip).at[pl.ds(number * half, half)],
            self.second.at[e],
            self.first.at[e],
            (self.plane_sems.at[0, e], self.plane_sems.at[1, e]),
            self.stage,
        )

    def out_copy(self, e):
        slot = lax.rem(e, 2)
        return pltpu.make_async_copy(
            self.staged.at[slot], self.target(e), self.out_sems.at[slot]
        )

    def prepare(self, e):
        self.load(e).start()
        if self.place.sizes[2] > 1:
            for share in self.shares(e):
                share.start()

    def begin(self):
        for e in range(self.ahead):
            self.prepare(e)

    def ready(self, e):
        self.load(e).wait()
        if self.place.sizes[2] > 1:
            for share in self.shares(e):
                share.wait_recv()
        return self.core_held.at[e]

    def start(self, e):
        when(e + self.ahead < self.count, lambda: self.prepare(e + self.ahead))
        held = self.ready(e)
        if self.place.sizes[2] > 1:
            for chip in range(self.chips):
                add_rows(self.block(e, chip), held.at[chip])
        self.inside(e).first()

    def middle(self, e):
        self.inside(e).second()

    def close(self, e):
        self.inside(e).third()
        when(e >= 2, lambda: self.out_copy(e - 2).wait())
        slot = lax.rem(e, 2)
        own = self.block(e, self.place.chip_of(self.place.at))
        self.staged[slot] = own[...].astype(f32)
        self.out_copy(e).start()

    def tick(self, t):
        for lag, action in ((0, self.start), (LAG, self.middle), (2 * LAG, self.close)):
            e = t - lag
            when((e >= 0) & (e < self.count), functools.partial(action, e))

    def finish(self):
        for e in range(max(self.count - 2, 0), self.count):
            self.out_copy(e).wait()

        def done(e, carry):
            if self.place.sizes[2] > 1:
                for share in self.shares(e):
                    share.wait_send()
            self.inside(e).finish()
            return carry

        lax.fori_loop(0, self.count, done, 0)


class InnerSumInPlace(InnerSum):
    def __init__(self, place, terms, target, chunk, refs, stage):
        self.place, self.terms, self.target, self.chunk = place, terms, target, chunk
        self.core_held, self.second, self.first, self.staged = refs[:4]
        self.core_sems, self.plane_sems, self.out_sems = refs[4:]
        self.count = terms.shape[1] // chunk
        self.ahead = self.count
        self.chips, self.deep = self.core_held.shape[1:3]
        self.core_stage, self.core_stage_sem = stage[:2]
        self.stage = stage[2:]

    @staticmethod
    def stage_scratch(sizes, deep, chunk):
        shapes = InnerSum.held_shapes(sizes, deep, chunk, chunk)
        return [
            pltpu.VMEM(shapes[0][1:], bf16),
            pltpu.SemaphoreType.DMA,
            pltpu.VMEM(shapes[2][1:], bf16),
            pltpu.VMEM(shapes[1][1:], bf16),
            pltpu.SemaphoreType.DMA(shapes[2][1:3]),
            pltpu.SemaphoreType.DMA(shapes[1][1:3]),
        ]

    def rows(self, e, chip, core):
        row = chip * self.place.sizes[2] + core
        return self.terms.at[
            pl.ds(pl.multiple_of(row * self.deep, self.deep), self.deep),
            pl.ds(pl.multiple_of(e * self.chunk, self.chunk), self.chunk),
        ]

    def block(self, e, chip):
        return self.rows(e, chip, self.place.at[2])

    def shares(self, e):
        return [
            remote(
                self.rows(e, chip, self.other()),
                self.core_held.at[e, chip],
                self.core_sems.at[0, e, chip],
                self.core_sems.at[1, e, chip],
                self.place.device(2, 1),
            )
            for chip in range(self.chips)
        ]

    def prepare(self, e):
        if self.place.sizes[2] > 1:
            for share in self.shares(e):
                share.start()

    def ready(self, e):
        if self.place.sizes[2] > 1:
            for share in self.shares(e):
                share.wait_recv()
            copy = pltpu.make_async_copy(
                self.core_held.at[e], self.core_stage, self.core_stage_sem
            )
            copy.start()
            copy.wait()
        return self.core_stage


class SmallSum:
    def __init__(self, place, own, total, ring_held, line_held, ring_sems, line_sems):
        self.place, self.own, self.total = place, own, total
        self.held, self.sems = ring_held, ring_sems
        self.line = LineGather(
            place, total, lambda j: line_held.at[j], line_sems.at[0], line_sems.at[1]
        )
        self.line_held = line_held
        self.stages = []
        for axis in range(3):
            for step in range(1, place.sizes[axis]):
                self.stages.append(functools.partial(self.ring_send, axis, step))
                self.stages.append(functools.partial(self.ring_receive, axis, step))
            if place.sizes[axis] > 1:
                self.stages.append(functools.partial(self.ring_add, axis))
        self.stages.append(self.line_start)
        for step in range(1, place.cols):
            self.stages.append(functools.partial(self.line_step, step))
        self.stages.append(self.line_add)

    def begin(self):
        self.total[...] = self.own[...]

    def block(self, axis, step):
        at = self.place.moved(axis, -step)[axis]
        return self.held.at[axis, at]

    def ring_copy(self, axis, step):
        source = self.total if step == 1 else self.block(axis, step - 1)
        target = self.held.at[axis, self.place.moved(axis, 1 - step)[axis]]
        return remote(
            source,
            target,
            self.sems.at[0, axis, step - 1],
            self.sems.at[1, axis, step - 1],
            self.place.device(axis, 1),
        )

    def ring_send(self, axis, step):
        self.ring_copy(axis, step).start()

    def ring_receive(self, axis, step):
        ref = self.block(axis, step)
        remote(
            ref,
            ref,
            self.sems.at[0, axis, step - 1],
            self.sems.at[1, axis, step - 1],
            self.place.device(axis, 1),
        ).wait_recv()

    def ring_add(self, axis):
        for step in range(1, self.place.sizes[axis]):
            self.ring_copy(axis, step).wait_send()
        own_at = self.place.at[axis]
        total = None
        for at in range(self.place.sizes[axis]):
            term = jnp.where(own_at == at, self.total[...], self.held[axis, at])
            total = term if total is None else total + term
        self.total[...] = total

    def line_start(self):
        for way in (0, 1):
            self.line.send(way, 1)

    def line_step(self, step):
        for way in (0, 1):
            self.line.receive(way, step)

    def line_add(self):
        self.line.finish()
        total = None
        for at in range(self.place.cols):
            term = jnp.where(self.place.col == at, self.total[...], self.line_held[at])
            total = term if total is None else total + term
        self.total[...] = total


def norm_rows(dxn, x, dh, gain, out, part):
    rows, width = x.shape
    piece = 32

    def body(n, carry):
        at = pl.ds(pl.multiple_of(n * piece, piece), piece)
        values = x[at].astype(f32)
        scale = lax.rsqrt(jnp.mean(values * values, axis=1, keepdims=True) + epsilon)
        grad = dxn[at]
        weighted = grad * gain[...]
        inner = jnp.mean(weighted * values, axis=1, keepdims=True)
        result = dh[at] + scale * weighted - values * (scale * scale * scale) * inner
        out[at] = result.astype(out.dtype)
        part[0:1] += jnp.sum(grad * values * scale, axis=0, keepdims=True)
        return carry

    part[0:1] = jnp.zeros((1, width), f32)
    lax.fori_loop(0, rows // piece, body, 0)


def add_out(hidden, term, out):
    rows = hidden.shape[0]
    piece = 32

    def body(n, carry):
        at = pl.ds(pl.multiple_of(n * piece, piece), piece)
        out[at] = (hidden[at] + term[at].astype(f32)).astype(out.dtype)
        return carry

    lax.fori_loop(0, rows // piece, body, 0)


def sum_kernel(sizes, count, *refs):
    row_count, col_count = sizes
    place = Place(row_count, col_count)
    cores = place.sizes[2]
    lefts, rights = refs[: cores * count], refs[cores * count : 2 * cores * count]
    refs = refs[2 * cores * count :]
    dxn, x, dh, gain, hidden, out_sum, mid_part = refs[:7]
    outs = refs[7 : 8 + count]
    tokens_out, block_out, small_out = refs[8 + count : 11 + count]
    refs = refs[11 + count :]
    per = [refs[7 * n : 7 * n + 7] for n in range(count)]
    load_sems, out_sems, ps, pr, zs, zr = refs[7 * count : 7 * count + 6]
    ring_held, line_held, ring_sems, line_sems, chip_sems, small = refs[7 * count + 6 :]

    entries = [(n, nearby(place, k)) for k in range(col_count - 1, -1, -1) for n in range(count)]

    acc = [per[n][0] for n in range(count)]
    lines = [
        LineSum(
            place,
            lambda j, n=n: acc[n].at[j, place.chip_of(place.at)],
            per[n][3],
            zs.at[n],
            zr.at[n],
        )
        for n in range(count)
    ]
    tokens = lefts[0].shape[0]
    chips, deep = acc[0].shape[1:3]

    def loads():
        for n in range(count):
            left, right = per[n][5], per[n][6]
            for k in range(cores):
                at = pl.ds(k * tokens, tokens)
                if k == 0:
                    for chip in range(chips):
                        yield pltpu.make_async_copy(
                            lefts[n * cores].at[:, core_rows(place, chip, 0, deep)],
                            left.at[at, pl.ds(chip * deep, deep)],
                            chip_sems.at[n, chip],
                        )
                else:
                    yield pltpu.make_async_copy(
                        lefts[n * cores + k], left.at[at], load_sems.at[0, n * cores + k]
                    )
                yield pltpu.make_async_copy(
                    rights[n * cores + k], right.at[:, at], load_sems.at[1, n * cores + k]
                )

    for copy in loads():
        copy.start()
    place.greet(True, True)
    smalls = SmallSum(place, small, small_out, ring_held, line_held, ring_sems, line_sems)
    stages = [functools.partial(norm_rows, dxn, x, dh, gain, tokens_out, small)]
    stages += [functools.partial(add_out, hidden, out_sum, block_out), smalls.begin]
    stages += smalls.stages
    small[1:2] = mid_part[...]
    for copy in loads():
        copy.wait()

    def inside(n, col):
        return PlaneSum(
            place,
            halves_of(acc[n].at[col]),
            per[n][1].at[col],
            per[n][2].at[col],
            (ps.at[n, col], pr.at[n, col]),
        )

    parts = [inside(n, col) for n, col in entries]
    final = len(entries) - count
    total = len(entries)

    def start(number):
        n, col = entries[number]
        left, right = per[n][5], per[n][6]
        deep = acc[n].shape[2]

        def chip_rows(chip, carry):
            at = pl.ds(pl.multiple_of(chip * deep, deep), deep)
            acc[n][col, chip] = dot_tokens(left[:, at], right[col]).astype(bf16)
            return carry

        lax.fori_loop(0, acc[n].shape[1], chip_rows, 0)
        parts[number].first()

    split = outs[0].shape[1]

    def out_copies(n):
        if n > 0:
            return [pltpu.make_async_copy(per[n][4], outs[n + 1], out_sems.at[n + 1])]
        rest = pl.ds(split, outs[1].shape[1])
        return [
            pltpu.make_async_copy(per[0][4].at[:, pl.ds(0, split)], outs[0], out_sems.at[0]),
            pltpu.make_async_copy(per[0][4].at[:, rest], outs[1], out_sems.at[1]),
        ]

    def close(number):
        parts[number].third()
        n, col = entries[number]
        if number < final:
            lines[n].early(col, True)
            if number >= count:
                lines[n].late(entries[number - count][1], True)
            if number >= final - count:
                lines[n].late(col, True)

    def finish_lines():
        for n in range(count):
            lines[n].last(per[n][4])
            for copy in out_copies(n):
                copy.start()

    for number in range(total + 2 * LAG):
        if number < total:
            start(number)
        if LAG <= number < total + LAG:
            parts[number - LAG].second()
        if 2 * LAG <= number:
            close(number - 2 * LAG)
        if number >= 1:
            for stage in stages[:2]:
                stage()
            del stages[:2]
    for stage in stages:
        stage()
    finish_lines()
    for n in range(count):
        for copy in out_copies(n):
            copy.wait()
    for part in parts:
        part.finish()
    for line in lines:
        line.finish()


def sum_all(lefts, rights, split, extras, row_count, col_count):
    count = len(rights)
    sizes = plane_sizes(row_count)
    na, nb, nk = sizes
    chips = na * nb
    tokens, model = lefts[0][0].shape
    deep = lefts[0][0].shape[1] // row_count
    steps = max(col_count - 1, 1)
    firsts, seconds = PlaneSum.counts_of(sizes)
    widths = [right[0].shape[2] for right in rights]
    scratch = []
    for width in widths:
        scratch += [
            pltpu.VMEM((col_count, chips, deep, width), bf16),
            pltpu.VMEM((col_count, 2, max(seconds, 1), deep // 2, width), bf16),
            pltpu.VMEM((col_count, 2, max(firsts, 1), deep // 2, width), bf16),
            pltpu.VMEM((2, steps, deep, width), bf16),
            pltpu.VMEM((deep, width), f32),
            pltpu.VMEM((nk * tokens, chips * deep), bf16),
            pltpu.VMEM((col_count, nk * tokens, width), bf16),
        ]
    plane_sems = (count, col_count, 2, max(PlaneSum.sem_count(sizes), 1))
    scratch += [
        pltpu.SemaphoreType.DMA((2, count * nk)),
        pltpu.SemaphoreType.DMA((count + 1,)),
        pltpu.SemaphoreType.DMA(plane_sems),
        pltpu.SemaphoreType.DMA(plane_sems),
        pltpu.SemaphoreType.DMA((count, 2, steps)),
        pltpu.SemaphoreType.DMA((count, 2, steps)),
        pltpu.VMEM((3, max(sizes), 2, model), f32),
        pltpu.VMEM((col_count, 2, model), f32),
        pltpu.SemaphoreType.DMA((2, 3, max(max(sizes) - 1, 1))),
        pltpu.SemaphoreType.DMA((2, 2, steps)),
        pltpu.SemaphoreType.DMA((count, chips)),
        pltpu.VMEM((2, model), f32),
    ]
    outs = [split, widths[0] - split] + widths[1:]
    vmem = pl.BlockSpec(memory_space=pltpu.VMEM)
    flops = sum(2 * nk * tokens * chips * deep * width * col_count for width in widths)
    return pl.pallas_call(
        functools.partial(sum_kernel, (row_count, col_count), count),
        out_shape=[jax.ShapeDtypeStruct((deep, width), f32) for width in outs]
        + [
            jax.ShapeDtypeStruct((tokens, model), bf16),
            jax.ShapeDtypeStruct((tokens, model), bf16),
            jax.ShapeDtypeStruct((2, model), f32),
        ],
        in_specs=[ANY] * (2 * count * nk) + [vmem] * 7,
        out_specs=[ANY] * (count + 1) + [vmem] * 3,
        scratch_shapes=scratch,
        compiler_params=pltpu.CompilerParams(
            collective_id=1, has_side_effects=True, vmem_limit_bytes=63 << 20
        ),
        cost_estimate=pl.CostEstimate(
            flops=flops, bytes_accessed=flops // 256, transcendentals=0
        ),
        name="sum_weights",
    )(
        *[left for pair in lefts for left in pair],
        *[right for pair in rights for right in pair],
        *extras,
    )


LANES = 2 * HD


def lower_lanes():
    return lax.broadcasted_iota(jnp.int32, (1, LANES), 1) < HD


def rope_lanes(values, cosine, sinusoid):
    lane = lax.broadcasted_iota(jnp.int32, (1, LANES), 1)
    other = jnp.where(
        lane % HD < HD // 2,
        pltpu.roll(values, LANES - HD // 2, 1),
        pltpu.roll(values, HD // 2, 1),
    )
    return values * cosine + other * sinusoid


def head_at(tile, head, upper):
    if (head % 2 == 1) != upper:
        tile = pltpu.roll(tile, HD, 1)
    keep = lower_lanes()
    if upper:
        keep = jnp.logical_not(keep)
    return jnp.where(keep, tile, 0.0)


def tile_of(head):
    return slice(head // 2 * LANES, head // 2 * LANES + LANES)


def pair_tile(even, odd, upper):
    if upper:
        even = pltpu.roll(even, HD, 1)
    else:
        odd = pltpu.roll(odd, HD, 1)
    return jnp.where(lower_lanes(), even, odd)


def attend_kernel(sizes, heads, group, back, *refs):
    xn, x, wf_in, wo_in, bias, cosq, sinq, coskv, sinkv, gain, tiles_in = refs[:11]
    q_out, kv_out, mixed_out, lse_out, full_tiles, hidden, hn = refs[11:18]
    q, kv, mixed, lse, wf, wo, w_sems, o_sems, sends, recvs, t_sems, ps, pr = refs[18:31]
    tiles, tiles_sem = refs[31:]
    place = Place(*sizes)
    cols, col = place.cols, place.col
    tokens = xn.shape[0]
    query_width = heads * HD
    own_rows = pl.ds(back * tokens, tokens)
    pairs = heads // group

    def weight_copies(z):
        return (
            pltpu.make_async_copy(wf_in.at[z], wf.at[z], w_sems.at[0, z]),
            pltpu.make_async_copy(wo_in.at[z], wo.at[z], w_sems.at[1, z]),
        )

    count, _, tile = tiles.shape
    tile = tile // 2
    hidden_units = tiles_in.shape[1] // 2
    fetches = [
        pltpu.make_async_copy(
            tiles_in.at[:, pl.ds(number * hidden_units + f * tile, tile)],
            tiles.at[f, :, pl.ds(number * tile, tile)],
            tiles_sem.at[f, number],
        )
        for f in range(count)
        for number in (0, 1)
    ]
    for fetch in fetches:
        fetch.start()
    for step in range(1, back + 1):

        @pl.when(col < step)
        def _():
            kv[:, (back - step) * tokens : (back - step + 1) * tokens] = jnp.zeros(
                (cols, tokens, kv.shape[2]), bf16
            )

    keeps = [
        pltpu.make_async_copy(
            tiles.at[f],
            full_tiles.at[f, pl.ds(place.row * tiles.shape[1], tiles.shape[1])],
            t_sems.at[f],
        )
        for f in range(tiles.shape[0])
    ]
    place.greet(True, True)
    for fetch in fetches:
        fetch.wait()
    parts = [
        tile_gather(place, full_tiles.at[f], tiles.at[f], ps.at[f], pr.at[f])
        for f in range(tiles.shape[0])
    ]
    for part in parts:
        part.first()
    for number in (0, 1):
        for z in range(cols):
            weight_copies(z)[number].start()
    for keep in keeps:
        keep.start()

    def hop(z, step):
        source = kv.at[z, pl.ds((back - step + 1) * tokens, tokens)]
        target = kv.at[z, pl.ds((back - step) * tokens, tokens)]
        return remote(
            source, target, sends.at[step - 1, z], recvs.at[step - 1, z], (place.row, col + 1)
        )

    def goes(step):
        return (col < cols - 1) & (col >= step - 1)

    def send(z, step):
        pl.when(goes(step))(lambda: hop(z, step).start())

    def receive(z, step):
        ref = kv.at[z, pl.ds((back - step) * tokens, tokens)]

        @pl.when(col >= step)
        def _():
            remote(
                ref, ref, sends.at[step - 1, z], recvs.at[step - 1, z], (place.row, col + 1)
            ).wait_recv()

    def project(z, carry):
        weight_copies(z)[0].wait()
        pre = matmul(xn[...], wf[z])
        for n in range(query_width // LANES):
            at = slice(n * LANES, (n + 1) * LANES)
            q[z, :, at] = rope_lanes(pre[:, at], cosq[...], sinq[...]).astype(bf16)
        for n in range(pairs):
            at = slice(n * LANES, (n + 1) * LANES)
            tile = pre[:, query_width + n * LANES : query_width + (n + 1) * LANES]
            kv[z, own_rows, at] = rope_lanes(tile, coskv[...], sinkv[...]).astype(bf16)
        if back > 0:
            send(z, 1)
        return carry

    lax.fori_loop(0, cols, project, 0)
    if parts:
        parts[0].second()
    for step in range(1, back):
        for z in range(cols):
            receive(z, step)
            send(z, step + 1)

    def attend(z, carry):
        if back > 0:
            receive(z, back)
        lane = lax.broadcasted_iota(jnp.int32, (1, LANES), 1)
        logs = jnp.zeros((tokens, LANES), f32)
        outs = []
        for head in range(heads):
            pair = head // group
            keyval = kv[z, :, pair * LANES : (pair + 1) * LANES]
            query = head_at(q[z, :, tile_of(head)].astype(f32), head, False) * HD**-0.5
            scores = against(query.astype(bf16), keyval) + bias[...]
            summit = jnp.max(scores, axis=1, keepdims=True)
            weights = jnp.exp(scores - summit)
            total = jnp.sum(weights, axis=1, keepdims=True)
            chances = (weights * (1.0 / total)).astype(bf16)
            outs.append(matmul(chances, keyval))
            logs = jnp.where(lane == head, summit + jnp.log(total), logs)
            if head % 2 == 1:
                mixed[z, :, tile_of(head)] = pair_tile(outs[-2], outs[-1], True).astype(bf16)
        lse[z] = jnp.transpose(logs)[:heads]

        @pl.when(z == 0)
        def _():
            for part in parts[1:]:
                part.second()

        @pl.when(z == max(cols - 2, 1))
        def _():
            for part in parts[:-1]:
                part.third()

        return carry

    lax.fori_loop(0, cols, attend, 0)
    outputs = [
        pltpu.make_async_copy(source, target, o_sems.at[n])
        for n, (source, target) in enumerate(
            ((q, q_out), (kv, kv_out), (mixed, mixed_out), (lse, lse_out))
        )
    ]
    for copy in outputs:
        copy.start()
    hidden[...] = x[...].astype(f32)

    def project_out(z, carry):
        weight_copies(z)[1].wait()
        hidden[...] += against(mixed[z], wo[z])
        return carry

    lax.fori_loop(0, cols, project_out, 0)
    total = hidden[...]
    scale = lax.rsqrt(jnp.mean(total * total, axis=1, keepdims=True) + epsilon)
    hn[...] = (total * scale * gain[...]).astype(bf16)
    if parts:
        parts[-1].third()
    for part in parts:
        part.finish()
    for copy in keeps + outputs:
        copy.wait()
    for step in range(1, back + 1):
        for z in range(cols):
            pl.when(goes(step))(lambda: hop(z, step).wait_send())


def attend(
    xn, x, wf, wo, bias, tables, gain, tiles, count, tile, heads, group, back, sizes, cid
):
    row_count, col_count = sizes
    tokens, width = xn.shape
    query_width = heads * HD
    kv_shape = (col_count, (back + 1) * tokens, heads // group * LANES)
    q_shape = (col_count, tokens, query_width)
    lse_shape = (col_count, heads, tokens)
    vmem = pl.BlockSpec(memory_space=pltpu.VMEM)
    keys = (back + 1) * tokens
    plane_sems = (count, 2, PlaneGather.sem_count(plane_sizes(row_count)))
    return pl.pallas_call(
        functools.partial(attend_kernel, (row_count, col_count), heads, group, back),
        out_shape=[
            jax.ShapeDtypeStruct(q_shape, bf16),
            jax.ShapeDtypeStruct(kv_shape, bf16),
            jax.ShapeDtypeStruct(q_shape, bf16),
            jax.ShapeDtypeStruct(lse_shape, f32),
            jax.ShapeDtypeStruct((count, row_count * tiles.shape[0], 2 * tile), bf16),
            jax.ShapeDtypeStruct((tokens, width), f32),
            jax.ShapeDtypeStruct((tokens, width), bf16),
        ],
        in_specs=[vmem, vmem, ANY, ANY] + [vmem] * 6 + [ANY],
        out_specs=[ANY] * 5 + [vmem] * 2,
        scratch_shapes=[
            pltpu.VMEM(q_shape, bf16),
            pltpu.VMEM(kv_shape, bf16),
            pltpu.VMEM(q_shape, bf16),
            pltpu.VMEM(lse_shape, f32),
            pltpu.VMEM(wf.shape, bf16),
            pltpu.VMEM(wo.shape, bf16),
            pltpu.SemaphoreType.DMA((2, col_count)),
            pltpu.SemaphoreType.DMA((4,)),
            pltpu.SemaphoreType.DMA((max(back, 1), col_count)),
            pltpu.SemaphoreType.DMA((max(back, 1), col_count)),
            pltpu.SemaphoreType.DMA((count,)),
            pltpu.SemaphoreType.DMA(plane_sems),
            pltpu.SemaphoreType.DMA(plane_sems),
            pltpu.VMEM((count, tiles.shape[0], 2 * tile), bf16),
            pltpu.SemaphoreType.DMA((count, 2)),
        ],
        compiler_params=pltpu.CompilerParams(
            collective_id=cid, has_side_effects=True, vmem_limit_bytes=56 << 20
        ),
        cost_estimate=pl.CostEstimate(
            flops=2 * tokens * (wf.size + wo.size) + 4 * col_count * heads * tokens * keys * HD,
            bytes_accessed=(wf.size + wo.size) * 2,
            transcendentals=col_count * heads * tokens * keys,
        ),
        name="attend",
    )(xn, x, wf, wo, bias, *tables, gain, tiles)


def attend_back_kernel(sizes, heads, group, back, chunk, *refs):
    dhb, xn, lse, bias, cosq, sinq, coskv, sinkv = refs[:8]
    mixed_in, q_in, kv_in, wo_in, wf_in, terms = refs[8:14]
    dxn, dqkv_out, sum_out, xn_sib, dhb_sib, mixed_sib, dqkv_sib = refs[14:21]
    q, kv, wo, wf, dmix, dkv, dqkv, going, coming, dst, pst, rhs_q, rhs_o = refs[21:34]
    in_sems, wo_sems, wf_sems, out_sems, pair_sems, row_sems, sends, recvs = refs[34:42]
    place = Place(*sizes)
    cols, col = place.cols, place.col
    cores = place.sizes[2]
    tokens = dhb.shape[0]
    query_width = heads * HD
    pairs = heads // group
    hidden = sum_out.shape[1] // 2

    def inner_target(e):
        at = lax.rem(e, 2) * hidden + e // 2 * chunk
        return sum_out.at[:, pl.ds(pl.multiple_of(at, chunk), chunk)]

    def inner_terms(e, core):
        at = pl.multiple_of(lax.rem(e, 2) * chunk, chunk)
        return terms.at[e // 2, :, core, :, pl.ds(at, chunk)]

    inner = InnerSum(place, 2 * hidden // chunk, inner_terms, inner_target, refs[42:])

    in_copies = [
        pltpu.make_async_copy(q_in, q, in_sems.at[0]),
        pltpu.make_async_copy(kv_in, kv, in_sems.at[1]),
    ]

    def wo_copy(z):
        slot = lax.rem(z, 2)
        return pltpu.make_async_copy(wo_in.at[z], wo.at[slot], wo_sems.at[slot])

    def wf_copy(z):
        slot = lax.rem(z, 2)
        return pltpu.make_async_copy(wf_in.at[z], wf.at[slot], wf_sems.at[slot])

    wo_copy(0).start()
    for copy in in_copies:
        copy.start()
    for z in range(min(2, cols)):
        wf_copy(z).start()
    place.greet(True, True)

    other = place.device(2, 1)
    exchanges = []
    if cores > 1:
        chips, deep = terms.shape[1], terms.shape[3]
        moves = [(mixed_in, mixed_sib)]
        for chip in range(chips):
            to, rows = pl.ds(chip * deep, deep), core_rows(place, chip, 1, deep)
            moves += [(xn.at[:, rows], xn_sib.at[:, to]), (dhb.at[:, rows], dhb_sib.at[:, to])]
        exchanges = [
            remote(source, target, pair_sems.at[0, n], pair_sems.at[1, n], other)
            for n, (source, target) in enumerate(moves)
        ]

    def row_exchange(z):
        return remote(dqkv.at[z], dqkv_sib.at[z], row_sems.at[0, z], row_sems.at[1, z], other)

    def out_copy(z):
        return pltpu.make_async_copy(dqkv.at[z], dqkv_out.at[z], out_sems.at[z])

    inner.begin()
    for exchange in exchanges:
        exchange.start()
    dxn[...] = jnp.zeros_like(dxn)
    for copy in in_copies:
        copy.wait()

    def hop(z, step):
        return remote(
            going.at[step - 1, z],
            coming.at[step - 1, z],
            sends.at[step - 1, z],
            recvs.at[step - 1, z],
            (place.row, col - 1),
        )

    def goes(step):
        return col - back + step - 1 >= 0

    def comes(step):
        return (col < cols - 1) & (col + step - back >= 0)

    def send(z, step):
        pl.when(goes(step))(lambda: hop(z, step).start())

    def chunk_rows(step):
        return slice(step * tokens, (step + 1) * tokens)

    def halo(step, z):
        if step > 0:
            pl.when(comes(step))(lambda: hop(z, step).wait_recv())
            term = jnp.where(comes(step), coming[step - 1, z].astype(f32), 0.0)
            total = dkv[z, chunk_rows(step)] + term
        else:
            total = dkv[z, chunk_rows(step)]
        if step < back:
            going[step, z] = total.astype(bf16)
            send(z, step + 1)
            return
        for n in range(pairs):
            at = slice(n * LANES, (n + 1) * LANES)
            dqkv[z, :, query_width + n * LANES : query_width + (n + 1) * LANES] = rope_lanes(
                total[:, at], coskv[...], sinkv[...]
            ).astype(bf16)
        out_copy(z).start()
        if cores > 1:
            row_exchange(z).start()
        wf_copy(z).wait()
        dxn[...] += against(dqkv[z], wf[lax.rem(z, 2)])
        when(z + 2 < cols, lambda: wf_copy(z + 2).start())

    def halos(z):
        for step in range(1, back + 1):
            at = z - step
            when((at >= 0) & (at < cols), lambda: halo(step, at))

    def one_col(z, carry):
        wo_copy(z).wait()
        when(z + 1 < cols, lambda: wo_copy(z + 1).start())
        dmix[...] = matmul(dhb[...], wo[lax.rem(z, 2)]).astype(bf16)
        for n in range(pairs):
            keyval = kv[z, :, n * LANES : (n + 1) * LANES]
            for i in range(group):
                head = n * group + i
                at = slice(i * tokens, (i + 1) * tokens)
                query = head_at(q[z, :, tile_of(head)].astype(f32), head, False) * HD**-0.5
                query = query.astype(bf16)
                grad = head_at(dmix[:, tile_of(head)].astype(f32), head, True).astype(bf16)
                rhs_q[at] = query
                rhs_o[at] = grad
                chances = jnp.exp(against(keyval, query) + bias[...] - lse[z, head : head + 1])
                grad_chance = against(keyval, grad)
                centre = jnp.sum(chances * grad_chance, axis=0, keepdims=True)
                dst[:, at] = (chances * (grad_chance - centre)).astype(bf16)
                pst[:, at] = chances.astype(bf16)
            dkv[z, :, n * LANES : (n + 1) * LANES] = matmul(dst[...], rhs_q[...]) + matmul(
                pst[...], rhs_o[...]
            )
            grad_rows = dot_tokens(keyval, dst[...])
            for i in range(0, group, 2):
                tile = jnp.concatenate(
                    [
                        grad_rows[:HD, i * tokens : (i + 1) * tokens],
                        grad_rows[:HD, (i + 1) * tokens : (i + 2) * tokens],
                    ],
                    axis=0,
                )
                turned = rope_lanes(jnp.transpose(tile), cosq[...], sinq[...]) * HD**-0.5
                dqkv[z, :, tile_of(n * group + i)] = turned.astype(bf16)
            inner.tick(z * pairs + n)
        halo(0, z)
        halos(z)
        return carry

    lax.fori_loop(0, cols, one_col, 0)
    ticks = list(range(cols * pairs, inner.count + 2 * LAG))
    for z in range(cols, cols + back):
        if ticks:
            inner.tick(ticks.pop(0))
        halos(z)
    for t in ticks:
        inner.tick(t)
    for z in range(cols):
        out_copy(z).wait()
        if cores > 1:
            row_exchange(z).wait_send()
            row_exchange(z).wait_recv()
    for exchange in exchanges:
        exchange.wait_send()
        exchange.wait_recv()
    for step in range(1, back + 1):
        for z in range(cols):
            pl.when(goes(step))(lambda: hop(z, step).wait_send())
    inner.finish()


def attend_back(
    dhb, xn, lse, bias, tables, mixed, q, kv, wo, wf, terms, group, sizes, cid
):
    row_count, col_count = sizes
    plane = plane_sizes(row_count)
    chips = plane[0] * plane[1]
    tokens, width = dhb.shape
    heads = lse.shape[1]
    back = kv.shape[1] // tokens - 1
    pairs = heads // group
    keys = kv.shape[1]
    all_width = wf.shape[2]
    tiles, _, chunk = terms.shape
    chunk = chunk // 2
    inner_width = 2 * tiles * chunk
    deep = terms.shape[1] // row_count
    row_shape = (col_count, tokens, all_width)
    halo_shape = (max(back, 1), col_count, tokens, kv.shape[2])
    vmem = pl.BlockSpec(memory_space=pltpu.VMEM)
    return pl.pallas_call(
        functools.partial(attend_back_kernel, sizes, heads, group, back, chunk),
        out_shape=[
            jax.ShapeDtypeStruct((tokens, width), f32),
            jax.ShapeDtypeStruct(row_shape, bf16),
            jax.ShapeDtypeStruct((deep, inner_width), f32),
            jax.ShapeDtypeStruct((tokens, chips * deep), bf16),
            jax.ShapeDtypeStruct((tokens, chips * deep), bf16),
            jax.ShapeDtypeStruct(mixed.shape, bf16),
            jax.ShapeDtypeStruct(row_shape, bf16),
        ],
        in_specs=[vmem] * 8 + [ANY] * 6,
        out_specs=[vmem] + [ANY] * 6,
        scratch_shapes=[
            pltpu.VMEM(q.shape, bf16),
            pltpu.VMEM(kv.shape, bf16),
            pltpu.VMEM((2,) + wo.shape[1:], bf16),
            pltpu.VMEM((2,) + wf.shape[1:], bf16),
            pltpu.VMEM((tokens, heads * HD), bf16),
            pltpu.VMEM(kv.shape, f32),
            pltpu.VMEM(row_shape, bf16),
            pltpu.VMEM(halo_shape, bf16),
            pltpu.VMEM(halo_shape, bf16),
            pltpu.VMEM((keys, group * tokens), bf16),
            pltpu.VMEM((keys, group * tokens), bf16),
            pltpu.VMEM((group * tokens, LANES), bf16),
            pltpu.VMEM((group * tokens, LANES), bf16),
            pltpu.SemaphoreType.DMA((2,)),
            pltpu.SemaphoreType.DMA((2,)),
            pltpu.SemaphoreType.DMA((2,)),
            pltpu.SemaphoreType.DMA((col_count,)),
            pltpu.SemaphoreType.DMA((2, 1 + 2 * chips)),
            pltpu.SemaphoreType.DMA((2, col_count)),
            pltpu.SemaphoreType.DMA((max(back, 1), col_count)),
            pltpu.SemaphoreType.DMA((max(back, 1), col_count)),
        ]
        + InnerSum.scratch(plane, deep, inner_width, chunk),
        compiler_params=pltpu.CompilerParams(
            collective_id=cid, has_side_effects=True, vmem_limit_bytes=62 << 20
        ),
        cost_estimate=pl.CostEstimate(
            flops=2 * tokens * (wf.size + wo.size) + 10 * col_count * heads * tokens * keys * HD,
            bytes_accessed=(wf.size + wo.size + terms.size) * 2,
            transcendentals=col_count * heads * tokens * keys,
        ),
        name="attend_back",
    )(
        dhb,
        xn,
        lse,
        bias,
        *tables,
        mixed,
        q,
        kv,
        wo,
        wf,
        terms.reshape(tiles, chips, plane[2], deep, 2 * chunk),
    )


def rope_tables(position):
    indices = jnp.arange(HD // 2, dtype=f32)
    frequency = rope_base ** (-(indices * 2.0 / HD))
    wavelen = 2.0 * jnp.pi / frequency
    smooth = (8192.0 / wavelen - 1.0) / 3.0
    scaled = jnp.where(
        wavelen > 8192.0, frequency / 32.0, (1.0 - smooth) * frequency / 32.0 + smooth * frequency
    )
    frequency = jnp.where(wavelen < 2048.0, frequency, scaled)
    angles = position.astype(f32)[:, None] * frequency[None, :]
    return (jnp.cos(angles), jnp.sin(angles))


def rotate(values, cosine, sinusoid):
    halfway = values.shape[-1] // 2
    former = values[..., :halfway]
    latter = values[..., halfway:]
    cos_wide = cosine[:, None, :]
    sin_wide = sinusoid[:, None, :]
    return jnp.concatenate(
        [former * cos_wide - latter * sin_wide, latter * cos_wide + former * sin_wide], axis=-1
    )


def normalize(values, gain):
    scale = lax.rsqrt(jnp.mean(values * values, axis=1, keepdims=True) + epsilon)
    return ((values * scale * gain).astype(bf16), scale)


def norm_back(grad_in, values, scale, gain):
    weighted = grad_in * gain
    inner_sum = jnp.mean(weighted * values, axis=1, keepdims=True)
    return (
        scale * weighted - values * (scale * scale * scale) * inner_sum,
        jnp.sum(grad_in * values * scale, axis=0),
    )


def against(left, right):
    return lax.dot_general(left, right, (((1,), (1,)), ((), ())), preferred_element_type=f32)


def over_rows(left, right):
    return lax.dot_general(left, right, (((0,), (0,)), ((), ())), preferred_element_type=f32)


def matmul(left, right):
    return jnp.dot(left, right, preferred_element_type=f32)


def shift(values, step, col_count):
    if step > 0:
        pairs = [(i, i + step) for i in range(col_count - step)]
    else:
        pairs = [(i, i + step) for i in range(-step, col_count)]
    return lax.ppermute(values, "col", pairs)


def shards(
    tokens,
    seq_lens,
    attn_gain,
    query_weight,
    keyvalue_weight,
    output_weight,
    mlp_gain,
    hidden_weight,
    down_weight,
    out_grad,
):
    row_count, col_count = lax.axis_size("row"), lax.axis_size("col")
    local = tokens.shape[0]
    block_rows = local * col_count
    col = lax.axis_index("col")
    deep = query_weight.shape[0]
    width = tokens.shape[1]
    query_width = query_weight.shape[1]
    pairs = keyvalue_weight.shape[1]
    heads = query_width // HD
    group = heads // pairs
    hidden = down_weight.shape[1]
    back = min(-(-(SEQ_MAX - 1) // local), col_count - 1)

    lengths = seq_lens[0]
    finish = jnp.cumsum(lengths)
    indices = jnp.arange(block_rows, dtype=jnp.int32)
    passed = indices[:, None] >= finish[None, :]
    segment = jnp.sum(passed.astype(jnp.int32), axis=1, dtype=jnp.int32)
    position = indices - jnp.sum(jnp.where(passed, lengths[None, :], 0), axis=1, dtype=jnp.int32)
    own_position = lax.dynamic_slice(position, (col * local,), (local,))
    own_segment = lax.dynamic_slice(segment, (col * local,), (local,))
    padded = jnp.concatenate([jnp.full((back * local,), -1, jnp.int32), segment])
    key_segment = lax.dynamic_slice(padded, (col * local,), ((back + 1) * local,))
    key_index = jnp.arange((back + 1) * local, dtype=jnp.int32) - back * local
    query_index = jnp.arange(local, dtype=jnp.int32)
    allowed = (own_segment[:, None] == key_segment[None, :]) & (
        key_index[None, :] <= query_index[:, None]
    )
    cosine, sinusoid = rope_tables(own_position)
    gain_first = attn_gain.astype(f32)
    gain_second = mlp_gain.astype(f32)

    first_weight = jnp.concatenate(
        [query_weight, keyvalue_weight.reshape(deep, pairs * 2 * HD)], axis=1
    )
    full_first, full_output, full_down, rows_grad = gather_all(
        [first_weight, output_weight], [down_weight], out_grad, row_count, col_count
    )

    tile = min(512, hidden)
    tiles = hidden // tile
    early = max(tiles // 2, 1)
    hidden_flat = hidden_weight.reshape(deep, 2 * hidden)

    inputs = tokens.astype(f32)
    normal_in, scale_in = normalize(inputs, gain_first)
    halves = jnp.concatenate([cosine, cosine], axis=1)
    signed = jnp.concatenate([-sinusoid, sinusoid], axis=1)
    tables = (
        jnp.concatenate([halves, halves], axis=1),
        jnp.concatenate([signed, signed], axis=1),
        jnp.concatenate([halves, jnp.ones_like(halves)], axis=1),
        jnp.concatenate([signed, jnp.zeros_like(signed)], axis=1),
    )
    bias = jnp.where(allowed, 0.0, blocked).astype(f32)
    queries, all_keyvals, mixed, lse, early_tiles, hidden_in, normal_mid = attend(
        normal_in,
        tokens,
        full_first,
        full_output,
        bias,
        tables,
        gain_second[None],
        hidden_flat,
        early,
        tile,
        heads,
        group,
        back,
        (row_count, col_count),
        4,
    )
    scale_mid = lax.rsqrt(jnp.mean(hidden_in * hidden_in, axis=1, keepdims=True) + epsilon)

    grad_mid, out_terms, grad_hidden_part, sum_down = mlp(
        normal_mid,
        rows_grad,
        early_tiles,
        hidden_flat,
        full_down,
        row_count,
        col_count,
        3,
    )
    out_sum = lax.psum_scatter(out_terms, "col", scatter_dimension=0, tiled=True)
    back_mid, gain_mid_part = norm_back(grad_mid, hidden_in, scale_mid, gain_second)
    grad_hidden_in = out_grad.astype(f32) + back_mid
    grad_low = grad_hidden_in.astype(bf16)
    cores = plane_sizes(row_count)[2]
    tables_back = (tables[0], -tables[1], tables[2], -tables[3])
    grad_in, grad_first, sum_hidden, normal_sib, grad_low_sib, mixed_sib, grad_first_sib = (
        attend_back(
            grad_low,
            normal_in,
            lse,
            bias.T,
            tables_back,
            mixed,
            queries,
            all_keyvals,
            full_output,
            full_first,
            grad_hidden_part,
            group,
            (row_count, col_count),
            5,
        )
    )
    lefts = [
        (normal_in, normal_sib)[:cores],
        (grad_low, grad_low_sib)[:cores],
    ]
    rights = [(grad_first, grad_first_sib)[:cores], (mixed, mixed_sib)[:cores]]
    extras = (
        grad_in,
        tokens,
        grad_hidden_in,
        gain_first[None],
        hidden_in,
        out_sum,
        gain_mid_part[None],
    )
    sum_query, sum_keyvalue, sum_output, grad_tokens, block_out, gain_sums = sum_all(
        lefts, rights, query_width, extras, row_count, col_count
    )
    return (
        block_out,
        grad_tokens,
        gain_sums[0],
        sum_query,
        sum_keyvalue.reshape(deep, pairs, 2 * HD),
        sum_output,
        gain_sums[1],
        sum_hidden.reshape(deep, 2, hidden),
        sum_down,
    )


def solution(mesh):
    return jax.shard_map(
        shards,
        mesh=mesh,
        in_specs=(
            P(("row", "col"), None),
            P("row", None),
            P(),
            P("row", "col"),
            P("row", "col", None),
            P("row", "col"),
            P(),
            P("row", None, "col"),
            P("row", "col"),
            P(("row", "col"), None),
        ),
        out_specs=(
            P(("row", "col"), None),
            P(("row", "col"), None),
            P(),
            P("row", "col"),
            P("row", "col", None),
            P("row", "col"),
            P(),
            P("row", None, "col"),
            P("row", "col"),
        ),
        check_vma=False,
    )
```

```python
import functools

import jax
import jax.numpy as jnp
from jax import lax
from jax.experimental import pallas as pl
from jax.experimental.pallas import tpu as pltpu
from jax.sharding import PartitionSpec as P

HD = 64
SEQ_MAX = 512
MESH = pl.DeviceIdType.MESH
LAG = 2
ANY = pl.BlockSpec(memory_space=pl.ANY)

epsilon = 1e-05
rope_base = 500000.0
blocked = -1e30
bf16 = jnp.bfloat16
f32 = jnp.float32


def plane_sizes(row_count):
    cores = 2 if row_count % 2 == 0 else 1
    chips = row_count // cores
    first = 2 if chips % 2 == 0 else 1
    return first, chips // first, cores


class Place:
    def __init__(self, row_count, col_count):
        self.rows, self.cols = row_count, col_count
        self.sizes = plane_sizes(row_count)
        na, nb, nk = self.sizes
        self.row = lax.axis_index("row")
        self.col = lax.axis_index("col")
        self.at = (self.row // (nb * nk), (self.row // nk) % nb, self.row % nk)

    def row_of(self, at):
        _, nb, nk = self.sizes
        return (at[0] * nb + at[1]) * nk + at[2]

    def chip_of(self, at):
        return at[0] * self.sizes[1] + at[1]

    def moved(self, axis, step, at=None):
        at = list(self.at if at is None else at)
        size = self.sizes[axis]
        at[axis] = lax.rem(at[axis] + (step % size), size)
        return tuple(at)

    def device(self, axis, step):
        return (self.row_of(self.moved(axis, step)), self.col)

    def greet(self, plane, line):
        barrier = pltpu.get_barrier_semaphore()
        count = 0
        if plane:
            for axis in range(3):
                size = self.sizes[axis]
                for step in {1 % size, (size - 1) % size} - {0}:
                    pl.semaphore_signal(
                        barrier, inc=1, device_id=self.device(axis, step), device_id_type=MESH
                    )
                    count += 1
        if line and self.cols > 1:
            for step, there in self.line_ways():

                @pl.when(there)
                def _(step=step):
                    pl.semaphore_signal(
                        barrier, inc=1, device_id=(self.row, self.col + step), device_id_type=MESH
                    )

        if line and self.cols > 1:
            last = self.cols - 1
            count = count + jnp.minimum(self.col, 1) + jnp.minimum(last - self.col, 1)
        if not isinstance(count, int) or count:
            pl.semaphore_wait(barrier, count)

    def line_ways(self):
        return ((1, self.col < self.cols - 1), (-1, self.col > 0))


def when(condition, action):
    if condition is None or condition is True:
        action()
    elif condition is False:
        pass
    else:
        pl.when(condition)(action)


def remote(src, dst, send_sem, recv_sem, device):
    return pltpu.make_async_remote_copy(
        src_ref=src,
        dst_ref=dst,
        send_sem=send_sem,
        recv_sem=recv_sem,
        device_id=device,
        device_id_type=MESH,
    )


class LineGather:
    def __init__(self, place, own, block, send_sems, recv_sems):
        self.place, self.own, self.block = place, own, block
        self.sends, self.recvs = send_sems, recv_sems

    def copy(self, way, step, origin):
        place = self.place
        source = self.own if step == 1 else self.block(origin)
        return remote(
            source,
            self.block(origin),
            self.sends.at[way, step - 1],
            self.recvs.at[way, step - 1],
            (place.row, place.col + (1, -1)[way]),
        )

    def sends_at(self, way, step):
        col, last = self.place.col, self.place.cols - 1
        if way == 0:
            return (col >= step - 1) & (col < last), col - (step - 1)
        return (col + step - 1 <= last) & (col > 0), col + (step - 1)

    def gets_at(self, way, step):
        col, last = self.place.col, self.place.cols - 1
        if way == 0:
            return col >= step, col - step
        return col + step <= last, col + step

    def send(self, way, step):
        condition, origin = self.sends_at(way, step)
        when(condition, lambda: self.copy(way, step, origin).start())

    def receive(self, way, step):
        condition, origin = self.gets_at(way, step)

        def action():
            self.copy(way, step, origin).wait_recv()

        when(condition, action)
        if step < self.place.cols - 1:
            self.send(way, step + 1)

    def finish(self):
        for step in range(1, self.place.cols):
            for way in (0, 1):
                condition, origin = self.sends_at(way, step)
                when(condition, lambda: self.copy(way, step, origin).wait_send())


class PlaneGather:
    def __init__(self, place, block, own, send_sems, recv_sems):
        self.place, self.block, self.own = place, block, own
        self.sends, self.recvs = send_sems, recv_sems

    @staticmethod
    def sem_count(sizes):
        na, nb, _ = sizes
        return 2 * na * nb - 1

    def axes(self, half):
        return (1, 0) if half == 0 else (0, 1)

    def counts(self, half):
        first, second = self.axes(half)
        return self.place.sizes[first], self.place.sizes[second]

    def origin(self, half, i, j, core_step=0):
        first, second = self.axes(half)
        at = self.place.moved(first, -i)
        at = self.place.moved(second, -j, at)
        if core_step:
            at = self.place.moved(2, 1, at)
        return self.place.row_of(at)

    def copy(self, half, kind, i, j):
        np_, nq = self.counts(half)
        if kind == 0:
            number, device = i - 1, self.place.device(self.axes(half)[0], 1)
        elif kind == 1:
            number = (np_ - 1) + i * (nq - 1) + (j - 1)
            device = self.place.device(self.axes(half)[1], 1)
        else:
            number = (np_ * nq - 1) + i * nq + j
            device = self.place.device(2, 1)
        return number, device

    def sender(self, half, kind, i, j):
        number, device = self.copy(half, kind, i, j)
        oi, oj = (i - 1, j) if kind == 0 else ((i, j - 1) if kind == 1 else (i, j))
        ref = self.block(self.origin(half, oi, oj), half)
        source = self.own(half) if (oi, oj) == (0, 0) else ref
        return remote(source, ref, self.sends.at[half, number], self.recvs.at[half, number], device)

    def receiver(self, half, kind, i, j):
        number, device = self.copy(half, kind, i, j)
        ref = self.block(self.origin(half, i, j, 1 if kind == 2 else 0), half)
        return remote(ref, ref, self.sends.at[half, number], self.recvs.at[half, number], device)

    def all_copies(self):
        for half in (0, 1):
            np_, nq = self.counts(half)
            for i in range(1, np_):
                yield half, 0, i, 0
            for i in range(np_):
                for j in range(1, nq):
                    yield half, 1, i, j
            if self.place.sizes[2] > 1:
                for i in range(np_):
                    for j in range(nq):
                        yield half, 2, i, j

    def share(self, half, i, j):
        if self.place.sizes[2] > 1:
            self.sender(half, 2, i, j).start()

    def first(self):
        for half in (0, 1):
            if self.counts(half)[0] > 1:
                self.sender(half, 0, 1, 0).start()
        for half in (0, 1):
            self.share(half, 0, 0)

    def second(self):
        for half in (0, 1):
            np_, nq = self.counts(half)
            for i in range(np_):
                if i > 0:
                    self.receiver(half, 0, i, 0).wait_recv()
                    if i < np_ - 1:
                        self.sender(half, 0, i + 1, 0).start()
                if nq > 1:
                    self.sender(half, 1, i, 1).start()
                if i > 0:
                    self.share(half, i, 0)

    def third(self):
        for half in (0, 1):
            np_, nq = self.counts(half)
            for j in range(1, nq):
                for i in range(np_):
                    self.receiver(half, 1, i, j).wait_recv()
                    if j < nq - 1:
                        self.sender(half, 1, i, j + 1).start()
                    self.share(half, i, j)

    def shared(self):
        for copy in self.all_copies():
            if copy[1] == 2:
                self.receiver(*copy).wait_recv()

    def sent(self):
        for copy in self.all_copies():
            self.sender(*copy).wait_send()

    def finish(self):
        self.shared()
        self.sent()


def tile_gather(place, full, own, send_sems, recv_sems):
    deep = full.shape[0] // place.rows
    half = deep // 2

    def block(row, number):
        return full.at[pl.ds(row * deep + number * half, half)]

    def mine(number):
        if own is None:
            return block(place.row, number)
        return own.at[pl.ds(number * half, half)]

    return PlaneGather(place, block, mine, send_sems, recv_sems)


def nearby(place, number):
    low, high = place.col, place.cols - 1 - place.col
    both = jnp.minimum(low, high)
    way = jnp.minimum(jnp.maximum(high - low, -1), 1)
    step = (number + 1) // 2 * (-1 if number % 2 else 1)
    paired = jnp.minimum(jnp.maximum(2 * both - number + 1, 0), 1)
    return place.col + paired * step + (1 - paired) * way * (number - both)


def gather_kernel(sizes, count, inner, *refs):
    row_count, col_count = sizes
    every = count + inner
    splits = min(2, col_count)
    own, own_act = refs[:every], refs[every]
    full, full_act = refs[every + 1 : 2 * every + 1], refs[2 * every + 1]
    local_sems, zs, zr, ps, pr = refs[2 * every + 2 :]
    place = Place(row_count, col_count)
    place.greet(True, True)
    token_rows = own_act.shape[0]

    def at(n, col, row):
        deep = own[n].shape[0]
        if n < count:
            return full[n].at[col, pl.ds(row * deep, deep)]
        return full[n].at[pl.ds(row * deep, deep)]

    lines = [
        LineGather(place, own[n], lambda j, n=n: at(n, j, place.row), zs.at[n], zr.at[n])
        for n in range(count)
    ]
    acts = LineGather(
        place,
        own_act,
        lambda j: full_act.at[pl.ds(j * token_rows, token_rows)],
        zs.at[count],
        zr.at[count],
    )

    def keep(n):
        if n == every:
            return pltpu.make_async_copy(own_act, acts.block(place.col), local_sems.at[n])
        return pltpu.make_async_copy(own[n], at(n, place.col, place.row), local_sems.at[n])

    for n in range(every + 1):
        keep(n).start()
    for line in lines:
        for way in (0, 1):
            line.send(way, 1)

    def inside(n, col, near):
        deep = own[n].shape[0]
        half = deep // 2
        wide = own[n].shape[1] // splits
        columns = pl.ds(col * wide, wide) if n >= count else slice(None)

        def block(row, number):
            rows = pl.ds(row * deep + number * half, half)
            return full[n].at[col, rows] if n < count else full[n].at[rows, columns]

        def mine(number):
            rows = pl.ds(number * half, half)
            return own[n].at[rows, columns] if near else block(place.row, number)

        return PlaneGather(place, block, mine, ps.at[n, col], pr.at[n, col])

    entries = [(n, k) for k in range(col_count) for n in range(count)]
    parts = [inside(n, nearby(place, k), k == 0) for n, k in entries]
    entries += [(n, 0) for n in range(count, every) for _ in range(splits)]
    parts += [inside(n, part, True) for n in range(count, every) for part in range(splits)]
    act_steps = list(range(1, col_count))

    def act_step():
        if act_steps:
            for way in (0, 1):
                acts.receive(way, act_steps[0])
            act_steps.pop(0)

    for number in range(len(parts) + 2):
        if number < len(parts):
            n, k = entries[number]
            if n == 0 and k > 0:
                for line in lines:
                    for way in (0, 1):
                        line.receive(way, k)
                if k == 1:
                    for way in (0, 1):
                        acts.send(way, 1)
                if k >= 3:
                    act_step()
            parts[number].first()
        if 1 <= number <= len(parts):
            parts[number - 1].second()
        if 2 <= number:
            parts[number - 2].third()
        if number >= len(parts):
            act_step()
    while act_steps:
        act_step()
    for n in range(every + 1):
        keep(n).wait()
    for part in parts:
        part.finish()
    for line in lines + [acts]:
        line.finish()


def gather_all(weights, inner_weights, act, row_count, col_count):
    count, inner = len(weights), len(inner_weights)
    sizes = plane_sizes(row_count)
    steps = max(col_count - 1, 1)
    every = list(weights) + list(inner_weights)
    plane_sems = (count + inner, col_count, 2, PlaneGather.sem_count(sizes))
    moved = sum(w.size for w in weights) * row_count * col_count * 2
    return pl.pallas_call(
        functools.partial(gather_kernel, (row_count, col_count), count, inner),
        out_shape=[
            jax.ShapeDtypeStruct((col_count, row_count * w.shape[0], w.shape[1]), bf16)
            for w in weights
        ]
        + [
            jax.ShapeDtypeStruct((row_count * w.shape[0], w.shape[1]), bf16) for w in inner_weights
        ]
        + [jax.ShapeDtypeStruct((col_count * act.shape[0], act.shape[1]), bf16)],
        in_specs=[pl.BlockSpec(memory_space=pltpu.VMEM)] * (len(every) + 1),
        out_specs=[ANY] * (len(every) + 1),
        scratch_shapes=[
            pltpu.SemaphoreType.DMA((len(every) + 1,)),
            pltpu.SemaphoreType.DMA((count + 1, 2, steps)),
            pltpu.SemaphoreType.DMA((count + 1, 2, steps)),
            pltpu.SemaphoreType.DMA(plane_sems),
            pltpu.SemaphoreType.DMA(plane_sems),
        ],
        compiler_params=pltpu.CompilerParams(collective_id=0, has_side_effects=True),
        cost_estimate=pl.CostEstimate(flops=0, bytes_accessed=moved, transcendentals=0),
        name="gather_weights",
    )(*every, act)


def line_gather_kernel(sizes, own, full, local_sem, sends, recvs):
    place = Place(*sizes)
    place.greet(False, True)
    rows = own.shape[0]
    line = LineGather(place, own, lambda j: full.at[pl.ds(j * rows, rows)], sends, recvs)
    for way in (0, 1):
        line.send(way, 1)
    keep = pltpu.make_async_copy(own, full.at[pl.ds(place.col * rows, rows)], local_sem)
    keep.start()
    for step in range(1, place.cols):
        for way in (0, 1):
            line.receive(way, step)
    keep.wait()
    line.finish()


def line_gather(own, row_count, col_count, collective_id):
    steps = max(col_count - 1, 1)
    return pl.pallas_call(
        functools.partial(line_gather_kernel, (row_count, col_count)),
        out_shape=jax.ShapeDtypeStruct((col_count * own.shape[0], own.shape[1]), own.dtype),
        in_specs=[pl.BlockSpec(memory_space=pltpu.VMEM)],
        out_specs=ANY,
        scratch_shapes=[
            pltpu.SemaphoreType.DMA,
            pltpu.SemaphoreType.DMA((2, steps)),
            pltpu.SemaphoreType.DMA((2, steps)),
        ],
        compiler_params=pltpu.CompilerParams(collective_id=collective_id, has_side_effects=True),
        cost_estimate=pl.CostEstimate(
            flops=0, bytes_accessed=own.size * 2 * col_count, transcendentals=0
        ),
        name="gather_line",
    )(own)


def add_rows(target, source):
    rows = target.shape[0]
    piece = 32 if rows % 32 == 0 else 16

    def body(n, carry):
        at = pl.ds(pl.multiple_of(n * piece, piece), piece)
        target[at] = (target[at].astype(f32) + source[at].astype(f32)).astype(target.dtype)
        return carry

    lax.fori_loop(0, rows // piece, body, 0)


class LineSum:
    def __init__(self, place, own, held, send_sems, recv_sems):
        self.place, self.own, self.held = place, own, held
        self.sends, self.recvs = send_sems, recv_sems

    def distance(self, way, col):
        return col - self.place.col if way == 0 else self.place.col - col

    def feeds(self, way):
        return self.place.col > 0 if way == 0 else self.place.col < self.place.cols - 1

    def copy(self, way, distance, source):
        return remote(
            source,
            self.held.at[way, distance - 1],
            self.sends.at[way, distance - 1],
            self.recvs.at[way, distance - 1],
            (self.place.row, self.place.col + (1, -1)[way]),
        )

    def arrived(self, way, distance):
        ref = self.held.at[way, distance]
        return remote(
            ref,
            ref,
            self.sends.at[way, distance],
            self.recvs.at[way, distance],
            (self.place.row, self.place.col + (1, -1)[way]),
        )

    def early(self, col, allowed):
        for way in (0, 1):
            far = self.distance(way, col)

            @pl.when(allowed & (far > 0) & jnp.logical_not(self.feeds(way)))
            def _():
                self.copy(way, far, self.own(col)).start()

    def late(self, col, allowed):
        for way in (0, 1):
            far = self.distance(way, col)

            @pl.when(allowed & (far > 0) & self.feeds(way))
            def _():
                self.arrived(way, far).wait_recv()
                add_rows(self.own(col), self.held.at[way, far])
                self.copy(way, far, self.own(col)).start()

    def last(self, out):
        if self.place.cols > 1:
            for way in (0, 1):
                when(self.feeds(way), lambda: self.arrived(way, 0).wait_recv())
        own = self.own(self.place.col)
        rows = own.shape[0]
        piece = 32 if rows % 32 == 0 else 16
        has = [self.feeds(way) for way in (0, 1)]

        def body(n, carry):
            at = pl.ds(pl.multiple_of(n * piece, piece), piece)
            total = own[at].astype(f32)
            if self.place.cols > 1:
                for way in (0, 1):
                    term = self.held[way, 0, at].astype(f32)
                    total = total + jnp.where(has[way], term, 0.0)
            out[at] = total.astype(out.dtype)
            return carry

        lax.fori_loop(0, rows // piece, body, 0)

    def finish(self):
        for distance in range(1, self.place.cols):
            for way in (0, 1):
                col = self.place.col + (distance if way == 0 else -distance)
                there = col < self.place.cols if way == 0 else col >= 0
                when(there, lambda: self.copy(way, distance, self.own(col)).wait_send())


def dot_tokens(left, right):
    return lax.dot_general(left, right, (((0,), (0,)), ((), ())), preferred_element_type=f32)


def plan_units(cols, tiles, early, hop_us, tile_us, unit_us):
    begin = 4.0
    chunk_at = [0.0] + [begin + hop_us * k for k in range(1, cols)]
    tile_at = [0.0] * early + [begin + 2.0 + tile_us * (n + 1) for n in range(tiles - early)]
    events = [(chunk_at[k], ("chunk", k)) for k in range(1, cols)]
    for f in range(early, tiles):
        second_at = begin + 1.0 + 0.35 * tile_us * (f - early + 1)
        events.append((second_at, ("second", f)))
        events.append((tile_at[f], ("third", f)))
    events.sort(key=lambda event: event[0])
    units = [(max(chunk_at[k], tile_at[f]), k, f) for k in range(cols) for f in range(tiles)]
    units.sort()
    plan, now, after = [], 0.0, []
    while units or events or after:
        while events and events[0][0] <= now:
            plan.append(events.pop(0)[1])
        if after and (not units or units[0][0] > now):
            step, cost = after.pop(0)
            plan.append(step)
            now += cost
            continue
        if units and units[0][0] <= now:
            _, k, f = units.pop(0)
            plan.append(("unit", k, f))
            now += unit_us
            if not any(unit[1] == k for unit in units):
                if k > 0:
                    after.append((("grad", k), 2.6 * unit_us))
                after.append((("y", k), 1.3 * unit_us))
                after.sort(key=lambda item: -item[0][1] if item[0][0] == "grad" else 1)
            continue
        now = min([events[0][0]] * bool(events) + [units[0][0]] * bool(units))
    return plan


def mlp_kernel(sizes, early, wide, *refs):
    hn_own, dy_in, wh_in, wh_own, wd_in = refs[:5]
    grad_out, y_out, dwh_out, down_out = refs[5:9]
    hn, dy, wh, wd, act, dgu, terms, staged, held, grad_staged, down_staged = refs[9:20]
    token_sems, tile_sems, wd_sems, y_sem, dw_sems, sends, recvs = refs[20:27]
    hs, hr, ps, pr, own_sem, grad_sems = refs[27:33]
    first_held, inner_sems = refs[33], refs[34:]
    place = Place(*sizes)
    cols = place.cols
    width, hidden = wd.shape
    tiles = wh.shape[0]
    tile = hidden // tiles
    wides = width // wide
    tokens = hn.shape[1]
    deep = wh_own.shape[0]

    def wide_at(n):
        return pl.ds(pl.multiple_of(n * wide, wide), wide)

    def piece(n):
        return LineSum(
            place, lambda j: terms.at[j, :, wide_at(n)], held.at[n], sends.at[n], recvs.at[n]
        )

    near = [nearby(place, k) for k in range(cols)]

    def dy_copy(j):
        return pltpu.make_async_copy(dy_in.at[j], dy.at[j], token_sems.at[j])

    def wd_copy(f):
        at = slice(f * tile, (f + 1) * tile)
        return pltpu.make_async_copy(wd_in.at[:, at], wd.at[:, at], wd_sems.at[f])

    def tile_copies(f):
        if f < early:
            return [pltpu.make_async_copy(wh_in.at[f], wh.at[f], tile_sems.at[f, 0])]
        rows = pl.ds(place.row * deep, deep)
        return [
            pltpu.make_async_copy(
                wh_own.at[:, pl.ds(number * hidden + f * tile, tile)],
                wh.at[f, rows, pl.ds(number * tile, tile)],
                tile_sems.at[f, number],
            )
            for number in (0, 1)
        ]

    own_copy = pltpu.make_async_copy(hn_own, hn.at[place.col], own_sem)
    own_copy.start()
    for f in range(early, tiles):
        for copy in tile_copies(f):
            copy.start()
    place.greet(True, True)
    own_copy.wait()
    line = LineGather(place, hn.at[place.col], lambda j: hn.at[j], hs, hr)
    for way in (0, 1):
        line.send(way, 1)
    parts = {
        f: tile_gather(place, wh.at[f], None, ps.at[f - early], pr.at[f - early])
        for f in range(early, tiles)
    }
    for f in range(early, tiles):
        for copy in tile_copies(f):
            copy.wait()
        parts[f].first()
    dy_copy(near[0]).start()
    for f in range(tiles):
        if f < early:
            tile_copies(f)[0].start()
        wd_copy(f).start()
    for k in range(1, cols):
        dy_copy(near[k]).start()

    def out_copy(j):
        return pltpu.make_async_copy(staged, y_out.at[j], y_sem)

    def unit(k, f):
        j = near[k]
        at = slice(f * tile, (f + 1) * tile)
        gate_up = matmul(hn[j], wh[f])
        gate, up = gate_up[:, :tile], gate_up[:, tile:]
        back = matmul(dy[j], wd[:, at])
        sigmoid = jax.nn.sigmoid(gate)
        silu = gate * sigmoid
        act[j, :, at] = (silu * up).astype(bf16)
        dgate = back * up * sigmoid * (1.0 + gate * (1.0 - sigmoid))
        dgu[j, :, 2 * f * tile : (2 * f + 1) * tile] = dgate.astype(bf16)
        dgu[j, :, (2 * f + 1) * tile : (2 * f + 2) * tile] = (back * silu).astype(bf16)

    def grad(k):
        j = near[k]

        def body(n, carry):
            at = wide_at(n)
            total = 0.0
            for f in range(tiles):
                total += against(dgu[j, :, 2 * f * tile : 2 * (f + 1) * tile], wh[f, at])
            terms[j, :, at] = total.astype(bf16)
            piece(n).early(j, True)
            return carry

        lax.fori_loop(0, wides, body, 0)

    stored = []

    def y_part(k):
        j = near[k]
        if stored:
            out_copy(near[stored[-1]]).wait()

        def body(n, carry):
            at = wide_at(n)
            staged[:, at] = against(act[j], wd[at]).astype(bf16)
            return carry

        lax.fori_loop(0, wides, body, 0)
        out_copy(j).start()
        stored.append(k)

    def late(number):
        low, high = place.col, cols - 1 - place.col
        up_first = jnp.minimum(jnp.maximum(high - low, 0), 1)
        side = up_first * high + (1 - up_first) * low
        way = 2 * up_first - 1
        first = jnp.minimum(jnp.maximum(side - number, 0), 1)
        col = place.col + first * way * (number + 1) - (1 - first) * way * (number + 1 - side)
        return col

    calls = [(number, n) for number in range(cols - 1) for n in range(wides)]

    def do_late(call):
        number, n = call
        piece(n).late(late(number), True)

    def next_late():
        if calls:
            do_late(calls.pop(0))

    seen_tiles, seen_chunks = set(), set()
    for step in plan_units(cols, tiles, early, 24.0, 18.0, 2.1):
        if step[0] == "chunk":
            for way in (0, 1):
                line.receive(way, step[1])
        elif step[0] == "second":
            parts[step[1]].second()
        elif step[0] == "third":
            parts[step[1]].third()
            parts[step[1]].shared()
        elif step[0] == "unit":
            _, k, f = step
            if f not in seen_tiles:
                seen_tiles.add(f)
                if f < early:
                    tile_copies(f)[0].wait()
                wd_copy(f).wait()
            if k not in seen_chunks:
                seen_chunks.add(k)
                dy_copy(near[k]).wait()
            unit(k, f)
        elif step[0] == "grad":
            grad(step[1])
            if step[1] == cols - 1:
                next_late()
        else:
            y_part(step[1])
            if step[1] == cols - 1:
                next_late()

    for f in parts:
        parts[f].sent()
    strips = width // 256

    def flat(ref):
        return ref[...].reshape(cols * tokens, ref.shape[2])

    def columns(ref, at):
        return jnp.concatenate([ref[j, :, at] for j in range(cols)], axis=0)

    def down_strip(n, carry):
        at = pl.ds(pl.multiple_of(n * 256, 256), 256)
        wd[at] = dot_tokens(columns(dy, at), flat(act)).astype(bf16)
        return carry

    for begin, end in ((0, strips // 2), (strips // 2, strips)):
        lax.fori_loop(begin, end, down_strip, 0)
        next_late()
    chunk = down_staged.shape[2]
    inner = InnerSumInPlace(
        place,
        wd,
        lambda e: down_out.at[:, pl.ds(pl.multiple_of(e * chunk, chunk), chunk)],
        chunk,
        dy,
        act,
        first_held,
        down_staged,
        inner_sems,
    )
    inner.begin()
    inner.tick(0)
    inner.tick(1)
    grad(0)
    beside = []
    for number in ((1, 3) + (2,) * strips)[:strips]:
        beside.append(calls[:number])
        del calls[:number]

    def hidden_strip(n, carry):
        at = pl.ds(pl.multiple_of(n * 256, 256), 256)
        left = columns(hn, at)
        for f in range(tiles):
            span = slice(2 * f * tile, 2 * (f + 1) * tile)
            right = dgu[:, :, span].reshape(cols * tokens, 2 * tile)
            wh[f, at] = dot_tokens(left, right).astype(bf16)
        pltpu.make_async_copy(wh.at[:, at], dwh_out.at[:, at], dw_sems.at[n]).start()
        inner.tick(n + 2)
        for number, some in enumerate(beside):
            for call in some:
                pl.when(n == number)(functools.partial(do_late, call))
        return carry

    lax.fori_loop(0, strips, hidden_strip, 0)
    for t in range(strips + 2, inner.count + 2 * LAG):
        inner.tick(t)
    while calls:
        next_late()

    def grad_copy(n):
        return pltpu.make_async_copy(
            grad_staged.at[n % 2], grad_out.at[:, wide_at(n)], grad_sems.at[n % 2]
        )

    for n in range(wides):
        if n >= 2:
            grad_copy(n - 2).wait()
        piece(n).last(grad_staged.at[n % 2])
        grad_copy(n).start()
    for n in range(max(wides - 2, 0), wides):
        grad_copy(n).wait()
    out_copy(near[stored[-1]]).wait()

    def finish(n, carry):
        at = pl.ds(pl.multiple_of(n * 256, 256), 256)
        pltpu.make_async_copy(wh.at[:, at], dwh_out.at[:, at], dw_sems.at[n]).wait()
        return carry

    lax.fori_loop(0, strips, finish, 0)
    inner.finish()
    line.finish()
    for n in range(wides):
        piece(n).finish()


def mlp(hn, dy, wh, wh_own, wd, row_count, col_count, collective_id):
    steps = max(col_count - 1, 1)
    rows, width = hn.shape
    hidden = wd.shape[1]
    early, tile = wh.shape[0], wh.shape[2] // 2
    tiles = hidden // tile
    left = tiles - early
    wide = min(512, width)
    shape = (col_count, rows, width)
    total = col_count * rows
    wh_shape = (tiles, width, 2 * tile)
    plane = plane_sizes(row_count)
    plane_sems = (left, 2, PlaneGather.sem_count(plane))
    deep = width // row_count
    chunk = min(512, hidden)
    count = hidden // chunk
    inner_sems = InnerSum.sems(plane, count)
    inner_sems[0] = pltpu.SemaphoreType.DMA((2, count, plane[0] * plane[1]))
    grad, y, dwh, sum_down = pl.pallas_call(
        functools.partial(mlp_kernel, (row_count, col_count), early, wide),
        out_shape=[
            jax.ShapeDtypeStruct((rows, width), f32),
            jax.ShapeDtypeStruct(shape, bf16),
            jax.ShapeDtypeStruct(wh_shape, bf16),
            jax.ShapeDtypeStruct((deep, hidden), f32),
        ],
        in_specs=[ANY] * 5,
        out_specs=[ANY] * 4,
        scratch_shapes=[
            pltpu.VMEM(shape, bf16),
            pltpu.VMEM(shape, bf16),
            pltpu.VMEM(wh_shape, bf16),
            pltpu.VMEM(wd.shape, bf16),
            pltpu.VMEM((col_count, rows, hidden), bf16),
            pltpu.VMEM((col_count, rows, 2 * hidden), bf16),
            pltpu.VMEM(shape, bf16),
            pltpu.VMEM((rows, width), bf16),
            pltpu.VMEM((width // wide, 2, steps, rows, wide), bf16),
            pltpu.VMEM((2, rows, wide), f32),
            pltpu.VMEM((2, deep, chunk), f32),
            pltpu.SemaphoreType.DMA((col_count,)),
            pltpu.SemaphoreType.DMA((tiles, 2)),
            pltpu.SemaphoreType.DMA((tiles,)),
            pltpu.SemaphoreType.DMA,
            pltpu.SemaphoreType.DMA((width // 256,)),
            pltpu.SemaphoreType.DMA((width // wide, 2, steps)),
            pltpu.SemaphoreType.DMA((width // wide, 2, steps)),
            pltpu.SemaphoreType.DMA((2, steps)),
            pltpu.SemaphoreType.DMA((2, steps)),
            pltpu.SemaphoreType.DMA(plane_sems),
            pltpu.SemaphoreType.DMA(plane_sems),
            pltpu.SemaphoreType.DMA,
            pltpu.SemaphoreType.DMA((2,)),
        ]
        + [pltpu.VMEM(InnerSum.held_shapes(plane, deep, hidden, chunk)[2], bf16)]
        + inner_sems
        + [pltpu.SemaphoreType.REGULAR],
        compiler_params=pltpu.CompilerParams(
            collective_id=collective_id, has_side_effects=True, vmem_limit_bytes=63 << 20
        ),
        cost_estimate=pl.CostEstimate(
            flops=2 * 9 * total * width * hidden,
            bytes_accessed=6 * width * hidden * 2,
            transcendentals=total * hidden,
        ),
        name="feed_forward",
    )(hn, dy.reshape(shape), wh, wh_own, wd)
    return grad, y.reshape(total, width), dwh, sum_down


class PlaneSum:
    def __init__(self, place, block, held, sems):
        self.place, self.block, self.held = place, block, held
        self.sends, self.recvs = sems

    @staticmethod
    def counts_of(sizes):
        na, nb, _ = sizes
        return max(na, nb) - 1, max((na - 1) * nb, (nb - 1) * na)

    @staticmethod
    def sem_count(sizes):
        na, nb, _ = sizes
        return na * nb - 1

    def axes(self, half):
        return (1, 0) if half == 0 else (0, 1)

    def counts(self, half):
        first, second = self.axes(half)
        return self.place.sizes[first], self.place.sizes[second]

    def part(self, half, i, j):
        first, second = self.axes(half)
        at = self.place.moved(second, j, self.place.moved(first, i))
        return self.block(self.place.chip_of(at), half)

    def number(self, half, kind, step, i):
        return (step - 1) * self.counts(half)[0] + i if kind == 1 else step - 1

    def copy(self, half, kind, step, i):
        np_, nq = self.counts(half)
        number = self.number(half, kind, step, i)
        if kind == 1:
            source, sem = self.part(half, i, nq - step), number
        else:
            source, sem = self.part(half, np_ - step, 0), (nq - 1) * np_ + number
        target = self.held(kind, half, number)
        device = self.place.device(self.axes(half)[1 if kind == 1 else 0], 1)
        return remote(source, target, self.sends.at[half, sem], self.recvs.at[half, sem], device)

    def add(self, pieces):
        for half, kind, step, i in pieces:
            np_, nq = self.counts(half)
            self.copy(half, kind, step, i).wait_recv()
            if kind == 1:
                target = self.part(half, i, nq - step - 1)
            else:
                target = self.part(half, np_ - step - 1, 0)
            add_rows(target, self.held(kind, half, self.number(half, kind, step, i)))
            yield half, i

    def first(self):
        for half in (0, 1):
            np_, nq = self.counts(half)
            if nq > 1:
                for i in range(np_ - 1, -1, -1):
                    self.copy(half, 1, 1, i).start()

    def second(self):
        for half in (0, 1):
            np_, nq = self.counts(half)
            if nq == 1 and np_ > 1:
                self.copy(half, 0, 1, 0).start()
        for step in range(1, max(self.place.sizes[:2])):
            pieces = []
            for half in (0, 1):
                np_, nq = self.counts(half)
                if step < nq:
                    pieces += [(half, 1, step, i) for i in range(np_ - 1, -1, -1)]
            for half, i in self.add(pieces):
                np_, nq = self.counts(half)
                if step < nq - 1:
                    self.copy(half, 1, step + 1, i).start()
                elif i == np_ - 1 and np_ > 1:
                    self.copy(half, 0, 1, 0).start()

    def third(self):
        for step in range(1, max(self.place.sizes[:2])):
            pieces = [(half, 0, step, 0) for half in (0, 1) if step < self.counts(half)[0]]
            for half, _ in self.add(pieces):
                if step < self.counts(half)[0] - 1:
                    self.copy(half, 0, step + 1, 0).start()

    def finish(self):
        for half in (0, 1):
            np_, nq = self.counts(half)
            for step in range(1, nq):
                for i in range(np_):
                    self.copy(half, 1, step, i).wait_send()
            for step in range(1, np_):
                self.copy(half, 0, step, 0).wait_send()


def landing(first, second):
    return lambda kind, half, number: (first, second)[kind].at[half, number]


def halves_of(acc):
    half = acc.shape[1] // 2
    return lambda chip, number: acc.at[chip, pl.ds(number * half, half)]


def core_rows(place, chip, step, deep):
    cores = place.sizes[2]
    row = chip * cores + lax.rem(place.at[2] + step, cores)
    return pl.ds(pl.multiple_of(row * deep, deep), deep)


class InnerSum:
    def __init__(self, place, count, terms, target, refs):
        self.place, self.count, self.terms, self.target = place, count, terms, target
        self.acc, self.core_held, self.second, self.first, self.staged = refs[:5]
        self.load_sems, self.core_sems, self.plane_sems, self.out_sems = refs[5:9]
        self.ahead = min(3, self.count)
        self.chips, self.deep = self.core_held.shape[1:3]

    def held(self, e):
        return landing(self.first.at[e], self.second.at[e])

    def core_block(self, e, chip):
        return self.core_held.at[e, chip]

    @staticmethod
    def held_shapes(sizes, deep, width, chunk):
        na, nb, _ = sizes
        firsts, seconds = PlaneSum.counts_of(sizes)
        return [
            (width // chunk, na * nb, deep, chunk),
            (width // chunk, 2, max(seconds, 1), deep // 2, chunk),
            (width // chunk, 2, max(firsts, 1), deep // 2, chunk),
        ]

    @staticmethod
    def sems(sizes, count):
        return [
            pltpu.SemaphoreType.DMA((2, count)),
            pltpu.SemaphoreType.DMA((2, count, 2, max(PlaneSum.sem_count(sizes), 1))),
            pltpu.SemaphoreType.DMA((2,)),
        ]

    @staticmethod
    def scratch(sizes, deep, width, chunk, staged):
        shapes = InnerSum.held_shapes(sizes, deep, width, chunk)
        count = width // chunk
        return (
            [pltpu.VMEM(shape, bf16) for shape in shapes[:1] + shapes]
            + [pltpu.VMEM(staged, f32), pltpu.SemaphoreType.DMA((count,))]
            + InnerSum.sems(sizes, count)
        )

    def load(self, e):
        source = self.terms(e, self.place.at[2])
        return pltpu.make_async_copy(source, self.acc.at[e], self.load_sems.at[e])

    def other(self):
        return lax.rem(self.place.at[2] + 1, self.place.sizes[2])

    def shares(self, e):
        return [
            remote(
                self.terms(e, self.other()),
                self.core_held.at[e],
                self.core_sems.at[0, e],
                self.core_sems.at[1, e],
                self.place.device(2, 1),
            )
        ]

    def block(self, e, chip):
        return self.acc.at[e, chip]

    def inside(self, e):
        half = self.deep // 2
        return PlaneSum(
            self.place,
            lambda chip, number: self.block(e, chip).at[pl.ds(number * half, half)],
            self.held(e),
            (self.plane_sems.at[0, e], self.plane_sems.at[1, e]),
        )

    def out_copy(self, e):
        slot = lax.rem(e, 2)
        return pltpu.make_async_copy(
            self.staged.at[slot], self.target(e), self.out_sems.at[slot]
        )

    def prepare(self, e):
        self.load(e).start()
        if self.place.sizes[2] > 1:
            for share in self.shares(e):
                share.start()

    def begin(self):
        for e in range(self.ahead):
            self.prepare(e)

    def ready(self, e):
        self.load(e).wait()
        if self.place.sizes[2] > 1:
            for share in self.shares(e):
                share.wait_recv()

    def start(self, e):
        when(e + self.ahead < self.count, lambda: self.prepare(e + self.ahead))
        self.ready(e)
        if self.place.sizes[2] > 1:
            for chip in range(self.chips):
                add_rows(self.block(e, chip), self.core_block(e, chip))
        self.inside(e).first()

    def middle(self, e):
        self.inside(e).second()

    def close(self, e):
        self.inside(e).third()
        when(e >= 2, lambda: self.out_copy(e - 2).wait())
        slot = lax.rem(e, 2)
        own = self.block(e, self.place.chip_of(self.place.at))
        self.staged[slot] = own[...].astype(f32)
        self.out_copy(e).start()

    def tick(self, t):
        for lag, action in ((0, self.start), (LAG, self.middle), (2 * LAG, self.close)):
            e = t - lag
            when((e >= 0) & (e < self.count), functools.partial(action, e))

    def last_outs(self):
        return range(max(self.count - 2, 0), self.count)

    def finish(self):
        for e in self.last_outs():
            self.out_copy(e).wait()

        def done(e, carry):
            if self.place.sizes[2] > 1:
                for share in self.shares(e):
                    share.wait_send()
            self.inside(e).finish()
            return carry

        lax.fori_loop(0, self.count, done, 0)


class PairSum(InnerSum):
    def out_copy(self, f):
        return pltpu.make_async_copy(self.staged.at[0], self.target(f), self.out_sems.at[0])

    def close(self, e):
        self.inside(e).third()
        f, part = e // 2, lax.rem(e, 2)
        when((part == 0) & (f >= 1), lambda: self.out_copy(f - 1).wait())
        own = self.block(e, self.place.chip_of(self.place.at))
        for number in (0, 1):

            @pl.when(part == number)
            def _(number=number):
                self.staged[0, :, number, :] = own[...].astype(f32)

        when(part == 1, lambda: self.out_copy(f).start())

    def last_outs(self):
        return range(self.count // 2 - 1, self.count // 2)


class InnerSumInPlace(InnerSum):
    def __init__(self, place, terms, target, chunk, core_land, land, first, staged, sems):
        self.place, self.terms, self.target, self.chunk = place, terms, target, chunk
        self.core_land, self.land, self.first, self.staged = core_land, land, first, staged
        self.core_sems, self.plane_sems, self.out_sems, self.free_sem = sems
        self.count = terms.shape[1] // chunk
        self.ahead = self.count
        self.chips = place.sizes[0] * place.sizes[1]
        self.deep = terms.shape[0] // place.rows

    def columns(self, e):
        return pl.ds(pl.multiple_of(e * self.chunk, self.chunk), self.chunk)

    def rows(self, e, chip, core):
        row = chip * self.place.sizes[2] + core
        return self.terms.at[
            pl.ds(pl.multiple_of(row * self.deep, self.deep), self.deep), self.columns(e)
        ]

    def block(self, e, chip):
        return self.rows(e, chip, self.place.at[2])

    def core_block(self, e, chip):
        return self.core_land.at[chip, :, self.columns(e)]

    def held(self, e):
        half_deep = self.deep // 2

        def place_of(kind, half, number):
            if kind == 0:
                return self.first.at[e, half, number]
            return self.land.at[number, pl.ds(half * half_deep, half_deep), self.columns(e)]

        return place_of

    def shares(self, e):
        return [
            remote(
                self.rows(e, chip, self.other()),
                self.core_block(e, chip),
                self.core_sems.at[0, e, chip],
                self.core_sems.at[1, e, chip],
                self.place.device(2, 1),
            )
            for chip in range(self.chips)
        ]

    def prepare(self, e):
        if self.place.sizes[2] > 1:
            for share in self.shares(e):
                share.start()

    def begin(self):
        peers = [axis for axis in range(3) if self.place.sizes[axis] > 1]
        for axis in peers:
            pl.semaphore_signal(
                self.free_sem, inc=1, device_id=self.place.device(axis, -1), device_id_type=MESH
            )
        if peers:
            pl.semaphore_wait(self.free_sem, len(peers))
        super().begin()

    def ready(self, e):
        if self.place.sizes[2] > 1:
            for share in self.shares(e):
                share.wait_recv()


class SmallSum:
    def __init__(self, place, own, total, ring_held, line_held, ring_sems, line_sems):
        self.place, self.own, self.total = place, own, total
        self.held, self.sems = ring_held, ring_sems
        self.line = LineGather(
            place, total, lambda j: line_held.at[j], line_sems.at[0], line_sems.at[1]
        )
        self.line_held = line_held
        self.stages = []
        for axis in range(3):
            for step in range(1, place.sizes[axis]):
                self.stages.append(functools.partial(self.ring_send, axis, step))
                self.stages.append(functools.partial(self.ring_receive, axis, step))
            if place.sizes[axis] > 1:
                self.stages.append(functools.partial(self.ring_add, axis))
        self.stages.append(self.line_start)
        for step in range(1, place.cols):
            self.stages.append(functools.partial(self.line_step, step))
        self.stages.append(self.line_add)

    def begin(self):
        self.total[...] = self.own[...]

    def block(self, axis, step):
        at = self.place.moved(axis, -step)[axis]
        return self.held.at[axis, at]

    def ring_copy(self, axis, step):
        source = self.total if step == 1 else self.block(axis, step - 1)
        target = self.held.at[axis, self.place.moved(axis, 1 - step)[axis]]
        return remote(
            source,
            target,
            self.sems.at[0, axis, step - 1],
            self.sems.at[1, axis, step - 1],
            self.place.device(axis, 1),
        )

    def ring_send(self, axis, step):
        self.ring_copy(axis, step).start()

    def ring_receive(self, axis, step):
        ref = self.block(axis, step)
        remote(
            ref,
            ref,
            self.sems.at[0, axis, step - 1],
            self.sems.at[1, axis, step - 1],
            self.place.device(axis, 1),
        ).wait_recv()

    def ring_add(self, axis):
        for step in range(1, self.place.sizes[axis]):
            self.ring_copy(axis, step).wait_send()
        own_at = self.place.at[axis]
        total = None
        for at in range(self.place.sizes[axis]):
            term = jnp.where(own_at == at, self.total[...], self.held[axis, at])
            total = term if total is None else total + term
        self.total[...] = total

    def line_start(self):
        for way in (0, 1):
            self.line.send(way, 1)

    def line_step(self, step):
        for way in (0, 1):
            self.line.receive(way, step)

    def line_add(self):
        self.line.finish()
        total = None
        for at in range(self.place.cols):
            term = jnp.where(self.place.col == at, self.total[...], self.line_held[at])
            total = term if total is None else total + term
        self.total[...] = total


def norm_rows(dxn, x, dh, gain, out, part):
    rows, width = x.shape
    piece = 32

    def body(n, carry):
        at = pl.ds(pl.multiple_of(n * piece, piece), piece)
        values = x[at].astype(f32)
        scale = lax.rsqrt(jnp.mean(values * values, axis=1, keepdims=True) + epsilon)
        grad = dxn[at]
        weighted = grad * gain[...]
        inner = jnp.mean(weighted * values, axis=1, keepdims=True)
        result = dh[at].astype(f32) + scale * weighted - values * (scale * scale * scale) * inner
        out[at] = result.astype(out.dtype)
        part[0:1] += jnp.sum(grad * values * scale, axis=0, keepdims=True)
        return carry

    part[0:1] = jnp.zeros((1, width), f32)
    lax.fori_loop(0, rows // piece, body, 0)


def sum_kernel(sizes, count, *refs):
    row_count, col_count = sizes
    place = Place(row_count, col_count)
    cores = place.sizes[2]
    lefts, rights = refs[: cores * count], refs[cores * count : 2 * cores * count]
    refs = refs[2 * cores * count :]
    dxn, x, dh, gain, mid_part = refs[:5]
    outs = refs[5 : 6 + count]
    tokens_out, small_out = refs[6 + count : 8 + count]
    refs = refs[8 + count :]
    per = [refs[7 * n : 7 * n + 7] for n in range(count)]
    load_sems, out_sems, ps, pr, zs, zr = refs[7 * count : 7 * count + 6]
    ring_held, line_held, ring_sems, line_sems, chip_sems, small = refs[7 * count + 6 :]

    entries = [(n, nearby(place, k)) for k in range(col_count - 1, -1, -1) for n in range(count)]

    acc = [per[n][0] for n in range(count)]
    lines = [
        LineSum(
            place,
            lambda j, n=n: acc[n].at[j, place.chip_of(place.at)],
            per[n][3],
            zs.at[n],
            zr.at[n],
        )
        for n in range(count)
    ]
    tokens = lefts[0].shape[0]
    chips, deep = acc[0].shape[1:3]

    def loads():
        for n in range(count):
            left, right = per[n][5], per[n][6]
            for k in range(cores):
                at = pl.ds(k * tokens, tokens)
                if k == 0:
                    for chip in range(chips):
                        yield pltpu.make_async_copy(
                            lefts[n * cores].at[:, core_rows(place, chip, 0, deep)],
                            left.at[at, pl.ds(chip * deep, deep)],
                            chip_sems.at[n, chip],
                        )
                else:
                    yield pltpu.make_async_copy(
                        lefts[n * cores + k], left.at[at], load_sems.at[0, n * cores + k]
                    )
                yield pltpu.make_async_copy(
                    rights[n * cores + k], right.at[:, at], load_sems.at[1, n * cores + k]
                )

    for copy in loads():
        copy.start()
    place.greet(True, True)
    smalls = SmallSum(place, small, small_out, ring_held, line_held, ring_sems, line_sems)
    stages = [functools.partial(norm_rows, dxn, x, dh, gain, tokens_out, small)]
    stages += [smalls.begin] + smalls.stages
    small[1:2] = mid_part[...]
    for copy in loads():
        copy.wait()

    def inside(n, col):
        return PlaneSum(
            place,
            halves_of(acc[n].at[col]),
            landing(per[n][2].at[col], per[n][1].at[col]),
            (ps.at[n, col], pr.at[n, col]),
        )

    parts = [inside(n, col) for n, col in entries]
    final = len(entries) - count
    total = len(entries)

    def start(number):
        n, col = entries[number]
        left, right = per[n][5], per[n][6]
        deep = acc[n].shape[2]

        def chip_rows(chip, carry):
            at = pl.ds(pl.multiple_of(chip * deep, deep), deep)
            acc[n][col, chip] = dot_tokens(left[:, at], right[col]).astype(bf16)
            return carry

        lax.fori_loop(0, acc[n].shape[1], chip_rows, 0)
        parts[number].first()

    split = outs[0].shape[1]

    def out_copies(n):
        if n > 0:
            return [pltpu.make_async_copy(per[n][4], outs[n + 1], out_sems.at[n + 1])]
        rest = pl.ds(split, outs[1].shape[1])
        return [
            pltpu.make_async_copy(per[0][4].at[:, pl.ds(0, split)], outs[0], out_sems.at[0]),
            pltpu.make_async_copy(per[0][4].at[:, rest], outs[1], out_sems.at[1]),
        ]

    def close(number):
        parts[number].third()
        n, col = entries[number]
        if number < final:
            lines[n].early(col, True)
            if number >= count:
                lines[n].late(entries[number - count][1], True)
            if number >= final - count:
                lines[n].late(col, True)

    def finish_lines():
        for n in range(count):
            lines[n].last(per[n][4])
            for copy in out_copies(n):
                copy.start()

    for number in range(total + 2 * LAG):
        if number < total:
            start(number)
        if LAG <= number < total + LAG:
            parts[number - LAG].second()
        if 2 * LAG <= number:
            close(number - 2 * LAG)
        if number >= 1:
            for stage in stages[:2]:
                stage()
            del stages[:2]
    for stage in stages:
        stage()
    finish_lines()
    for n in range(count):
        for copy in out_copies(n):
            copy.wait()
    for part in parts:
        part.finish()
    for line in lines:
        line.finish()


def sum_all(lefts, rights, split, extras, row_count, col_count):
    count = len(rights)
    sizes = plane_sizes(row_count)
    na, nb, nk = sizes
    chips = na * nb
    tokens, model = lefts[0][0].shape
    deep = lefts[0][0].shape[1] // row_count
    steps = max(col_count - 1, 1)
    firsts, seconds = PlaneSum.counts_of(sizes)
    widths = [right[0].shape[2] for right in rights]
    scratch = []
    for width in widths:
        scratch += [
            pltpu.VMEM((col_count, chips, deep, width), bf16),
            pltpu.VMEM((col_count, 2, max(seconds, 1), deep // 2, width), bf16),
            pltpu.VMEM((col_count, 2, max(firsts, 1), deep // 2, width), bf16),
            pltpu.VMEM((2, steps, deep, width), bf16),
            pltpu.VMEM((deep, width), f32),
            pltpu.VMEM((nk * tokens, chips * deep), bf16),
            pltpu.VMEM((col_count, nk * tokens, width), bf16),
        ]
    plane_sems = (count, col_count, 2, max(PlaneSum.sem_count(sizes), 1))
    scratch += [
        pltpu.SemaphoreType.DMA((2, count * nk)),
        pltpu.SemaphoreType.DMA((count + 1,)),
        pltpu.SemaphoreType.DMA(plane_sems),
        pltpu.SemaphoreType.DMA(plane_sems),
        pltpu.SemaphoreType.DMA((count, 2, steps)),
        pltpu.SemaphoreType.DMA((count, 2, steps)),
        pltpu.VMEM((3, max(sizes), 2, model), f32),
        pltpu.VMEM((col_count, 2, model), f32),
        pltpu.SemaphoreType.DMA((2, 3, max(max(sizes) - 1, 1))),
        pltpu.SemaphoreType.DMA((2, 2, steps)),
        pltpu.SemaphoreType.DMA((count, chips)),
        pltpu.VMEM((2, model), f32),
    ]
    outs = [split, widths[0] - split] + widths[1:]
    vmem = pl.BlockSpec(memory_space=pltpu.VMEM)
    flops = sum(2 * nk * tokens * chips * deep * width * col_count for width in widths)
    return pl.pallas_call(
        functools.partial(sum_kernel, (row_count, col_count), count),
        out_shape=[jax.ShapeDtypeStruct((deep, width), f32) for width in outs]
        + [
            jax.ShapeDtypeStruct((tokens, model), bf16),
            jax.ShapeDtypeStruct((2, model), f32),
        ],
        in_specs=[ANY] * (2 * count * nk) + [vmem] * 5,
        out_specs=[ANY] * (count + 1) + [vmem] * 2,
        scratch_shapes=scratch,
        compiler_params=pltpu.CompilerParams(
            collective_id=1, has_side_effects=True, vmem_limit_bytes=63 << 20
        ),
        cost_estimate=pl.CostEstimate(
            flops=flops, bytes_accessed=flops // 256, transcendentals=0
        ),
        name="sum_weights",
    )(
        *[left for pair in lefts for left in pair],
        *[right for pair in rights for right in pair],
        *extras,
    )


LANES = 2 * HD


def lower_lanes():
    return lax.broadcasted_iota(jnp.int32, (1, LANES), 1) < HD


def rope_lanes(values, cosine, sinusoid):
    lane = lax.broadcasted_iota(jnp.int32, (1, LANES), 1)
    other = jnp.where(
        lane % HD < HD // 2,
        pltpu.roll(values, LANES - HD // 2, 1),
        pltpu.roll(values, HD // 2, 1),
    )
    return values * cosine + other * sinusoid


def head_at(tile, head, upper):
    if (head % 2 == 1) != upper:
        tile = pltpu.roll(tile, HD, 1)
    keep = lower_lanes()
    if upper:
        keep = jnp.logical_not(keep)
    return jnp.where(keep, tile, 0.0)


def tile_of(head):
    return slice(head // 2 * LANES, head // 2 * LANES + LANES)


def pair_tile(even, odd, upper):
    if upper:
        even = pltpu.roll(even, HD, 1)
    else:
        odd = pltpu.roll(odd, HD, 1)
    return jnp.where(lower_lanes(), even, odd)


def attend_kernel(sizes, heads, group, back, *refs):
    xn, x, wf_in, wo_in, bias, cosq, sinq, coskv, sinkv, gain, tiles_in = refs[:11]
    q_out, kv_out, mixed_out, lse_out, full_tiles, hidden, hn = refs[11:18]
    q, kv, mixed, lse, wf, wo, w_sems, o_sems, sends, recvs, t_sems, ps, pr = refs[18:31]
    tiles, tiles_sem = refs[31:]
    place = Place(*sizes)
    cols, col = place.cols, place.col
    tokens = xn.shape[0]
    query_width = heads * HD
    own_rows = pl.ds(back * tokens, tokens)
    pairs = heads // group

    def weight_copies(z):
        return (
            pltpu.make_async_copy(wf_in.at[z], wf.at[z], w_sems.at[0, z]),
            pltpu.make_async_copy(wo_in.at[z], wo.at[z], w_sems.at[1, z]),
        )

    count, _, tile = tiles.shape
    tile = tile // 2
    hidden_units = tiles_in.shape[1] // 2
    fetches = [
        pltpu.make_async_copy(
            tiles_in.at[:, pl.ds(number * hidden_units + f * tile, tile)],
            tiles.at[f, :, pl.ds(number * tile, tile)],
            tiles_sem.at[f, number],
        )
        for f in range(count)
        for number in (0, 1)
    ]
    for fetch in fetches:
        fetch.start()
    for step in range(1, back + 1):

        @pl.when(col < step)
        def _():
            kv[:, (back - step) * tokens : (back - step + 1) * tokens] = jnp.zeros(
                (cols, tokens, kv.shape[2]), bf16
            )

    keeps = [
        pltpu.make_async_copy(
            tiles.at[f],
            full_tiles.at[f, pl.ds(place.row * tiles.shape[1], tiles.shape[1])],
            t_sems.at[f],
        )
        for f in range(tiles.shape[0])
    ]
    place.greet(True, True)
    for fetch in fetches:
        fetch.wait()
    parts = [
        tile_gather(place, full_tiles.at[f], tiles.at[f], ps.at[f], pr.at[f])
        for f in range(tiles.shape[0])
    ]
    for part in parts:
        part.first()
    for number in (0, 1):
        for z in range(cols):
            weight_copies(z)[number].start()
    for keep in keeps:
        keep.start()

    def hop(z, step):
        source = kv.at[z, pl.ds((back - step + 1) * tokens, tokens)]
        target = kv.at[z, pl.ds((back - step) * tokens, tokens)]
        return remote(
            source, target, sends.at[step - 1, z], recvs.at[step - 1, z], (place.row, col + 1)
        )

    def goes(step):
        return (col < cols - 1) & (col >= step - 1)

    def send(z, step):
        pl.when(goes(step))(lambda: hop(z, step).start())

    def receive(z, step):
        ref = kv.at[z, pl.ds((back - step) * tokens, tokens)]

        @pl.when(col >= step)
        def _():
            remote(
                ref, ref, sends.at[step - 1, z], recvs.at[step - 1, z], (place.row, col + 1)
            ).wait_recv()

    def project(z, carry):
        weight_copies(z)[0].wait()
        pre = matmul(xn[...], wf[z])
        for n in range(query_width // LANES):
            at = slice(n * LANES, (n + 1) * LANES)
            q[z, :, at] = rope_lanes(pre[:, at], cosq[...], sinq[...]).astype(bf16)
        for n in range(pairs):
            at = slice(n * LANES, (n + 1) * LANES)
            tile = pre[:, query_width + n * LANES : query_width + (n + 1) * LANES]
            kv[z, own_rows, at] = rope_lanes(tile, coskv[...], sinkv[...]).astype(bf16)
        if back > 0:
            send(z, 1)
        return carry

    lax.fori_loop(0, cols, project, 0)
    if parts:
        parts[0].second()
    for step in range(1, back):
        for z in range(cols):
            receive(z, step)
            send(z, step + 1)

    def attend(z, carry):
        if back > 0:
            receive(z, back)
        lane = lax.broadcasted_iota(jnp.int32, (1, LANES), 1)
        logs = jnp.zeros((tokens, LANES), f32)
        outs = []
        for head in range(heads):
            pair = head // group
            keyval = kv[z, :, pair * LANES : (pair + 1) * LANES]
            query = head_at(q[z, :, tile_of(head)].astype(f32), head, False) * HD**-0.5
            scores = against(query.astype(bf16), keyval) + bias[...]
            summit = jnp.max(scores, axis=1, keepdims=True)
            weights = jnp.exp(scores - summit)
            total = jnp.sum(weights, axis=1, keepdims=True)
            chances = (weights * (1.0 / total)).astype(bf16)
            outs.append(matmul(chances, keyval))
            logs = jnp.where(lane == head, summit + jnp.log(total), logs)
            if head % 2 == 1:
                mixed[z, :, tile_of(head)] = pair_tile(outs[-2], outs[-1], True).astype(bf16)
        lse[z] = jnp.transpose(logs)[:heads]

        @pl.when(z == 0)
        def _():
            for part in parts[1:]:
                part.second()

        @pl.when(z == max(cols - 2, 1))
        def _():
            for part in parts[:-1]:
                part.third()

        return carry

    lax.fori_loop(0, cols, attend, 0)
    outputs = [
        pltpu.make_async_copy(source, target, o_sems.at[n])
        for n, (source, target) in enumerate(
            ((q, q_out), (kv, kv_out), (mixed, mixed_out), (lse, lse_out))
        )
    ]
    for copy in outputs:
        copy.start()
    hidden[...] = x[...].astype(f32)

    def project_out(z, carry):
        weight_copies(z)[1].wait()
        hidden[...] += against(mixed[z], wo[z])
        return carry

    lax.fori_loop(0, cols, project_out, 0)
    total = hidden[...]
    scale = lax.rsqrt(jnp.mean(total * total, axis=1, keepdims=True) + epsilon)
    hn[...] = (total * scale * gain[...]).astype(bf16)
    if parts:
        parts[-1].third()
    for part in parts:
        part.finish()
    for copy in keeps + outputs:
        copy.wait()
    for step in range(1, back + 1):
        for z in range(cols):
            pl.when(goes(step))(lambda: hop(z, step).wait_send())


def attend(
    xn, x, wf, wo, bias, tables, gain, tiles, count, tile, heads, group, back, sizes, cid
):
    row_count, col_count = sizes
    tokens, width = xn.shape
    query_width = heads * HD
    kv_shape = (col_count, (back + 1) * tokens, heads // group * LANES)
    q_shape = (col_count, tokens, query_width)
    lse_shape = (col_count, heads, tokens)
    vmem = pl.BlockSpec(memory_space=pltpu.VMEM)
    keys = (back + 1) * tokens
    plane_sems = (count, 2, PlaneGather.sem_count(plane_sizes(row_count)))
    return pl.pallas_call(
        functools.partial(attend_kernel, (row_count, col_count), heads, group, back),
        out_shape=[
            jax.ShapeDtypeStruct(q_shape, bf16),
            jax.ShapeDtypeStruct(kv_shape, bf16),
            jax.ShapeDtypeStruct(q_shape, bf16),
            jax.ShapeDtypeStruct(lse_shape, f32),
            jax.ShapeDtypeStruct((count, row_count * tiles.shape[0], 2 * tile), bf16),
            jax.ShapeDtypeStruct((tokens, width), f32),
            jax.ShapeDtypeStruct((tokens, width), bf16),
        ],
        in_specs=[vmem, vmem, ANY, ANY] + [vmem] * 6 + [ANY],
        out_specs=[ANY] * 5 + [vmem] * 2,
        scratch_shapes=[
            pltpu.VMEM(q_shape, bf16),
            pltpu.VMEM(kv_shape, bf16),
            pltpu.VMEM(q_shape, bf16),
            pltpu.VMEM(lse_shape, f32),
            pltpu.VMEM(wf.shape, bf16),
            pltpu.VMEM(wo.shape, bf16),
            pltpu.SemaphoreType.DMA((2, col_count)),
            pltpu.SemaphoreType.DMA((4,)),
            pltpu.SemaphoreType.DMA((max(back, 1), col_count)),
            pltpu.SemaphoreType.DMA((max(back, 1), col_count)),
            pltpu.SemaphoreType.DMA((count,)),
            pltpu.SemaphoreType.DMA(plane_sems),
            pltpu.SemaphoreType.DMA(plane_sems),
            pltpu.VMEM((count, tiles.shape[0], 2 * tile), bf16),
            pltpu.SemaphoreType.DMA((count, 2)),
        ],
        compiler_params=pltpu.CompilerParams(
            collective_id=cid, has_side_effects=True, vmem_limit_bytes=56 << 20
        ),
        cost_estimate=pl.CostEstimate(
            flops=2 * tokens * (wf.size + wo.size) + 4 * col_count * heads * tokens * keys * HD,
            bytes_accessed=(wf.size + wo.size) * 2,
            transcendentals=col_count * heads * tokens * keys,
        ),
        name="attend",
    )(xn, x, wf, wo, bias, *tables, gain, tiles)


def attend_back_kernel(sizes, heads, group, back, chunk, *refs):
    grad_hn, hidden_in, dy, gain, xn, lse, bias, cosq, sinq, coskv, sinkv = refs[:11]
    mixed_in, q_in, kv_in, wo_in, wf_in, terms = refs[11:17]
    dxn, dh, dhb, mid_part = refs[17:21]
    dqkv_out, sum_out, xn_sib, dhb_sib, mixed_sib, dqkv_sib = refs[21:27]
    q, kv, wo, wf, dmix, dkv, dqkv, going, coming, dst, pst, rhs_q, rhs_o = refs[27:40]
    in_sems, wo_sems, wf_sems, out_sems, pair_sems, row_sems, sends, recvs = refs[40:48]
    place = Place(*sizes)
    cols, col = place.cols, place.col
    cores = place.sizes[2]
    tokens = dhb.shape[0]
    query_width = heads * HD
    pairs = heads // group
    hidden = sum_out.shape[2]

    def inner_target(f):
        return sum_out.at[:, :, pl.ds(pl.multiple_of(f * chunk, chunk), chunk)]

    def inner_terms(e, core):
        at = pl.multiple_of(lax.rem(e, 2) * chunk, chunk)
        return terms.at[e // 2, :, core, :, pl.ds(at, chunk)]

    inner = PairSum(place, 2 * hidden // chunk, inner_terms, inner_target, refs[48:])

    in_copies = [
        pltpu.make_async_copy(q_in, q, in_sems.at[0]),
        pltpu.make_async_copy(kv_in, kv, in_sems.at[1]),
    ]

    def wo_copy(z):
        slot = lax.rem(z, 2)
        return pltpu.make_async_copy(wo_in.at[z], wo.at[slot], wo_sems.at[slot])

    def wf_copy(z):
        return pltpu.make_async_copy(wf_in.at[z], wf, wf_sems.at[0])

    wo_copy(0).start()
    for copy in in_copies:
        copy.start()
    wf_copy(0).start()
    place.greet(True, True)

    other = place.device(2, 1)
    chips, deep = terms.shape[1], terms.shape[3]
    exchanges = []
    if cores > 1:
        moves = [(mixed_in, mixed_sib)]
        for source, target in ((xn, xn_sib), (dhb, dhb_sib)):
            for chip in range(chips):
                to, rows = pl.ds(chip * deep, deep), core_rows(place, chip, 1, deep)
                moves.append((source.at[:, rows], target.at[:, to]))
        exchanges = [
            remote(source, target, pair_sems.at[0, n], pair_sems.at[1, n], other)
            for n, (source, target) in enumerate(moves)
        ]

    def row_exchange(z):
        return remote(dqkv.at[z], dqkv_sib.at[z], row_sems.at[0, z], row_sems.at[1, z], other)

    def out_copy(z):
        return pltpu.make_async_copy(dqkv.at[z], dqkv_out.at[z], out_sems.at[z])

    inner.begin()
    for exchange in exchanges[: 1 + chips]:
        exchange.start()
    norm_rows(grad_hn, hidden_in, dy, gain, dh, mid_part)
    dhb[...] = dh[...].astype(bf16)
    for exchange in exchanges[1 + chips :]:
        exchange.start()
    dxn[...] = jnp.zeros_like(dxn)
    for copy in in_copies:
        copy.wait()

    def hop(z, step):
        return remote(
            going.at[step - 1, z],
            coming.at[step - 1, z],
            sends.at[step - 1, z],
            recvs.at[step - 1, z],
            (place.row, col - 1),
        )

    def goes(step):
        return col - back + step - 1 >= 0

    def comes(step):
        return (col < cols - 1) & (col + step - back >= 0)

    def send(z, step):
        pl.when(goes(step))(lambda: hop(z, step).start())

    def chunk_rows(step):
        return slice(step * tokens, (step + 1) * tokens)

    def halo(step, z):
        if step > 0:
            pl.when(comes(step))(lambda: hop(z, step).wait_recv())
            term = jnp.where(comes(step), coming[step - 1, z].astype(f32), 0.0)
            total = dkv[z, chunk_rows(step)] + term
        else:
            total = dkv[z, chunk_rows(step)]
        if step < back:
            going[step, z] = total.astype(bf16)
            send(z, step + 1)
            return
        for n in range(pairs):
            at = slice(n * LANES, (n + 1) * LANES)
            dqkv[z, :, query_width + n * LANES : query_width + (n + 1) * LANES] = rope_lanes(
                total[:, at], coskv[...], sinkv[...]
            ).astype(bf16)
        out_copy(z).start()
        if cores > 1:
            row_exchange(z).start()
        wf_copy(z).wait()
        dxn[...] += against(dqkv[z], wf[...])
        when(z + 1 < cols, lambda: wf_copy(z + 1).start())

    def halos(z):
        for step in range(1, back + 1):
            at = z - step
            when((at >= 0) & (at < cols), lambda: halo(step, at))

    def one_col(z, carry):
        wo_copy(z).wait()
        when(z + 1 < cols, lambda: wo_copy(z + 1).start())
        dmix[...] = matmul(dhb[...], wo[lax.rem(z, 2)]).astype(bf16)
        for n in range(pairs):
            keyval = kv[z, :, n * LANES : (n + 1) * LANES]
            for i in range(group):
                head = n * group + i
                at = slice(i * tokens, (i + 1) * tokens)
                query = head_at(q[z, :, tile_of(head)].astype(f32), head, False) * HD**-0.5
                query = query.astype(bf16)
                grad = head_at(dmix[:, tile_of(head)].astype(f32), head, True).astype(bf16)
                rhs_q[at] = query
                rhs_o[at] = grad
                chances = jnp.exp(against(keyval, query) + bias[...] - lse[z, head : head + 1])
                grad_chance = against(keyval, grad)
                centre = jnp.sum(chances * grad_chance, axis=0, keepdims=True)
                dst[:, at] = (chances * (grad_chance - centre)).astype(bf16)
                pst[:, at] = chances.astype(bf16)
            dkv[z, :, n * LANES : (n + 1) * LANES] = matmul(dst[...], rhs_q[...]) + matmul(
                pst[...], rhs_o[...]
            )
            grad_rows = dot_tokens(keyval, dst[...])
            for i in range(0, group, 2):
                tile = jnp.concatenate(
                    [
                        grad_rows[:HD, i * tokens : (i + 1) * tokens],
                        grad_rows[:HD, (i + 1) * tokens : (i + 2) * tokens],
                    ],
                    axis=0,
                )
                turned = rope_lanes(jnp.transpose(tile), cosq[...], sinq[...]) * HD**-0.5
                dqkv[z, :, tile_of(n * group + i)] = turned.astype(bf16)
            inner.tick(z * pairs + n)
        halo(0, z)
        halos(z)
        return carry

    lax.fori_loop(0, cols, one_col, 0)
    ticks = list(range(cols * pairs, inner.count + 2 * LAG))
    for z in range(cols, cols + back):
        if ticks:
            inner.tick(ticks.pop(0))
        halos(z)
    for t in ticks:
        inner.tick(t)
    for z in range(cols):
        out_copy(z).wait()
        if cores > 1:
            row_exchange(z).wait_send()
            row_exchange(z).wait_recv()
    for exchange in exchanges:
        exchange.wait_send()
        exchange.wait_recv()
    for step in range(1, back + 1):
        for z in range(cols):
            pl.when(goes(step))(lambda: hop(z, step).wait_send())
    inner.finish()


def attend_back(
    mid, xn, lse, bias, tables, mixed, q, kv, wo, wf, terms, group, sizes, cid
):
    row_count, col_count = sizes
    plane = plane_sizes(row_count)
    chips = plane[0] * plane[1]
    tokens, width = xn.shape
    heads = lse.shape[1]
    back = kv.shape[1] // tokens - 1
    pairs = heads // group
    keys = kv.shape[1]
    all_width = wf.shape[2]
    tiles, _, chunk = terms.shape
    chunk = chunk // 2
    inner_width = 2 * tiles * chunk
    deep = terms.shape[1] // row_count
    row_shape = (col_count, tokens, all_width)
    halo_shape = (max(back, 1), col_count, tokens, kv.shape[2])
    vmem = pl.BlockSpec(memory_space=pltpu.VMEM)
    return pl.pallas_call(
        functools.partial(attend_back_kernel, sizes, heads, group, back, chunk),
        out_shape=[
            jax.ShapeDtypeStruct((tokens, width), f32),
            jax.ShapeDtypeStruct((tokens, width), f32),
            jax.ShapeDtypeStruct((tokens, width), bf16),
            jax.ShapeDtypeStruct((1, width), f32),
            jax.ShapeDtypeStruct(row_shape, bf16),
            jax.ShapeDtypeStruct((deep, 2, tiles * chunk), f32),
            jax.ShapeDtypeStruct((tokens, chips * deep), bf16),
            jax.ShapeDtypeStruct((tokens, chips * deep), bf16),
            jax.ShapeDtypeStruct(mixed.shape, bf16),
            jax.ShapeDtypeStruct(row_shape, bf16),
        ],
        in_specs=[vmem] * 11 + [ANY] * 6,
        out_specs=[vmem] * 4 + [ANY] * 6,
        scratch_shapes=[
            pltpu.VMEM(q.shape, bf16),
            pltpu.VMEM(kv.shape, bf16),
            pltpu.VMEM((2,) + wo.shape[1:], bf16),
            pltpu.VMEM(wf.shape[1:], bf16),
            pltpu.VMEM((tokens, heads * HD), bf16),
            pltpu.VMEM(kv.shape, f32),
            pltpu.VMEM(row_shape, bf16),
            pltpu.VMEM(halo_shape, bf16),
            pltpu.VMEM(halo_shape, bf16),
            pltpu.VMEM((keys, group * tokens), bf16),
            pltpu.VMEM((keys, group * tokens), bf16),
            pltpu.VMEM((group * tokens, LANES), bf16),
            pltpu.VMEM((group * tokens, LANES), bf16),
            pltpu.SemaphoreType.DMA((2,)),
            pltpu.SemaphoreType.DMA((2,)),
            pltpu.SemaphoreType.DMA((2,)),
            pltpu.SemaphoreType.DMA((col_count,)),
            pltpu.SemaphoreType.DMA((2, 1 + 2 * chips)),
            pltpu.SemaphoreType.DMA((2, col_count)),
            pltpu.SemaphoreType.DMA((max(back, 1), col_count)),
            pltpu.SemaphoreType.DMA((max(back, 1), col_count)),
        ]
        + InnerSum.scratch(plane, deep, inner_width, chunk, (1, deep, 2, chunk)),
        compiler_params=pltpu.CompilerParams(
            collective_id=cid, has_side_effects=True, vmem_limit_bytes=62 << 20
        ),
        cost_estimate=pl.CostEstimate(
            flops=2 * tokens * (wf.size + wo.size) + 10 * col_count * heads * tokens * keys * HD,
            bytes_accessed=(wf.size + wo.size + terms.size) * 2,
            transcendentals=col_count * heads * tokens * keys,
        ),
        name="attend_back",
    )(
        *mid,
        xn,
        lse,
        bias,
        *tables,
        mixed,
        q,
        kv,
        wo,
        wf,
        terms.reshape(tiles, chips, plane[2], deep, 2 * chunk),
    )


def rope_tables(position):
    indices = jnp.arange(HD // 2, dtype=f32)
    frequency = rope_base ** (-(indices * 2.0 / HD))
    wavelen = 2.0 * jnp.pi / frequency
    smooth = (8192.0 / wavelen - 1.0) / 3.0
    scaled = jnp.where(
        wavelen > 8192.0, frequency / 32.0, (1.0 - smooth) * frequency / 32.0 + smooth * frequency
    )
    frequency = jnp.where(wavelen < 2048.0, frequency, scaled)
    angles = position.astype(f32)[:, None] * frequency[None, :]
    return (jnp.cos(angles), jnp.sin(angles))


def rotate(values, cosine, sinusoid):
    halfway = values.shape[-1] // 2
    former = values[..., :halfway]
    latter = values[..., halfway:]
    cos_wide = cosine[:, None, :]
    sin_wide = sinusoid[:, None, :]
    return jnp.concatenate(
        [former * cos_wide - latter * sin_wide, latter * cos_wide + former * sin_wide], axis=-1
    )


def normalize(values, gain):
    scale = lax.rsqrt(jnp.mean(values * values, axis=1, keepdims=True) + epsilon)
    return ((values * scale * gain).astype(bf16), scale)


def against(left, right):
    return lax.dot_general(left, right, (((1,), (1,)), ((), ())), preferred_element_type=f32)


def over_rows(left, right):
    return lax.dot_general(left, right, (((0,), (0,)), ((), ())), preferred_element_type=f32)


def matmul(left, right):
    return jnp.dot(left, right, preferred_element_type=f32)


def shift(values, step, col_count):
    if step > 0:
        pairs = [(i, i + step) for i in range(col_count - step)]
    else:
        pairs = [(i, i + step) for i in range(-step, col_count)]
    return lax.ppermute(values, "col", pairs)


def shards(
    tokens,
    seq_lens,
    attn_gain,
    query_weight,
    keyvalue_weight,
    output_weight,
    mlp_gain,
    hidden_weight,
    down_weight,
    out_grad,
):
    row_count, col_count = lax.axis_size("row"), lax.axis_size("col")
    local = tokens.shape[0]
    block_rows = local * col_count
    col = lax.axis_index("col")
    deep = query_weight.shape[0]
    width = tokens.shape[1]
    query_width = query_weight.shape[1]
    pairs = keyvalue_weight.shape[1]
    heads = query_width // HD
    group = heads // pairs
    hidden = down_weight.shape[1]
    back = min(-(-(SEQ_MAX - 1) // local), col_count - 1)

    lengths = seq_lens[0]
    finish = jnp.cumsum(lengths)
    indices = jnp.arange(block_rows, dtype=jnp.int32)
    passed = indices[:, None] >= finish[None, :]
    segment = jnp.sum(passed.astype(jnp.int32), axis=1, dtype=jnp.int32)
    position = indices - jnp.sum(jnp.where(passed, lengths[None, :], 0), axis=1, dtype=jnp.int32)
    own_position = lax.dynamic_slice(position, (col * local,), (local,))
    own_segment = lax.dynamic_slice(segment, (col * local,), (local,))
    padded = jnp.concatenate([jnp.full((back * local,), -1, jnp.int32), segment])
    key_segment = lax.dynamic_slice(padded, (col * local,), ((back + 1) * local,))
    key_index = jnp.arange((back + 1) * local, dtype=jnp.int32) - back * local
    query_index = jnp.arange(local, dtype=jnp.int32)
    allowed = (own_segment[:, None] == key_segment[None, :]) & (
        key_index[None, :] <= query_index[:, None]
    )
    cosine, sinusoid = rope_tables(own_position)
    gain_first = attn_gain.astype(f32)
    gain_second = mlp_gain.astype(f32)

    first_weight = jnp.concatenate(
        [query_weight, keyvalue_weight.reshape(deep, pairs * 2 * HD)], axis=1
    )
    full_first, full_output, full_down, rows_grad = gather_all(
        [first_weight, output_weight], [down_weight], out_grad, row_count, col_count
    )

    tile = min(512, hidden)
    tiles = hidden // tile
    early = max(tiles // 2, 1)
    hidden_flat = hidden_weight.reshape(deep, 2 * hidden)

    inputs = tokens.astype(f32)
    normal_in, scale_in = normalize(inputs, gain_first)
    halves = jnp.concatenate([cosine, cosine], axis=1)
    signed = jnp.concatenate([-sinusoid, sinusoid], axis=1)
    tables = (
        jnp.concatenate([halves, halves], axis=1),
        jnp.concatenate([signed, signed], axis=1),
        jnp.concatenate([halves, jnp.ones_like(halves)], axis=1),
        jnp.concatenate([signed, jnp.zeros_like(signed)], axis=1),
    )
    bias = jnp.where(allowed, 0.0, blocked).astype(f32)
    queries, all_keyvals, mixed, lse, early_tiles, hidden_in, normal_mid = attend(
        normal_in,
        tokens,
        full_first,
        full_output,
        bias,
        tables,
        gain_second[None],
        hidden_flat,
        early,
        tile,
        heads,
        group,
        back,
        (row_count, col_count),
        4,
    )
    grad_mid, out_terms, grad_hidden_part, sum_down = mlp(
        normal_mid,
        rows_grad,
        early_tiles,
        hidden_flat,
        full_down,
        row_count,
        col_count,
        3,
    )
    out_sum = lax.psum_scatter(out_terms, "col", scatter_dimension=0, tiled=True)
    cores = plane_sizes(row_count)[2]
    tables_back = (tables[0], -tables[1], tables[2], -tables[3])
    grad_in, grad_hidden_in, grad_low, gain_mid_part, grad_first, sum_hidden, *siblings = (
        attend_back(
            (grad_mid, hidden_in, out_grad, gain_second[None]),
            normal_in,
            lse,
            bias.T,
            tables_back,
            mixed,
            queries,
            all_keyvals,
            full_output,
            full_first,
            grad_hidden_part,
            group,
            (row_count, col_count),
            5,
        )
    )
    normal_sib, grad_low_sib, mixed_sib, grad_first_sib = siblings
    lefts = [
        (normal_in, normal_sib)[:cores],
        (grad_low, grad_low_sib)[:cores],
    ]
    rights = [(grad_first, grad_first_sib)[:cores], (mixed, mixed_sib)[:cores]]
    extras = (
        grad_in,
        tokens,
        grad_hidden_in,
        gain_first[None],
        gain_mid_part,
    )
    sum_query, sum_keyvalue, sum_output, grad_tokens, gain_sums = sum_all(
        lefts, rights, query_width, extras, row_count, col_count
    )
    out_sum, gain_sums = lax.optimization_barrier((out_sum, gain_sums))
    block_out = (hidden_in + out_sum.astype(f32)).astype(bf16)
    return (
        block_out,
        grad_tokens,
        gain_sums[0],
        sum_query,
        sum_keyvalue.reshape(deep, pairs, 2 * HD),
        sum_output,
        gain_sums[1],
        sum_hidden,
        sum_down,
    )


def solution(mesh):
    return jax.shard_map(
        shards,
        mesh=mesh,
        in_specs=(
            P(("row", "col"), None),
            P("row", None),
            P(),
            P("row", "col"),
            P("row", "col", None),
            P("row", "col"),
            P(),
            P("row", None, "col"),
            P("row", "col"),
            P(("row", "col"), None),
        ),
        out_specs=(
            P(("row", "col"), None),
            P(("row", "col"), None),
            P(),
            P("row", "col"),
            P("row", "col", None),
            P("row", "col"),
            P(),
            P("row", None, "col"),
            P("row", "col"),
        ),
        check_vma=False,
    )
```

```python
import functools

import jax
import jax.numpy as jnp
from jax import lax
from jax.experimental import pallas as pl
from jax.experimental.pallas import tpu as pltpu
from jax.sharding import PartitionSpec as P

HD = 64
SEQ_MAX = 512
MESH = pl.DeviceIdType.MESH
LAG = 2
ANY = pl.BlockSpec(memory_space=pl.ANY)

epsilon = 1e-05
rope_base = 500000.0
blocked = -1e30
bf16 = jnp.bfloat16
f32 = jnp.float32


def plane_sizes(row_count):
    cores = 2 if row_count % 2 == 0 else 1
    chips = row_count // cores
    first = 2 if chips % 2 == 0 else 1
    return first, chips // first, cores


class Place:
    def __init__(self, row_count, col_count):
        self.rows, self.cols = row_count, col_count
        self.sizes = plane_sizes(row_count)
        na, nb, nk = self.sizes
        self.row = lax.axis_index("row")
        self.col = lax.axis_index("col")
        self.at = (self.row // (nb * nk), (self.row // nk) % nb, self.row % nk)

    def row_of(self, at):
        _, nb, nk = self.sizes
        return (at[0] * nb + at[1]) * nk + at[2]

    def chip_of(self, at):
        return at[0] * self.sizes[1] + at[1]

    def moved(self, axis, step, at=None):
        at = list(self.at if at is None else at)
        size = self.sizes[axis]
        at[axis] = lax.rem(at[axis] + (step % size), size)
        return tuple(at)

    def device(self, axis, step):
        return (self.row_of(self.moved(axis, step)), self.col)

    def greet(self, plane, line):
        barrier = pltpu.get_barrier_semaphore()
        count = 0
        if plane:
            for axis in range(3):
                size = self.sizes[axis]
                for step in {1 % size, (size - 1) % size} - {0}:
                    pl.semaphore_signal(
                        barrier, inc=1, device_id=self.device(axis, step), device_id_type=MESH
                    )
                    count += 1
        if line and self.cols > 1:
            for step, there in self.line_ways():

                @pl.when(there)
                def _(step=step):
                    pl.semaphore_signal(
                        barrier, inc=1, device_id=(self.row, self.col + step), device_id_type=MESH
                    )

        if line and self.cols > 1:
            last = self.cols - 1
            count = count + jnp.minimum(self.col, 1) + jnp.minimum(last - self.col, 1)
        if not isinstance(count, int) or count:
            pl.semaphore_wait(barrier, count)

    def line_ways(self):
        return ((1, self.col < self.cols - 1), (-1, self.col > 0))


def when(condition, action):
    if condition is None or condition is True:
        action()
    elif condition is False:
        pass
    else:
        pl.when(condition)(action)


def remote(src, dst, send_sem, recv_sem, device):
    return pltpu.make_async_remote_copy(
        src_ref=src,
        dst_ref=dst,
        send_sem=send_sem,
        recv_sem=recv_sem,
        device_id=device,
        device_id_type=MESH,
    )


class LineGather:
    def __init__(self, place, own, block, send_sems, recv_sems):
        self.place, self.own, self.block = place, own, block
        self.sends, self.recvs = send_sems, recv_sems

    def copy(self, way, step, origin):
        place = self.place
        source = self.own if step == 1 else self.block(origin)
        return remote(
            source,
            self.block(origin),
            self.sends.at[way, step - 1],
            self.recvs.at[way, step - 1],
            (place.row, place.col + (1, -1)[way]),
        )

    def sends_at(self, way, step):
        col, last = self.place.col, self.place.cols - 1
        if way == 0:
            return (col >= step - 1) & (col < last), col - (step - 1)
        return (col + step - 1 <= last) & (col > 0), col + (step - 1)

    def gets_at(self, way, step):
        col, last = self.place.col, self.place.cols - 1
        if way == 0:
            return col >= step, col - step
        return col + step <= last, col + step

    def send(self, way, step):
        condition, origin = self.sends_at(way, step)
        when(condition, lambda: self.copy(way, step, origin).start())

    def receive(self, way, step):
        condition, origin = self.gets_at(way, step)

        def action():
            self.copy(way, step, origin).wait_recv()

        when(condition, action)
        if step < self.place.cols - 1:
            self.send(way, step + 1)

    def finish(self):
        for step in range(1, self.place.cols):
            for way in (0, 1):
                condition, origin = self.sends_at(way, step)
                when(condition, lambda: self.copy(way, step, origin).wait_send())


class PlaneGather:
    def __init__(self, place, block, own, send_sems, recv_sems):
        self.place, self.block, self.own = place, block, own
        self.sends, self.recvs = send_sems, recv_sems

    @staticmethod
    def sem_count(sizes):
        na, nb, _ = sizes
        return 2 * na * nb - 1

    def axes(self, half):
        return (1, 0) if half == 0 else (0, 1)

    def counts(self, half):
        first, second = self.axes(half)
        return self.place.sizes[first], self.place.sizes[second]

    def origin(self, half, i, j, core_step=0):
        first, second = self.axes(half)
        at = self.place.moved(first, -i)
        at = self.place.moved(second, -j, at)
        if core_step:
            at = self.place.moved(2, 1, at)
        return self.place.row_of(at)

    def copy(self, half, kind, i, j):
        np_, nq = self.counts(half)
        if kind == 0:
            number, device = i - 1, self.place.device(self.axes(half)[0], 1)
        elif kind == 1:
            number = (np_ - 1) + i * (nq - 1) + (j - 1)
            device = self.place.device(self.axes(half)[1], 1)
        else:
            number = (np_ * nq - 1) + i * nq + j
            device = self.place.device(2, 1)
        return number, device

    def sender(self, half, kind, i, j):
        number, device = self.copy(half, kind, i, j)
        oi, oj = (i - 1, j) if kind == 0 else ((i, j - 1) if kind == 1 else (i, j))
        ref = self.block(self.origin(half, oi, oj), half)
        source = self.own(half) if (oi, oj) == (0, 0) else ref
        return remote(source, ref, self.sends.at[half, number], self.recvs.at[half, number], device)

    def receiver(self, half, kind, i, j):
        number, device = self.copy(half, kind, i, j)
        ref = self.block(self.origin(half, i, j, 1 if kind == 2 else 0), half)
        return remote(ref, ref, self.sends.at[half, number], self.recvs.at[half, number], device)

    def all_copies(self):
        for half in (0, 1):
            np_, nq = self.counts(half)
            for i in range(1, np_):
                yield half, 0, i, 0
            for i in range(np_):
                for j in range(1, nq):
                    yield half, 1, i, j
            if self.place.sizes[2] > 1:
                for i in range(np_):
                    for j in range(nq):
                        yield half, 2, i, j

    def share(self, half, i, j):
        if self.place.sizes[2] > 1:
            self.sender(half, 2, i, j).start()

    def first(self):
        for half in (0, 1):
            if self.counts(half)[0] > 1:
                self.sender(half, 0, 1, 0).start()
        for half in (0, 1):
            self.share(half, 0, 0)

    def second(self):
        for half in (0, 1):
            np_, nq = self.counts(half)
            for i in range(np_):
                if i > 0:
                    self.receiver(half, 0, i, 0).wait_recv()
                    if i < np_ - 1:
                        self.sender(half, 0, i + 1, 0).start()
                if nq > 1:
                    self.sender(half, 1, i, 1).start()
                if i > 0:
                    self.share(half, i, 0)

    def third(self):
        for half in (0, 1):
            np_, nq = self.counts(half)
            for j in range(1, nq):
                for i in range(np_):
                    self.receiver(half, 1, i, j).wait_recv()
                    if j < nq - 1:
                        self.sender(half, 1, i, j + 1).start()
                    self.share(half, i, j)

    def shared(self):
        for copy in self.all_copies():
            if copy[1] == 2:
                self.receiver(*copy).wait_recv()

    def sent(self):
        for copy in self.all_copies():
            self.sender(*copy).wait_send()

    def finish(self):
        self.shared()
        self.sent()


def tile_gather(place, full, own, send_sems, recv_sems):
    deep = full.shape[0] // place.rows
    half = deep // 2

    def block(row, number):
        return full.at[pl.ds(row * deep + number * half, half)]

    def mine(number):
        if own is None:
            return block(place.row, number)
        return own.at[pl.ds(number * half, half)]

    return PlaneGather(place, block, mine, send_sems, recv_sems)


def nearby(place, number):
    low, high = place.col, place.cols - 1 - place.col
    both = jnp.minimum(low, high)
    way = jnp.minimum(jnp.maximum(high - low, -1), 1)
    step = (number + 1) // 2 * (-1 if number % 2 else 1)
    paired = jnp.minimum(jnp.maximum(2 * both - number + 1, 0), 1)
    return place.col + paired * step + (1 - paired) * way * (number - both)


def gather_kernel(sizes, count, inner, *refs):
    row_count, col_count = sizes
    every = count + inner
    splits = min(2, col_count)
    own, own_act = refs[:every], refs[every]
    full, full_act = refs[every + 1 : 2 * every + 1], refs[2 * every + 1]
    local_sems, zs, zr, ps, pr = refs[2 * every + 2 :]
    place = Place(row_count, col_count)
    place.greet(True, True)
    token_rows = own_act.shape[0]

    def at(n, col, row):
        deep = own[n].shape[0]
        if n < count:
            return full[n].at[col, pl.ds(row * deep, deep)]
        return full[n].at[pl.ds(row * deep, deep)]

    lines = [
        LineGather(place, own[n], lambda j, n=n: at(n, j, place.row), zs.at[n], zr.at[n])
        for n in range(count)
    ]
    acts = LineGather(
        place,
        own_act,
        lambda j: full_act.at[pl.ds(j * token_rows, token_rows)],
        zs.at[count],
        zr.at[count],
    )

    def keep(n):
        if n == every:
            return pltpu.make_async_copy(own_act, acts.block(place.col), local_sems.at[n])
        return pltpu.make_async_copy(own[n], at(n, place.col, place.row), local_sems.at[n])

    for n in range(every + 1):
        keep(n).start()
    for line in lines:
        for way in (0, 1):
            line.send(way, 1)

    def inside(n, col, near):
        deep = own[n].shape[0]
        half = deep // 2
        wide = own[n].shape[1] // splits
        columns = pl.ds(col * wide, wide) if n >= count else slice(None)

        def block(row, number):
            rows = pl.ds(row * deep + number * half, half)
            return full[n].at[col, rows] if n < count else full[n].at[rows, columns]

        def mine(number):
            rows = pl.ds(number * half, half)
            return own[n].at[rows, columns] if near else block(place.row, number)

        return PlaneGather(place, block, mine, ps.at[n, col], pr.at[n, col])

    entries = [(n, k) for k in range(col_count) for n in range(count)]
    parts = [inside(n, nearby(place, k), k == 0) for n, k in entries]
    entries += [(n, 0) for n in range(count, every) for _ in range(splits)]
    parts += [inside(n, part, True) for n in range(count, every) for part in range(splits)]
    act_steps = list(range(1, col_count))

    def act_step():
        if act_steps:
            for way in (0, 1):
                acts.receive(way, act_steps[0])
            act_steps.pop(0)

    for number in range(len(parts) + 2):
        if number < len(parts):
            n, k = entries[number]
            if n == 0 and k > 0:
                for line in lines:
                    for way in (0, 1):
                        line.receive(way, k)
                if k == 1:
                    for way in (0, 1):
                        acts.send(way, 1)
                if k >= 3:
                    act_step()
            parts[number].first()
        if 1 <= number <= len(parts):
            parts[number - 1].second()
        if 2 <= number:
            parts[number - 2].third()
        if number >= len(parts):
            act_step()
    while act_steps:
        act_step()
    for n in range(every + 1):
        keep(n).wait()
    for part in parts:
        part.finish()
    for line in lines + [acts]:
        line.finish()


def gather_all(weights, inner_weights, act, row_count, col_count):
    count, inner = len(weights), len(inner_weights)
    sizes = plane_sizes(row_count)
    steps = max(col_count - 1, 1)
    every = list(weights) + list(inner_weights)
    plane_sems = (count + inner, col_count, 2, PlaneGather.sem_count(sizes))
    moved = sum(w.size for w in weights) * row_count * col_count * 2
    return pl.pallas_call(
        functools.partial(gather_kernel, (row_count, col_count), count, inner),
        out_shape=[
            jax.ShapeDtypeStruct((col_count, row_count * w.shape[0], w.shape[1]), bf16)
            for w in weights
        ]
        + [
            jax.ShapeDtypeStruct((row_count * w.shape[0], w.shape[1]), bf16) for w in inner_weights
        ]
        + [jax.ShapeDtypeStruct((col_count * act.shape[0], act.shape[1]), bf16)],
        in_specs=[pl.BlockSpec(memory_space=pltpu.VMEM)] * (len(every) + 1),
        out_specs=[ANY] * (len(every) + 1),
        scratch_shapes=[
            pltpu.SemaphoreType.DMA((len(every) + 1,)),
            pltpu.SemaphoreType.DMA((count + 1, 2, steps)),
            pltpu.SemaphoreType.DMA((count + 1, 2, steps)),
            pltpu.SemaphoreType.DMA(plane_sems),
            pltpu.SemaphoreType.DMA(plane_sems),
        ],
        compiler_params=pltpu.CompilerParams(collective_id=0, has_side_effects=True),
        cost_estimate=pl.CostEstimate(flops=0, bytes_accessed=moved, transcendentals=0),
        name="gather_weights",
    )(*every, act)


def line_gather_kernel(sizes, own, full, local_sem, sends, recvs):
    place = Place(*sizes)
    place.greet(False, True)
    rows = own.shape[0]
    line = LineGather(place, own, lambda j: full.at[pl.ds(j * rows, rows)], sends, recvs)
    for way in (0, 1):
        line.send(way, 1)
    keep = pltpu.make_async_copy(own, full.at[pl.ds(place.col * rows, rows)], local_sem)
    keep.start()
    for step in range(1, place.cols):
        for way in (0, 1):
            line.receive(way, step)
    keep.wait()
    line.finish()


def line_gather(own, row_count, col_count, collective_id):
    steps = max(col_count - 1, 1)
    return pl.pallas_call(
        functools.partial(line_gather_kernel, (row_count, col_count)),
        out_shape=jax.ShapeDtypeStruct((col_count * own.shape[0], own.shape[1]), own.dtype),
        in_specs=[pl.BlockSpec(memory_space=pltpu.VMEM)],
        out_specs=ANY,
        scratch_shapes=[
            pltpu.SemaphoreType.DMA,
            pltpu.SemaphoreType.DMA((2, steps)),
            pltpu.SemaphoreType.DMA((2, steps)),
        ],
        compiler_params=pltpu.CompilerParams(collective_id=collective_id, has_side_effects=True),
        cost_estimate=pl.CostEstimate(
            flops=0, bytes_accessed=own.size * 2 * col_count, transcendentals=0
        ),
        name="gather_line",
    )(own)


def add_rows(target, source):
    rows = target.shape[0]
    piece = 32 if rows % 32 == 0 else 16

    def body(n, carry):
        at = pl.ds(pl.multiple_of(n * piece, piece), piece)
        target[at] = (target[at].astype(f32) + source[at].astype(f32)).astype(target.dtype)
        return carry

    lax.fori_loop(0, rows // piece, body, 0)


class LineSum:
    def __init__(self, place, own, held, send_sems, recv_sems):
        self.place, self.own, self.held = place, own, held
        self.sends, self.recvs = send_sems, recv_sems

    def distance(self, way, col):
        return col - self.place.col if way == 0 else self.place.col - col

    def feeds(self, way):
        return self.place.col > 0 if way == 0 else self.place.col < self.place.cols - 1

    def copy(self, way, distance, source):
        return remote(
            source,
            self.held.at[way, distance - 1],
            self.sends.at[way, distance - 1],
            self.recvs.at[way, distance - 1],
            (self.place.row, self.place.col + (1, -1)[way]),
        )

    def arrived(self, way, distance):
        ref = self.held.at[way, distance]
        return remote(
            ref,
            ref,
            self.sends.at[way, distance],
            self.recvs.at[way, distance],
            (self.place.row, self.place.col + (1, -1)[way]),
        )

    def early(self, col, allowed):
        for way in (0, 1):
            far = self.distance(way, col)

            @pl.when(allowed & (far > 0) & jnp.logical_not(self.feeds(way)))
            def _():
                self.copy(way, far, self.own(col)).start()

    def late(self, col, allowed):
        for way in (0, 1):
            far = self.distance(way, col)

            @pl.when(allowed & (far > 0) & self.feeds(way))
            def _():
                self.arrived(way, far).wait_recv()
                add_rows(self.own(col), self.held.at[way, far])
                self.copy(way, far, self.own(col)).start()

    def last(self, out):
        if self.place.cols > 1:
            for way in (0, 1):
                when(self.feeds(way), lambda: self.arrived(way, 0).wait_recv())
        own = self.own(self.place.col)
        rows = own.shape[0]
        piece = 32 if rows % 32 == 0 else 16
        has = [self.feeds(way) for way in (0, 1)]

        def body(n, carry):
            at = pl.ds(pl.multiple_of(n * piece, piece), piece)
            total = own[at].astype(f32)
            if self.place.cols > 1:
                for way in (0, 1):
                    term = self.held[way, 0, at].astype(f32)
                    total = total + jnp.where(has[way], term, 0.0)
            out[at] = total.astype(out.dtype)
            return carry

        lax.fori_loop(0, rows // piece, body, 0)

    def finish(self):
        for distance in range(1, self.place.cols):
            for way in (0, 1):
                col = self.place.col + (distance if way == 0 else -distance)
                there = col < self.place.cols if way == 0 else col >= 0
                when(there, lambda: self.copy(way, distance, self.own(col)).wait_send())


def dot_tokens(left, right):
    return lax.dot_general(left, right, (((0,), (0,)), ((), ())), preferred_element_type=f32)


def plan_units(cols, tiles, early, hop_us, tile_us, unit_us):
    begin = 4.0
    chunk_at = [0.0] + [begin + hop_us * k for k in range(1, cols)]
    tile_at = [0.0] * early + [begin + 2.0 + tile_us * (n + 1) for n in range(tiles - early)]
    events = [(chunk_at[k], ("chunk", k)) for k in range(1, cols)]
    for f in range(early, tiles):
        second_at = begin + 1.0 + 0.35 * tile_us * (f - early + 1)
        events.append((second_at, ("second", f)))
        events.append((tile_at[f], ("third", f)))
    events.sort(key=lambda event: event[0])
    units = [(max(chunk_at[k], tile_at[f]), k, f) for k in range(cols) for f in range(tiles)]
    units.sort()
    plan, now, after = [], 0.0, []
    while units or events or after:
        while events and events[0][0] <= now:
            plan.append(events.pop(0)[1])
        if after and (not units or units[0][0] > now):
            step, cost = after.pop(0)
            plan.append(step)
            now += cost
            continue
        if units and units[0][0] <= now:
            _, k, f = units.pop(0)
            plan.append(("unit", k, f))
            now += unit_us
            if not any(unit[1] == k for unit in units):
                if k > 0:
                    after.append((("grad", k), 2.6 * unit_us))
                after.append((("y", k), 1.3 * unit_us))
                after.sort(key=lambda item: -item[0][1] if item[0][0] == "grad" else 1)
            continue
        now = min([events[0][0]] * bool(events) + [units[0][0]] * bool(units))
    return plan


def mlp_kernel(sizes, early, wide, *refs):
    hn_own, dy_in, wh_in, wh_own, wd_in = refs[:5]
    grad_out, y_out, dwh_out, down_out = refs[5:9]
    hn, dy, wh, wd, act, dgu, terms, staged, held, grad_staged, down_staged = refs[9:20]
    token_sems, tile_sems, wd_sems, y_sem, dw_sems, sends, recvs = refs[20:27]
    hs, hr, ps, pr, own_sem, grad_sems = refs[27:33]
    first_held, inner_sems = refs[33], refs[34:]
    place = Place(*sizes)
    cols = place.cols
    width, hidden = wd.shape
    tiles = wh.shape[0]
    tile = hidden // tiles
    wides = width // wide
    tokens = hn.shape[1]
    deep = wh_own.shape[0]

    def wide_at(n):
        return pl.ds(pl.multiple_of(n * wide, wide), wide)

    def piece(n):
        return LineSum(
            place, lambda j: terms.at[j, :, wide_at(n)], held.at[n], sends.at[n], recvs.at[n]
        )

    near = [nearby(place, k) for k in range(cols)]

    def dy_copy(j):
        return pltpu.make_async_copy(dy_in.at[j], dy.at[j], token_sems.at[j])

    def wd_copy(f):
        at = slice(f * tile, (f + 1) * tile)
        return pltpu.make_async_copy(wd_in.at[:, at], wd.at[:, at], wd_sems.at[f])

    def tile_copies(f):
        if f < early:
            return [pltpu.make_async_copy(wh_in.at[f], wh.at[f], tile_sems.at[f, 0])]
        rows = pl.ds(place.row * deep, deep)
        return [
            pltpu.make_async_copy(
                wh_own.at[:, pl.ds(number * hidden + f * tile, tile)],
                wh.at[f, rows, pl.ds(number * tile, tile)],
                tile_sems.at[f, number],
            )
            for number in (0, 1)
        ]

    own_copy = pltpu.make_async_copy(hn_own, hn.at[place.col], own_sem)
    own_copy.start()
    for f in range(early, tiles):
        for copy in tile_copies(f):
            copy.start()
    place.greet(True, True)
    own_copy.wait()
    line = LineGather(place, hn.at[place.col], lambda j: hn.at[j], hs, hr)
    for way in (0, 1):
        line.send(way, 1)
    parts = {
        f: tile_gather(place, wh.at[f], None, ps.at[f - early], pr.at[f - early])
        for f in range(early, tiles)
    }
    for f in range(early, tiles):
        for copy in tile_copies(f):
            copy.wait()
        parts[f].first()
    dy_copy(near[0]).start()
    for f in range(tiles):
        if f < early:
            tile_copies(f)[0].start()
        wd_copy(f).start()
    for k in range(1, cols):
        dy_copy(near[k]).start()

    def out_copy(j):
        return pltpu.make_async_copy(staged, y_out.at[j], y_sem)

    def unit(k, f):
        j = near[k]
        at = slice(f * tile, (f + 1) * tile)
        gate_up = matmul(hn[j], wh[f])
        gate, up = gate_up[:, :tile], gate_up[:, tile:]
        back = matmul(dy[j], wd[:, at])
        sigmoid = jax.nn.sigmoid(gate)
        silu = gate * sigmoid
        act[j, :, at] = (silu * up).astype(bf16)
        dgate = back * up * sigmoid * (1.0 + gate * (1.0 - sigmoid))
        dgu[j, :, 2 * f * tile : (2 * f + 1) * tile] = dgate.astype(bf16)
        dgu[j, :, (2 * f + 1) * tile : (2 * f + 2) * tile] = (back * silu).astype(bf16)

    def grad(k):
        j = near[k]

        def body(n, carry):
            at = wide_at(n)
            total = 0.0
            for f in range(tiles):
                total += against(dgu[j, :, 2 * f * tile : 2 * (f + 1) * tile], wh[f, at])
            terms[j, :, at] = total.astype(bf16)
            piece(n).early(j, True)
            return carry

        lax.fori_loop(0, wides, body, 0)

    stored = []

    def y_part(k):
        j = near[k]
        if stored:
            out_copy(near[stored[-1]]).wait()

        def body(n, carry):
            at = wide_at(n)
            staged[:, at] = against(act[j], wd[at]).astype(bf16)
            return carry

        lax.fori_loop(0, wides, body, 0)
        out_copy(j).start()
        stored.append(k)

    def late(number):
        low, high = place.col, cols - 1 - place.col
        up_first = jnp.minimum(jnp.maximum(high - low, 0), 1)
        side = up_first * high + (1 - up_first) * low
        way = 2 * up_first - 1
        first = jnp.minimum(jnp.maximum(side - number, 0), 1)
        col = place.col + first * way * (number + 1) - (1 - first) * way * (number + 1 - side)
        return col

    calls = [(number, n) for number in range(cols - 1) for n in range(wides)]

    def do_late(call):
        number, n = call
        piece(n).late(late(number), True)

    def next_late():
        if calls:
            do_late(calls.pop(0))

    seen_tiles, seen_chunks = set(), set()
    for step in plan_units(cols, tiles, early, 24.0, 18.0, 2.1):
        if step[0] == "chunk":
            for way in (0, 1):
                line.receive(way, step[1])
        elif step[0] == "second":
            parts[step[1]].second()
        elif step[0] == "third":
            parts[step[1]].third()
            parts[step[1]].shared()
        elif step[0] == "unit":
            _, k, f = step
            if f not in seen_tiles:
                seen_tiles.add(f)
                if f < early:
                    tile_copies(f)[0].wait()
                wd_copy(f).wait()
            if k not in seen_chunks:
                seen_chunks.add(k)
                dy_copy(near[k]).wait()
            unit(k, f)
        elif step[0] == "grad":
            grad(step[1])
            if step[1] == cols - 1:
                next_late()
        else:
            y_part(step[1])
            if step[1] == cols - 1:
                next_late()

    for f in parts:
        parts[f].sent()
    strips = width // 256

    def flat(ref):
        return ref[...].reshape(cols * tokens, ref.shape[2])

    def columns(ref, at):
        return jnp.concatenate([ref[j, :, at] for j in range(cols)], axis=0)

    def down_strip(n, carry):
        at = pl.ds(pl.multiple_of(n * 256, 256), 256)
        wd[at] = dot_tokens(columns(dy, at), flat(act)).astype(bf16)
        return carry

    for begin, end in ((0, strips // 2), (strips // 2, strips)):
        lax.fori_loop(begin, end, down_strip, 0)
        next_late()
    chunk = down_staged.shape[2]
    inner = InnerSumInPlace(
        place,
        wd,
        lambda e: down_out.at[:, pl.ds(pl.multiple_of(e * chunk, chunk), chunk)],
        chunk,
        dy,
        act,
        first_held,
        down_staged,
        inner_sems,
    )
    inner.begin()
    inner.tick(0)
    inner.tick(1)
    grad(0)
    beside = []
    for number in ((1, 3) + (2,) * strips)[:strips]:
        beside.append(calls[:number])
        del calls[:number]

    def hidden_strip(n, carry):
        at = pl.ds(pl.multiple_of(n * 256, 256), 256)
        left = columns(hn, at)
        for f in range(tiles):
            span = slice(2 * f * tile, 2 * (f + 1) * tile)
            right = dgu[:, :, span].reshape(cols * tokens, 2 * tile)
            wh[f, at] = dot_tokens(left, right).astype(bf16)
        pltpu.make_async_copy(wh.at[:, at], dwh_out.at[:, at], dw_sems.at[n]).start()
        inner.tick(n + 2)
        for number, some in enumerate(beside):
            for call in some:
                pl.when(n == number)(functools.partial(do_late, call))
        return carry

    lax.fori_loop(0, strips, hidden_strip, 0)
    for t in range(strips + 2, inner.count + 2 * inner.lag):
        inner.tick(t)
    while calls:
        next_late()

    def grad_copy(n):
        return pltpu.make_async_copy(
            grad_staged.at[n % 2], grad_out.at[:, wide_at(n)], grad_sems.at[n % 2]
        )

    for n in range(wides):
        if n >= 2:
            grad_copy(n - 2).wait()
        piece(n).last(grad_staged.at[n % 2])
        grad_copy(n).start()
    for n in range(max(wides - 2, 0), wides):
        grad_copy(n).wait()
    out_copy(near[stored[-1]]).wait()

    def finish(n, carry):
        at = pl.ds(pl.multiple_of(n * 256, 256), 256)
        pltpu.make_async_copy(wh.at[:, at], dwh_out.at[:, at], dw_sems.at[n]).wait()
        return carry

    lax.fori_loop(0, strips, finish, 0)
    inner.finish()
    line.finish()
    for n in range(wides):
        piece(n).finish()


def mlp(hn, dy, wh, wh_own, wd, row_count, col_count, collective_id):
    steps = max(col_count - 1, 1)
    rows, width = hn.shape
    hidden = wd.shape[1]
    early, tile = wh.shape[0], wh.shape[2] // 2
    tiles = hidden // tile
    left = tiles - early
    wide = min(512, width)
    shape = (col_count, rows, width)
    total = col_count * rows
    wh_shape = (tiles, width, 2 * tile)
    plane = plane_sizes(row_count)
    plane_sems = (left, 2, PlaneGather.sem_count(plane))
    deep = width // row_count
    chunk = min(512, hidden)
    count = hidden // chunk
    inner_sems = InnerSum.sems(plane, count)
    inner_sems[0] = pltpu.SemaphoreType.DMA((2, count, plane[0] * plane[1]))
    grad, y, dwh, sum_down = pl.pallas_call(
        functools.partial(mlp_kernel, (row_count, col_count), early, wide),
        out_shape=[
            jax.ShapeDtypeStruct((rows, width), f32),
            jax.ShapeDtypeStruct(shape, bf16),
            jax.ShapeDtypeStruct(wh_shape, bf16),
            jax.ShapeDtypeStruct((deep, hidden), f32),
        ],
        in_specs=[ANY] * 5,
        out_specs=[ANY] * 4,
        scratch_shapes=[
            pltpu.VMEM(shape, bf16),
            pltpu.VMEM(shape, bf16),
            pltpu.VMEM(wh_shape, bf16),
            pltpu.VMEM(wd.shape, bf16),
            pltpu.VMEM((col_count, rows, hidden), bf16),
            pltpu.VMEM((col_count, rows, 2 * hidden), bf16),
            pltpu.VMEM(shape, bf16),
            pltpu.VMEM((rows, width), bf16),
            pltpu.VMEM((width // wide, 2, steps, rows, wide), bf16),
            pltpu.VMEM((2, rows, wide), f32),
            pltpu.VMEM((2, deep, chunk), f32),
            pltpu.SemaphoreType.DMA((col_count,)),
            pltpu.SemaphoreType.DMA((tiles, 2)),
            pltpu.SemaphoreType.DMA((tiles,)),
            pltpu.SemaphoreType.DMA,
            pltpu.SemaphoreType.DMA((width // 256,)),
            pltpu.SemaphoreType.DMA((width // wide, 2, steps)),
            pltpu.SemaphoreType.DMA((width // wide, 2, steps)),
            pltpu.SemaphoreType.DMA((2, steps)),
            pltpu.SemaphoreType.DMA((2, steps)),
            pltpu.SemaphoreType.DMA(plane_sems),
            pltpu.SemaphoreType.DMA(plane_sems),
            pltpu.SemaphoreType.DMA,
            pltpu.SemaphoreType.DMA((2,)),
        ]
        + [pltpu.VMEM(InnerSum.held_shapes(plane, deep, hidden, chunk)[2], bf16)]
        + inner_sems
        + [pltpu.SemaphoreType.REGULAR],
        compiler_params=pltpu.CompilerParams(
            collective_id=collective_id, has_side_effects=True, vmem_limit_bytes=63 << 20
        ),
        cost_estimate=pl.CostEstimate(
            flops=2 * 9 * total * width * hidden,
            bytes_accessed=6 * width * hidden * 2,
            transcendentals=total * hidden,
        ),
        name="feed_forward",
    )(hn, dy.reshape(shape), wh, wh_own, wd)
    return grad, y.reshape(total, width), dwh, sum_down


class PlaneSum:
    def __init__(self, place, block, held, sems):
        self.place, self.block, self.held = place, block, held
        self.sends, self.recvs = sems

    @staticmethod
    def counts_of(sizes):
        na, nb, _ = sizes
        return max(na, nb) - 1, max((na - 1) * nb, (nb - 1) * na)

    @staticmethod
    def sem_count(sizes):
        na, nb, _ = sizes
        return na * nb - 1

    def axes(self, half):
        return (1, 0) if half == 0 else (0, 1)

    def counts(self, half):
        first, second = self.axes(half)
        return self.place.sizes[first], self.place.sizes[second]

    def part(self, half, i, j):
        first, second = self.axes(half)
        at = self.place.moved(second, j, self.place.moved(first, i))
        return self.block(self.place.chip_of(at), half)

    def number(self, half, kind, step, i):
        return (step - 1) * self.counts(half)[0] + i if kind == 1 else step - 1

    def copy(self, half, kind, step, i):
        np_, nq = self.counts(half)
        number = self.number(half, kind, step, i)
        if kind == 1:
            source, sem = self.part(half, i, nq - step), number
        else:
            source, sem = self.part(half, np_ - step, 0), (nq - 1) * np_ + number
        target = self.held(kind, half, number)
        device = self.place.device(self.axes(half)[1 if kind == 1 else 0], 1)
        return remote(source, target, self.sends.at[half, sem], self.recvs.at[half, sem], device)

    def add(self, pieces):
        for half, kind, step, i in pieces:
            np_, nq = self.counts(half)
            self.copy(half, kind, step, i).wait_recv()
            if kind == 1:
                target = self.part(half, i, nq - step - 1)
            else:
                target = self.part(half, np_ - step - 1, 0)
            add_rows(target, self.held(kind, half, self.number(half, kind, step, i)))
            yield half, i

    def first(self):
        for half in (0, 1):
            np_, nq = self.counts(half)
            if nq > 1:
                for i in range(np_ - 1, -1, -1):
                    self.copy(half, 1, 1, i).start()

    def second(self):
        for half in (0, 1):
            np_, nq = self.counts(half)
            if nq == 1 and np_ > 1:
                self.copy(half, 0, 1, 0).start()
        for step in range(1, max(self.place.sizes[:2])):
            pieces = []
            for half in (0, 1):
                np_, nq = self.counts(half)
                if step < nq:
                    pieces += [(half, 1, step, i) for i in range(np_ - 1, -1, -1)]
            for half, i in self.add(pieces):
                np_, nq = self.counts(half)
                if step < nq - 1:
                    self.copy(half, 1, step + 1, i).start()
                elif i == np_ - 1 and np_ > 1:
                    self.copy(half, 0, 1, 0).start()

    def third(self):
        for step in range(1, max(self.place.sizes[:2])):
            pieces = [(half, 0, step, 0) for half in (0, 1) if step < self.counts(half)[0]]
            for half, _ in self.add(pieces):
                if step < self.counts(half)[0] - 1:
                    self.copy(half, 0, step + 1, 0).start()

    def finish(self):
        for half in (0, 1):
            np_, nq = self.counts(half)
            for step in range(1, nq):
                for i in range(np_):
                    self.copy(half, 1, step, i).wait_send()
            for step in range(1, np_):
                self.copy(half, 0, step, 0).wait_send()


def landing(first, second):
    return lambda kind, half, number: (first, second)[kind].at[half, number]


def halves_of(acc):
    half = acc.shape[1] // 2
    return lambda chip, number: acc.at[chip, pl.ds(number * half, half)]


def core_rows(place, chip, step, deep):
    cores = place.sizes[2]
    row = chip * cores + lax.rem(place.at[2] + step, cores)
    return pl.ds(pl.multiple_of(row * deep, deep), deep)


class InnerSum:
    lag = LAG

    def __init__(self, place, count, terms, target, refs):
        self.place, self.count, self.terms, self.target = place, count, terms, target
        self.acc, self.core_held, self.second, self.first, self.staged = refs[:5]
        self.load_sems, self.core_sems, self.plane_sems, self.out_sems = refs[5:9]
        self.ahead = min(3, self.count)
        self.chips, self.deep = self.core_held.shape[1:3]

    def held(self, e):
        return landing(self.first.at[e], self.second.at[e])

    def core_block(self, e, chip):
        return self.core_held.at[e, chip]

    @staticmethod
    def held_shapes(sizes, deep, width, chunk):
        na, nb, _ = sizes
        firsts, seconds = PlaneSum.counts_of(sizes)
        return [
            (width // chunk, na * nb, deep, chunk),
            (width // chunk, 2, max(seconds, 1), deep // 2, chunk),
            (width // chunk, 2, max(firsts, 1), deep // 2, chunk),
        ]

    @staticmethod
    def sems(sizes, count):
        return [
            pltpu.SemaphoreType.DMA((2, count)),
            pltpu.SemaphoreType.DMA((2, count, 2, max(PlaneSum.sem_count(sizes), 1))),
            pltpu.SemaphoreType.DMA((2,)),
        ]

    @staticmethod
    def scratch(sizes, deep, width, chunk, staged):
        shapes = InnerSum.held_shapes(sizes, deep, width, chunk)
        count = width // chunk
        return (
            [pltpu.VMEM(shape, bf16) for shape in shapes[:1] + shapes]
            + [pltpu.VMEM(staged, f32), pltpu.SemaphoreType.DMA((count,))]
            + InnerSum.sems(sizes, count)
        )

    def load(self, e):
        source = self.terms(e, self.place.at[2])
        return pltpu.make_async_copy(source, self.acc.at[e], self.load_sems.at[e])

    def other(self):
        return lax.rem(self.place.at[2] + 1, self.place.sizes[2])

    def shares(self, e):
        return [
            remote(
                self.terms(e, self.other()),
                self.core_held.at[e],
                self.core_sems.at[0, e],
                self.core_sems.at[1, e],
                self.place.device(2, 1),
            )
        ]

    def block(self, e, chip):
        return self.acc.at[e, chip]

    def inside(self, e):
        half = self.deep // 2
        return PlaneSum(
            self.place,
            lambda chip, number: self.block(e, chip).at[pl.ds(number * half, half)],
            self.held(e),
            (self.plane_sems.at[0, e], self.plane_sems.at[1, e]),
        )

    def out_copy(self, e):
        slot = lax.rem(e, 2)
        return pltpu.make_async_copy(
            self.staged.at[slot], self.target(e), self.out_sems.at[slot]
        )

    def prepare(self, e):
        self.load(e).start()
        if self.place.sizes[2] > 1:
            for share in self.shares(e):
                share.start()

    def begin(self):
        for e in range(self.ahead):
            self.prepare(e)

    def ready(self, e):
        self.load(e).wait()
        if self.place.sizes[2] > 1:
            for share in self.shares(e):
                share.wait_recv()

    def start(self, e):
        when(e + self.ahead < self.count, lambda: self.prepare(e + self.ahead))
        self.ready(e)
        if self.place.sizes[2] > 1:
            for chip in range(self.chips):
                add_rows(self.block(e, chip), self.core_block(e, chip))
        self.inside(e).first()

    def middle(self, e):
        self.inside(e).second()

    def close(self, e):
        self.inside(e).third()
        when(e >= 2, lambda: self.out_copy(e - 2).wait())
        slot = lax.rem(e, 2)
        own = self.block(e, self.place.chip_of(self.place.at))
        self.staged[slot] = own[...].astype(f32)
        self.out_copy(e).start()

    def tick(self, t):
        steps = ((0, self.start), (self.lag, self.middle), (2 * self.lag, self.close))
        for lag, action in steps:
            e = t - lag
            when((e >= 0) & (e < self.count), functools.partial(action, e))

    def last_outs(self):
        return range(max(self.count - 2, 0), self.count)

    def finish(self):
        for e in self.last_outs():
            self.out_copy(e).wait()

        def done(e, carry):
            if self.place.sizes[2] > 1:
                for share in self.shares(e):
                    share.wait_send()
            self.inside(e).finish()
            return carry

        lax.fori_loop(0, self.count, done, 0)


class PairSum(InnerSum):
    def out_copy(self, f):
        return pltpu.make_async_copy(self.staged.at[0], self.target(f), self.out_sems.at[0])

    def close(self, e):
        self.inside(e).third()
        f, part = e // 2, lax.rem(e, 2)
        when((part == 0) & (f >= 1), lambda: self.out_copy(f - 1).wait())
        own = self.block(e, self.place.chip_of(self.place.at))
        for number in (0, 1):

            @pl.when(part == number)
            def _(number=number):
                self.staged[0, :, number, :] = own[...].astype(f32)

        when(part == 1, lambda: self.out_copy(f).start())

    def last_outs(self):
        return range(self.count // 2 - 1, self.count // 2)


class InnerSumInPlace(InnerSum):
    lag = LAG + 1

    def __init__(self, place, terms, target, chunk, core_land, land, first, staged, sems):
        self.place, self.terms, self.target, self.chunk = place, terms, target, chunk
        self.core_land, self.land, self.first, self.staged = core_land, land, first, staged
        self.core_sems, self.plane_sems, self.out_sems, self.free_sem = sems
        self.count = terms.shape[1] // chunk
        self.ahead = self.count
        self.chips = place.sizes[0] * place.sizes[1]
        self.deep = terms.shape[0] // place.rows

    def columns(self, e):
        return pl.ds(pl.multiple_of(e * self.chunk, self.chunk), self.chunk)

    def rows(self, e, chip, core):
        row = chip * self.place.sizes[2] + core
        return self.terms.at[
            pl.ds(pl.multiple_of(row * self.deep, self.deep), self.deep), self.columns(e)
        ]

    def block(self, e, chip):
        return self.rows(e, chip, self.place.at[2])

    def core_block(self, e, chip):
        return self.core_land.at[chip, :, self.columns(e)]

    def held(self, e):
        half_deep = self.deep // 2

        def place_of(kind, half, number):
            if kind == 0:
                return self.first.at[e, half, number]
            return self.land.at[number, pl.ds(half * half_deep, half_deep), self.columns(e)]

        return place_of

    def shares(self, e):
        return [
            remote(
                self.rows(e, chip, self.other()),
                self.core_block(e, chip),
                self.core_sems.at[0, e, chip],
                self.core_sems.at[1, e, chip],
                self.place.device(2, 1),
            )
            for chip in range(self.chips)
        ]

    def prepare(self, e):
        if self.place.sizes[2] > 1:
            for share in self.shares(e):
                share.start()

    def begin(self):
        peers = [axis for axis in range(3) if self.place.sizes[axis] > 1]
        for axis in peers:
            pl.semaphore_signal(
                self.free_sem, inc=1, device_id=self.place.device(axis, -1), device_id_type=MESH
            )
        if peers:
            pl.semaphore_wait(self.free_sem, len(peers))
        super().begin()

    def ready(self, e):
        if self.place.sizes[2] > 1:
            for share in self.shares(e):
                share.wait_recv()


class SmallSum:
    def __init__(self, place, own, total, ring_held, line_held, ring_sems, line_sems):
        self.place, self.own, self.total = place, own, total
        self.held, self.sems = ring_held, ring_sems
        self.line = LineGather(
            place, total, lambda j: line_held.at[j], line_sems.at[0], line_sems.at[1]
        )
        self.line_held = line_held
        self.stages = []
        for axis in range(3):
            for step in range(1, place.sizes[axis]):
                self.stages.append(functools.partial(self.ring_send, axis, step))
                self.stages.append(functools.partial(self.ring_receive, axis, step))
            if place.sizes[axis] > 1:
                self.stages.append(functools.partial(self.ring_add, axis))
        self.stages.append(self.line_start)
        for step in range(1, place.cols):
            self.stages.append(functools.partial(self.line_step, step))
        self.stages.append(self.line_add)

    def begin(self):
        self.total[...] = self.own[...]

    def block(self, axis, step):
        at = self.place.moved(axis, -step)[axis]
        return self.held.at[axis, at]

    def ring_copy(self, axis, step):
        source = self.total if step == 1 else self.block(axis, step - 1)
        target = self.held.at[axis, self.place.moved(axis, 1 - step)[axis]]
        return remote(
            source,
            target,
            self.sems.at[0, axis, step - 1],
            self.sems.at[1, axis, step - 1],
            self.place.device(axis, 1),
        )

    def ring_send(self, axis, step):
        self.ring_copy(axis, step).start()

    def ring_receive(self, axis, step):
        ref = self.block(axis, step)
        remote(
            ref,
            ref,
            self.sems.at[0, axis, step - 1],
            self.sems.at[1, axis, step - 1],
            self.place.device(axis, 1),
        ).wait_recv()

    def ring_add(self, axis):
        for step in range(1, self.place.sizes[axis]):
            self.ring_copy(axis, step).wait_send()
        own_at = self.place.at[axis]
        total = None
        for at in range(self.place.sizes[axis]):
            term = jnp.where(own_at == at, self.total[...], self.held[axis, at])
            total = term if total is None else total + term
        self.total[...] = total

    def line_start(self):
        for way in (0, 1):
            self.line.send(way, 1)

    def line_step(self, step):
        for way in (0, 1):
            self.line.receive(way, step)

    def line_add(self):
        self.line.finish()
        total = None
        for at in range(self.place.cols):
            term = jnp.where(self.place.col == at, self.total[...], self.line_held[at])
            total = term if total is None else total + term
        self.total[...] = total


def norm_rows(dxn, x, dh, gain, out, part):
    rows, width = x.shape
    piece = 32

    def body(n, carry):
        at = pl.ds(pl.multiple_of(n * piece, piece), piece)
        values = x[at].astype(f32)
        scale = lax.rsqrt(jnp.mean(values * values, axis=1, keepdims=True) + epsilon)
        grad = dxn[at]
        weighted = grad * gain[...]
        inner = jnp.mean(weighted * values, axis=1, keepdims=True)
        result = dh[at].astype(f32) + scale * weighted - values * (scale * scale * scale) * inner
        out[at] = result.astype(out.dtype)
        part[0:1] += jnp.sum(grad * values * scale, axis=0, keepdims=True)
        return carry

    part[0:1] = jnp.zeros((1, width), f32)
    lax.fori_loop(0, rows // piece, body, 0)


def sum_kernel(sizes, count, *refs):
    row_count, col_count = sizes
    place = Place(row_count, col_count)
    cores = place.sizes[2]
    lefts, rights = refs[: cores * count], refs[cores * count : 2 * cores * count]
    refs = refs[2 * cores * count :]
    dxn, x, dh, gain, mid_part = refs[:5]
    outs = refs[5 : 6 + count]
    tokens_out, small_out = refs[6 + count : 8 + count]
    refs = refs[8 + count :]
    per = [refs[7 * n : 7 * n + 7] for n in range(count)]
    load_sems, out_sems, ps, pr, zs, zr = refs[7 * count : 7 * count + 6]
    ring_held, line_held, ring_sems, line_sems, chip_sems, small = refs[7 * count + 6 :]

    entries = [(n, nearby(place, k)) for k in range(col_count - 1, -1, -1) for n in range(count)]

    acc = [per[n][0] for n in range(count)]
    lines = [
        LineSum(
            place,
            lambda j, n=n: acc[n].at[j, place.chip_of(place.at)],
            per[n][3],
            zs.at[n],
            zr.at[n],
        )
        for n in range(count)
    ]
    tokens = lefts[0].shape[0]
    chips, deep = acc[0].shape[1:3]

    def loads():
        for n in range(count):
            left, right = per[n][5], per[n][6]
            for k in range(cores):
                at = pl.ds(k * tokens, tokens)
                if k == 0:
                    for chip in range(chips):
                        yield pltpu.make_async_copy(
                            lefts[n * cores].at[:, core_rows(place, chip, 0, deep)],
                            left.at[at, pl.ds(chip * deep, deep)],
                            chip_sems.at[n, chip],
                        )
                else:
                    yield pltpu.make_async_copy(
                        lefts[n * cores + k], left.at[at], load_sems.at[0, n * cores + k]
                    )
                yield pltpu.make_async_copy(
                    rights[n * cores + k], right.at[:, at], load_sems.at[1, n * cores + k]
                )

    for copy in loads():
        copy.start()
    place.greet(True, True)
    smalls = SmallSum(place, small, small_out, ring_held, line_held, ring_sems, line_sems)
    stages = [functools.partial(norm_rows, dxn, x, dh, gain, tokens_out, small)]
    stages += [smalls.begin] + smalls.stages
    small[1:2] = mid_part[...]
    for copy in loads():
        copy.wait()

    def inside(n, col):
        return PlaneSum(
            place,
            halves_of(acc[n].at[col]),
            landing(per[n][2].at[col], per[n][1].at[col]),
            (ps.at[n, col], pr.at[n, col]),
        )

    parts = [inside(n, col) for n, col in entries]
    final = len(entries) - count
    total = len(entries)

    def start(number):
        n, col = entries[number]
        left, right = per[n][5], per[n][6]
        deep = acc[n].shape[2]

        def chip_rows(chip, carry):
            at = pl.ds(pl.multiple_of(chip * deep, deep), deep)
            acc[n][col, chip] = dot_tokens(left[:, at], right[col]).astype(bf16)
            return carry

        lax.fori_loop(0, acc[n].shape[1], chip_rows, 0)
        parts[number].first()

    split = outs[0].shape[1]

    def out_copies(n):
        if n > 0:
            return [pltpu.make_async_copy(per[n][4], outs[n + 1], out_sems.at[n + 1])]
        rest = pl.ds(split, outs[1].shape[1])
        return [
            pltpu.make_async_copy(per[0][4].at[:, pl.ds(0, split)], outs[0], out_sems.at[0]),
            pltpu.make_async_copy(per[0][4].at[:, rest], outs[1], out_sems.at[1]),
        ]

    def close(number):
        parts[number].third()
        n, col = entries[number]
        if number < final:
            lines[n].early(col, True)
            if number >= count:
                lines[n].late(entries[number - count][1], True)
            if number >= final - count:
                lines[n].late(col, True)

    def finish_lines():
        for n in range(count):
            lines[n].last(per[n][4])
            for copy in out_copies(n):
                copy.start()

    for number in range(total + 2 * LAG):
        if number < total:
            start(number)
        if LAG <= number < total + LAG:
            parts[number - LAG].second()
        if 2 * LAG <= number:
            close(number - 2 * LAG)
        if number >= 1:
            for stage in stages[:2]:
                stage()
            del stages[:2]
    for stage in stages:
        stage()
    finish_lines()
    for n in range(count):
        for copy in out_copies(n):
            copy.wait()
    for part in parts:
        part.finish()
    for line in lines:
        line.finish()


def sum_all(lefts, rights, split, extras, row_count, col_count):
    count = len(rights)
    sizes = plane_sizes(row_count)
    na, nb, nk = sizes
    chips = na * nb
    tokens, model = lefts[0][0].shape
    deep = lefts[0][0].shape[1] // row_count
    steps = max(col_count - 1, 1)
    firsts, seconds = PlaneSum.counts_of(sizes)
    widths = [right[0].shape[2] for right in rights]
    scratch = []
    for width in widths:
        scratch += [
            pltpu.VMEM((col_count, chips, deep, width), bf16),
            pltpu.VMEM((col_count, 2, max(seconds, 1), deep // 2, width), bf16),
            pltpu.VMEM((col_count, 2, max(firsts, 1), deep // 2, width), bf16),
            pltpu.VMEM((2, steps, deep, width), bf16),
            pltpu.VMEM((deep, width), f32),
            pltpu.VMEM((nk * tokens, chips * deep), bf16),
            pltpu.VMEM((col_count, nk * tokens, width), bf16),
        ]
    plane_sems = (count, col_count, 2, max(PlaneSum.sem_count(sizes), 1))
    scratch += [
        pltpu.SemaphoreType.DMA((2, count * nk)),
        pltpu.SemaphoreType.DMA((count + 1,)),
        pltpu.SemaphoreType.DMA(plane_sems),
        pltpu.SemaphoreType.DMA(plane_sems),
        pltpu.SemaphoreType.DMA((count, 2, steps)),
        pltpu.SemaphoreType.DMA((count, 2, steps)),
        pltpu.VMEM((3, max(sizes), 2, model), f32),
        pltpu.VMEM((col_count, 2, model), f32),
        pltpu.SemaphoreType.DMA((2, 3, max(max(sizes) - 1, 1))),
        pltpu.SemaphoreType.DMA((2, 2, steps)),
        pltpu.SemaphoreType.DMA((count, chips)),
        pltpu.VMEM((2, model), f32),
    ]
    outs = [split, widths[0] - split] + widths[1:]
    vmem = pl.BlockSpec(memory_space=pltpu.VMEM)
    flops = sum(2 * nk * tokens * chips * deep * width * col_count for width in widths)
    return pl.pallas_call(
        functools.partial(sum_kernel, (row_count, col_count), count),
        out_shape=[jax.ShapeDtypeStruct((deep, width), f32) for width in outs]
        + [
            jax.ShapeDtypeStruct((tokens, model), bf16),
            jax.ShapeDtypeStruct((2, model), f32),
        ],
        in_specs=[ANY] * (2 * count * nk) + [vmem] * 5,
        out_specs=[ANY] * (count + 1) + [vmem] * 2,
        scratch_shapes=scratch,
        compiler_params=pltpu.CompilerParams(
            collective_id=1, has_side_effects=True, vmem_limit_bytes=63 << 20
        ),
        cost_estimate=pl.CostEstimate(
            flops=flops, bytes_accessed=flops // 256, transcendentals=0
        ),
        name="sum_weights",
    )(
        *[left for pair in lefts for left in pair],
        *[right for pair in rights for right in pair],
        *extras,
    )


LANES = 2 * HD


def lower_lanes():
    return lax.broadcasted_iota(jnp.int32, (1, LANES), 1) < HD


def rope_lanes(values, cosine, sinusoid):
    lane = lax.broadcasted_iota(jnp.int32, (1, LANES), 1)
    other = jnp.where(
        lane % HD < HD // 2,
        pltpu.roll(values, LANES - HD // 2, 1),
        pltpu.roll(values, HD // 2, 1),
    )
    return values * cosine + other * sinusoid


def head_at(tile, head, upper):
    if (head % 2 == 1) != upper:
        tile = pltpu.roll(tile, HD, 1)
    keep = lower_lanes()
    if upper:
        keep = jnp.logical_not(keep)
    return jnp.where(keep, tile, 0.0)


def tile_of(head):
    return slice(head // 2 * LANES, head // 2 * LANES + LANES)


def pair_tile(even, odd, upper):
    if upper:
        even = pltpu.roll(even, HD, 1)
    else:
        odd = pltpu.roll(odd, HD, 1)
    return jnp.where(lower_lanes(), even, odd)


def attend_kernel(sizes, heads, group, back, *refs):
    xn, x, wf_in, wo_in, bias, cosq, sinq, coskv, sinkv, gain, tiles_in = refs[:11]
    q_out, kv_out, mixed_out, lse_out, full_tiles, hidden, hn = refs[11:18]
    q, kv, mixed, lse, wf, wo, w_sems, o_sems, sends, recvs, t_sems, ps, pr = refs[18:31]
    tiles, tiles_sem = refs[31:]
    place = Place(*sizes)
    cols, col = place.cols, place.col
    tokens = xn.shape[0]
    query_width = heads * HD
    own_rows = pl.ds(back * tokens, tokens)
    pairs = heads // group

    def weight_copies(z):
        return (
            pltpu.make_async_copy(wf_in.at[z], wf.at[z], w_sems.at[0, z]),
            pltpu.make_async_copy(wo_in.at[z], wo.at[z], w_sems.at[1, z]),
        )

    count, _, tile = tiles.shape
    tile = tile // 2
    hidden_units = tiles_in.shape[1] // 2
    fetches = [
        pltpu.make_async_copy(
            tiles_in.at[:, pl.ds(number * hidden_units + f * tile, tile)],
            tiles.at[f, :, pl.ds(number * tile, tile)],
            tiles_sem.at[f, number],
        )
        for f in range(count)
        for number in (0, 1)
    ]
    for fetch in fetches:
        fetch.start()
    for step in range(1, back + 1):

        @pl.when(col < step)
        def _():
            kv[:, (back - step) * tokens : (back - step + 1) * tokens] = jnp.zeros(
                (cols, tokens, kv.shape[2]), bf16
            )

    keeps = [
        pltpu.make_async_copy(
            tiles.at[f],
            full_tiles.at[f, pl.ds(place.row * tiles.shape[1], tiles.shape[1])],
            t_sems.at[f],
        )
        for f in range(tiles.shape[0])
    ]
    place.greet(True, True)
    for fetch in fetches:
        fetch.wait()
    parts = [
        tile_gather(place, full_tiles.at[f], tiles.at[f], ps.at[f], pr.at[f])
        for f in range(tiles.shape[0])
    ]
    for part in parts:
        part.first()
    for number in (0, 1):
        for z in range(cols):
            weight_copies(z)[number].start()
    for keep in keeps:
        keep.start()

    def hop(z, step):
        source = kv.at[z, pl.ds((back - step + 1) * tokens, tokens)]
        target = kv.at[z, pl.ds((back - step) * tokens, tokens)]
        return remote(
            source, target, sends.at[step - 1, z], recvs.at[step - 1, z], (place.row, col + 1)
        )

    def goes(step):
        return (col < cols - 1) & (col >= step - 1)

    def send(z, step):
        pl.when(goes(step))(lambda: hop(z, step).start())

    def receive(z, step):
        ref = kv.at[z, pl.ds((back - step) * tokens, tokens)]

        @pl.when(col >= step)
        def _():
            remote(
                ref, ref, sends.at[step - 1, z], recvs.at[step - 1, z], (place.row, col + 1)
            ).wait_recv()

    def project(z, carry):
        weight_copies(z)[0].wait()
        pre = matmul(xn[...], wf[z])
        for n in range(query_width // LANES):
            at = slice(n * LANES, (n + 1) * LANES)
            q[z, :, at] = rope_lanes(pre[:, at], cosq[...], sinq[...]).astype(bf16)
        for n in range(pairs):
            at = slice(n * LANES, (n + 1) * LANES)
            tile = pre[:, query_width + n * LANES : query_width + (n + 1) * LANES]
            kv[z, own_rows, at] = rope_lanes(tile, coskv[...], sinkv[...]).astype(bf16)
        if back > 0:
            send(z, 1)
        return carry

    lax.fori_loop(0, cols, project, 0)
    if parts:
        parts[0].second()
    for step in range(1, back):
        for z in range(cols):
            receive(z, step)
            send(z, step + 1)

    def attend(z, carry):
        if back > 0:
            receive(z, back)
        lane = lax.broadcasted_iota(jnp.int32, (1, LANES), 1)
        logs = jnp.zeros((tokens, LANES), f32)
        outs = []
        for head in range(heads):
            pair = head // group
            keyval = kv[z, :, pair * LANES : (pair + 1) * LANES]
            query = head_at(q[z, :, tile_of(head)].astype(f32), head, False) * HD**-0.5
            scores = against(query.astype(bf16), keyval) + bias[...]
            summit = jnp.max(scores, axis=1, keepdims=True)
            weights = jnp.exp(scores - summit)
            total = jnp.sum(weights, axis=1, keepdims=True)
            chances = (weights * (1.0 / total)).astype(bf16)
            outs.append(matmul(chances, keyval))
            logs = jnp.where(lane == head, summit + jnp.log(total), logs)
            if head % 2 == 1:
                mixed[z, :, tile_of(head)] = pair_tile(outs[-2], outs[-1], True).astype(bf16)
        lse[z] = jnp.transpose(logs)[:heads]

        @pl.when(z == 0)
        def _():
            for part in parts[1:]:
                part.second()

        @pl.when(z == max(cols - 2, 1))
        def _():
            for part in parts[:-1]:
                part.third()

        return carry

    lax.fori_loop(0, cols, attend, 0)
    outputs = [
        pltpu.make_async_copy(source, target, o_sems.at[n])
        for n, (source, target) in enumerate(
            ((q, q_out), (kv, kv_out), (mixed, mixed_out), (lse, lse_out))
        )
    ]
    for copy in outputs:
        copy.start()
    hidden[...] = x[...].astype(f32)

    def project_out(z, carry):
        weight_copies(z)[1].wait()
        hidden[...] += against(mixed[z], wo[z])
        return carry

    lax.fori_loop(0, cols, project_out, 0)
    total = hidden[...]
    scale = lax.rsqrt(jnp.mean(total * total, axis=1, keepdims=True) + epsilon)
    hn[...] = (total * scale * gain[...]).astype(bf16)
    if parts:
        parts[-1].third()
    for part in parts:
        part.finish()
    for copy in keeps + outputs:
        copy.wait()
    for step in range(1, back + 1):
        for z in range(cols):
            pl.when(goes(step))(lambda: hop(z, step).wait_send())


def attend(
    xn, x, wf, wo, bias, tables, gain, tiles, count, tile, heads, group, back, sizes, cid
):
    row_count, col_count = sizes
    tokens, width = xn.shape
    query_width = heads * HD
    kv_shape = (col_count, (back + 1) * tokens, heads // group * LANES)
    q_shape = (col_count, tokens, query_width)
    lse_shape = (col_count, heads, tokens)
    vmem = pl.BlockSpec(memory_space=pltpu.VMEM)
    keys = (back + 1) * tokens
    plane_sems = (count, 2, PlaneGather.sem_count(plane_sizes(row_count)))
    return pl.pallas_call(
        functools.partial(attend_kernel, (row_count, col_count), heads, group, back),
        out_shape=[
            jax.ShapeDtypeStruct(q_shape, bf16),
            jax.ShapeDtypeStruct(kv_shape, bf16),
            jax.ShapeDtypeStruct(q_shape, bf16),
            jax.ShapeDtypeStruct(lse_shape, f32),
            jax.ShapeDtypeStruct((count, row_count * tiles.shape[0], 2 * tile), bf16),
            jax.ShapeDtypeStruct((tokens, width), f32),
            jax.ShapeDtypeStruct((tokens, width), bf16),
        ],
        in_specs=[vmem, vmem, ANY, ANY] + [vmem] * 6 + [ANY],
        out_specs=[ANY] * 5 + [vmem] * 2,
        scratch_shapes=[
            pltpu.VMEM(q_shape, bf16),
            pltpu.VMEM(kv_shape, bf16),
            pltpu.VMEM(q_shape, bf16),
            pltpu.VMEM(lse_shape, f32),
            pltpu.VMEM(wf.shape, bf16),
            pltpu.VMEM(wo.shape, bf16),
            pltpu.SemaphoreType.DMA((2, col_count)),
            pltpu.SemaphoreType.DMA((4,)),
            pltpu.SemaphoreType.DMA((max(back, 1), col_count)),
            pltpu.SemaphoreType.DMA((max(back, 1), col_count)),
            pltpu.SemaphoreType.DMA((count,)),
            pltpu.SemaphoreType.DMA(plane_sems),
            pltpu.SemaphoreType.DMA(plane_sems),
            pltpu.VMEM((count, tiles.shape[0], 2 * tile), bf16),
            pltpu.SemaphoreType.DMA((count, 2)),
        ],
        compiler_params=pltpu.CompilerParams(
            collective_id=cid, has_side_effects=True, vmem_limit_bytes=56 << 20
        ),
        cost_estimate=pl.CostEstimate(
            flops=2 * tokens * (wf.size + wo.size) + 4 * col_count * heads * tokens * keys * HD,
            bytes_accessed=(wf.size + wo.size) * 2,
            transcendentals=col_count * heads * tokens * keys,
        ),
        name="attend",
    )(xn, x, wf, wo, bias, *tables, gain, tiles)


def attend_back_kernel(sizes, heads, group, back, chunk, *refs):
    grad_hn, hidden_in, dy, gain, xn, lse, bias, cosq, sinq, coskv, sinkv = refs[:11]
    mixed_in, q_in, kv_in, wo_in, wf_in, terms = refs[11:17]
    dxn, dh, dhb, mid_part = refs[17:21]
    dqkv_out, sum_out, xn_sib, dhb_sib, mixed_sib, dqkv_sib = refs[21:27]
    q, kv, wo, wf, dmix, dkv, dqkv, going, coming, dst, pst, rhs_q, rhs_o = refs[27:40]
    in_sems, wo_sems, wf_sems, out_sems, pair_sems, row_sems, sends, recvs = refs[40:48]
    place = Place(*sizes)
    cols, col = place.cols, place.col
    cores = place.sizes[2]
    tokens = dhb.shape[0]
    query_width = heads * HD
    pairs = heads // group
    hidden = sum_out.shape[2]

    def inner_target(f):
        return sum_out.at[:, :, pl.ds(pl.multiple_of(f * chunk, chunk), chunk)]

    def inner_terms(e, core):
        at = pl.multiple_of(lax.rem(e, 2) * chunk, chunk)
        return terms.at[e // 2, :, core, :, pl.ds(at, chunk)]

    inner = PairSum(place, 2 * hidden // chunk, inner_terms, inner_target, refs[48:])

    in_copies = [
        pltpu.make_async_copy(q_in, q, in_sems.at[0]),
        pltpu.make_async_copy(kv_in, kv, in_sems.at[1]),
    ]

    def wo_copy(z):
        slot = lax.rem(z, 2)
        return pltpu.make_async_copy(wo_in.at[z], wo.at[slot], wo_sems.at[slot])

    def wf_copy(z):
        return pltpu.make_async_copy(wf_in.at[z], wf, wf_sems.at[0])

    wo_copy(0).start()
    for copy in in_copies:
        copy.start()
    wf_copy(0).start()
    place.greet(True, True)

    other = place.device(2, 1)
    chips, deep = terms.shape[1], terms.shape[3]
    exchanges = []
    if cores > 1:
        moves = [(mixed_in, mixed_sib)]
        for source, target in ((xn, xn_sib), (dhb, dhb_sib)):
            for chip in range(chips):
                to, rows = pl.ds(chip * deep, deep), core_rows(place, chip, 1, deep)
                moves.append((source.at[:, rows], target.at[:, to]))
        exchanges = [
            remote(source, target, pair_sems.at[0, n], pair_sems.at[1, n], other)
            for n, (source, target) in enumerate(moves)
        ]

    def row_exchange(z):
        return remote(dqkv.at[z], dqkv_sib.at[z], row_sems.at[0, z], row_sems.at[1, z], other)

    def out_copy(z):
        return pltpu.make_async_copy(dqkv.at[z], dqkv_out.at[z], out_sems.at[z])

    inner.begin()
    for exchange in exchanges[: 1 + chips]:
        exchange.start()
    norm_rows(grad_hn, hidden_in, dy, gain, dh, mid_part)
    dhb[...] = dh[...].astype(bf16)
    for exchange in exchanges[1 + chips :]:
        exchange.start()
    dxn[...] = jnp.zeros_like(dxn)
    for copy in in_copies:
        copy.wait()

    def hop(z, step):
        return remote(
            going.at[step - 1, z],
            coming.at[step - 1, z],
            sends.at[step - 1, z],
            recvs.at[step - 1, z],
            (place.row, col - 1),
        )

    def goes(step):
        return col - back + step - 1 >= 0

    def comes(step):
        return (col < cols - 1) & (col + step - back >= 0)

    def send(z, step):
        pl.when(goes(step))(lambda: hop(z, step).start())

    def chunk_rows(step):
        return slice(step * tokens, (step + 1) * tokens)

    def halo(step, z):
        if step > 0:
            pl.when(comes(step))(lambda: hop(z, step).wait_recv())
            term = jnp.where(comes(step), coming[step - 1, z].astype(f32), 0.0)
            total = dkv[z, chunk_rows(step)] + term
        else:
            total = dkv[z, chunk_rows(step)]
        if step < back:
            going[step, z] = total.astype(bf16)
            send(z, step + 1)
            return
        for n in range(pairs):
            at = slice(n * LANES, (n + 1) * LANES)
            dqkv[z, :, query_width + n * LANES : query_width + (n + 1) * LANES] = rope_lanes(
                total[:, at], coskv[...], sinkv[...]
            ).astype(bf16)
        out_copy(z).start()
        if cores > 1:
            row_exchange(z).start()
        wf_copy(z).wait()
        dxn[...] += against(dqkv[z], wf[...])
        when(z + 1 < cols, lambda: wf_copy(z + 1).start())

    def halos(z):
        for step in range(1, back + 1):
            at = z - step
            when((at >= 0) & (at < cols), lambda: halo(step, at))

    def one_col(z, carry):
        wo_copy(z).wait()
        when(z + 1 < cols, lambda: wo_copy(z + 1).start())
        dmix[...] = matmul(dhb[...], wo[lax.rem(z, 2)]).astype(bf16)
        for n in range(pairs):
            keyval = kv[z, :, n * LANES : (n + 1) * LANES]
            for i in range(group):
                head = n * group + i
                at = slice(i * tokens, (i + 1) * tokens)
                query = head_at(q[z, :, tile_of(head)].astype(f32), head, False) * HD**-0.5
                query = query.astype(bf16)
                grad = head_at(dmix[:, tile_of(head)].astype(f32), head, True).astype(bf16)
                rhs_q[at] = query
                rhs_o[at] = grad
                chances = jnp.exp(against(keyval, query) + bias[...] - lse[z, head : head + 1])
                grad_chance = against(keyval, grad)
                centre = jnp.sum(chances * grad_chance, axis=0, keepdims=True)
                dst[:, at] = (chances * (grad_chance - centre)).astype(bf16)
                pst[:, at] = chances.astype(bf16)
            dkv[z, :, n * LANES : (n + 1) * LANES] = matmul(dst[...], rhs_q[...]) + matmul(
                pst[...], rhs_o[...]
            )
            grad_rows = dot_tokens(keyval, dst[...])
            for i in range(0, group, 2):
                tile = jnp.concatenate(
                    [
                        grad_rows[:HD, i * tokens : (i + 1) * tokens],
                        grad_rows[:HD, (i + 1) * tokens : (i + 2) * tokens],
                    ],
                    axis=0,
                )
                turned = rope_lanes(jnp.transpose(tile), cosq[...], sinq[...]) * HD**-0.5
                dqkv[z, :, tile_of(n * group + i)] = turned.astype(bf16)
            inner.tick(z * pairs + n)
        halo(0, z)
        halos(z)
        return carry

    lax.fori_loop(0, cols, one_col, 0)
    ticks = list(range(cols * pairs, inner.count + 2 * LAG))
    for z in range(cols, cols + back):
        if ticks:
            inner.tick(ticks.pop(0))
        halos(z)
    for t in ticks:
        inner.tick(t)
    for z in range(cols):
        out_copy(z).wait()
        if cores > 1:
            row_exchange(z).wait_send()
            row_exchange(z).wait_recv()
    for exchange in exchanges:
        exchange.wait_send()
        exchange.wait_recv()
    for step in range(1, back + 1):
        for z in range(cols):
            pl.when(goes(step))(lambda: hop(z, step).wait_send())
    inner.finish()


def attend_back(
    mid, xn, lse, bias, tables, mixed, q, kv, wo, wf, terms, group, sizes, cid
):
    row_count, col_count = sizes
    plane = plane_sizes(row_count)
    chips = plane[0] * plane[1]
    tokens, width = xn.shape
    heads = lse.shape[1]
    back = kv.shape[1] // tokens - 1
    pairs = heads // group
    keys = kv.shape[1]
    all_width = wf.shape[2]
    tiles, _, chunk = terms.shape
    chunk = chunk // 2
    inner_width = 2 * tiles * chunk
    deep = terms.shape[1] // row_count
    row_shape = (col_count, tokens, all_width)
    halo_shape = (max(back, 1), col_count, tokens, kv.shape[2])
    vmem = pl.BlockSpec(memory_space=pltpu.VMEM)
    return pl.pallas_call(
        functools.partial(attend_back_kernel, sizes, heads, group, back, chunk),
        out_shape=[
            jax.ShapeDtypeStruct((tokens, width), f32),
            jax.ShapeDtypeStruct((tokens, width), f32),
            jax.ShapeDtypeStruct((tokens, width), bf16),
            jax.ShapeDtypeStruct((1, width), f32),
            jax.ShapeDtypeStruct(row_shape, bf16),
            jax.ShapeDtypeStruct((deep, 2, tiles * chunk), f32),
            jax.ShapeDtypeStruct((tokens, chips * deep), bf16),
            jax.ShapeDtypeStruct((tokens, chips * deep), bf16),
            jax.ShapeDtypeStruct(mixed.shape, bf16),
            jax.ShapeDtypeStruct(row_shape, bf16),
        ],
        in_specs=[vmem] * 11 + [ANY] * 6,
        out_specs=[vmem] * 4 + [ANY] * 6,
        scratch_shapes=[
            pltpu.VMEM(q.shape, bf16),
            pltpu.VMEM(kv.shape, bf16),
            pltpu.VMEM((2,) + wo.shape[1:], bf16),
            pltpu.VMEM(wf.shape[1:], bf16),
            pltpu.VMEM((tokens, heads * HD), bf16),
            pltpu.VMEM(kv.shape, f32),
            pltpu.VMEM(row_shape, bf16),
            pltpu.VMEM(halo_shape, bf16),
            pltpu.VMEM(halo_shape, bf16),
            pltpu.VMEM((keys, group * tokens), bf16),
            pltpu.VMEM((keys, group * tokens), bf16),
            pltpu.VMEM((group * tokens, LANES), bf16),
            pltpu.VMEM((group * tokens, LANES), bf16),
            pltpu.SemaphoreType.DMA((2,)),
            pltpu.SemaphoreType.DMA((2,)),
            pltpu.SemaphoreType.DMA((2,)),
            pltpu.SemaphoreType.DMA((col_count,)),
            pltpu.SemaphoreType.DMA((2, 1 + 2 * chips)),
            pltpu.SemaphoreType.DMA((2, col_count)),
            pltpu.SemaphoreType.DMA((max(back, 1), col_count)),
            pltpu.SemaphoreType.DMA((max(back, 1), col_count)),
        ]
        + InnerSum.scratch(plane, deep, inner_width, chunk, (1, deep, 2, chunk)),
        compiler_params=pltpu.CompilerParams(
            collective_id=cid, has_side_effects=True, vmem_limit_bytes=62 << 20
        ),
        cost_estimate=pl.CostEstimate(
            flops=2 * tokens * (wf.size + wo.size) + 10 * col_count * heads * tokens * keys * HD,
            bytes_accessed=(wf.size + wo.size + terms.size) * 2,
            transcendentals=col_count * heads * tokens * keys,
        ),
        name="attend_back",
    )(
        *mid,
        xn,
        lse,
        bias,
        *tables,
        mixed,
        q,
        kv,
        wo,
        wf,
        terms.reshape(tiles, chips, plane[2], deep, 2 * chunk),
    )


def rope_tables(position):
    indices = jnp.arange(HD // 2, dtype=f32)
    frequency = rope_base ** (-(indices * 2.0 / HD))
    wavelen = 2.0 * jnp.pi / frequency
    smooth = (8192.0 / wavelen - 1.0) / 3.0
    scaled = jnp.where(
        wavelen > 8192.0, frequency / 32.0, (1.0 - smooth) * frequency / 32.0 + smooth * frequency
    )
    frequency = jnp.where(wavelen < 2048.0, frequency, scaled)
    angles = position.astype(f32)[:, None] * frequency[None, :]
    return (jnp.cos(angles), jnp.sin(angles))


def rotate(values, cosine, sinusoid):
    halfway = values.shape[-1] // 2
    former = values[..., :halfway]
    latter = values[..., halfway:]
    cos_wide = cosine[:, None, :]
    sin_wide = sinusoid[:, None, :]
    return jnp.concatenate(
        [former * cos_wide - latter * sin_wide, latter * cos_wide + former * sin_wide], axis=-1
    )


def normalize(values, gain):
    scale = lax.rsqrt(jnp.mean(values * values, axis=1, keepdims=True) + epsilon)
    return ((values * scale * gain).astype(bf16), scale)


def against(left, right):
    return lax.dot_general(left, right, (((1,), (1,)), ((), ())), preferred_element_type=f32)


def over_rows(left, right):
    return lax.dot_general(left, right, (((0,), (0,)), ((), ())), preferred_element_type=f32)


def matmul(left, right):
    return jnp.dot(left, right, preferred_element_type=f32)


def shift(values, step, col_count):
    if step > 0:
        pairs = [(i, i + step) for i in range(col_count - step)]
    else:
        pairs = [(i, i + step) for i in range(-step, col_count)]
    return lax.ppermute(values, "col", pairs)


def shards(
    tokens,
    seq_lens,
    attn_gain,
    query_weight,
    keyvalue_weight,
    output_weight,
    mlp_gain,
    hidden_weight,
    down_weight,
    out_grad,
):
    row_count, col_count = lax.axis_size("row"), lax.axis_size("col")
    local = tokens.shape[0]
    block_rows = local * col_count
    col = lax.axis_index("col")
    deep = query_weight.shape[0]
    width = tokens.shape[1]
    query_width = query_weight.shape[1]
    pairs = keyvalue_weight.shape[1]
    heads = query_width // HD
    group = heads // pairs
    hidden = down_weight.shape[1]
    back = min(-(-(SEQ_MAX - 1) // local), col_count - 1)

    lengths = seq_lens[0]
    finish = jnp.cumsum(lengths)
    indices = jnp.arange(block_rows, dtype=jnp.int32)
    passed = indices[:, None] >= finish[None, :]
    segment = jnp.sum(passed.astype(jnp.int32), axis=1, dtype=jnp.int32)
    position = indices - jnp.sum(jnp.where(passed, lengths[None, :], 0), axis=1, dtype=jnp.int32)
    own_position = lax.dynamic_slice(position, (col * local,), (local,))
    own_segment = lax.dynamic_slice(segment, (col * local,), (local,))
    padded = jnp.concatenate([jnp.full((back * local,), -1, jnp.int32), segment])
    key_segment = lax.dynamic_slice(padded, (col * local,), ((back + 1) * local,))
    key_index = jnp.arange((back + 1) * local, dtype=jnp.int32) - back * local
    query_index = jnp.arange(local, dtype=jnp.int32)
    allowed = (own_segment[:, None] == key_segment[None, :]) & (
        key_index[None, :] <= query_index[:, None]
    )
    cosine, sinusoid = rope_tables(own_position)
    gain_first = attn_gain.astype(f32)
    gain_second = mlp_gain.astype(f32)

    first_weight = jnp.concatenate(
        [query_weight, keyvalue_weight.reshape(deep, pairs * 2 * HD)], axis=1
    )
    full_first, full_output, full_down, rows_grad = gather_all(
        [first_weight, output_weight], [down_weight], out_grad, row_count, col_count
    )

    tile = min(512, hidden)
    tiles = hidden // tile
    early = max(tiles // 2, 1)
    hidden_flat = hidden_weight.reshape(deep, 2 * hidden)

    inputs = tokens.astype(f32)
    normal_in, scale_in = normalize(inputs, gain_first)
    halves = jnp.concatenate([cosine, cosine], axis=1)
    signed = jnp.concatenate([-sinusoid, sinusoid], axis=1)
    tables = (
        jnp.concatenate([halves, halves], axis=1),
        jnp.concatenate([signed, signed], axis=1),
        jnp.concatenate([halves, jnp.ones_like(halves)], axis=1),
        jnp.concatenate([signed, jnp.zeros_like(signed)], axis=1),
    )
    bias = jnp.where(allowed, 0.0, blocked).astype(f32)
    queries, all_keyvals, mixed, lse, early_tiles, hidden_in, normal_mid = attend(
        normal_in,
        tokens,
        full_first,
        full_output,
        bias,
        tables,
        gain_second[None],
        hidden_flat,
        early,
        tile,
        heads,
        group,
        back,
        (row_count, col_count),
        4,
    )
    grad_mid, out_terms, grad_hidden_part, sum_down = mlp(
        normal_mid,
        rows_grad,
        early_tiles,
        hidden_flat,
        full_down,
        row_count,
        col_count,
        3,
    )
    out_sum = lax.psum_scatter(out_terms, "col", scatter_dimension=0, tiled=True)
    cores = plane_sizes(row_count)[2]
    tables_back = (tables[0], -tables[1], tables[2], -tables[3])
    grad_in, grad_hidden_in, grad_low, gain_mid_part, grad_first, sum_hidden, *siblings = (
        attend_back(
            (grad_mid, hidden_in, out_grad, gain_second[None]),
            normal_in,
            lse,
            bias.T,
            tables_back,
            mixed,
            queries,
            all_keyvals,
            full_output,
            full_first,
            grad_hidden_part,
            group,
            (row_count, col_count),
            5,
        )
    )
    normal_sib, grad_low_sib, mixed_sib, grad_first_sib = siblings
    lefts = [
        (normal_in, normal_sib)[:cores],
        (grad_low, grad_low_sib)[:cores],
    ]
    rights = [(grad_first, grad_first_sib)[:cores], (mixed, mixed_sib)[:cores]]
    extras = (
        grad_in,
        tokens,
        grad_hidden_in,
        gain_first[None],
        gain_mid_part,
    )
    sum_query, sum_keyvalue, sum_output, grad_tokens, gain_sums = sum_all(
        lefts, rights, query_width, extras, row_count, col_count
    )
    out_sum, gain_sums = lax.optimization_barrier((out_sum, gain_sums))
    block_out = (hidden_in + out_sum.astype(f32)).astype(bf16)
    return (
        block_out,
        grad_tokens,
        gain_sums[0],
        sum_query,
        sum_keyvalue.reshape(deep, pairs, 2 * HD),
        sum_output,
        gain_sums[1],
        sum_hidden,
        sum_down,
    )


def solution(mesh):
    return jax.shard_map(
        shards,
        mesh=mesh,
        in_specs=(
            P(("row", "col"), None),
            P("row", None),
            P(),
            P("row", "col"),
            P("row", "col", None),
            P("row", "col"),
            P(),
            P("row", None, "col"),
            P("row", "col"),
            P(("row", "col"), None),
        ),
        out_specs=(
            P(("row", "col"), None),
            P(("row", "col"), None),
            P(),
            P("row", "col"),
            P("row", "col", None),
            P("row", "col"),
            P(),
            P("row", None, "col"),
            P("row", "col"),
        ),
        check_vma=False,
    )
```
